32 devices in a mesh: band: 2 (over y), domain: 16 (over z, x, core).
Axes of the slice: x: 2, y: 2, z: 4, core: 2. Of those that a mesh axis runs over, the one named last changes fastest.
Arguments:
- orbital_block: bfloat16 [256, 192, 16, 128], P('band', 'domain'), may hold values from -8 to 8
- block_scale: float32 [256, 192], P('band', 'domain'), may hold values from 0.5 to 6
- potential: float32 [192, 16, 128], P('domain'), may hold values from -4 to 0
Outputs:
- orthonormal: bfloat16 [256, 192, 16, 128], P('band', 'domain')
The draws below stay inside these ranges and needn't reach their ends.
All inputs are finite; a program needn't handle non-finite values.
Results may differ from the reference program's by a relative error of at most 0.015.
Values may be sent and summed in bfloat16 or wider, within the bound.
No kernel may reach another device: no remote copies, remote signals or barrier semaphores. Data moves between devices by JAX's collectives and lax.ppermute only.
A program may use at most 128 MiB of HBM per device.

```python
import math
import jax
import jax.numpy as jnp
from jax import lax

NBANDS = 256
CX = 12
NY = 16
NZ = 128
NX = 192


def draw_orbital_block(key, part):
    fields = jnp.clip(jax.random.normal(key, (NBANDS + 1, NX, NY, NZ), jnp.float32), -4.0, 4.0)
    mixed = fields[:NBANDS] + 0.5 * fields[1:]
    return mixed.astype(jnp.bfloat16)


def draw_block_scale(key, part):
    slab_count = NX // CX
    heavy_slab = jax.random.randint(jax.random.fold_in(key, 11), (), 0, slab_count)
    plane_slab = lax.broadcasted_iota(jnp.int32, (NBANDS, NX), 1) // CX
    heavy = plane_slab == heavy_slab
    draw_key = jax.random.fold_in(key, 23)
    unit = jax.random.uniform(draw_key, (NBANDS, NX), jnp.float32, 0.0, 1.0)
    background = jnp.exp(math.log(0.5) + unit * math.log(1.4))
    loud = jnp.exp(math.log(4.0) + unit * math.log(1.5))
    return jnp.where(heavy, loud, background)


def level_of(own_key, shape, cuts, smallest, high):
    loudness, own = 1.0, jax.random.fold_in(own_key, 6)
    for position, shards_of in cuts:
        draws = jnp.exp(jax.random.uniform(jax.random.fold_in(own, position), (shards_of,), jnp.float32, smallest / len(cuts), high / len(cuts)))
        loudness = loudness * jnp.repeat(draws, shape[position] // shards_of).reshape([-1 if axis == position else 1 for axis in range(len(shape))])
    return loudness


def setup_inputs(seed: int = 0) -> dict:
    splits = jax.random.split(jax.random.key(seed), 4)
    orbital_block = draw_orbital_block(jax.random.fold_in(splits[3], 71), 0)
    block_scale = draw_block_scale(jax.random.fold_in(splits[3], 71), 0)
    potential = jnp.clip(-4.0 + 4.0 * jax.random.uniform(splits[2], (NX, NY, NZ), jnp.float32) ** level_of(splits[2], (NX, NY, NZ), ((0, 16),), -0.2, 0.2), -4.0, 0.0)
    return dict(orbital_block=orbital_block, block_scale=block_scale, potential=potential)


grid_step = 0.5
stencil_coef = (-5369.0 / 1800.0, 12.0 / 7.0, -15.0 / 56.0, 10.0 / 189.0, -1.0 / 112.0, 2.0 / 1925.0, -1.0 / 16632.0)
lower_end = -4.0
cut_energy = 6.0
upper_end = 43.0

def filter_terms():
    width_e = (upper_end - cut_energy) / 2.0
    centre = (upper_end + cut_energy) / 2.0
    sigma_one = width_e / (lower_end - centre)
    gamma_term = 2.0 / sigma_one
    sigma_two = 1.0 / (gamma_term - sigma_one)
    sigma_three = 1.0 / (gamma_term - sigma_two)
    return (width_e, centre, sigma_one, sigma_two, sigma_three)

def hamiltonian(padded, potential):
    count_x = padded.shape[1] - 12
    count_y = padded.shape[2] - 12
    count_z = padded.shape[3] - 12

    def window(shift_x, shift_y, shift_z):
        return padded[:, 6 + shift_x:6 + shift_x + count_x, 6 + shift_y:6 + shift_y + count_y, 6 + shift_z:6 + shift_z + count_z].astype(jnp.float32)
    kinetic = -0.5 / (grid_step * grid_step)
    result = (3.0 * stencil_coef[0] * kinetic + potential[None]) * window(0, 0, 0)
    for offset in range(1, 7):
        neighbours = window(offset, 0, 0) + window(-offset, 0, 0) + window(0, offset, 0) + window(0, -offset, 0) + window(0, 0, offset) + window(0, 0, -offset)
        result = result + kinetic * stencil_coef[offset] * neighbours
    return result

def filter_group(orbitals, scales, potential):
    scaled = (orbitals.astype(jnp.float32) * scales[:, :, None, None]).astype(jnp.bfloat16)
    width_e, centre, sigma_one, sigma_two, sigma_three = filter_terms()

    def shifted(source_field):
        padded = jnp.pad(source_field, ((0, 0), (6, 6), (6, 6), (6, 6)))
        return hamiltonian(padded, potential) - centre * source_field.astype(jnp.float32)
    first_iter = (shifted(scaled) * (sigma_one / width_e)).astype(jnp.bfloat16)
    second = (2.0 * sigma_two / width_e * shifted(first_iter) - sigma_one * sigma_two * scaled.astype(jnp.float32)).astype(jnp.bfloat16)
    third_iter = (2.0 * sigma_three / width_e * shifted(second) - sigma_two * sigma_three * first_iter.astype(jnp.float32)).astype(jnp.bfloat16)
    return third_iter

def reference(orbital_block, block_scale, potential):
    group_rows = min(32, NBANDS)
    blocks = orbital_block.reshape(NBANDS // group_rows, group_rows, NX, NY, NZ)
    scale_blocks = block_scale.reshape(NBANDS // group_rows, group_rows, NX)
    filtered = lax.map(lambda pieces: filter_group(pieces[0], pieces[1], potential), (blocks, scale_blocks))
    filtered = filtered.reshape(NBANDS, NX, NY * NZ)

    def add_plane(plane_index, gram_sum):
        plane_rows = lax.dynamic_index_in_dim(filtered, plane_index, 1, keepdims=False)
        return gram_sum + lax.dot_general(plane_rows.astype(jnp.float32), plane_rows.astype(jnp.float32), (((1,), (1,)), ((), ())), preferred_element_type=jnp.float32)
    gram_sum = lax.fori_loop(0, NX, add_plane, jnp.zeros((NBANDS, NBANDS), jnp.float32))
    correlation = gram_sum / float(NX * NY * NZ)
    lower_factor = jnp.linalg.cholesky(correlation)
    inverse = jax.scipy.linalg.solve_triangular(lower_factor, jnp.eye(NBANDS, dtype=jnp.float32), lower=True)
    rotation = inverse.astype(jnp.bfloat16)

    def rotate_plane(plane_index, rotated):
        plane_rows = lax.dynamic_index_in_dim(filtered, plane_index, 1, keepdims=False)
        mixed = jnp.dot(rotation.astype(jnp.float32), plane_rows.astype(jnp.float32), preferred_element_type=jnp.float32).astype(jnp.bfloat16)
        return lax.dynamic_update_index_in_dim(rotated, mixed, plane_index, 1)
    rotated = lax.fori_loop(0, NX, rotate_plane, jnp.zeros((NBANDS, NX, NY * NZ), jnp.bfloat16))
    return rotated.reshape(NBANDS, NX, NY, NZ)
```

```python
import functools

import jax
import jax.numpy as jnp
import numpy as np
from jax import lax
from jax.experimental import pallas as pl
from jax.experimental.pallas import tpu as pltpu
from jax.sharding import PartitionSpec as P

grid_step = 0.5
stencil_coef = (
    -5369.0 / 1800.0,
    12.0 / 7.0,
    -15.0 / 56.0,
    10.0 / 189.0,
    -1.0 / 112.0,
    2.0 / 1925.0,
    -1.0 / 16632.0,
)
lower_end = -4.0
cut_energy = 6.0
upper_end = 43.0
kinetic = -0.5 / (grid_step * grid_step)
coef_scale = 7.0
reach = 6
edge = 3 * reach
chunk = 16
F32, BF16 = jnp.float32, jnp.bfloat16
vmem_bytes = 50 * 2**20


def filter_terms():
    width_e = (upper_end - cut_energy) / 2.0
    centre = (upper_end + cut_energy) / 2.0
    sigma_one = width_e / (lower_end - centre)
    gamma_term = 2.0 / sigma_one
    sigma_two = 1.0 / (gamma_term - sigma_one)
    sigma_three = 1.0 / (gamma_term - sigma_two)
    return (width_e, centre, sigma_one, sigma_two, sigma_three)


def stencil_line(count):
    line = np.zeros((count, count), np.float64)
    for offset in range(1, reach + 1):
        value = kinetic * stencil_coef[offset] * coef_scale
        line += value * (np.eye(count, k=offset) + np.eye(count, k=-offset))
    return line


def xy_matrix(planes, rows_y):
    along_x = np.zeros((planes, planes + 2 * reach), np.float64)
    along_x[:, :] = stencil_line(planes + 2 * reach)[reach : reach + planes]
    middle = np.eye(planes, planes + 2 * reach, k=reach)
    full = np.kron(along_x, np.eye(rows_y)) + np.kron(middle, stencil_line(rows_y))
    return jnp.asarray(full, BF16)


def z_matrix(count_z):
    return jnp.asarray(np.kron(np.eye(2), stencil_line(count_z)), BF16)


def swap_matrix():
    full = np.zeros((256, 256), np.float32)
    for a in range(16):
        for b in range(16):
            full[a * 16 + b, b * 16 + a] = 1.0
    return jnp.asarray(full, BF16)


def params(flops=0, moved=0, grid_dims=1):
    return dict(
        compiler_params=pltpu.CompilerParams(
            vmem_limit_bytes=vmem_bytes, dimension_semantics=("arbitrary",) * grid_dims
        ),
        cost_estimate=pl.CostEstimate(flops=flops, bytes_accessed=moved, transcendentals=0),
    )


def prepare(info, orbitals, scale, potential, part, group, with_potential):
    bands, planes, rows_y, rows_z = orbitals.shape
    own = bands // group
    steps = chunk // 2
    total = chunk + (2 if with_potential else 0)

    def kernel(info_ref, *refs):
        sources, scale_ref, potential_ref = refs[:group], refs[group], refs[group + 1]
        outs = refs[group + 2 :]
        i = pl.program_id(0)

        @pl.when(i < steps)
        def _():
            for r in range(group):
                base = (info_ref[0] ^ r) * own + part * chunk + 2 * i
                for b in range(2):
                    for p in range(planes):
                        value = sources[r][b, p].astype(F32) * scale_ref[base + b, p]
                        outs[r][b, p] = value.astype(BF16)

        if with_potential:

            @pl.when(i == steps)
            def _():
                high = potential_ref[...].astype(BF16)
                low = (potential_ref[...] - high.astype(F32)).astype(BF16)
                for r in range(group):
                    outs[r][0] = high
                    outs[r][1] = low

    def source_spec(r):
        def index(i, info_ref):
            first = ((info_ref[0] ^ r) * own + part * chunk) // 2
            return (first + jnp.minimum(i, steps - 1), 0, 0, 0)

        return pl.BlockSpec((2, planes, rows_y, rows_z), index)

    shape = jax.ShapeDtypeStruct((total, planes, rows_y, rows_z), BF16)
    return pl.pallas_call(
        kernel,
        grid_spec=pltpu.PrefetchScalarGridSpec(
            num_scalar_prefetch=1,
            grid=(total // 2,),
            in_specs=[source_spec(r) for r in range(group)]
            + [
                pl.BlockSpec(memory_space=pltpu.SMEM),
                pl.BlockSpec((planes, rows_y, rows_z), lambda i, info_ref: (0, 0, 0)),
            ],
            out_specs=[
                pl.BlockSpec((2, planes, rows_y, rows_z), lambda i, info_ref: (i, 0, 0, 0))
            ]
            * group,
        ),
        out_shape=[shape] * group,
        name="prepare",
        **params(moved=2 * group * total * planes * rows_y * rows_z * 2),
    )(info, *([orbitals] * group), scale, potential)


def edges(info, pieces):
    group = len(pieces)
    total, planes, rows_y, rows_z = pieces[0].shape
    rest = edge - planes

    def kernel(info_ref, *refs):
        sources, (up, down) = refs[:group], refs[group:]
        for r in range(group):
            slab = info_ref[0] ^ r

            @pl.when(slab == group - 1)
            def _():
                up[:, rest:] = sources[r][...]

            @pl.when(slab == group - 2)
            def _():
                up[:, :rest] = sources[r][:, planes - rest :]

            @pl.when(slab == 0)
            def _():
                down[:, :planes] = sources[r][...]

            @pl.when(slab == 1)
            def _():
                down[:, planes:] = sources[r][:, :rest]

    shape = jax.ShapeDtypeStruct((total, edge, rows_y, rows_z), BF16)
    block = lambda count: pl.BlockSpec(
        (2, count, rows_y, rows_z), lambda i, info_ref: (i, 0, 0, 0)
    )
    return pl.pallas_call(
        kernel,
        grid_spec=pltpu.PrefetchScalarGridSpec(
            num_scalar_prefetch=1,
            grid=(total // 2,),
            in_specs=[block(planes)] * group,
            out_specs=[block(edge)] * 2,
        ),
        out_shape=[shape] * 2,
        name="edges",
        **params(moved=(group * planes + 2 * edge) * total * rows_y * rows_z * 2),
    )(info, *pieces)


def chebyshev(info, left, right, pieces, left_pot, right_pot, pieces_pot):
    group = len(pieces)
    _, planes, rows_y, rows_z = pieces[0].shape
    slab = group * planes
    steps = chunk // 2
    width_e, centre, sigma_one, sigma_two, sigma_three = filter_terms()
    diagonal = 3.0 * stencil_coef[0] * kinetic - centre
    tile_rows = planes * rows_y
    xy, zz, swap = xy_matrix(planes, rows_y), z_matrix(rows_z), swap_matrix()
    count_0, count_1, count_2 = slab + 6 * reach, slab + 4 * reach, slab + 2 * reach

    def kernel(info_ref, *refs):
        left_ref, right_ref = refs[:2]
        piece_refs = refs[2 : 2 + group]
        left_pot_ref, right_pot_ref = refs[2 + group : 4 + group]
        pot_refs = refs[4 + group : 4 + 2 * group]
        xy_ref, zz_ref, swap_ref = refs[4 + 2 * group : 7 + 2 * group]
        outs = refs[7 + 2 * group : 7 + 3 * group]
        field, first, second, energy, result = refs[7 + 3 * group :]
        i = pl.program_id(0)
        me = info_ref[0]
        at_left, at_right = info_ref[1] == 1, info_ref[2] == 1

        @pl.when(i == 0)
        def _():
            def store(start, count, source, begin):
                total = source[0, begin : begin + count].astype(F32) + source[
                    1, begin : begin + count
                ].astype(F32)
                energy[pl.ds(start, count)] = coef_scale * (total + diagonal)

            store(0, 2 * reach, left_pot_ref, reach)
            store(slab + 2 * reach, 2 * reach, right_pot_ref, 0)
            for r in range(group):
                store(2 * reach + planes * (me ^ r), planes, pot_refs[r], 0)

        for b in range(2):
            lanes = slice(b * rows_z, (b + 1) * rows_z)
            field[0:edge, :, lanes] = left_ref[b]
            field[edge + slab : edge + slab + edge, :, lanes] = right_ref[b]
            for r in range(group):
                field[pl.ds(edge + planes * (me ^ r), planes), :, lanes] = piece_refs[r][b]

        def apply(source, start, energy_start):
            rows = source[pl.ds(start, planes + 2 * reach)].reshape(-1, 2 * rows_z)
            middle = source[pl.ds(start + reach, planes)].reshape(tile_rows, 2 * rows_z)
            total = jnp.dot(xy_ref[...], rows, preferred_element_type=F32)
            total += jnp.dot(middle, zz_ref[...], preferred_element_type=F32)
            factor = energy[pl.ds(energy_start, planes)].reshape(tile_rows, rows_z)
            factor = jnp.concatenate([factor, factor], axis=1)
            return total + factor * middle.astype(F32)

        def block(value):
            return value.astype(BF16).reshape(planes, rows_y, 2 * rows_z)

        def previous(source, start):
            return source[pl.ds(start, planes)].reshape(tile_rows, 2 * rows_z).astype(F32)

        for t in range(count_1 // planes):
            at = t * planes
            value = apply(field, at, at) * (sigma_one / width_e / coef_scale)
            first[at : at + planes] = block(value)

        @pl.when(at_left)
        def _():
            first[: 2 * reach] = jnp.zeros((2 * reach, rows_y, 2 * rows_z), BF16)

        @pl.when(at_right)
        def _():
            first[count_1 - 2 * reach :] = jnp.zeros((2 * reach, rows_y, 2 * rows_z), BF16)

        for t in range(count_2 // planes):
            at = t * planes
            value = apply(first, at, at + reach) * (2.0 * sigma_two / width_e / coef_scale)
            value -= sigma_one * sigma_two * previous(field, at + 2 * reach)
            second[at : at + planes] = block(value)

        @pl.when(at_left)
        def _():
            second[:reach] = jnp.zeros((reach, rows_y, 2 * rows_z), BF16)

        @pl.when(at_right)
        def _():
            second[count_2 - reach :] = jnp.zeros((reach, rows_y, 2 * rows_z), BF16)

        for t in range(group):
            at = t * planes
            value = apply(second, at, at + 2 * reach) * (2.0 * sigma_three / width_e / coef_scale)
            value -= sigma_two * sigma_three * previous(first, at + 2 * reach)
            value = block(value)
            for b in range(2):
                result[at : at + planes, 2 * i + b] = value[:, :, b * rows_z : (b + 1) * rows_z]

        @pl.when(i == steps - 1)
        def _():
            for r in range(group):
                start = planes * (me ^ r)
                for p in range(0, planes, 2):
                    pair = [
                        result[start + p + k].reshape(chunk * rows_y, rows_z) for k in range(2)
                    ]
                    moved = jnp.dot(
                        swap_ref[...], jnp.concatenate(pair, axis=1), preferred_element_type=F32
                    ).astype(BF16)
                    for k in range(2):
                        part = moved[:, k * rows_z : (k + 1) * rows_z]
                        outs[r][:, p + k] = part.reshape(rows_y, chunk, rows_z)

    def block_spec(count, index):
        return pl.BlockSpec((2, count, rows_y, rows_z), index)

    def whole_spec(shape):
        return pl.BlockSpec(shape, lambda i, info_ref: (0,) * len(shape))

    moving = lambda i, info_ref: (i, 0, 0, 0)
    fixed = lambda i, info_ref: (steps, 0, 0, 0)
    shape = jax.ShapeDtypeStruct((rows_y, planes, chunk, rows_z), BF16)
    cells = chunk * rows_y * rows_z
    return pl.pallas_call(
        kernel,
        grid_spec=pltpu.PrefetchScalarGridSpec(
            num_scalar_prefetch=1,
            grid=(steps,),
            in_specs=[block_spec(edge, moving)] * 2
            + [block_spec(planes, moving)] * group
            + [block_spec(edge, fixed)] * 2
            + [block_spec(planes, fixed)] * group
            + [whole_spec(xy.shape), whole_spec(zz.shape), whole_spec(swap.shape)],
            out_specs=[whole_spec(shape.shape)] * group,
            scratch_shapes=[
                pltpu.VMEM((count_0, rows_y, 2 * rows_z), BF16),
                pltpu.VMEM((count_1, rows_y, 2 * rows_z), BF16),
                pltpu.VMEM((count_2, rows_y, 2 * rows_z), BF16),
                pltpu.VMEM((count_1, rows_y, rows_z), F32),
                pltpu.VMEM((slab, chunk, rows_y, rows_z), BF16),
            ],
        ),
        out_shape=[shape] * group,
        name="chebyshev",
        **params(
            flops=2 * cells * (3 * group + 3) * planes * (xy.shape[1] + zz.shape[0]),
            moved=2 * cells * (2 * slab + 2 * edge),
        ),
    )(info, left, right, *pieces, left_pot, right_pot, *pieces_pot, xy, zz, swap)


def fill_own(info_ref, rows, refs, bands, group):
    own = bands // group
    for c, pieces in enumerate(refs):
        for r, piece in enumerate(pieces):
            start = info_ref[3] * bands + (info_ref[0] ^ r) * own + c * chunk
            rows[:, pl.ds(pl.multiple_of(start, chunk), chunk), :] = piece[:, 0]


def fill_other(info_ref, rows, piece, c, shift, part, count, bands, group):
    own = bands // group
    parts = info_ref[4]
    source = lax.rem(info_ref[3] + parts - shift, parts)
    per = piece.shape[1]
    first = 0 if part is None else lax.rem(info_ref[3] + part, parts) * per
    for r in range(group):
        start = source * bands + (info_ref[0] ^ r) * own + c * chunk
        where = pl.ds(pl.multiple_of(start, chunk), chunk)
        rows[pl.ds(first, per), where, :] = piece[r, :, 0]


def gram(info, own, others, bands, bands_all):
    chunks, group = len(own), len(own[0])
    rows_y, planes, _, rows_z = own[0][0].shape
    per = others[0][0].shape[1]
    flat_own = [piece for pieces in own for piece in pieces]
    flat_others = [piece for pieces in others for piece in pieces]

    def kernel(info_ref, *refs):
        own_refs = refs[: len(flat_own)]
        other_refs = refs[len(flat_own) : len(flat_own) + len(flat_others)]
        out, rows = refs[len(flat_own) + len(flat_others) :]
        nested = [own_refs[c * group : (c + 1) * group] for c in range(chunks)]
        fill_own(info_ref, rows, nested, bands, group)
        for k, piece in enumerate(other_refs):
            fill_other(
                info_ref, rows, piece, k % chunks, k // chunks + 1, None, per, bands, group
            )
        block = jnp.concatenate([rows[y] for y in range(per)], axis=1)
        total = lax.dot_general(
            block, block, (((1,), (1,)), ((), ())), preferred_element_type=F32
        )

        @pl.when(pl.program_id(0) == 0)
        def _():
            out[...] = total

        @pl.when(pl.program_id(0) > 0)
        def _():
            out[...] += total

    own_spec = pl.BlockSpec(
        (per, 1, chunk, rows_z), lambda i, info_ref: (info_ref[3], i, 0, 0)
    )
    other_spec = pl.BlockSpec(
        (group, per, 1, chunk, rows_z), lambda i, info_ref: (0, 0, i, 0, 0)
    )
    return pl.pallas_call(
        kernel,
        grid_spec=pltpu.PrefetchScalarGridSpec(
            num_scalar_prefetch=1,
            grid=(planes,),
            in_specs=[own_spec] * len(flat_own) + [other_spec] * len(flat_others),
            out_specs=pl.BlockSpec((bands_all, bands_all), lambda i, info_ref: (0, 0)),
            scratch_shapes=[pltpu.VMEM((per, bands_all, rows_z), BF16)],
        ),
        out_shape=jax.ShapeDtypeStruct((bands_all, bands_all), F32),
        name="gram",
        **params(
            flops=2 * bands_all**2 * per * planes * rows_z,
            moved=2 * bands_all * per * planes * rows_z,
        ),
    )(info, *flat_own, *flat_others)


def rotate(info, rotation, own, others, later, bands, bands_all):
    chunks, group = len(own), len(own[0])
    rows_y, planes, _, rows_z = own[0][0].shape
    per = others[0][0].shape[1]
    swap = swap_matrix()
    flat_own = [piece for pieces in own for piece in pieces]
    keys = [(s + 1, 0, c) for s in range(len(others)) for c in range(chunks)]
    flat_others = [piece for pieces in others for piece in pieces]
    for (s, t), pieces in later.items():
        keys += [(s, t, c) for c in range(chunks)]
        flat_others += pieces

    def kernel(info_ref, *refs):
        own_refs = refs[: len(flat_own)]
        other_refs = refs[len(flat_own) : len(flat_own) + len(flat_others)]
        rotation_ref, swap_ref, out, rows, mixed = refs[len(flat_own) + len(flat_others) :]
        nested = [own_refs[c * group : (c + 1) * group] for c in range(chunks)]
        fill_own(info_ref, rows, nested, bands, group)
        for (s, t, c), piece in zip(keys, other_refs):
            fill_other(info_ref, rows, piece, c, s, t, per, bands, group)
        for y in range(0, rows_y, 2):
            pair = jnp.concatenate([rows[y], rows[y + 1]], axis=1)
            value = jnp.dot(rotation_ref[...], pair, preferred_element_type=F32).astype(BF16)
            for k in range(bands // 16):
                for b in range(2):
                    mixed[k, y + b] = value[
                        16 * k : 16 * k + 16, b * rows_z : (b + 1) * rows_z
                    ]
        for k in range(0, bands // 16, 2):
            pair = [mixed[k + b].reshape(16 * rows_y, rows_z) for b in range(2)]
            moved = jnp.dot(
                swap_ref[...], jnp.concatenate(pair, axis=1), preferred_element_type=F32
            ).astype(BF16)
            for b in range(2):
                part = moved[:, b * rows_z : (b + 1) * rows_z].reshape(16, rows_y, rows_z)
                out[16 * (k + b) : 16 * (k + b) + 16, 0] = part

    own_spec = pl.BlockSpec((rows_y, 1, chunk, rows_z), lambda i, info_ref: (0, i, 0, 0))
    other_spec = pl.BlockSpec(
        (group, per, 1, chunk, rows_z), lambda i, info_ref: (0, 0, i, 0, 0)
    )
    return pl.pallas_call(
        kernel,
        grid_spec=pltpu.PrefetchScalarGridSpec(
            num_scalar_prefetch=1,
            grid=(planes,),
            in_specs=[own_spec] * len(flat_own)
            + [other_spec] * len(flat_others)
            + [
                pl.BlockSpec((bands, bands_all), lambda i, info_ref: (info_ref[3], 0)),
                pl.BlockSpec(swap.shape, lambda i, info_ref: (0, 0)),
            ],
            out_specs=pl.BlockSpec((bands, 1, rows_y, rows_z), lambda i, info_ref: (0, i, 0, 0)),
            scratch_shapes=[
                pltpu.VMEM((rows_y, bands_all, rows_z), BF16),
                pltpu.VMEM((bands // 16, rows_y, 16, rows_z), BF16),
            ],
        ),
        out_shape=jax.ShapeDtypeStruct((bands, planes, rows_y, rows_z), BF16),
        name="rotate",
        **params(
            flops=4 * bands * bands_all * rows_y * planes * rows_z,
            moved=2 * (bands + bands_all) * rows_y * planes * rows_z,
        ),
    )(info, *flat_own, *flat_others, rotation, swap)


def pairwise_sum(value, axis, count, bits):
    for bit in bits:
        value = value + lax.ppermute(value, axis, [(i, i ^ bit) for i in range(count)])
    return value


def body(orbital_block, block_scale, potential):
    bands, planes, rows_y, rows_z = orbital_block.shape
    parts, slabs = lax.axis_size("band"), lax.axis_size("domain")
    bands_all = bands * parts
    group = 4 if bands // 4 >= chunk else 2
    chunks = bands // group // chunk
    per = rows_y // parts
    where, band = lax.axis_index("domain"), lax.axis_index("band")
    info = jnp.stack(
        [
            lax.rem(where, group),
            (where < group).astype(jnp.int32),
            (where >= slabs - group).astype(jnp.int32),
            band,
            jnp.int32(parts),
        ]
    ).astype(jnp.int32)

    def swapped(pieces):
        return [pieces[0]] + [
            lax.ppermute(pieces[r], "domain", [(i, i ^ r) for i in range(slabs)])
            for r in range(1, group)
        ]

    arrived = [
        swapped(prepare(info, orbital_block, block_scale, potential, c, group, c == 0))
        for c in range(chunks)
    ]
    own = []
    sides_pot = None
    for c in range(chunks):
        up, down = edges(info, arrived[c])
        left = lax.ppermute(up, "domain", [(i, i + group) for i in range(slabs - group)])
        right = lax.ppermute(down, "domain", [(i + group, i) for i in range(slabs - group)])
        if c == 0:
            sides_pot = (left, right)
        filtered = chebyshev(info, left, right, arrived[c], *sides_pot, arrived[0])
        own.append(swapped(filtered))

    def part_of(pieces, which):
        start = lax.rem(which, parts) * per
        return jnp.stack([lax.dynamic_slice_in_dim(piece, start, per, 0) for piece in pieces])

    others = []
    for s in range(1, parts):
        pairs = [(q, (q + s) % parts) for q in range(parts)]
        others.append([lax.ppermute(part_of(pieces, band + s), "band", pairs) for pieces in own])
    total = gram(info, own, others, bands, bands_all)
    later = {}
    for s in range(1, parts):
        pairs = [(q, q + s) for q in range(parts - s)]
        for t in range(1, parts):
            later[(s, t)] = [
                lax.ppermute(part_of(pieces, band + s + t), "band", pairs) for pieces in own
            ]
    bits = lambda count: [1 << k for k in range(count.bit_length() - 1)]
    total = pairwise_sum(total, "band", parts, bits(parts))
    total = pairwise_sum(total, "domain", slabs, bits(slabs))
    correlation = total / float(planes * rows_y * rows_z * slabs)
    lower_factor = jnp.linalg.cholesky(correlation)
    inverse = jax.scipy.linalg.solve_triangular(
        lower_factor, jnp.eye(bands_all, dtype=F32), lower=True
    )
    rotation = jnp.tril(inverse).astype(BF16)
    return rotate(info, rotation, own, others, later, bands, bands_all)


def solution(mesh):
    in_specs = (P("band", "domain", None, None), P("band", "domain"), P("domain", None, None))
    out_specs = P("band", "domain", None, None)
    return jax.shard_map(body, mesh=mesh, in_specs=in_specs, out_specs=out_specs, check_vma=False)
```

```python
import jax
import jax.numpy as jnp
import numpy as np
from jax import lax
from jax.experimental import pallas as pl
from jax.experimental.pallas import tpu as pltpu
from jax.sharding import PartitionSpec as P

grid_step = 0.5
stencil_coef = (
    -5369.0 / 1800.0,
    12.0 / 7.0,
    -15.0 / 56.0,
    10.0 / 189.0,
    -1.0 / 112.0,
    2.0 / 1925.0,
    -1.0 / 16632.0,
)
lower_end = -4.0
cut_energy = 6.0
upper_end = 43.0
kinetic = -0.5 / (grid_step * grid_step)
coef_scale = 7.0
reach = 6
edge = 3 * reach
chunk = 16
F32, BF16 = jnp.float32, jnp.bfloat16
vmem_bytes = 50 * 2**20


def filter_terms():
    width_e = (upper_end - cut_energy) / 2.0
    centre = (upper_end + cut_energy) / 2.0
    sigma_one = width_e / (lower_end - centre)
    gamma_term = 2.0 / sigma_one
    sigma_two = 1.0 / (gamma_term - sigma_one)
    sigma_three = 1.0 / (gamma_term - sigma_two)
    return (width_e, centre, sigma_one, sigma_two, sigma_three)


def stencil_line(count):
    line = np.zeros((count, count), np.float64)
    for offset in range(1, reach + 1):
        value = kinetic * stencil_coef[offset] * coef_scale
        line += value * (np.eye(count, k=offset) + np.eye(count, k=-offset))
    return line


def xy_matrix(planes, rows_y):
    along_x = np.zeros((planes, planes + 2 * reach), np.float64)
    along_x[:, :] = stencil_line(planes + 2 * reach)[reach : reach + planes]
    middle = np.eye(planes, planes + 2 * reach, k=reach)
    full = np.kron(along_x, np.eye(rows_y)) + np.kron(middle, stencil_line(rows_y))
    return jnp.asarray(full, BF16)


def z_matrix(count_z):
    return jnp.asarray(np.kron(np.eye(2), stencil_line(count_z)), BF16)


def swap_matrix():
    full = np.zeros((256, 256), np.float32)
    for a in range(16):
        for b in range(16):
            full[a * 16 + b, b * 16 + a] = 1.0
    return jnp.asarray(full, BF16)


def params():
    return dict(
        compiler_params=pltpu.CompilerParams(
            vmem_limit_bytes=vmem_bytes, dimension_semantics=("arbitrary",)
        ),
        cost_estimate=pl.CostEstimate(flops=1, bytes_accessed=1, transcendentals=0),
    )


def prepare(info, orbitals, scale, potential, part, group, with_potential):
    bands, planes, rows_y, rows_z = orbitals.shape
    own = bands // group
    steps = chunk // 2
    total = chunk + (2 if with_potential else 0)

    def kernel(info_ref, *refs):
        sources, scales, potential_ref = refs[:group], refs[group : 2 * group], refs[2 * group]
        outs = refs[2 * group + 1 :]
        i = pl.program_id(0)

        @pl.when(i < steps)
        def _():
            for r in range(group):
                for b in range(2):
                    value = sources[r][b].astype(F32) * scales[r][b][:, None, :]
                    outs[r][b] = value.astype(BF16)

        if with_potential:

            @pl.when(i == steps)
            def _():
                high = potential_ref[...].astype(BF16)
                low = (potential_ref[...] - high.astype(F32)).astype(BF16)
                for r in range(group):
                    outs[r][0] = high
                    outs[r][1] = low

    def first(r, i, info_ref):
        start = ((info_ref[0] ^ r) * own + part * chunk) // 2
        return start + jnp.minimum(i, steps - 1)

    def source_spec(r):
        return pl.BlockSpec(
            (2, planes, rows_y, rows_z), lambda i, info_ref: (first(r, i, info_ref), 0, 0, 0)
        )

    def scale_spec(r):
        return pl.BlockSpec(
            (2, planes, rows_z), lambda i, info_ref: (first(r, i, info_ref), 0, 0)
        )

    shape = jax.ShapeDtypeStruct((total, planes, rows_y, rows_z), BF16)
    return pl.pallas_call(
        kernel,
        grid_spec=pltpu.PrefetchScalarGridSpec(
            num_scalar_prefetch=1,
            grid=(total // 2,),
            in_specs=[source_spec(r) for r in range(group)]
            + [scale_spec(r) for r in range(group)]
            + [pl.BlockSpec((planes, rows_y, rows_z), lambda i, info_ref: (0, 0, 0))],
            out_specs=[
                pl.BlockSpec((2, planes, rows_y, rows_z), lambda i, info_ref: (i, 0, 0, 0))
            ]
            * group,
        ),
        out_shape=[shape] * group,
        name="prepare",
        **params(),
    )(info, *([orbitals] * group), *([scale] * group), potential)


def edges(info, pieces):
    group = len(pieces)
    total, planes, rows_y, rows_z = pieces[0].shape
    rest = edge - planes
    at_once = 6 if total % 6 == 0 else 4

    def kernel(info_ref, *refs):
        sources, (up, down) = refs[:group], refs[group:]
        for r in range(group):
            slab = info_ref[0] ^ r

            @pl.when(slab == group - 1)
            def _():
                up[:, rest:] = sources[r][...]

            @pl.when(slab == group - 2)
            def _():
                up[:, :rest] = sources[r][:, planes - rest :]

            @pl.when(slab == 0)
            def _():
                down[:, :planes] = sources[r][...]

            @pl.when(slab == 1)
            def _():
                down[:, planes:] = sources[r][:, :rest]

    shape = jax.ShapeDtypeStruct((total, edge, rows_y, rows_z), BF16)
    block = lambda count: pl.BlockSpec(
        (at_once, count, rows_y, rows_z), lambda i, info_ref: (i, 0, 0, 0)
    )
    return pl.pallas_call(
        kernel,
        grid_spec=pltpu.PrefetchScalarGridSpec(
            num_scalar_prefetch=1,
            grid=(total // at_once,),
            in_specs=[block(planes)] * group,
            out_specs=[block(edge)] * 2,
        ),
        out_shape=[shape] * 2,
        name="edges",
        **params(),
    )(info, *pieces)


def chebyshev(info, left, right, pieces, left_pot, right_pot, pieces_pot, parts):
    group = len(pieces)
    _, planes, rows_y, rows_z = pieces[0].shape
    slab = group * planes
    per = rows_y // parts
    steps = chunk // 2
    width_e, centre, sigma_one, sigma_two, sigma_three = filter_terms()
    diagonal = 3.0 * stencil_coef[0] * kinetic - centre
    tile_rows = planes * rows_y
    xy, zz, swap = xy_matrix(planes, rows_y), z_matrix(rows_z), swap_matrix()
    count_0, count_1, count_2 = slab + 6 * reach, slab + 4 * reach, slab + 2 * reach

    def kernel(info_ref, *refs):
        left_ref, right_ref = refs[:2]
        piece_refs = refs[2 : 2 + group]
        left_pot_ref, right_pot_ref = refs[2 + group : 4 + group]
        pot_refs = refs[4 + group : 4 + 2 * group]
        xy_ref, zz_ref, swap_ref = refs[4 + 2 * group : 7 + 2 * group]
        outs = refs[7 + 2 * group : 7 + (2 + parts) * group]
        field, first, second, energy, result = refs[7 + (2 + parts) * group :]
        i = pl.program_id(0)
        me = info_ref[0]
        at_left, at_right = info_ref[1] == 1, info_ref[2] == 1

        @pl.when(i == 0)
        def _():
            def store(start, count, source, begin):
                total = source[0, begin : begin + count].astype(F32) + source[
                    1, begin : begin + count
                ].astype(F32)
                energy[pl.ds(start, count)] = coef_scale * (total + diagonal)

            store(0, 2 * reach, left_pot_ref, reach)
            store(slab + 2 * reach, 2 * reach, right_pot_ref, 0)
            for r in range(group):
                store(2 * reach + planes * (me ^ r), planes, pot_refs[r], 0)

        for b in range(2):
            lanes = slice(b * rows_z, (b + 1) * rows_z)
            field[0:edge, :, lanes] = left_ref[b]
            field[edge + slab : edge + slab + edge, :, lanes] = right_ref[b]
            for r in range(group):
                field[pl.ds(edge + planes * (me ^ r), planes), :, lanes] = piece_refs[r][b]

        def apply(source, start, energy_start):
            rows = source[pl.ds(start, planes + 2 * reach)].reshape(-1, 2 * rows_z)
            middle = source[pl.ds(start + reach, planes)].reshape(tile_rows, 2 * rows_z)
            total = jnp.dot(xy_ref[...], rows, preferred_element_type=F32)
            total += jnp.dot(middle, zz_ref[...], preferred_element_type=F32)
            factor = energy[pl.ds(energy_start, planes)].reshape(tile_rows, rows_z)
            factor = jnp.concatenate([factor, factor], axis=1)
            return total + factor * middle.astype(F32)

        def block(value):
            return value.astype(BF16).reshape(planes, rows_y, 2 * rows_z)

        def previous(source, start):
            return source[pl.ds(start, planes)].reshape(tile_rows, 2 * rows_z).astype(F32)

        for t in range(count_1 // planes):
            at = t * planes
            value = apply(field, at, at) * (sigma_one / width_e / coef_scale)
            first[at : at + planes] = block(value)

        @pl.when(at_left)
        def _():
            first[: 2 * reach] = jnp.zeros((2 * reach, rows_y, 2 * rows_z), BF16)

        @pl.when(at_right)
        def _():
            first[count_1 - 2 * reach :] = jnp.zeros((2 * reach, rows_y, 2 * rows_z), BF16)

        for t in range(count_2 // planes):
            at = t * planes
            value = apply(first, at, at + reach) * (2.0 * sigma_two / width_e / coef_scale)
            value -= sigma_one * sigma_two * previous(field, at + 2 * reach)
            second[at : at + planes] = block(value)

        @pl.when(at_left)
        def _():
            second[:reach] = jnp.zeros((reach, rows_y, 2 * rows_z), BF16)

        @pl.when(at_right)
        def _():
            second[count_2 - reach :] = jnp.zeros((reach, rows_y, 2 * rows_z), BF16)

        for t in range(group):
            at = t * planes
            value = apply(second, at, at + 2 * reach) * (2.0 * sigma_three / width_e / coef_scale)
            value -= sigma_two * sigma_three * previous(first, at + 2 * reach)
            value = block(value)
            for b in range(2):
                result[at : at + planes, 2 * i + b] = value[:, :, b * rows_z : (b + 1) * rows_z]

        @pl.when(i == steps - 1)
        def _():
            for r in range(group):
                start = planes * (me ^ r)
                for p in range(0, planes, 2):
                    pair = [
                        result[start + p + k].reshape(chunk * rows_y, rows_z) for k in range(2)
                    ]
                    pair = jnp.concatenate(pair, axis=1)
                    for t in range(parts):
                        begin = lax.rem(info_ref[3] + t, parts) * (per * chunk)
                        begin = pl.multiple_of(begin, per * chunk)
                        moved = jnp.dot(
                            swap_ref[pl.ds(begin, per * chunk), :],
                            pair,
                            preferred_element_type=F32,
                        ).astype(BF16)
                        for k in range(2):
                            value = moved[:, k * rows_z : (k + 1) * rows_z]
                            outs[r * parts + t][:, p + k] = value.reshape(per, chunk, rows_z)

    def block_spec(count, index):
        return pl.BlockSpec((2, count, rows_y, rows_z), index)

    def whole_spec(shape):
        return pl.BlockSpec(shape, lambda i, info_ref: (0,) * len(shape))

    moving = lambda i, info_ref: (i, 0, 0, 0)
    fixed = lambda i, info_ref: (steps, 0, 0, 0)
    shape = jax.ShapeDtypeStruct((per, planes, chunk, rows_z), BF16)
    flat = pl.pallas_call(
        kernel,
        grid_spec=pltpu.PrefetchScalarGridSpec(
            num_scalar_prefetch=1,
            grid=(steps,),
            in_specs=[block_spec(edge, moving)] * 2
            + [block_spec(planes, moving)] * group
            + [block_spec(edge, fixed)] * 2
            + [block_spec(planes, fixed)] * group
            + [whole_spec(xy.shape), whole_spec(zz.shape), whole_spec(swap.shape)],
            out_specs=[whole_spec(shape.shape)] * (group * parts),
            scratch_shapes=[
                pltpu.VMEM((count_0, rows_y, 2 * rows_z), BF16),
                pltpu.VMEM((count_1, rows_y, 2 * rows_z), BF16),
                pltpu.VMEM((count_2, rows_y, 2 * rows_z), BF16),
                pltpu.VMEM((count_1, rows_y, rows_z), F32),
                pltpu.VMEM((slab, chunk, rows_y, rows_z), BF16),
            ],
        ),
        out_shape=[shape] * (group * parts),
        name="chebyshev",
        **params(),
    )(info, left, right, *pieces, left_pot, right_pot, *pieces_pot, xy, zz, swap)
    return [flat[r * parts : (r + 1) * parts] for r in range(group)]


def fill(info_ref, rows, piece, source, part, r, c, bands, group):
    own = bands // group
    start = source * bands + (info_ref[0] ^ r) * own + c * chunk
    where = pl.ds(pl.multiple_of(start, chunk), chunk)
    per, planes = piece.shape[0], piece.shape[1]
    for p in range(planes):
        rows[p, pl.ds(part * per, per), where, :] = piece[:, p]


def gram(info, pieces, bands, bands_all):
    group = 1 + max(r for r, t, c in pieces)
    per, planes, _, rows_z = next(iter(pieces.values())).shape
    at_once = 3 if planes % 3 == 0 else 1

    def kernel(info_ref, *refs):
        out, rows = refs[len(pieces) :]
        parts = info_ref[4]
        for (r, t, c), piece in zip(pieces, refs):
            source = lax.rem(info_ref[3] + parts - t, parts)
            fill(info_ref, rows, piece, source, 0, r, c, bands, group)
        block = jnp.concatenate([rows[p, y] for p in range(at_once) for y in range(per)], axis=1)
        total = lax.dot_general(
            block, block, (((1,), (1,)), ((), ())), preferred_element_type=F32
        )

        @pl.when(pl.program_id(0) == 0)
        def _():
            out[...] = total

        @pl.when(pl.program_id(0) > 0)
        def _():
            out[...] += total

    spec = pl.BlockSpec((per, at_once, chunk, rows_z), lambda i, info_ref: (0, i, 0, 0))
    return pl.pallas_call(
        kernel,
        grid_spec=pltpu.PrefetchScalarGridSpec(
            num_scalar_prefetch=1,
            grid=(planes // at_once,),
            in_specs=[spec] * len(pieces),
            out_specs=pl.BlockSpec((bands_all, bands_all), lambda i, info_ref: (0, 0)),
            scratch_shapes=[pltpu.VMEM((at_once, per, bands_all, rows_z), BF16)],
        ),
        out_shape=jax.ShapeDtypeStruct((bands_all, bands_all), F32),
        name="gram",
        **params(),
    )(info, *pieces.values())


def inverse_factor(correlation):
    count = correlation.shape[0]
    half = count // 2

    def exact(a, b, transposed):
        dims = (((1,), (1 if transposed else 0,)), ((), ()))
        return lax.dot_general(
            a, b, dims, precision=lax.Precision.HIGHEST, preferred_element_type=F32
        )

    def eliminate(block):
        groups = half // 8
        row = lax.broadcasted_iota(jnp.int32, (8, half), 0)
        column = lax.broadcasted_iota(jnp.int32, (8, half), 1)
        left = [block[8 * g : 8 * g + 8] for g in range(groups)]
        right = [jnp.where(column == row + 8 * g, 1.0, 0.0).astype(F32) for g in range(groups)]
        for c in range(half):
            at, k = c // 8, c % 8
            spread = [
                jnp.broadcast_to(left[g][:, c : c + 1], (8, half)) for g in range(at, groups)
            ]
            pivot = jnp.broadcast_to(spread[0][k : k + 1], (8, half))
            scale = lax.rsqrt(pivot)
            scale = scale * (1.5 - 0.5 * pivot * scale * scale)
            row_left = jnp.broadcast_to(left[at][k : k + 1], (8, half)) * scale
            row_right = jnp.broadcast_to(right[at][k : k + 1], (8, half)) * scale
            for g in range(at, groups):
                factor = spread[g - at] * scale
                if g == at:
                    factor = jnp.where(row > k, factor, 0.0)
                left[g] = left[g] - factor * row_left
                right[g] = right[g] - factor * row_right
            left[at] = jnp.where(row == k, row_left, left[at])
            right[at] = jnp.where(row == k, row_right, right[at])
        return jnp.concatenate(right, axis=0)

    def kernel(source, out):
        scale = source[...]
        top = eliminate(scale[:half, :half])
        below = exact(scale[half:, :half], top, True)
        rest = scale[half:, half:] - exact(below, below, True)
        bottom = eliminate(rest)
        out[:half, :half] = top.astype(BF16)
        out[:half, half:] = jnp.zeros((half, half), BF16)
        out[half:, :half] = (-exact(bottom, exact(below, top, False), False)).astype(BF16)
        out[half:, half:] = bottom.astype(BF16)

    return pl.pallas_call(
        kernel,
        out_shape=jax.ShapeDtypeStruct((count, count), BF16),
        name="inverse_factor",
        compiler_params=pltpu.CompilerParams(vmem_limit_bytes=vmem_bytes),
        cost_estimate=pl.CostEstimate(flops=1, bytes_accessed=1, transcendentals=0),
    )(correlation)


def rotate(info, rotation, pieces, packed, chunks, bands, bands_all, rows_y):
    group = 1 + max(r for r, t, u, c in pieces)
    per, planes, _, rows_z = next(iter(pieces.values())).shape
    swap = swap_matrix()
    at_once = 2 if planes % 2 == 0 else 1

    def kernel(info_ref, *refs):
        packed_refs = refs[len(pieces) : len(pieces) + len(packed)]
        rotation_ref, swap_ref, out, rows, mixed = refs[len(pieces) + len(packed) :]
        me, parts = info_ref[3], info_ref[4]
        for (r, t, u, c), piece in zip(pieces, refs):
            source = lax.rem(me + parts - t, parts)
            fill(info_ref, rows, piece, source, lax.rem(me + u, parts), r, c, bands, group)
        for (s, t), piece in zip(packed, packed_refs):
            source = lax.rem(me + parts - s, parts)
            part = lax.rem(source + t, parts)
            for c in range(chunks):
                for r in range(group):
                    at = piece.at[c * group + r]
                    fill(info_ref, rows, at, source, part, r, c, bands, group)
        for p in range(at_once):
            for y in range(0, rows_y, 2):
                pair = jnp.concatenate([rows[p, y], rows[p, y + 1]], axis=1)
                value = jnp.dot(rotation_ref[...], pair, preferred_element_type=F32)
                value = value.astype(BF16)
                for k in range(bands // 16):
                    for b in range(2):
                        mixed[p, k, y + b] = value[
                            16 * k : 16 * k + 16, b * rows_z : (b + 1) * rows_z
                        ]
            for k in range(0, bands // 16, 2):
                pair = [mixed[p, k + b].reshape(16 * rows_y, rows_z) for b in range(2)]
                moved = jnp.dot(
                    swap_ref[...], jnp.concatenate(pair, axis=1), preferred_element_type=F32
                ).astype(BF16)
                for b in range(2):
                    part = moved[:, b * rows_z : (b + 1) * rows_z].reshape(16, rows_y, rows_z)
                    out[16 * (k + b) : 16 * (k + b) + 16, p] = part

    spec = pl.BlockSpec((per, at_once, chunk, rows_z), lambda i, info_ref: (0, i, 0, 0))
    packed_spec = pl.BlockSpec(
        (chunks * group, per, at_once, chunk, rows_z), lambda i, info_ref: (0, 0, i, 0, 0)
    )
    return pl.pallas_call(
        kernel,
        grid_spec=pltpu.PrefetchScalarGridSpec(
            num_scalar_prefetch=1,
            grid=(planes // at_once,),
            in_specs=[spec] * len(pieces)
            + [packed_spec] * len(packed)
            + [
                pl.BlockSpec((bands, bands_all), lambda i, info_ref: (info_ref[3], 0)),
                pl.BlockSpec(swap.shape, lambda i, info_ref: (0, 0)),
            ],
            out_specs=pl.BlockSpec(
                (bands, at_once, rows_y, rows_z), lambda i, info_ref: (0, i, 0, 0)
            ),
            scratch_shapes=[
                pltpu.VMEM((at_once, rows_y, bands_all, rows_z), BF16),
                pltpu.VMEM((at_once, bands // 16, rows_y, 16, rows_z), BF16),
            ],
        ),
        out_shape=jax.ShapeDtypeStruct((bands, planes, rows_y, rows_z), BF16),
        name="rotate",
        **params(),
    )(info, *pieces.values(), *packed.values(), rotation, swap)


def pairwise_sum(value, axis, count):
    for k in range(count.bit_length() - 1):
        value = value + lax.ppermute(value, axis, [(i, i ^ (1 << k)) for i in range(count)])
    return value


def body(orbital_block, block_scale, potential):
    bands, planes, rows_y, rows_z = orbital_block.shape
    parts, slabs = lax.axis_size("band"), lax.axis_size("domain")
    bands_all = bands * parts
    group = 4 if bands // 4 >= chunk else 2
    chunks = bands // group // chunk
    where, band = lax.axis_index("domain"), lax.axis_index("band")
    info = jnp.stack(
        [
            lax.rem(where, group),
            (where < group).astype(jnp.int32),
            (where >= slabs - group).astype(jnp.int32),
            band,
            jnp.int32(parts),
        ]
    ).astype(jnp.int32)

    def send(value, r, t):
        if r == 0 and t == 0:
            return value
        pairs = [
            (q * slabs + i, (q + t) % parts * slabs + (i ^ r))
            for q in range(parts)
            for i in range(slabs)
        ]
        return lax.ppermute(value, ("band", "domain"), pairs)

    scale = jnp.broadcast_to(block_scale[:, :, None], (bands, planes, rows_z))
    far_first = sorted(range(group), reverse=True)
    arrived = []
    for c in range(chunks):
        pieces = prepare(info, orbital_block, scale, potential, c, group, c == 0)
        sent = {r: send(pieces[r], r, 0) for r in far_first}
        arrived.append([sent[r] for r in range(group)])
    pieces, own = {}, {}
    sides_pot = None
    for c in range(chunks):
        up, down = edges(info, arrived[c])
        left = lax.ppermute(up, "domain", [(i, i + group) for i in range(slabs - group)])
        right = lax.ppermute(down, "domain", [(i + group, i) for i in range(slabs - group)])
        if c == 0:
            sides_pot = (left, right)
        filtered = chebyshev(info, left, right, arrived[c], *sides_pot, arrived[0], parts)
        for r in far_first:
            for t in range(parts):
                pieces[(r, t, c)] = send(filtered[r][t], r, t)
                own[(r, t, c)] = filtered[r][t]

    total = gram(info, pieces, bands, bands_all)
    total, pieces, own = lax.optimization_barrier((total, pieces, own))
    known = {(r, t, 0, c): value for (r, t, c), value in pieces.items()}
    for c in range(chunks):
        for r in far_first:
            for t in range(1, parts):
                known[(r, 0, t, c)] = send(own[(r, t, c)], r, 0)
    packed = {}
    for s in range(1, parts):
        pairs = [(q, q + s) for q in range(parts - s)]
        for t in range(parts):
            if t != s:
                buffer = jnp.stack(
                    [known[(r, 0, t, c)] for c in range(chunks) for r in range(group)]
                )
                packed[(s, t)] = lax.ppermute(buffer, "band", pairs)
    total = pairwise_sum(total, "band", parts)
    total = pairwise_sum(total, "domain", slabs)
    rotation = inverse_factor(total / float(planes * rows_y * rows_z * slabs))
    return rotate(info, rotation, known, packed, chunks, bands, bands_all, rows_y)


def solution(mesh):
    in_specs = (P("band", "domain", None, None), P("band", "domain"), P("domain", None, None))
    out_specs = P("band", "domain", None, None)
    return jax.shard_map(body, mesh=mesh, in_specs=in_specs, out_specs=out_specs, check_vma=False)
```

```python
import jax
import jax.numpy as jnp
import numpy as np
from jax import lax
from jax.experimental import pallas as pl
from jax.experimental.pallas import tpu as pltpu
from jax.sharding import PartitionSpec as P

grid_step = 0.5
stencil_coef = (
    -5369.0 / 1800.0,
    12.0 / 7.0,
    -15.0 / 56.0,
    10.0 / 189.0,
    -1.0 / 112.0,
    2.0 / 1925.0,
    -1.0 / 16632.0,
)
lower_end = -4.0
cut_energy = 6.0
upper_end = 43.0
kinetic = -0.5 / (grid_step * grid_step)
coef_scale = 7.0
reach = 6
edge = 3 * reach
chunk = 16
F32, BF16 = jnp.float32, jnp.bfloat16
vmem_bytes = 50 * 2**20


def filter_terms():
    width_e = (upper_end - cut_energy) / 2.0
    centre = (upper_end + cut_energy) / 2.0
    sigma_one = width_e / (lower_end - centre)
    gamma_term = 2.0 / sigma_one
    sigma_two = 1.0 / (gamma_term - sigma_one)
    sigma_three = 1.0 / (gamma_term - sigma_two)
    return (width_e, centre, sigma_one, sigma_two, sigma_three)


def stencil_line(count):
    line = np.zeros((count, count), np.float64)
    for offset in range(1, reach + 1):
        value = kinetic * stencil_coef[offset] * coef_scale
        line += value * (np.eye(count, k=offset) + np.eye(count, k=-offset))
    return line


def xy_matrix(planes, rows_y):
    along_x = np.zeros((planes, planes + 2 * reach), np.float64)
    along_x[:, :] = stencil_line(planes + 2 * reach)[reach : reach + planes]
    middle = np.eye(planes, planes + 2 * reach, k=reach)
    full = np.kron(along_x, np.eye(rows_y)) + np.kron(middle, stencil_line(rows_y))
    return jnp.asarray(full, BF16)


def z_matrix(count_z):
    return jnp.asarray(np.kron(np.eye(2), stencil_line(count_z)), BF16)


def swap_matrix():
    full = np.zeros((256, 256), np.float32)
    for a in range(16):
        for b in range(16):
            full[a * 16 + b, b * 16 + a] = 1.0
    return jnp.asarray(full, BF16)


def params(flops=1):
    return dict(
        compiler_params=pltpu.CompilerParams(
            vmem_limit_bytes=vmem_bytes, dimension_semantics=("arbitrary",)
        ),
        cost_estimate=pl.CostEstimate(flops=flops, bytes_accessed=1, transcendentals=0),
    )


def prepare(info, orbitals, scale, potential, part, group, with_potential):
    bands, planes, rows_y, rows_z = orbitals.shape
    own = bands // group
    at_once = 8
    steps = chunk // at_once
    total = chunk + (2 if with_potential else 0)

    def kernel(info_ref, *refs):
        sources, scales, potential_ref = refs[:group], refs[group : 2 * group], refs[2 * group]
        outs = refs[2 * group + 1 :]
        i = pl.program_id(0)
        for r in range(group):
            for b in range(at_once):
                value = sources[r][b].astype(F32) * scales[r][b][:, None, :]
                outs[r][i * at_once + b] = value.astype(BF16)

        if with_potential:

            @pl.when(i == 0)
            def _():
                high = potential_ref[...].astype(BF16)
                low = (potential_ref[...] - high.astype(F32)).astype(BF16)
                for r in range(group):
                    outs[r][chunk] = high
                    outs[r][chunk + 1] = low

    def first(r, i, info_ref):
        return ((info_ref[0] ^ r) * own + part * chunk) // at_once + i

    def source_spec(r):
        return pl.BlockSpec(
            (at_once, planes, rows_y, rows_z),
            lambda i, info_ref: (first(r, i, info_ref), 0, 0, 0),
        )

    def scale_spec(r):
        return pl.BlockSpec(
            (at_once, planes, rows_z), lambda i, info_ref: (first(r, i, info_ref), 0, 0)
        )

    shape = jax.ShapeDtypeStruct((total, planes, rows_y, rows_z), BF16)
    return pl.pallas_call(
        kernel,
        grid_spec=pltpu.PrefetchScalarGridSpec(
            num_scalar_prefetch=1,
            grid=(steps,),
            in_specs=[source_spec(r) for r in range(group)]
            + [scale_spec(r) for r in range(group)]
            + [pl.BlockSpec((planes, rows_y, rows_z), lambda i, info_ref: (0, 0, 0))],
            out_specs=[pl.BlockSpec(shape.shape, lambda i, info_ref: (0, 0, 0, 0))] * group,
        ),
        out_shape=[shape] * group,
        name="prepare",
        **params(),
    )(info, *([orbitals] * group), *([scale] * group), potential)


def edges(info, pieces):
    group = len(pieces)
    total, planes, rows_y, rows_z = pieces[0].shape
    rest = edge - planes
    at_once = 6 if total % 6 == 0 else 4

    def kernel(info_ref, *refs):
        sources, (up, down) = refs[:group], refs[group:]
        for r in range(group):
            slab = info_ref[0] ^ r

            @pl.when(slab == group - 1)
            def _():
                up[:, rest:] = sources[r][...]

            @pl.when(slab == group - 2)
            def _():
                up[:, :rest] = sources[r][:, planes - rest :]

            @pl.when(slab == 0)
            def _():
                down[:, :planes] = sources[r][...]

            @pl.when(slab == 1)
            def _():
                down[:, planes:] = sources[r][:, :rest]

    shape = jax.ShapeDtypeStruct((total, edge, rows_y, rows_z), BF16)
    block = lambda count: pl.BlockSpec(
        (at_once, count, rows_y, rows_z), lambda i, info_ref: (i, 0, 0, 0)
    )
    return pl.pallas_call(
        kernel,
        grid_spec=pltpu.PrefetchScalarGridSpec(
            num_scalar_prefetch=1,
            grid=(total // at_once,),
            in_specs=[block(planes)] * group,
            out_specs=[block(edge)] * 2,
        ),
        out_shape=[shape] * 2,
        name="edges",
        **params(),
    )(info, *pieces)


def chebyshev(info, left, right, pieces, left_pot, right_pot, pieces_pot, parts):
    group = len(pieces)
    _, planes, rows_y, rows_z = pieces[0].shape
    slab = group * planes
    per = rows_y // parts
    steps = chunk // 2
    width_e, centre, sigma_one, sigma_two, sigma_three = filter_terms()
    diagonal = 3.0 * stencil_coef[0] * kinetic - centre
    tile_rows = planes * rows_y
    xy, zz, swap = xy_matrix(planes, rows_y), z_matrix(rows_z), swap_matrix()
    count_0, count_1, count_2 = slab + 6 * reach, slab + 4 * reach, slab + 2 * reach

    def kernel(info_ref, *refs):
        left_ref, right_ref = refs[:2]
        piece_refs = refs[2 : 2 + group]
        left_pot_ref, right_pot_ref = refs[2 + group : 4 + group]
        pot_refs = refs[4 + group : 4 + 2 * group]
        xy_ref, zz_ref, swap_ref = refs[4 + 2 * group : 7 + 2 * group]
        outs = refs[7 + 2 * group : 7 + (2 + parts) * group]
        field, first, second, energy, result = refs[7 + (2 + parts) * group :]
        i = pl.program_id(0)
        me = info_ref[0]
        at_left, at_right = info_ref[1] == 1, info_ref[2] == 1

        @pl.when(i == 0)
        def _():
            def store(start, count, source, begin):
                total = source[0, begin : begin + count].astype(F32) + source[
                    1, begin : begin + count
                ].astype(F32)
                energy[pl.ds(start, count)] = coef_scale * (total + diagonal)

            store(0, 2 * reach, left_pot_ref, reach)
            store(slab + 2 * reach, 2 * reach, right_pot_ref, 0)
            for r in range(group):
                store(2 * reach + planes * (me ^ r), planes, pot_refs[r], 0)

        for b in range(2):
            lanes = slice(b * rows_z, (b + 1) * rows_z)
            field[0:edge, :, lanes] = left_ref[b]
            field[edge + slab : edge + slab + edge, :, lanes] = right_ref[b]
            for r in range(group):
                field[pl.ds(edge + planes * (me ^ r), planes), :, lanes] = piece_refs[r][b]

        def apply(source, start, energy_start):
            rows = source[pl.ds(start, planes + 2 * reach)].reshape(-1, 2 * rows_z)
            middle = source[pl.ds(start + reach, planes)].reshape(tile_rows, 2 * rows_z)
            total = jnp.dot(xy_ref[...], rows, preferred_element_type=F32)
            total += jnp.dot(middle, zz_ref[...], preferred_element_type=F32)
            factor = energy[pl.ds(energy_start, planes)].reshape(tile_rows, rows_z)
            factor = jnp.concatenate([factor, factor], axis=1)
            return total + factor * middle.astype(F32)

        def block(value):
            return value.astype(BF16).reshape(planes, rows_y, 2 * rows_z)

        def previous(source, start):
            return source[pl.ds(start, planes)].reshape(tile_rows, 2 * rows_z).astype(F32)

        for t in range(count_1 // planes):
            at = t * planes
            value = apply(field, at, at) * (sigma_one / width_e / coef_scale)
            first[at : at + planes] = block(value)

        @pl.when(at_left)
        def _():
            first[: 2 * reach] = jnp.zeros((2 * reach, rows_y, 2 * rows_z), BF16)

        @pl.when(at_right)
        def _():
            first[count_1 - 2 * reach :] = jnp.zeros((2 * reach, rows_y, 2 * rows_z), BF16)

        for t in range(count_2 // planes):
            at = t * planes
            value = apply(first, at, at + reach) * (2.0 * sigma_two / width_e / coef_scale)
            value -= sigma_one * sigma_two * previous(field, at + 2 * reach)
            second[at : at + planes] = block(value)

        @pl.when(at_left)
        def _():
            second[:reach] = jnp.zeros((reach, rows_y, 2 * rows_z), BF16)

        @pl.when(at_right)
        def _():
            second[count_2 - reach :] = jnp.zeros((reach, rows_y, 2 * rows_z), BF16)

        for t in range(group):
            at = t * planes
            value = apply(second, at, at + 2 * reach) * (2.0 * sigma_three / width_e / coef_scale)
            value -= sigma_two * sigma_three * previous(first, at + 2 * reach)
            value = block(value)
            for b in range(2):
                result[at : at + planes, 2 * i + b] = value[:, :, b * rows_z : (b + 1) * rows_z]

        @pl.when(i == steps - 1)
        def _():
            for r in range(group):
                start = planes * (me ^ r)
                for p in range(0, planes, 2):
                    pair = [
                        result[start + p + k].reshape(chunk * rows_y, rows_z) for k in range(2)
                    ]
                    pair = jnp.concatenate(pair, axis=1)
                    for t in range(parts):
                        begin = lax.rem(info_ref[3] + t, parts) * (per * chunk)
                        begin = pl.multiple_of(begin, per * chunk)
                        moved = jnp.dot(
                            swap_ref[pl.ds(begin, per * chunk), :],
                            pair,
                            preferred_element_type=F32,
                        ).astype(BF16)
                        for k in range(2):
                            value = moved[:, k * rows_z : (k + 1) * rows_z]
                            outs[r * parts + t][:, p + k] = value.reshape(per, chunk, rows_z)

    def block_spec(count, index):
        return pl.BlockSpec((2, count, rows_y, rows_z), index)

    def whole_spec(shape):
        return pl.BlockSpec(shape, lambda i, info_ref: (0,) * len(shape))

    moving = lambda i, info_ref: (i, 0, 0, 0)
    fixed = lambda i, info_ref: (steps, 0, 0, 0)
    shape = jax.ShapeDtypeStruct((per, planes, chunk, rows_z), BF16)
    flat = pl.pallas_call(
        kernel,
        grid_spec=pltpu.PrefetchScalarGridSpec(
            num_scalar_prefetch=1,
            grid=(steps,),
            in_specs=[block_spec(edge, moving)] * 2
            + [block_spec(planes, moving)] * group
            + [block_spec(edge, fixed)] * 2
            + [block_spec(planes, fixed)] * group
            + [whole_spec(xy.shape), whole_spec(zz.shape), whole_spec(swap.shape)],
            out_specs=[whole_spec(shape.shape)] * (group * parts),
            scratch_shapes=[
                pltpu.VMEM((count_0, rows_y, 2 * rows_z), BF16),
                pltpu.VMEM((count_1, rows_y, 2 * rows_z), BF16),
                pltpu.VMEM((count_2, rows_y, 2 * rows_z), BF16),
                pltpu.VMEM((count_1, rows_y, rows_z), F32),
                pltpu.VMEM((slab, chunk, rows_y, rows_z), BF16),
            ],
        ),
        out_shape=[shape] * (group * parts),
        name="chebyshev",
        **params(),
    )(info, left, right, *pieces, left_pot, right_pot, *pieces_pot, xy, zz, swap)
    return [flat[r * parts : (r + 1) * parts] for r in range(group)]


def fill(info_ref, rows, piece, source, part, r, c, bands, group):
    own = bands // group
    start = source * bands + (info_ref[0] ^ r) * own + c * chunk
    where = pl.ds(pl.multiple_of(start, chunk), chunk)
    per, planes = piece.shape[0], piece.shape[1]
    for p in range(planes):
        rows[p, pl.ds(part * per, per), where, :] = piece[:, p]


def gram(info, pieces, bands, bands_all):
    group = 1 + max(r for r, t, c in pieces)
    chunks = 1 + max(c for r, t, c in pieces)
    per, planes, _, rows_z = next(iter(pieces.values())).shape
    at_once = 3 if planes % 3 == 0 else 1

    def kernel(info_ref, *refs):
        out, packed, rows = refs[len(pieces) :]
        parts = info_ref[4]
        for (r, t, c), piece in zip(pieces, refs):
            if t == 0:
                packed[c * group + r] = piece[...]
            source = lax.rem(info_ref[3] + parts - t, parts)
            fill(info_ref, rows, piece, source, 0, r, c, bands, group)
        block = jnp.concatenate([rows[p, y] for p in range(at_once) for y in range(per)], axis=1)
        total = lax.dot_general(
            block, block, (((1,), (1,)), ((), ())), preferred_element_type=F32
        )

        @pl.when(pl.program_id(0) == 0)
        def _():
            out[...] = total

        @pl.when(pl.program_id(0) > 0)
        def _():
            out[...] += total

    spec = pl.BlockSpec((per, at_once, chunk, rows_z), lambda i, info_ref: (0, i, 0, 0))
    return pl.pallas_call(
        kernel,
        grid_spec=pltpu.PrefetchScalarGridSpec(
            num_scalar_prefetch=1,
            grid=(planes // at_once,),
            in_specs=[spec] * len(pieces),
            out_specs=[
                pl.BlockSpec((bands_all, bands_all), lambda i, info_ref: (0, 0)),
                pl.BlockSpec(
                    (chunks * group, per, at_once, chunk, rows_z),
                    lambda i, info_ref: (0, 0, i, 0, 0),
                ),
            ],
            scratch_shapes=[pltpu.VMEM((at_once, per, bands_all, rows_z), BF16)],
        ),
        out_shape=[
            jax.ShapeDtypeStruct((bands_all, bands_all), F32),
            jax.ShapeDtypeStruct((chunks * group, per, planes, chunk, rows_z), BF16),
        ],
        name="gram",
        **params(),
    )(info, *pieces.values())


def inverse_factor(correlation):
    count = correlation.shape[0]
    half = count // 2

    def exact(a, b, transposed):
        dims = (((1,), (1 if transposed else 0,)), ((), ()))
        return lax.dot_general(
            a, b, dims, precision=lax.Precision.HIGHEST, preferred_element_type=F32
        )

    def eliminate(block):
        groups = half // 8
        row = lax.broadcasted_iota(jnp.int32, (8, half), 0)
        column = lax.broadcasted_iota(jnp.int32, (8, half), 1)
        left = [block[8 * g : 8 * g + 8] for g in range(groups)]
        right = [jnp.where(column == row + 8 * g, 1.0, 0.0).astype(F32) for g in range(groups)]
        for at in range(groups):
            later = range(at, groups)
            spread = [
                [
                    jnp.broadcast_to(left[g][:, 8 * at + k : 8 * at + k + 1], (8, half))
                    for g in later
                ]
                for k in range(8)
            ]
            factors, rows_left, rows_right = [], [], []
            for k in range(8):
                pivot = jnp.broadcast_to(spread[k][0][k : k + 1], (8, half))
                scale = lax.rsqrt(pivot)
                scale = scale * (1.5 - 0.5 * pivot * scale * scale)
                factor = [value * scale for value in spread[k]]
                for m in range(k + 1, 8):
                    other = jnp.broadcast_to(factor[0][m : m + 1], (8, half))
                    spread[m] = [value - f * other for value, f in zip(spread[m], factor)]
                row_left = jnp.broadcast_to(left[at][k : k + 1], (8, half)) * scale
                row_right = jnp.broadcast_to(right[at][k : k + 1], (8, half)) * scale
                inside = jnp.where(row > k, factor[0], 0.0)
                left[at] = jnp.where(row == k, row_left, left[at] - inside * row_left)
                right[at] = jnp.where(row == k, row_right, right[at] - inside * row_right)
                factors.append(factor)
                rows_left.append(row_left)
                rows_right.append(row_right)
            for g in range(at + 1, groups):
                for k in range(8):
                    left[g] = left[g] - factors[k][g - at] * rows_left[k]
                    right[g] = right[g] - factors[k][g - at] * rows_right[k]
        return jnp.concatenate(right, axis=0)

    def kernel(source, out):
        scale = source[...]
        top = eliminate(scale[:half, :half])
        below = exact(scale[half:, :half], top, True)
        rest = scale[half:, half:] - exact(below, below, True)
        bottom = eliminate(rest)
        out[:half, :half] = top.astype(BF16)
        out[:half, half:] = jnp.zeros((half, half), BF16)
        out[half:, :half] = (-exact(bottom, exact(below, top, False), False)).astype(BF16)
        out[half:, half:] = bottom.astype(BF16)

    return pl.pallas_call(
        kernel,
        out_shape=jax.ShapeDtypeStruct((count, count), BF16),
        name="inverse_factor",
        compiler_params=pltpu.CompilerParams(vmem_limit_bytes=vmem_bytes),
        cost_estimate=pl.CostEstimate(flops=1, bytes_accessed=1, transcendentals=0),
    )(correlation)


def rotate(info, rotation, pieces, packed, chunks, bands, bands_all, rows_y):
    group = 1 + max(r for r, t, u, c in pieces)
    per, planes, _, rows_z = next(iter(pieces.values())).shape
    swap = swap_matrix()
    at_once = 2 if planes % 2 == 0 else 1

    def kernel(info_ref, *refs):
        packed_refs = refs[len(pieces) : len(pieces) + len(packed)]
        rotation_ref, swap_ref, out, rows, mixed = refs[len(pieces) + len(packed) :]
        me, parts = info_ref[3], info_ref[4]
        for (r, t, u, c), piece in zip(pieces, refs):
            source = lax.rem(me + parts - t, parts)
            fill(info_ref, rows, piece, source, lax.rem(me + u, parts), r, c, bands, group)
        for (s, t), piece in zip(packed, packed_refs):
            source = lax.rem(me + parts - s, parts)
            part = lax.rem(source + t, parts)
            for c in range(chunks):
                for r in range(group):
                    at = piece.at[c * group + r]
                    fill(info_ref, rows, at, source, part, r, c, bands, group)
        for p in range(at_once):
            for y in range(0, rows_y, 2):
                pair = jnp.concatenate([rows[p, y], rows[p, y + 1]], axis=1)
                value = jnp.dot(rotation_ref[...], pair, preferred_element_type=F32)
                value = value.astype(BF16)
                for k in range(bands // 16):
                    for b in range(2):
                        mixed[p, k, y + b] = value[
                            16 * k : 16 * k + 16, b * rows_z : (b + 1) * rows_z
                        ]
            for k in range(0, bands // 16, 2):
                pair = [mixed[p, k + b].reshape(16 * rows_y, rows_z) for b in range(2)]
                moved = jnp.dot(
                    swap_ref[...], jnp.concatenate(pair, axis=1), preferred_element_type=F32
                ).astype(BF16)
                for b in range(2):
                    part = moved[:, b * rows_z : (b + 1) * rows_z].reshape(16, rows_y, rows_z)
                    out[16 * (k + b) : 16 * (k + b) + 16, p] = part

    spec = pl.BlockSpec((per, at_once, chunk, rows_z), lambda i, info_ref: (0, i, 0, 0))
    packed_spec = pl.BlockSpec(
        (chunks * group, per, at_once, chunk, rows_z), lambda i, info_ref: (0, 0, i, 0, 0)
    )
    return pl.pallas_call(
        kernel,
        grid_spec=pltpu.PrefetchScalarGridSpec(
            num_scalar_prefetch=1,
            grid=(planes // at_once,),
            in_specs=[spec] * len(pieces)
            + [packed_spec] * len(packed)
            + [
                pl.BlockSpec((bands, bands_all), lambda i, info_ref: (info_ref[3], 0)),
                pl.BlockSpec(swap.shape, lambda i, info_ref: (0, 0)),
            ],
            out_specs=pl.BlockSpec(
                (bands, at_once, rows_y, rows_z), lambda i, info_ref: (0, i, 0, 0)
            ),
            scratch_shapes=[
                pltpu.VMEM((at_once, rows_y, bands_all, rows_z), BF16),
                pltpu.VMEM((at_once, bands // 16, rows_y, 16, rows_z), BF16),
            ],
        ),
        out_shape=jax.ShapeDtypeStruct((bands, planes, rows_y, rows_z), BF16),
        name="rotate",
        **params(),
    )(info, *pieces.values(), *packed.values(), rotation, swap)


def pairwise_sum(value, axis, count, low, high):
    bit = max(low, 1)
    while bit < high:
        value = value + lax.ppermute(value, axis, [(i, i ^ bit) for i in range(count)])
        bit *= 2
    return value


def body(orbital_block, block_scale, potential):
    bands, planes, rows_y, rows_z = orbital_block.shape
    parts, slabs = lax.axis_size("band"), lax.axis_size("domain")
    bands_all = bands * parts
    group = 4 if bands // 4 >= chunk else 2
    chunks = bands // group // chunk
    where, band = lax.axis_index("domain"), lax.axis_index("band")
    info = jnp.stack(
        [
            lax.rem(where, group),
            (where < group).astype(jnp.int32),
            (where >= slabs - group).astype(jnp.int32),
            band,
            jnp.int32(parts),
        ]
    ).astype(jnp.int32)

    def send(value, r, t):
        if r == 0 and t == 0:
            return value
        pairs = [
            (q * slabs + i, (q + t) % parts * slabs + (i ^ r))
            for q in range(parts)
            for i in range(slabs)
        ]
        return lax.ppermute(value, ("band", "domain"), pairs)

    scale = jnp.broadcast_to(block_scale[:, :, None], (bands, planes, rows_z))
    far_first = sorted(range(group), reverse=True)
    arrived = []
    for c in range(chunks):
        pieces = prepare(info, orbital_block, scale, potential, c, group, c == 0)
        sent = {r: send(pieces[r], r, 0) for r in far_first}
        arrived.append([sent[r] for r in range(group)])
    def after(value, *others):
        return lax.optimization_barrier((value, *others))[0]

    sides = []
    for c in range(chunks):
        up, down = edges(info, arrived[c])
        left = lax.ppermute(up, "domain", [(i, i + group) for i in range(slabs - group)])
        right = lax.ppermute(down, "domain", [(i + group, i) for i in range(slabs - group)])
        sides.append((left, right))
        last_up = up
    pieces, own = {}, {}
    order = after(info, last_up)
    for c in range(chunks):
        filtered = chebyshev(order, *sides[c], arrived[c], *sides[0], arrived[0], parts)
        order = after(info, filtered[0][0])
        for r in far_first:
            for t in reversed(range(parts)):
                value = filtered[r][t]
                own[(r, t, c)] = value
                if c > 0:
                    value = after(value, pieces[(r, t, c - 1)])
                pieces[(r, t, c)] = send(value, r, t)

    known = {(r, t, 0, c): value for (r, t, c), value in pieces.items()}
    total, buffer = gram(info, pieces, bands, bands_all)
    total = pairwise_sum(total, "band", parts, 0, parts)
    buffer = after(buffer, total)
    packed = {}
    for s in range(1, parts):
        packed[(s, 0)] = lax.ppermute(buffer, "band", [(q, q + s) for q in range(parts - s)])
    total = pairwise_sum(total, "domain", slabs, 0, group)
    for c in range(chunks):
        for r in far_first:
            for t in range(1, parts):
                known[(r, 0, t, c)] = send(after(own[(r, t, c)], total), r, 0)
    for t in range(1, parts):
        for s in range(1, parts):
            if t != s:
                buffer = jnp.stack(
                    [known[(r, 0, t, c)] for c in range(chunks) for r in range(group)]
                )
                pairs = [(q, q + s) for q in range(parts - s)]
                packed[(s, t)] = lax.ppermute(buffer, "band", pairs)
    total = pairwise_sum(total, "domain", slabs, group, slabs)
    rotation = inverse_factor(total / float(planes * rows_y * rows_z * slabs))
    return rotate(info, rotation, known, packed, chunks, bands, bands_all, rows_y)


def solution(mesh):
    in_specs = (P("band", "domain", None, None), P("band", "domain"), P("domain", None, None))
    out_specs = P("band", "domain", None, None)
    return jax.shard_map(body, mesh=mesh, in_specs=in_specs, out_specs=out_specs, check_vma=False)
```

```python
import math

import jax
import jax.numpy as jnp
import numpy as np
from jax import lax
from jax.experimental import pallas as pl
from jax.experimental.pallas import tpu as pltpu
from jax.sharding import PartitionSpec as P

grid_step = 0.5
stencil_coef = (
    -5369.0 / 1800.0,
    12.0 / 7.0,
    -15.0 / 56.0,
    10.0 / 189.0,
    -1.0 / 112.0,
    2.0 / 1925.0,
    -1.0 / 16632.0,
)
lower_end = -4.0
cut_energy = 6.0
upper_end = 43.0
kinetic = -0.5 / (grid_step * grid_step)
coef_scale = 7.0
reach = 6
edge = 3 * reach
chunk = 16
F32, BF16 = jnp.float32, jnp.bfloat16
vmem_bytes = 50 * 2**20


def filter_terms():
    width_e = (upper_end - cut_energy) / 2.0
    centre = (upper_end + cut_energy) / 2.0
    sigma_one = width_e / (lower_end - centre)
    gamma_term = 2.0 / sigma_one
    sigma_two = 1.0 / (gamma_term - sigma_one)
    sigma_three = 1.0 / (gamma_term - sigma_two)
    return (width_e, centre, sigma_one, sigma_two, sigma_three)


def stencil_line(count):
    line = np.zeros((count, count), np.float64)
    for offset in range(1, reach + 1):
        value = kinetic * stencil_coef[offset] * coef_scale
        line += value * (np.eye(count, k=offset) + np.eye(count, k=-offset))
    return line


def xy_matrix(planes, rows_y):
    along_x = np.zeros((planes, planes + 2 * reach), np.float64)
    along_x[:, :] = stencil_line(planes + 2 * reach)[reach : reach + planes]
    middle = np.eye(planes, planes + 2 * reach, k=reach)
    full = np.kron(along_x, np.eye(rows_y)) + np.kron(middle, stencil_line(rows_y))
    return jnp.asarray(full, BF16)


def z_matrix(count_z):
    return jnp.asarray(np.kron(np.eye(2), stencil_line(count_z)), BF16)


def swap_matrix():
    full = np.zeros((256, 256), np.float32)
    for a in range(16):
        for b in range(16):
            full[a * 16 + b, b * 16 + a] = 1.0
    return jnp.asarray(full, BF16)


def params(flops=1):
    return dict(
        compiler_params=pltpu.CompilerParams(
            vmem_limit_bytes=vmem_bytes, dimension_semantics=("arbitrary",)
        ),
        cost_estimate=pl.CostEstimate(flops=flops, bytes_accessed=1, transcendentals=0),
    )


def prepare(info, orbitals, scale, potential, part, group, with_potential):
    bands, planes, rows_y, rows_z = orbitals.shape
    own = bands // group
    at_once = 8
    steps = chunk // at_once
    total = chunk + (2 if with_potential else 0)

    def kernel(info_ref, *refs):
        sources, scales, potential_ref = refs[:group], refs[group : 2 * group], refs[2 * group]
        outs = refs[2 * group + 1 :]
        i = pl.program_id(0)
        for r in range(group):
            for b in range(at_once):
                value = sources[r][b].astype(F32) * scales[r][b][:, None, :]
                outs[r][i * at_once + b] = value.astype(BF16)

        if with_potential:

            @pl.when(i == 0)
            def _():
                high = potential_ref[...].astype(BF16)
                low = (potential_ref[...] - high.astype(F32)).astype(BF16)
                for r in range(group):
                    outs[r][chunk] = high
                    outs[r][chunk + 1] = low

    def first(r, i, info_ref):
        return ((info_ref[0] ^ r) * own + part * chunk) // at_once + i

    def source_spec(r):
        return pl.BlockSpec(
            (at_once, planes, rows_y, rows_z),
            lambda i, info_ref: (first(r, i, info_ref), 0, 0, 0),
        )

    def scale_spec(r):
        return pl.BlockSpec(
            (at_once, planes, rows_z), lambda i, info_ref: (first(r, i, info_ref), 0, 0)
        )

    shape = jax.ShapeDtypeStruct((total, planes, rows_y, rows_z), BF16)
    return pl.pallas_call(
        kernel,
        grid_spec=pltpu.PrefetchScalarGridSpec(
            num_scalar_prefetch=1,
            grid=(steps,),
            in_specs=[source_spec(r) for r in range(group)]
            + [scale_spec(r) for r in range(group)]
            + [pl.BlockSpec((planes, rows_y, rows_z), lambda i, info_ref: (0, 0, 0))],
            out_specs=[pl.BlockSpec(shape.shape, lambda i, info_ref: (0, 0, 0, 0))] * group,
        ),
        out_shape=[shape] * group,
        name="prepare",
        **params(),
    )(info, *([orbitals] * group), *([scale] * group), potential)


def edges(info, pieces):
    group = len(pieces)
    total, planes, rows_y, rows_z = pieces[0].shape
    rest = edge - planes
    at_once = 6 if total % 6 == 0 else 4
    half = chunk // 2
    counts = [half + total - chunk, half]

    def place(band):
        if band < half:
            return 0, band
        return (1, band - half) if band < chunk else (0, band - half)

    def kernel(info_ref, *refs):
        sources, outs = refs[:group], refs[group:]
        for step in range(total // at_once):

            @pl.when(pl.program_id(0) == step)
            def _():
                for r in range(group):
                    slab = info_ref[0] ^ r

                    def each(write):
                        for b in range(at_once):
                            which, to = place(step * at_once + b)
                            write(outs[2 * which], outs[2 * which + 1], to, sources[r].at[b])

                    @pl.when(slab == group - 1)
                    def _():
                        def write(up, down, to, source):
                            up[to, rest:] = source[...]

                        each(write)

                    @pl.when(slab == group - 2)
                    def _():
                        def write(up, down, to, source):
                            up[to, :rest] = source[planes - rest :]

                        each(write)

                    @pl.when(slab == 0)
                    def _():
                        def write(up, down, to, source):
                            down[to, :planes] = source[...]

                        each(write)

                    @pl.when(slab == 1)
                    def _():
                        def write(up, down, to, source):
                            down[to, planes:] = source[:rest]

                        each(write)

    shapes = [
        jax.ShapeDtypeStruct((count, edge, rows_y, rows_z), BF16)
        for count in counts
        for _ in range(2)
    ]
    flat = pl.pallas_call(
        kernel,
        grid_spec=pltpu.PrefetchScalarGridSpec(
            num_scalar_prefetch=1,
            grid=(total // at_once,),
            in_specs=[
                pl.BlockSpec(
                    (at_once, planes, rows_y, rows_z), lambda i, info_ref: (i, 0, 0, 0)
                )
            ]
            * group,
            out_specs=[
                pl.BlockSpec(shape.shape, lambda i, info_ref: (0, 0, 0, 0)) for shape in shapes
            ],
        ),
        out_shape=shapes,
        name="edges",
        **params(),
    )(info, *pieces)
    return flat[:2], flat[2:]


def chebyshev(info, left, right, pieces, left_pot, right_pot, pieces_pot, parts, before):
    group = len(pieces)
    _, planes, rows_y, rows_z = pieces[0].shape
    slab = group * planes
    per_p, per_y, cuts_y = shares(planes, rows_y, parts)
    at_once = 2 if per_p % 2 == 0 else 1
    half = chunk // 2
    steps = half // 2
    skip = 0 if before is None else steps
    given = [] if before is None else [before]
    count_out = 1 if before is None else group // 2 * parts
    width_e, centre, sigma_one, sigma_two, sigma_three = filter_terms()
    diagonal = 3.0 * stencil_coef[0] * kinetic - centre
    tile_rows = planes * rows_y
    xy, zz, swap = xy_matrix(planes, rows_y), z_matrix(rows_z), swap_matrix()
    count_0, count_1, count_2 = slab + 6 * reach, slab + 4 * reach, slab + 2 * reach

    def kernel(info_ref, *refs):
        left_ref, right_ref = refs[:2]
        piece_refs = refs[2 : 2 + group]
        left_pot_ref, right_pot_ref = refs[2 + group : 4 + group]
        pot_refs = refs[4 + group : 4 + 2 * group]
        xy_ref, zz_ref, swap_ref = refs[4 + 2 * group : 7 + 2 * group]
        given_refs = refs[7 + 2 * group : 7 + 2 * group + len(given)]
        outs = refs[7 + 2 * group + len(given) : 7 + 2 * group + len(given) + count_out]
        field, first, second, energy, *result = refs[
            7 + 2 * group + len(given) + count_out :
        ]
        i = pl.program_id(0)
        me = info_ref[0]
        at_left, at_right = info_ref[1] == 1, info_ref[2] == 1

        @pl.when(i == 0)
        def _():
            def store(start, count, source, begin):
                total = source[0, begin : begin + count].astype(F32) + source[
                    1, begin : begin + count
                ].astype(F32)
                energy[pl.ds(start, count)] = coef_scale * (total + diagonal)

            store(0, 2 * reach, left_pot_ref, reach)
            store(slab + 2 * reach, 2 * reach, right_pot_ref, 0)
            for r in range(group):
                store(2 * reach + planes * (me ^ r), planes, pot_refs[r], 0)

        for b in range(2):
            lanes = slice(b * rows_z, (b + 1) * rows_z)
            field[0:edge, :, lanes] = left_ref[b]
            field[edge + slab : edge + slab + edge, :, lanes] = right_ref[b]
            for r in range(group):
                field[pl.ds(edge + planes * (me ^ r), planes), :, lanes] = piece_refs[r][b]

        def apply(source, start, energy_start):
            rows = source[pl.ds(start, planes + 2 * reach)].reshape(-1, 2 * rows_z)
            middle = source[pl.ds(start + reach, planes)].reshape(tile_rows, 2 * rows_z)
            total = jnp.dot(xy_ref[...], rows, preferred_element_type=F32)
            total += jnp.dot(middle, zz_ref[...], preferred_element_type=F32)
            factor = energy[pl.ds(energy_start, planes)].reshape(tile_rows, rows_z)
            factor = jnp.concatenate([factor, factor], axis=1)
            return total + factor * middle.astype(F32)

        def block(value):
            return value.astype(BF16).reshape(planes, rows_y, 2 * rows_z)

        def previous(source, start):
            return source[pl.ds(start, planes)].reshape(tile_rows, 2 * rows_z).astype(F32)

        for t in range(count_1 // planes):
            at = t * planes
            value = apply(field, at, at) * (sigma_one / width_e / coef_scale)
            first[at : at + planes] = block(value)

        @pl.when(at_left)
        def _():
            first[: 2 * reach] = jnp.zeros((2 * reach, rows_y, 2 * rows_z), BF16)

        @pl.when(at_right)
        def _():
            first[count_1 - 2 * reach :] = jnp.zeros((2 * reach, rows_y, 2 * rows_z), BF16)

        for t in range(count_2 // planes):
            at = t * planes
            value = apply(first, at, at + reach) * (2.0 * sigma_two / width_e / coef_scale)
            value -= sigma_one * sigma_two * previous(field, at + 2 * reach)
            second[at : at + planes] = block(value)

        @pl.when(at_left)
        def _():
            second[:reach] = jnp.zeros((reach, rows_y, 2 * rows_z), BF16)

        @pl.when(at_right)
        def _():
            second[count_2 - reach :] = jnp.zeros((reach, rows_y, 2 * rows_z), BF16)

        for t in range(group):
            at = t * planes
            value = apply(second, at, at + 2 * reach) * (2.0 * sigma_three / width_e / coef_scale)
            value -= sigma_two * sigma_three * previous(first, at + 2 * reach)
            value = block(value)
            for b in range(2):
                part = value[:, :, b * rows_z : (b + 1) * rows_z]
                if before is None:
                    outs[0][at : at + planes, b] = part
                else:
                    result[0][at : at + planes, 2 * i + b] = part

        def exchange_order(p):
            pair = [
                jnp.concatenate(
                    [ref[p + k].reshape(half * rows_y, rows_z) for k in range(at_once)], axis=1
                )
                for ref in (given_refs[0], result[0])
            ]
            return jnp.concatenate(pair, axis=0)

        if before is not None:

            @pl.when(i == steps - 1)
            def _():
                for t in range(parts):
                    part = lax.rem(info_ref[3] + t, parts)
                    begin = lax.rem(part, cuts_y) * (per_y * chunk)
                    begin = pl.multiple_of(begin, per_y * chunk)
                    for r in range(group):
                        start = planes * (me ^ r) + part // cuts_y * per_p
                        for p in range(0, per_p, at_once):
                            moved = jnp.dot(
                                swap_ref[pl.ds(begin, per_y * chunk), :],
                                exchange_order(start + p),
                                preferred_element_type=F32,
                            ).astype(BF16)
                            for k in range(at_once):
                                value = moved[:, k * rows_z : (k + 1) * rows_z]
                                out = outs[r // 2 * parts + t]
                                out[r % 2, :, p + k] = value.reshape(per_y, chunk, rows_z)

    def block_spec(count, index):
        return pl.BlockSpec((2, count, rows_y, rows_z), index)

    def whole_spec(shape):
        return pl.BlockSpec(shape, lambda i, info_ref: (0,) * len(shape))

    moving = lambda i, info_ref: (i, 0, 0, 0)
    later = lambda i, info_ref: (skip + i, 0, 0, 0)
    side_pot = lambda i, info_ref: (steps, 0, 0, 0)
    piece_pot = lambda i, info_ref: (2 * steps, 0, 0, 0)
    if before is None:
        shape = jax.ShapeDtypeStruct((slab, half, rows_y, rows_z), BF16)
        out_spec = pl.BlockSpec((slab, 2, rows_y, rows_z), lambda i, info_ref: (0, i, 0, 0))
        kept = []
    else:
        shape = jax.ShapeDtypeStruct((2, per_y, per_p, chunk, rows_z), BF16)
        out_spec = whole_spec(shape.shape)
        kept = [pltpu.VMEM((slab, half, rows_y, rows_z), BF16)]
    flat = pl.pallas_call(
        kernel,
        grid_spec=pltpu.PrefetchScalarGridSpec(
            num_scalar_prefetch=1,
            grid=(steps,),
            in_specs=[block_spec(edge, moving)] * 2
            + [block_spec(planes, later)] * group
            + [block_spec(edge, side_pot)] * 2
            + [block_spec(planes, piece_pot)] * group
            + [whole_spec(xy.shape), whole_spec(zz.shape), whole_spec(swap.shape)]
            + [whole_spec(value.shape) for value in given],
            out_specs=[out_spec] * count_out,
            scratch_shapes=[
                pltpu.VMEM((count_0, rows_y, 2 * rows_z), BF16),
                pltpu.VMEM((count_1, rows_y, 2 * rows_z), BF16),
                pltpu.VMEM((count_2, rows_y, 2 * rows_z), BF16),
                pltpu.VMEM((count_1, rows_y, rows_z), F32),
            ]
            + kept,
        ),
        out_shape=[shape] * count_out,
        name="chebyshev",
        **params(),
    )(info, left, right, *pieces, left_pot, right_pot, *pieces_pot, xy, zz, swap, *given)
    if before is None:
        return flat[0]
    return [flat[a * parts : (a + 1) * parts] for a in range(group // 2)]


def shares(planes, rows_y, parts):
    cuts_p = math.gcd(planes, parts)
    cuts_y = parts // cuts_p
    return planes // cuts_p, rows_y // cuts_y, cuts_y


def fill(info_ref, rows, piece, source, first_p, first_y, r, c, bands, group):
    own = bands // group
    start = source * bands + (info_ref[0] ^ r) * own + c * chunk
    where = pl.ds(pl.multiple_of(start, chunk), chunk)
    for p in range(piece.shape[1]):
        rows[first_p + p, pl.ds(first_y, piece.shape[0]), where, :] = piece[:, p]


def gram(info, pieces, bands, bands_all):
    group = 1 + max(r for r, t, c in pieces)
    chunks = 1 + max(c for r, t, c in pieces)
    _, per_y, per_p, _, rows_z = next(iter(pieces.values()))[0].shape
    at_once = 2 if per_p % 2 == 0 else 1

    def kernel(info_ref, *refs):
        out, packed, rows = refs[len(pieces) :]
        parts = info_ref[4]
        i = pl.program_id(0)
        for (r, t, c), piece in zip(pieces, refs):
            source = lax.rem(info_ref[3] + parts - t, parts)
            fill(info_ref, rows, piece.at[0], source, 0, 0, r, c, bands, group)
            if t == 0:
                packed[c * group + r] = piece[0]
        block = jnp.concatenate(
            [rows[p, y] for p in range(at_once) for y in range(per_y)], axis=1
        )
        total = lax.dot_general(
            block, block, (((1,), (1,)), ((), ())), preferred_element_type=F32
        )

        @pl.when(i == 0)
        def _():
            out[...] = total

        @pl.when(i > 0)
        def _():
            out[...] += total

    def spec(index):
        return pl.BlockSpec(
            (1, per_y, at_once, chunk, rows_z), lambda i, info_ref: (index, 0, i, 0, 0)
        )

    return pl.pallas_call(
        kernel,
        grid_spec=pltpu.PrefetchScalarGridSpec(
            num_scalar_prefetch=1,
            grid=(per_p // at_once,),
            in_specs=[spec(index) for _, index in pieces.values()],
            out_specs=[
                pl.BlockSpec((bands_all, bands_all), lambda i, info_ref: (0, 0)),
                pl.BlockSpec(
                    (chunks * group, per_y, at_once, chunk, rows_z),
                    lambda i, info_ref: (0, 0, i, 0, 0),
                ),
            ],
            scratch_shapes=[pltpu.VMEM((at_once, per_y, bands_all, rows_z), BF16)],
        ),
        out_shape=[
            jax.ShapeDtypeStruct((bands_all, bands_all), F32),
            jax.ShapeDtypeStruct((chunks * group, per_y, per_p, chunk, rows_z), BF16),
        ],
        name="gram",
        **params(),
    )(info, *[value for value, _ in pieces.values()])


def inverse_factor(correlation):
    count = correlation.shape[0]
    half = count // 2

    def exact(a, b, transposed):
        dims = (((1,), (1 if transposed else 0,)), ((), ()))
        return lax.dot_general(
            a, b, dims, precision=lax.Precision.HIGHEST, preferred_element_type=F32
        )

    def eliminate(block):
        groups = half // 8
        row = lax.broadcasted_iota(jnp.int32, (8, half), 0)
        column = lax.broadcasted_iota(jnp.int32, (8, half), 1)
        left = [block[8 * g : 8 * g + 8] for g in range(groups)]
        right = [jnp.where(column == row + 8 * g, 1.0, 0.0).astype(F32) for g in range(groups)]
        for at in range(groups):
            later = range(at, groups)
            spread = [
                [
                    jnp.broadcast_to(left[g][:, 8 * at + k : 8 * at + k + 1], (8, half))
                    for g in later
                ]
                for k in range(8)
            ]
            factors, rows_left, rows_right = [], [], []
            for k in range(8):
                pivot = jnp.broadcast_to(spread[k][0][k : k + 1], (8, half))
                scale = lax.rsqrt(pivot)
                scale = scale * (1.5 - 0.5 * pivot * scale * scale)
                factor = [value * scale for value in spread[k]]
                for m in range(k + 1, 8):
                    other = jnp.broadcast_to(factor[0][m : m + 1], (8, half))
                    spread[m] = [value - f * other for value, f in zip(spread[m], factor)]
                row_left = jnp.broadcast_to(left[at][k : k + 1], (8, half)) * scale
                row_right = jnp.broadcast_to(right[at][k : k + 1], (8, half)) * scale
                inside = jnp.where(row > k, factor[0], 0.0)
                left[at] = jnp.where(row == k, row_left, left[at] - inside * row_left)
                right[at] = jnp.where(row == k, row_right, right[at] - inside * row_right)
                factors.append(factor)
                rows_left.append(row_left)
                rows_right.append(row_right)
            for g in range(at + 1, groups):
                for k in range(8):
                    left[g] = left[g] - factors[k][g - at] * rows_left[k]
                    right[g] = right[g] - factors[k][g - at] * rows_right[k]
        return jnp.concatenate(right, axis=0)

    def kernel(source, out):
        scale = source[...]
        top = eliminate(scale[:half, :half])
        below = exact(scale[half:, :half], top, True)
        rest = scale[half:, half:] - exact(below, below, True)
        bottom = eliminate(rest)
        out[:half, :half] = top.astype(BF16)
        out[:half, half:] = jnp.zeros((half, half), BF16)
        out[half:, :half] = (-exact(bottom, exact(below, top, False), False)).astype(BF16)
        out[half:, half:] = bottom.astype(BF16)

    return pl.pallas_call(
        kernel,
        out_shape=jax.ShapeDtypeStruct((count, count), BF16),
        name="inverse_factor",
        compiler_params=pltpu.CompilerParams(vmem_limit_bytes=vmem_bytes),
        cost_estimate=pl.CostEstimate(flops=1, bytes_accessed=1, transcendentals=0),
    )(correlation)


def rotate(info, rotation, pieces, bands, bands_all, planes, rows_y, only, before):
    group = 1 + max(r for r, t, u, c in pieces)
    _, per_y, per_p, _, rows_z = next(iter(pieces.values()))[0].shape
    swap = swap_matrix()
    cuts_y = rows_y // per_y
    at_once = 2 if only is not None and per_p % 2 == 0 else 1 if only is not None else per_p
    steps = per_p // at_once
    span = at_once if only is not None else planes
    given = [] if before is None else [before]
    arrays = {id(value): value for value, _ in pieces.values()}
    slots = {key: k for k, key in enumerate(arrays)}

    def kernel(info_ref, *refs):
        rotation_ref, swap_ref = refs[len(arrays) :][:2]
        out, rows, mixed = refs[-3:]
        me, parts = info_ref[3], info_ref[4]
        for (r, t, u, c), (value, index) in pieces.items():
            source = lax.rem(me + parts - t, parts)
            part = lax.rem(me + u, parts)
            first_p = 0 if only is not None else part // cuts_y * per_p
            first_y = 0 if only is not None else lax.rem(part, cuts_y) * per_y
            piece = refs[slots[id(value)]].at[index]
            fill(info_ref, rows, piece, source, first_p, first_y, r, c, bands, group)

        def plane(p):
            for y in range(0, rows_y, 2):
                pair = jnp.concatenate([rows[p, y], rows[p, y + 1]], axis=1)
                value = jnp.dot(rotation_ref[...], pair, preferred_element_type=F32)
                value = value.astype(BF16)
                for k in range(bands // 16):
                    for b in range(2):
                        mixed[k, y + b] = value[
                            16 * k : 16 * k + 16, b * rows_z : (b + 1) * rows_z
                        ]
            for k in range(0, bands // 16, 2):
                pair = [mixed[k + b].reshape(16 * rows_y, rows_z) for b in range(2)]
                moved = jnp.dot(
                    swap_ref[...], jnp.concatenate(pair, axis=1), preferred_element_type=F32
                ).astype(BF16)
                for b in range(2):
                    part = moved[:, b * rows_z : (b + 1) * rows_z].reshape(16, rows_y, rows_z)
                    out[16 * (k + b) : 16 * (k + b) + 16, p] = part

        if only is not None:
            for p in range(span):
                plane(p)
        else:
            pl.loop(0, span)(plane)

    def spec(value):
        return pl.BlockSpec(
            (value.shape[0], per_y, at_once, chunk, rows_z), lambda i, info_ref: (0, 0, i, 0, 0)
        )

    def out_index(i, info_ref):
        if only is None:
            return (0, 0, 0, 0)
        return (0, lax.rem(info_ref[3] + only, info_ref[4]) * steps + i, 0, 0)

    return pl.pallas_call(
        kernel,
        grid_spec=pltpu.PrefetchScalarGridSpec(
            num_scalar_prefetch=1,
            grid=(steps,),
            in_specs=[spec(value) for value in arrays.values()]
            + [
                pl.BlockSpec((bands, bands_all), lambda i, info_ref: (info_ref[3], 0)),
                pl.BlockSpec(swap.shape, lambda i, info_ref: (0, 0)),
            ]
            + [pl.BlockSpec(memory_space=pl.ANY)] * len(given),
            out_specs=pl.BlockSpec((bands, span, rows_y, rows_z), out_index),
            scratch_shapes=[
                pltpu.VMEM((span, rows_y, bands_all, rows_z), BF16),
                pltpu.VMEM((bands // 16, rows_y, 16, rows_z), BF16),
            ],
        ),
        out_shape=jax.ShapeDtypeStruct((bands, planes, rows_y, rows_z), BF16),
        input_output_aliases={3 + len(arrays): 0} if given else {},
        name="rotate",
        **params(),
    )(info, *arrays.values(), rotation, swap, *given)


def pairwise_sum(value, axis, count, low, high):
    bit = max(low, 1)
    while bit < high:
        value = value + lax.ppermute(value, axis, [(i, i ^ bit) for i in range(count)])
        bit *= 2
    return value


def body(orbital_block, block_scale, potential):
    bands, planes, rows_y, rows_z = orbital_block.shape
    parts, slabs = lax.axis_size("band"), lax.axis_size("domain")
    bands_all = bands * parts
    group = 4 if bands // 4 >= chunk else 2
    chunks = bands // group // chunk
    where, band = lax.axis_index("domain"), lax.axis_index("band")
    info = jnp.stack(
        [
            lax.rem(where, group),
            (where < group).astype(jnp.int32),
            (where >= slabs - group).astype(jnp.int32),
            band,
            jnp.int32(parts),
        ]
    ).astype(jnp.int32)

    def send(value, r, t):
        if r == 0 and t == 0:
            return value
        pairs = [
            (q * slabs + i, (q + t) % parts * slabs + (i ^ r))
            for q in range(parts)
            for i in range(slabs)
        ]
        return lax.ppermute(value, ("band", "domain"), pairs)

    scale = jnp.broadcast_to(block_scale[:, :, None], (bands, planes, rows_z))
    far_first = sorted(range(group), reverse=True)
    arrived = []
    for c in range(chunks):
        pieces = prepare(info, orbital_block, scale, potential, c, group, c == 0)
        sent = {r: send(pieces[r], r, 0) for r in far_first}
        arrived.append([sent[r] for r in range(group)])
    def after(value, *others):
        return lax.optimization_barrier((value, *others))[0]

    def shifted(value, by):
        pairs = [(i, i + by) for i in range(slabs) if 0 <= i + by < slabs]
        return lax.ppermute(value, "domain", pairs)

    sides = []
    for c in range(chunks):
        ups_downs = edges(info, arrived[c])
        sides.append([(shifted(up, group), shifted(down, -group)) for up, down in ups_downs])
        order = after(info, ups_downs[0][0])
    pieces, own, moved = {}, {}, {}
    for c in range(chunks):
        filtered = None
        for h in range(2):
            filtered = chebyshev(
                order, *sides[c][h], arrived[c], *sides[0][0], arrived[0], parts, filtered
            )
            order = after(info, filtered if h == 0 else filtered[0][0])
        for a in reversed(range(group // 2)):
            for t in reversed(range(parts)):
                value = filtered[a][t]
                own[(a, t, c)] = value
                if c > 0:
                    value = after(value, moved[(a, t, c - 1)])
                moved[(a, t, c)] = send(value, 2 * a, t)
        keys = [(a, t) for t in range(parts) for a in range(group // 2)]
        crossed = send(jnp.stack([moved[(a, t, c)][1] for a, t in keys]), 1, 0)
        for k, (a, t) in enumerate(keys):
            pieces[(2 * a, t, c)] = (moved[(a, t, c)], 0)
            pieces[(2 * a + 1, t, c)] = (crossed, k)

    total, buffer = gram(info, pieces, bands, bands_all)
    total = pairwise_sum(total, "band", parts, 0, parts)
    known = {(r, t, 0, c): value for (r, t, c), value in pieces.items()}

    def forward(buffer, t):
        for s in range(1, parts):
            if t != s:
                sent = lax.ppermute(buffer, "band", [(q, q + s) for q in range(parts - s)])
                for c in range(chunks):
                    for r in range(group):
                        known[(r, s, (t - s) % parts, c)] = (sent, c * group + r)

    forward(after(buffer, total), 0)
    total = pairwise_sum(total, "domain", slabs, 0, group)
    own = {key: after(value, total) for key, value in own.items()}
    total = pairwise_sum(total, "domain", slabs, group, slabs)
    rotation = inverse_factor(total / float(planes * rows_y * rows_z * slabs))
    for t in range(1, parts):
        keys = [(a, c) for c in range(chunks) for a in range(group // 2)]
        rest = {(a, c): send(own[(a, t, c)], 2 * a, 0) for a, c in keys}
        crossed = send(jnp.stack([after(rest[key], rotation)[1] for key in keys]), 1, 0)
        for k, (a, c) in enumerate(keys):
            known[(2 * a, 0, t, c)] = (rest[(a, c)], 0)
            known[(2 * a + 1, 0, t, c)] = (crossed, k)
        if parts > 2:
            chosen = [known[(r, 0, t, c)] for c in range(chunks) for r in range(group)]
            forward(jnp.stack([value[index] for value, index in chosen]), t)
    out = None
    for only in range(parts) if parts == 2 and planes % 2 == 0 else [None]:
        chosen = {key: value for key, value in known.items() if only in (None, key[2])}
        out = rotate(info, rotation, chosen, bands, bands_all, planes, rows_y, only, out)
    return out


def solution(mesh):
    in_specs = (P("band", "domain", None, None), P("band", "domain"), P("domain", None, None))
    out_specs = P("band", "domain", None, None)
    return jax.shard_map(body, mesh=mesh, in_specs=in_specs, out_specs=out_specs, check_vma=False)
```

```python
import math

import jax
import jax.numpy as jnp
import numpy as np
from jax import lax
from jax.experimental import pallas as pl
from jax.experimental.pallas import tpu as pltpu
from jax.sharding import PartitionSpec as P

grid_step = 0.5
stencil_coef = (
    -5369.0 / 1800.0,
    12.0 / 7.0,
    -15.0 / 56.0,
    10.0 / 189.0,
    -1.0 / 112.0,
    2.0 / 1925.0,
    -1.0 / 16632.0,
)
lower_end = -4.0
cut_energy = 6.0
upper_end = 43.0
kinetic = -0.5 / (grid_step * grid_step)
coef_scale = 7.0
reach = 6
edge = 3 * reach
chunk = 16
F32, BF16 = jnp.float32, jnp.bfloat16
vmem_bytes = 50 * 2**20


def filter_terms():
    width_e = (upper_end - cut_energy) / 2.0
    centre = (upper_end + cut_energy) / 2.0
    sigma_one = width_e / (lower_end - centre)
    gamma_term = 2.0 / sigma_one
    sigma_two = 1.0 / (gamma_term - sigma_one)
    sigma_three = 1.0 / (gamma_term - sigma_two)
    return (width_e, centre, sigma_one, sigma_two, sigma_three)


def stencil_line(count):
    line = np.zeros((count, count), np.float64)
    for offset in range(1, reach + 1):
        value = kinetic * stencil_coef[offset] * coef_scale
        line += value * (np.eye(count, k=offset) + np.eye(count, k=-offset))
    return line


def xy_matrix(planes, rows_y):
    along_x = np.zeros((planes, planes + 2 * reach), np.float64)
    along_x[:, :] = stencil_line(planes + 2 * reach)[reach : reach + planes]
    middle = np.eye(planes, planes + 2 * reach, k=reach)
    full = np.kron(along_x, np.eye(rows_y)) + np.kron(middle, stencil_line(rows_y))
    return jnp.asarray(full, BF16)


def z_matrix(count_z):
    return jnp.asarray(np.kron(np.eye(2), stencil_line(count_z)), BF16)


def swap_matrix():
    full = np.zeros((256, 256), np.float32)
    for a in range(16):
        for b in range(16):
            full[a * 16 + b, b * 16 + a] = 1.0
    return jnp.asarray(full, BF16)


def params(flops=1):
    return dict(
        compiler_params=pltpu.CompilerParams(
            vmem_limit_bytes=vmem_bytes, dimension_semantics=("arbitrary",)
        ),
        cost_estimate=pl.CostEstimate(flops=flops, bytes_accessed=1, transcendentals=0),
    )


def prepare(info, orbitals, scale, potential, part, group, with_potential):
    bands, planes, rows_y, rows_z = orbitals.shape
    own = bands // group
    at_once = 8
    steps = chunk // at_once
    total = chunk + (2 if with_potential else 0)

    def kernel(info_ref, *refs):
        sources, scales, potential_ref = refs[:group], refs[group : 2 * group], refs[2 * group]
        outs = refs[2 * group + 1 :]
        i = pl.program_id(0)
        for r in range(group):
            for b in range(at_once):
                value = sources[r][b].astype(F32) * scales[r][b][:, None, :]
                outs[r][i * at_once + b] = value.astype(BF16)

        if with_potential:

            @pl.when(i == 0)
            def _():
                high = potential_ref[...].astype(BF16)
                low = (potential_ref[...] - high.astype(F32)).astype(BF16)
                for r in range(group):
                    outs[r][chunk] = high
                    outs[r][chunk + 1] = low

    def first(r, i, info_ref):
        return ((info_ref[0] ^ r) * own + part * chunk) // at_once + i

    def source_spec(r):
        return pl.BlockSpec(
            (at_once, planes, rows_y, rows_z),
            lambda i, info_ref: (first(r, i, info_ref), 0, 0, 0),
        )

    def scale_spec(r):
        return pl.BlockSpec(
            (at_once, planes, rows_z), lambda i, info_ref: (first(r, i, info_ref), 0, 0)
        )

    shape = jax.ShapeDtypeStruct((total, planes, rows_y, rows_z), BF16)
    return pl.pallas_call(
        kernel,
        grid_spec=pltpu.PrefetchScalarGridSpec(
            num_scalar_prefetch=1,
            grid=(steps,),
            in_specs=[source_spec(r) for r in range(group)]
            + [scale_spec(r) for r in range(group)]
            + [pl.BlockSpec((planes, rows_y, rows_z), lambda i, info_ref: (0, 0, 0))],
            out_specs=[pl.BlockSpec(shape.shape, lambda i, info_ref: (0, 0, 0, 0))] * group,
        ),
        out_shape=[shape] * group,
        name="prepare",
        **params(),
    )(info, *([orbitals] * group), *([scale] * group), potential)


def edges(info, pieces, cuts):
    group = len(pieces)
    total, planes, rows_y, rows_z = pieces[0].shape
    rest = edge - planes
    width = edge // cuts
    at_once = 6 if total % 6 == 0 else 4

    def kernel(info_ref, *refs):
        sources, outs = refs[:group], refs[group:]

        def put(targets, to, source, begin, count):
            while count:
                size = min(count, width - to % width)
                target = targets[to // width]
                target[:, to % width : to % width + size] = source[:, begin : begin + size]
                to, begin, count = to + size, begin + size, count - size

        for odd in range(2):
            up, down = (outs[k * cuts : (k + 1) * cuts] for k in (odd, 1 - odd))
            for r in range(group):
                slab = jnp.where(info_ref[5] == odd, info_ref[0] ^ r, -1)

                @pl.when(slab == group - 1)
                def _():
                    put(up, rest, sources[r], 0, planes)

                @pl.when(slab == group - 2)
                def _():
                    put(up, 0, sources[r], planes - rest, rest)

                @pl.when(slab == 0)
                def _():
                    put(down, 0, sources[r], 0, planes)

                @pl.when(slab == 1)
                def _():
                    put(down, planes, sources[r], 0, rest)

    def spec(count):
        return pl.BlockSpec((at_once, count, rows_y, rows_z), lambda i, info_ref: (i, 0, 0, 0))

    flat = pl.pallas_call(
        kernel,
        grid_spec=pltpu.PrefetchScalarGridSpec(
            num_scalar_prefetch=1,
            grid=(total // at_once,),
            in_specs=[spec(planes)] * group,
            out_specs=[spec(width)] * (2 * cuts),
        ),
        out_shape=[jax.ShapeDtypeStruct((total, width, rows_y, rows_z), BF16)] * (2 * cuts),
        name="edges",
        **params(),
    )(info, *pieces)
    return flat[:cuts], flat[cuts:]


def chebyshev(info, sides, pieces, sides_pot, pieces_pot, parts):
    group = len(pieces)
    _, planes, rows_y, rows_z = pieces[0].shape
    slab = group * planes
    per_p, per_y, cuts_y = shares(planes, rows_y, parts)
    at_once = 2 if per_p % 2 == 0 else 1
    steps = chunk // 2
    count_out = group // 2 * parts
    flat_sides, flat_pot = ([value for side in both for value in side] for both in (sides, sides_pot))
    cuts, cuts_pot = len(sides[0]), len(sides_pot[0])
    width, width_pot = edge // cuts, edge // cuts_pot
    width_e, centre, sigma_one, sigma_two, sigma_three = filter_terms()
    diagonal = 3.0 * stencil_coef[0] * kinetic - centre
    tile_rows = planes * rows_y
    xy, zz, swap = xy_matrix(planes, rows_y), z_matrix(rows_z), swap_matrix()
    count_0, count_1, count_2 = slab + 6 * reach, slab + 4 * reach, slab + 2 * reach

    def kernel(info_ref, *refs):
        side_refs, refs = refs[: 2 * cuts], refs[2 * cuts :]
        side_pot_refs, refs = refs[: 2 * cuts_pot], refs[2 * cuts_pot :]
        piece_refs, pot_refs = refs[:group], refs[group : 2 * group]
        xy_ref, zz_ref, swap_ref = refs[2 * group : 3 + 2 * group]
        outs = refs[3 + 2 * group : 3 + 2 * group + count_out]
        field, first, second, energy, result = refs[3 + 2 * group + count_out :]
        i = pl.program_id(0)
        me = info_ref[0]
        at_left, at_right = info_ref[1] == 1, info_ref[2] == 1

        @pl.when(i == 0)
        def _():
            def store(start, source):
                total = source[0].astype(F32) + source[1].astype(F32)
                energy[pl.ds(start, source.shape[1])] = coef_scale * (total + diagonal)

            for side, base, low, high in (
                (side_pot_refs[cuts_pot:], -reach, 0, 2 * reach),
                (side_pot_refs[:cuts_pot], slab + 2 * reach, slab + 2 * reach, count_1),
            ):
                for k, ref in enumerate(side):
                    start = base + k * width_pot
                    begin, end = max(start, low), min(start + width_pot, high)
                    if begin < end:
                        store(begin, ref.at[:, begin - start : end - start])
            for r in range(group):
                store(2 * reach + planes * (me ^ r), pot_refs[r])

        for b in range(2):
            lanes = slice(b * rows_z, (b + 1) * rows_z)
            for k in range(2):
                start = (1 - (info_ref[5] ^ k)) * (edge + slab)
                for n in range(cuts):
                    where = pl.ds(start + n * width, width)
                    field[where, :, lanes] = side_refs[k * cuts + n][b]
            for r in range(group):
                field[pl.ds(edge + planes * (me ^ r), planes), :, lanes] = piece_refs[r][b]

        def apply(source, start, energy_start):
            rows = source[pl.ds(start, planes + 2 * reach)].reshape(-1, 2 * rows_z)
            middle = source[pl.ds(start + reach, planes)].reshape(tile_rows, 2 * rows_z)
            total = jnp.dot(xy_ref[...], rows, preferred_element_type=F32)
            total += jnp.dot(middle, zz_ref[...], preferred_element_type=F32)
            factor = energy[pl.ds(energy_start, planes)].reshape(tile_rows, rows_z)
            factor = jnp.concatenate([factor, factor], axis=1)
            return total + factor * middle.astype(F32)

        def block(value):
            return value.astype(BF16).reshape(planes, rows_y, 2 * rows_z)

        def previous(source, start):
            return source[pl.ds(start, planes)].reshape(tile_rows, 2 * rows_z).astype(F32)

        for t in range(count_1 // planes):
            at = t * planes
            value = apply(field, at, at) * (sigma_one / width_e / coef_scale)
            first[at : at + planes] = block(value)

        @pl.when(at_left)
        def _():
            first[: 2 * reach] = jnp.zeros((2 * reach, rows_y, 2 * rows_z), BF16)

        @pl.when(at_right)
        def _():
            first[count_1 - 2 * reach :] = jnp.zeros((2 * reach, rows_y, 2 * rows_z), BF16)

        for t in range(count_2 // planes):
            at = t * planes
            value = apply(first, at, at + reach) * (2.0 * sigma_two / width_e / coef_scale)
            value -= sigma_one * sigma_two * previous(field, at + 2 * reach)
            second[at : at + planes] = block(value)

        @pl.when(at_left)
        def _():
            second[:reach] = jnp.zeros((reach, rows_y, 2 * rows_z), BF16)

        @pl.when(at_right)
        def _():
            second[count_2 - reach :] = jnp.zeros((reach, rows_y, 2 * rows_z), BF16)

        for t in range(group):
            at = t * planes
            value = apply(second, at, at + 2 * reach) * (2.0 * sigma_three / width_e / coef_scale)
            value -= sigma_two * sigma_three * previous(first, at + 2 * reach)
            value = block(value)
            for b in range(2):
                part = value[:, :, b * rows_z : (b + 1) * rows_z]
                result[at : at + planes, 2 * i + b] = part

        @pl.when(i == steps - 1)
        def _():
            for t in range(parts):
                part = lax.rem(info_ref[3] + t, parts)
                begin = lax.rem(part, cuts_y) * (per_y * chunk)
                begin = pl.multiple_of(begin, per_y * chunk)
                for r in range(group):
                    start = planes * (me ^ r) + part // cuts_y * per_p
                    for p in range(0, per_p, at_once):
                        pair = [
                            result[start + p + k].reshape(chunk * rows_y, rows_z)
                            for k in range(at_once)
                        ]
                        moved = jnp.dot(
                            swap_ref[pl.ds(begin, per_y * chunk), :],
                            jnp.concatenate(pair, axis=1),
                            preferred_element_type=F32,
                        ).astype(BF16)
                        for k in range(at_once):
                            value = moved[:, k * rows_z : (k + 1) * rows_z]
                            out = outs[r // 2 * parts + t]
                            out[r % 2, :, p + k] = value.reshape(per_y, chunk, rows_z)

    def block_spec(count, index):
        return pl.BlockSpec((2, count, rows_y, rows_z), index)

    def whole_spec(shape):
        return pl.BlockSpec(shape, lambda i, info_ref: (0,) * len(shape))

    moving = lambda i, info_ref: (i, 0, 0, 0)
    fixed = lambda i, info_ref: (steps, 0, 0, 0)
    shape = jax.ShapeDtypeStruct((2, per_y, per_p, chunk, rows_z), BF16)
    flat = pl.pallas_call(
        kernel,
        grid_spec=pltpu.PrefetchScalarGridSpec(
            num_scalar_prefetch=1,
            grid=(steps,),
            in_specs=[block_spec(width, moving)] * (2 * cuts)
            + [block_spec(width_pot, fixed)] * (2 * cuts_pot)
            + [block_spec(planes, moving)] * group
            + [block_spec(planes, fixed)] * group
            + [whole_spec(xy.shape), whole_spec(zz.shape), whole_spec(swap.shape)],
            out_specs=[whole_spec(shape.shape)] * count_out,
            scratch_shapes=[
                pltpu.VMEM((count_0, rows_y, 2 * rows_z), BF16),
                pltpu.VMEM((count_1, rows_y, 2 * rows_z), BF16),
                pltpu.VMEM((count_2, rows_y, 2 * rows_z), BF16),
                pltpu.VMEM((count_1, rows_y, rows_z), F32),
                pltpu.VMEM((slab, chunk, rows_y, rows_z), BF16),
            ],
        ),
        out_shape=[shape] * count_out,
        name="chebyshev",
        **params(),
    )(info, *flat_sides, *flat_pot, *pieces, *pieces_pot, xy, zz, swap)
    return [flat[a * parts : (a + 1) * parts] for a in range(group // 2)]


def shares(planes, rows_y, parts):
    cuts_p = math.gcd(planes, parts)
    cuts_y = parts // cuts_p
    return planes // cuts_p, rows_y // cuts_y, cuts_y


def fill(info_ref, rows, piece, source, first_p, first_y, r, c, bands, group):
    own = bands // group
    start = source * bands + (info_ref[0] ^ r) * own + c * chunk
    where = pl.ds(pl.multiple_of(start, chunk), chunk)
    for p in range(piece.shape[1]):
        rows[first_p + p, pl.ds(first_y, piece.shape[0]), where, :] = piece[:, p]


def gram(info, pieces, packs, bands, bands_all):
    group = 1 + max(r for r, t, c in pieces)
    _, per_y, per_p, _, rows_z = next(iter(pieces.values()))[0].shape
    at_once = 2 if per_p % 2 == 0 else 1
    steps = per_p // at_once
    half = bands_all // 2

    def kernel(info_ref, *refs):
        mine, other, packed, rows, out = refs[len(pieces) :]
        parts = info_ref[4]
        i = pl.program_id(0)
        for (r, t, c), piece in zip(pieces, refs):
            source = lax.rem(info_ref[3] + parts - t, parts)
            fill(info_ref, rows, piece.at[0], source, 0, 0, r, c, bands, group)
            if t == 0 and (r, c) in packs:
                packed[packs.index((r, c))] = piece[0]
        block = jnp.concatenate(
            [rows[p, y] for p in range(at_once) for y in range(per_y)], axis=1
        )
        total = lax.dot_general(
            block, block, (((1,), (1,)), ((), ())), preferred_element_type=F32
        )

        total = [total[:half, :half], total[half:, :half], total[half:, half:]]
        total = jnp.concatenate(total, axis=1)

        @pl.when(i == 0)
        def _():
            out[...] = total

        @pl.when(i > 0)
        def _():
            out[...] += total

        @pl.when(i == steps - 1)
        def _():
            for ref, core in ((mine, info_ref[0] & 1), (other, 1 - (info_ref[0] & 1))):
                ref[...] = out[pl.ds(pl.multiple_of(core * (half // 2), half // 2), half // 2)]

    def spec(index):
        return pl.BlockSpec(
            (1, per_y, at_once, chunk, rows_z), lambda i, info_ref: (index, 0, i, 0, 0)
        )

    return pl.pallas_call(
        kernel,
        grid_spec=pltpu.PrefetchScalarGridSpec(
            num_scalar_prefetch=1,
            grid=(steps,),
            in_specs=[spec(index) for _, index in pieces.values()],
            out_specs=[pl.BlockSpec((half // 2, 3 * half), lambda i, info_ref: (0, 0))] * 2
            + [
                pl.BlockSpec(
                    (len(packs), per_y, at_once, chunk, rows_z),
                    lambda i, info_ref: (0, 0, i, 0, 0),
                ),
            ],
            scratch_shapes=[
                pltpu.VMEM((at_once, per_y, bands_all, rows_z), BF16),
                pltpu.VMEM((half, 3 * half), F32),
            ],
        ),
        out_shape=[jax.ShapeDtypeStruct((half // 2, 3 * half), F32)] * 2
        + [jax.ShapeDtypeStruct((len(packs), per_y, per_p, chunk, rows_z), BF16)],
        name="gram",
        **params(),
    )(info, *[value for value, _ in pieces.values()])


def inverse_factor(info, mine, other, cells):
    half = 2 * mine.shape[0]
    count = 2 * half

    def exact(a, b, transposed):
        dims = (((1,), (1 if transposed else 0,)), ((), ()))
        return lax.dot_general(
            a, b, dims, precision=lax.Precision.HIGHEST, preferred_element_type=F32
        )

    def eliminate(block):
        groups = half // 8
        row = lax.broadcasted_iota(jnp.int32, (8, half), 0)
        column = lax.broadcasted_iota(jnp.int32, (8, half), 1)
        left = [block[8 * g : 8 * g + 8] for g in range(groups)]
        right = [jnp.where(column == row + 8 * g, 1.0, 0.0).astype(F32) for g in range(groups)]
        for at in range(groups):
            later = range(at, groups)
            spread = [
                [
                    jnp.broadcast_to(left[g][:, 8 * at + k : 8 * at + k + 1], (8, half))
                    for g in later
                ]
                for k in range(8)
            ]
            factors, rows_left, rows_right = [], [], []
            for k in range(8):
                pivot = jnp.broadcast_to(spread[k][0][k : k + 1], (8, half))
                scale = lax.rsqrt(pivot)
                scale = scale * (1.5 - 0.5 * pivot * scale * scale)
                factor = [value * scale for value in spread[k]]
                for m in range(k + 1, 8):
                    other = jnp.broadcast_to(factor[0][m : m + 1], (8, half))
                    spread[m] = [value - f * other for value, f in zip(spread[m], factor)]
                row_left = jnp.broadcast_to(left[at][k : k + 1], (8, half)) * scale
                row_right = jnp.broadcast_to(right[at][k : k + 1], (8, half)) * scale
                inside = jnp.where(row > k, factor[0], 0.0)
                left[at] = jnp.where(row == k, row_left, left[at] - inside * row_left)
                right[at] = jnp.where(row == k, row_right, right[at] - inside * row_right)
                factors.append(factor)
                rows_left.append(row_left)
                rows_right.append(row_right)
            for g in range(at + 1, groups):
                for k in range(8):
                    left[g] = left[g] - factors[k][g - at] * rows_left[k]
                    right[g] = right[g] - factors[k][g - at] * rows_right[k]
        return jnp.concatenate(right, axis=0)

    def kernel(info_ref, mine_ref, other_ref, out, blocks):
        for ref, core in ((mine_ref, info_ref[0] & 1), (other_ref, 1 - (info_ref[0] & 1))):
            where = pl.ds(pl.multiple_of(core * (half // 2), half // 2), half // 2)
            blocks[where] = ref[...] * (1.0 / cells)
        top = eliminate(blocks[:, :half])
        below = exact(blocks[:, half:count], top, True)
        rest = blocks[:, count:] - exact(below, below, True)
        bottom = eliminate(rest)
        out[:half, :half] = top.astype(BF16)
        out[:half, half:] = jnp.zeros((half, half), BF16)
        out[half:, :half] = (-exact(bottom, exact(below, top, False), False)).astype(BF16)
        out[half:, half:] = bottom.astype(BF16)

    return pl.pallas_call(
        kernel,
        grid_spec=pltpu.PrefetchScalarGridSpec(
            num_scalar_prefetch=1,
            grid=(1,),
            in_specs=[pl.BlockSpec(mine.shape, lambda i, info_ref: (0, 0))] * 2,
            out_specs=pl.BlockSpec((count, count), lambda i, info_ref: (0, 0)),
            scratch_shapes=[pltpu.VMEM((half, 3 * half), F32)],
        ),
        out_shape=jax.ShapeDtypeStruct((count, count), BF16),
        name="inverse_factor",
        **params(),
    )(info, mine, other)


def rotate(info, rotation, pieces, bands, bands_all, planes, rows_y, only, before):
    group = 1 + max(r for r, t, u, c in pieces)
    _, per_y, per_p, _, rows_z = next(iter(pieces.values()))[0].shape
    swap = swap_matrix()
    cuts_y = rows_y // per_y
    at_once = 2 if only is not None and per_p % 2 == 0 else 1 if only is not None else per_p
    steps = per_p // at_once
    span = at_once if only is not None else planes
    given = [] if before is None else [before]
    arrays = {id(value): value for value, _ in pieces.values()}
    slots = {key: k for k, key in enumerate(arrays)}

    def kernel(info_ref, *refs):
        rotation_ref, swap_ref = refs[len(arrays) :][:2]
        out, rows, mixed = refs[-3:]
        me, parts = info_ref[3], info_ref[4]
        for (r, t, u, c), (value, index) in pieces.items():
            source = lax.rem(me + parts - t, parts)
            part = lax.rem(me + u, parts)
            first_p = 0 if only is not None else part // cuts_y * per_p
            first_y = 0 if only is not None else lax.rem(part, cuts_y) * per_y
            piece = refs[slots[id(value)]].at[index]
            fill(info_ref, rows, piece, source, first_p, first_y, r, c, bands, group)

        def plane(p):
            for y in range(0, rows_y, 2):
                pair = jnp.concatenate([rows[p, y], rows[p, y + 1]], axis=1)
                value = jnp.dot(rotation_ref[...], pair, preferred_element_type=F32)
                value = value.astype(BF16)
                for k in range(bands // 16):
                    for b in range(2):
                        mixed[k, y + b] = value[
                            16 * k : 16 * k + 16, b * rows_z : (b + 1) * rows_z
                        ]
            for k in range(0, bands // 16, 2):
                pair = [mixed[k + b].reshape(16 * rows_y, rows_z) for b in range(2)]
                moved = jnp.dot(
                    swap_ref[...], jnp.concatenate(pair, axis=1), preferred_element_type=F32
                ).astype(BF16)
                for b in range(2):
                    part = moved[:, b * rows_z : (b + 1) * rows_z].reshape(16, rows_y, rows_z)
                    out[16 * (k + b) : 16 * (k + b) + 16, p] = part

        if only is not None:
            for p in range(span):
                plane(p)
        else:
            pl.loop(0, span)(plane)

    def spec(value):
        return pl.BlockSpec(
            (value.shape[0], per_y, at_once, chunk, rows_z), lambda i, info_ref: (0, 0, i, 0, 0)
        )

    def out_index(i, info_ref):
        if only is None:
            return (0, 0, 0, 0)
        return (0, lax.rem(info_ref[3] + only, info_ref[4]) * steps + i, 0, 0)

    return pl.pallas_call(
        kernel,
        grid_spec=pltpu.PrefetchScalarGridSpec(
            num_scalar_prefetch=1,
            grid=(steps,),
            in_specs=[spec(value) for value in arrays.values()]
            + [
                pl.BlockSpec((bands, bands_all), lambda i, info_ref: (info_ref[3], 0)),
                pl.BlockSpec(swap.shape, lambda i, info_ref: (0, 0)),
            ]
            + [pl.BlockSpec(memory_space=pl.ANY)] * len(given),
            out_specs=pl.BlockSpec((bands, span, rows_y, rows_z), out_index),
            scratch_shapes=[
                pltpu.VMEM((span, rows_y, bands_all, rows_z), BF16),
                pltpu.VMEM((bands // 16, rows_y, 16, rows_z), BF16),
            ],
        ),
        out_shape=jax.ShapeDtypeStruct((bands, planes, rows_y, rows_z), BF16),
        input_output_aliases={3 + len(arrays): 0} if given else {},
        name="rotate",
        **params(),
    )(info, *arrays.values(), rotation, swap, *given)


def pairwise_sum(value, axis, count, low, high):
    bit = max(low, 1)
    while bit < high:
        value = value + lax.ppermute(value, axis, [(i, i ^ bit) for i in range(count)])
        bit *= 2
    return value


def body(orbital_block, block_scale, potential):
    bands, planes, rows_y, rows_z = orbital_block.shape
    parts, slabs = lax.axis_size("band"), lax.axis_size("domain")
    bands_all = bands * parts
    group = 4 if bands // 4 >= chunk else 2
    chunks = bands // group // chunk
    where, band = lax.axis_index("domain"), lax.axis_index("band")
    info = jnp.stack(
        [
            lax.rem(where, group),
            (where < group).astype(jnp.int32),
            (where >= slabs - group).astype(jnp.int32),
            band,
            jnp.int32(parts),
            jnp.int32(0),
        ]
    ).astype(jnp.int32)
    paired = info.at[5].set(lax.rem(where // group, 2))

    def send(value, r, t):
        if r == 0 and t == 0:
            return value
        pairs = [
            (q * slabs + i, (q + t) % parts * slabs + (i ^ r))
            for q in range(parts)
            for i in range(slabs)
        ]
        return lax.ppermute(value, ("band", "domain"), pairs)

    scale = jnp.broadcast_to(block_scale[:, :, None], (bands, planes, rows_z))
    far_first = sorted(range(group), reverse=True)
    arrived = []
    for c in range(chunks):
        pieces = prepare(info, orbital_block, scale, potential, c, group, c == 0)
        sent = {r: send(pieces[r], r, 0) for r in far_first}
        arrived.append([sent[r] for r in range(group)])
    def after(value, *others):
        return lax.optimization_barrier((value, *others))[0]

    def swapped(value, odd):
        lower = [i for i in range(slabs - group) if i // group % 2 == odd]
        pairs = [(i, i + group) for i in lower] + [(i + group, i) for i in lower]
        return lax.ppermute(value, "domain", pairs)

    def shifted(value, by):
        pairs = [(i, i + by) for i in range(slabs) if 0 <= i + by < slabs]
        return lax.ppermute(value, "domain", pairs)

    sides = []
    for c in range(chunks):
        first, second = edges(paired if c else info, arrived[c], 1 if c else 2)
        if c == 0:
            sides.append(
                [[shifted(end, -group) for end in second], [shifted(end, group) for end in first]]
            )
        else:
            sides.append([[swapped(end, 0) for end in first], [swapped(end, 1) for end in second]])
        last_end = first[0]
    pieces, own, moved, crossed = {}, {}, {}, {}
    ready = [last_end]
    for c in range(chunks):
        order = after(paired if c else info, *ready)
        filtered = chebyshev(order, sides[c], arrived[c], sides[0], arrived[0], parts)
        ready = [filtered[0][0]]
        for a in reversed(range(group // 2)):
            for t in reversed(range(parts)):
                value = filtered[a][t]
                own[(a, t, c)] = value
                if c > 0:
                    value = after(value, moved[(a, t, c - 1)])
                moved[(a, t, c)] = send(value, 2 * a, t)
        keys = [(a, t) for t in range(parts) for a in range(group // 2)]
        crossed[c] = send(jnp.stack([moved[(a, t, c)][1] for a, t in keys]), 1, 0)
        for k, (a, t) in enumerate(keys):
            pieces[(2 * a, t, c)] = (moved[(a, t, c)], 0)
            pieces[(2 * a + 1, t, c)] = (crossed[c], k)

    known = {(r, t, 0, c): value for (r, t, c), value in pieces.items()}
    late = {}
    last = [value for (a, t, c), value in moved.items() if c == chunks - 1]
    early = parts == 2 and chunks > 1
    if early:
        late[(group // 2 - 1, 1, 0)] = send(after(own[(group // 2 - 1, 1, 0)], *last), group - 2, 0)
        sent = lax.ppermute(after(crossed[0], *last)[: group // 2], "band", [(0, 1)])
        for a in range(group // 2):
            known[(2 * a + 1, 1, 1, 0)] = (sent, a)
    packs = [
        (r, c)
        for c in range(chunks)
        for r in range(group)
        if (r, 1, 1, c) not in known or parts > 2
    ]
    mine, other, buffer = gram(info, pieces, packs, bands, bands_all)
    mine = mine + send(other, 1, 0)
    if early:
        mine = after(mine, sent, *late.values())
    mine = pairwise_sum(mine, "band", parts, 0, parts)

    def forward(buffer, t, packs):
        for s in range(1, parts):
            if t != s:
                sent = lax.ppermute(buffer, "band", [(q, q + s) for q in range(parts - s)])
                for k, (r, c) in enumerate(packs):
                    known[(r, s, (t - s) % parts, c)] = (sent, k)

    forward(after(buffer, mine), 0, packs)
    mine = pairwise_sum(mine, "domain", slabs, 2, group)
    for key, value in own.items():
        if key[1] > 0 and key not in late:
            late[key] = send(after(value, mine), 2 * key[0], 0)
    mine = pairwise_sum(mine, "domain", slabs, group, slabs)
    rotation = inverse_factor(info, mine, send(mine, 1, 0), planes * rows_y * rows_z * slabs)
    for t in range(1, parts):
        keys = [(a, c) for c in range(chunks) for a in range(group // 2)]
        far = send(jnp.stack([after(late[(a, t, c)], rotation)[1] for a, c in keys]), 1, 0)
        for k, (a, c) in enumerate(keys):
            known[(2 * a, 0, t, c)] = (late[(a, t, c)], 0)
            known[(2 * a + 1, 0, t, c)] = (far, k)
        if parts > 2:
            chosen = [known[(r, 0, t, c)] for r, c in packs]
            forward(jnp.stack([value[index] for value, index in chosen]), t, packs)
    out = None
    for only in range(parts) if parts == 2 and planes % 2 == 0 else [None]:
        chosen = {key: value for key, value in known.items() if only in (None, key[2])}
        out = rotate(info, rotation, chosen, bands, bands_all, planes, rows_y, only, out)
    return out


def solution(mesh):
    in_specs = (P("band", "domain", None, None), P("band", "domain"), P("domain", None, None))
    out_specs = P("band", "domain", None, None)
    return jax.shard_map(body, mesh=mesh, in_specs=in_specs, out_specs=out_specs, check_vma=False)
```

```python
import math

import jax
import jax.numpy as jnp
import numpy as np
from jax import lax
from jax.experimental import pallas as pl
from jax.experimental.pallas import tpu as pltpu
from jax.sharding import PartitionSpec as P

grid_step = 0.5
stencil_coef = (
    -5369.0 / 1800.0,
    12.0 / 7.0,
    -15.0 / 56.0,
    10.0 / 189.0,
    -1.0 / 112.0,
    2.0 / 1925.0,
    -1.0 / 16632.0,
)
lower_end = -4.0
cut_energy = 6.0
upper_end = 43.0
kinetic = -0.5 / (grid_step * grid_step)
coef_scale = 7.0
reach = 6
edge = 3 * reach
chunk = 16
F32, BF16 = jnp.float32, jnp.bfloat16


def filter_terms():
    width_e = (upper_end - cut_energy) / 2.0
    centre = (upper_end + cut_energy) / 2.0
    sigma_one = width_e / (lower_end - centre)
    gamma_term = 2.0 / sigma_one
    sigma_two = 1.0 / (gamma_term - sigma_one)
    sigma_three = 1.0 / (gamma_term - sigma_two)
    return (width_e, centre, sigma_one, sigma_two, sigma_three)


def stencil_line(count):
    line = np.zeros((count, count), np.float64)
    for offset in range(1, reach + 1):
        value = kinetic * stencil_coef[offset] * coef_scale
        line += value * (np.eye(count, k=offset) + np.eye(count, k=-offset))
    return line


def xy_matrix(planes, rows_y):
    along_x = np.zeros((planes, planes + 2 * reach), np.float64)
    along_x[:, :] = stencil_line(planes + 2 * reach)[reach : reach + planes]
    middle = np.eye(planes, planes + 2 * reach, k=reach)
    full = np.kron(along_x, np.eye(rows_y)) + np.kron(middle, stencil_line(rows_y))
    return jnp.asarray(full, BF16)


def z_matrix(count_z):
    return jnp.asarray(np.kron(np.eye(2), stencil_line(count_z)), BF16)


def swap_matrix():
    full = np.zeros((256, 256), np.float32)
    for a in range(16):
        for b in range(16):
            full[a * 16 + b, b * 16 + a] = 1.0
    return jnp.asarray(full, BF16)


def params(mebibytes):
    return dict(
        compiler_params=pltpu.CompilerParams(
            vmem_limit_bytes=mebibytes * 2**20, dimension_semantics=("arbitrary",)
        ),
        cost_estimate=pl.CostEstimate(flops=1, bytes_accessed=1, transcendentals=0),
    )


def prepare(info, orbitals, scale, potential, part, group, with_potential):
    bands, planes, rows_y, rows_z = orbitals.shape
    own = bands // group
    at_once = 8
    steps = chunk // at_once
    total = chunk + (2 if with_potential else 0)

    def kernel(info_ref, *refs):
        sources, scales, potential_ref = refs[:group], refs[group : 2 * group], refs[2 * group]
        outs = refs[2 * group + 1 :]
        i = pl.program_id(0)
        for r in range(group):
            for b in range(at_once):
                value = sources[r][b].astype(F32) * scales[r][b][:, None, :]
                outs[r][i * at_once + b] = value.astype(BF16)

        if with_potential:

            @pl.when(i == 0)
            def _():
                high = potential_ref[...].astype(BF16)
                low = (potential_ref[...] - high.astype(F32)).astype(BF16)
                for r in range(group):
                    outs[r][chunk] = high
                    outs[r][chunk + 1] = low

    def first(r, i, info_ref):
        return ((info_ref[0] ^ r) * own + part * chunk) // at_once + i

    def source_spec(r):
        return pl.BlockSpec(
            (at_once, planes, rows_y, rows_z),
            lambda i, info_ref: (first(r, i, info_ref), 0, 0, 0),
        )

    def scale_spec(r):
        return pl.BlockSpec(
            (at_once, planes, rows_z), lambda i, info_ref: (first(r, i, info_ref), 0, 0)
        )

    shape = jax.ShapeDtypeStruct((total, planes, rows_y, rows_z), BF16)
    return pl.pallas_call(
        kernel,
        grid_spec=pltpu.PrefetchScalarGridSpec(
            num_scalar_prefetch=1,
            grid=(steps,),
            in_specs=[source_spec(r) for r in range(group)]
            + [scale_spec(r) for r in range(group)]
            + [pl.BlockSpec((planes, rows_y, rows_z), lambda i, info_ref: (0, 0, 0))],
            out_specs=[pl.BlockSpec(shape.shape, lambda i, info_ref: (0, 0, 0, 0))] * group,
        ),
        out_shape=[shape] * group,
        name="prepare",
        **params(24),
    )(info, *([orbitals] * group), *([scale] * group), potential)


def edges(info, pieces, cuts):
    group = len(pieces)
    total, planes, rows_y, rows_z = pieces[0].shape
    rest = edge - planes
    width = edge // cuts
    at_once = 6 if total % 6 == 0 else 4

    def kernel(info_ref, *refs):
        sources, outs = refs[:group], refs[group:]

        def put(targets, to, source, begin, count):
            while count:
                size = min(count, width - to % width)
                target = targets[to // width]
                target[:, to % width : to % width + size] = source[:, begin : begin + size]
                to, begin, count = to + size, begin + size, count - size

        for odd in range(2):
            up, down = (outs[k * cuts : (k + 1) * cuts] for k in (odd, 1 - odd))
            for r in range(group):
                slab = jnp.where(info_ref[5] == odd, info_ref[0] ^ r, -1)

                @pl.when(slab == group - 1)
                def _():
                    put(up, rest, sources[r], 0, planes)

                @pl.when(slab == group - 2)
                def _():
                    put(up, 0, sources[r], planes - rest, rest)

                @pl.when(slab == 0)
                def _():
                    put(down, 0, sources[r], 0, planes)

                @pl.when(slab == 1)
                def _():
                    put(down, planes, sources[r], 0, rest)

    def spec(count):
        return pl.BlockSpec((at_once, count, rows_y, rows_z), lambda i, info_ref: (i, 0, 0, 0))

    flat = pl.pallas_call(
        kernel,
        grid_spec=pltpu.PrefetchScalarGridSpec(
            num_scalar_prefetch=1,
            grid=(total // at_once,),
            in_specs=[spec(planes)] * group,
            out_specs=[spec(width)] * (2 * cuts),
        ),
        out_shape=[jax.ShapeDtypeStruct((total, width, rows_y, rows_z), BF16)] * (2 * cuts),
        name="edges",
        **params(16),
    )(info, *pieces)
    return flat[:cuts], flat[cuts:]


def chebyshev(info, sides, pieces, sides_pot, pieces_pot, parts):
    group = len(pieces)
    _, planes, rows_y, rows_z = pieces[0].shape
    slab = group * planes
    per_p, per_y, cuts_y = shares(planes, rows_y, parts)
    at_once = 2 if per_p % 2 == 0 else 1
    steps = chunk // 2
    count_out = group // 2 * parts
    flat_sides, flat_pot = ([value for side in both for value in side] for both in (sides, sides_pot))
    cuts, cuts_pot = len(sides[0]), len(sides_pot[0])
    width, width_pot = edge // cuts, edge // cuts_pot
    width_e, centre, sigma_one, sigma_two, sigma_three = filter_terms()
    diagonal = 3.0 * stencil_coef[0] * kinetic - centre
    tile_rows = planes * rows_y
    xy, zz, swap = xy_matrix(planes, rows_y), z_matrix(rows_z), swap_matrix()
    count_0, count_1, count_2 = slab + 6 * reach, slab + 4 * reach, slab + 2 * reach

    def kernel(info_ref, *refs):
        side_refs, refs = refs[: 2 * cuts], refs[2 * cuts :]
        side_pot_refs, refs = refs[: 2 * cuts_pot], refs[2 * cuts_pot :]
        piece_refs, pot_refs = refs[:group], refs[group : 2 * group]
        xy_ref, zz_ref, swap_ref = refs[2 * group : 3 + 2 * group]
        outs = refs[3 + 2 * group : 3 + 2 * group + count_out]
        field, first, second, energy, result = refs[3 + 2 * group + count_out :]
        i = pl.program_id(0)
        me = info_ref[0]
        at_left, at_right = info_ref[1] == 1, info_ref[2] == 1

        @pl.when(i == 0)
        def _():
            def store(start, source):
                total = source[0].astype(F32) + source[1].astype(F32)
                energy[pl.ds(start, source.shape[1])] = coef_scale * (total + diagonal)

            for side, base, low, high in (
                (side_pot_refs[cuts_pot:], -reach, 0, 2 * reach),
                (side_pot_refs[:cuts_pot], slab + 2 * reach, slab + 2 * reach, count_1),
            ):
                for k, ref in enumerate(side):
                    start = base + k * width_pot
                    begin, end = max(start, low), min(start + width_pot, high)
                    if begin < end:
                        store(begin, ref.at[:, begin - start : end - start])
            for r in range(group):
                store(2 * reach + planes * (me ^ r), pot_refs[r])

        for b in range(2):
            lanes = slice(b * rows_z, (b + 1) * rows_z)
            for k in range(2):
                start = (1 - (info_ref[5] ^ k)) * (edge + slab)
                for n in range(cuts):
                    where = pl.ds(start + n * width, width)
                    field[where, :, lanes] = side_refs[k * cuts + n][b]
            for r in range(group):
                field[pl.ds(edge + planes * (me ^ r), planes), :, lanes] = piece_refs[r][b]

        def apply(source, start, energy_start):
            rows = source[pl.ds(start, planes + 2 * reach)].reshape(-1, 2 * rows_z)
            middle = source[pl.ds(start + reach, planes)].reshape(tile_rows, 2 * rows_z)
            total = jnp.dot(xy_ref[...], rows, preferred_element_type=F32)
            total += jnp.dot(middle, zz_ref[...], preferred_element_type=F32)
            factor = energy[pl.ds(energy_start, planes)].reshape(tile_rows, rows_z)
            factor = jnp.concatenate([factor, factor], axis=1)
            return total + factor * middle.astype(F32)

        def block(value):
            return value.astype(BF16).reshape(planes, rows_y, 2 * rows_z)

        def previous(source, start):
            return source[pl.ds(start, planes)].reshape(tile_rows, 2 * rows_z).astype(F32)

        for t in range(count_1 // planes):
            at = t * planes
            value = apply(field, at, at) * (sigma_one / width_e / coef_scale)
            first[at : at + planes] = block(value)

        @pl.when(at_left)
        def _():
            first[: 2 * reach] = jnp.zeros((2 * reach, rows_y, 2 * rows_z), BF16)

        @pl.when(at_right)
        def _():
            first[count_1 - 2 * reach :] = jnp.zeros((2 * reach, rows_y, 2 * rows_z), BF16)

        for t in range(count_2 // planes):
            at = t * planes
            value = apply(first, at, at + reach) * (2.0 * sigma_two / width_e / coef_scale)
            value -= sigma_one * sigma_two * previous(field, at + 2 * reach)
            second[at : at + planes] = block(value)

        @pl.when(at_left)
        def _():
            second[:reach] = jnp.zeros((reach, rows_y, 2 * rows_z), BF16)

        @pl.when(at_right)
        def _():
            second[count_2 - reach :] = jnp.zeros((reach, rows_y, 2 * rows_z), BF16)

        for t in range(group):
            at = t * planes
            value = apply(second, at, at + 2 * reach) * (2.0 * sigma_three / width_e / coef_scale)
            value -= sigma_two * sigma_three * previous(first, at + 2 * reach)
            value = block(value)
            for b in range(2):
                part = value[:, :, b * rows_z : (b + 1) * rows_z]
                result[at : at + planes, 2 * i + b] = part

        @pl.when(i == steps - 1)
        def _():
            for t in range(parts):
                part = lax.rem(info_ref[3] + t, parts)
                begin = lax.rem(part, cuts_y) * (per_y * chunk)
                begin = pl.multiple_of(begin, per_y * chunk)
                for r in range(group):
                    start = planes * (me ^ r) + part // cuts_y * per_p
                    for p in range(0, per_p, at_once):
                        pair = [
                            result[start + p + k].reshape(chunk * rows_y, rows_z)
                            for k in range(at_once)
                        ]
                        moved = jnp.dot(
                            swap_ref[pl.ds(begin, per_y * chunk), :],
                            jnp.concatenate(pair, axis=1),
                            preferred_element_type=F32,
                        ).astype(BF16)
                        for k in range(at_once):
                            value = moved[:, k * rows_z : (k + 1) * rows_z]
                            out = outs[r // 2 * parts + t]
                            out[r % 2, :, p + k] = value.reshape(per_y, chunk, rows_z)

    def block_spec(count, index):
        return pl.BlockSpec((2, count, rows_y, rows_z), index)

    def whole_spec(shape):
        return pl.BlockSpec(shape, lambda i, info_ref: (0,) * len(shape))

    moving = lambda i, info_ref: (i, 0, 0, 0)
    fixed = lambda i, info_ref: (steps, 0, 0, 0)
    shape = jax.ShapeDtypeStruct((2, per_y, per_p, chunk, rows_z), BF16)
    flat = pl.pallas_call(
        kernel,
        grid_spec=pltpu.PrefetchScalarGridSpec(
            num_scalar_prefetch=1,
            grid=(steps,),
            in_specs=[block_spec(width, moving)] * (2 * cuts)
            + [block_spec(width_pot, fixed)] * (2 * cuts_pot)
            + [block_spec(planes, moving)] * group
            + [block_spec(planes, fixed)] * group
            + [whole_spec(xy.shape), whole_spec(zz.shape), whole_spec(swap.shape)],
            out_specs=[whole_spec(shape.shape)] * count_out,
            scratch_shapes=[
                pltpu.VMEM((count_0, rows_y, 2 * rows_z), BF16),
                pltpu.VMEM((count_1, rows_y, 2 * rows_z), BF16),
                pltpu.VMEM((count_2, rows_y, 2 * rows_z), BF16),
                pltpu.VMEM((count_1, rows_y, rows_z), F32),
                pltpu.VMEM((slab, chunk, rows_y, rows_z), BF16),
            ],
        ),
        out_shape=[shape] * count_out,
        name="chebyshev",
        **params(28),
    )(info, *flat_sides, *flat_pot, *pieces, *pieces_pot, xy, zz, swap)
    return [flat[a * parts : (a + 1) * parts] for a in range(group // 2)]


def shares(planes, rows_y, parts):
    cuts_p = math.gcd(planes, parts)
    cuts_y = parts // cuts_p
    return planes // cuts_p, rows_y // cuts_y, cuts_y


def fill(info_ref, rows, piece, source, first_p, first_y, r, c, bands, group):
    own = bands // group
    start = source * bands + (info_ref[0] ^ r) * own + c * chunk
    where = pl.ds(pl.multiple_of(start, chunk), chunk)
    for p in range(piece.shape[1]):
        rows[first_p + p, pl.ds(first_y, piece.shape[0]), where, :] = piece[:, p]


def gram(info, pieces, packs, bands, bands_all):
    group = 1 + max(r for r, t, c in pieces)
    _, per_y, per_p, _, rows_z = next(iter(pieces.values()))[0].shape
    at_once = 2 if per_p % 2 == 0 else 1
    steps = per_p // at_once
    half = bands_all // 2
    direct = half == bands
    own = bands // group
    ordered = sorted(pieces, key=lambda key: (key[1], key[0], key[2]))

    def in_order(info_ref, value, by_rows):
        axis = 0 if by_rows else 1
        count = value.shape[axis]
        place = lax.broadcasted_iota(jnp.int32, value.shape, axis)
        bit = 1
        while bit < group:
            step = bit * own
            if by_rows:
                blocks = [value[k : k + step] for k in range(0, count, step)]
                blocks = [blocks[k ^ 1] for k in range(len(blocks))]
                moved = jnp.concatenate(blocks, axis=0)
            else:
                low = pltpu.roll(value, count - step, 1)
                high = pltpu.roll(value, step, 1)
                moved = jnp.where(place & step == 0, low, high)
            value = jnp.where((info_ref[0] & bit) != 0, moved, value)
            bit *= 2
        return value

    def direct_blocks(info_ref, out):
        for odd in range(2):

            @pl.when(info_ref[3] == odd)
            def _():
                below = out[half:, :half] if odd == 0 else out[:half, half:bands_all]
                blocks = [out[:half, :half], below, out[half:, half:bands_all]]
                for k, block in enumerate(blocks if odd == 0 else blocks[::-1]):
                    value = in_order(info_ref, in_order(info_ref, block, True), False)
                    out[:half, k * half : (k + 1) * half] = value

    def direct_kernel(info_ref, *refs):
        mine, other, packed, _, out = refs[len(pieces) :]
        by_key = dict(zip(pieces, refs))
        i = pl.program_id(0)
        for k, (r, c) in enumerate(packs):
            packed[k] = by_key[(r, 0, c)][0]
        block = jnp.concatenate(
            [
                jnp.concatenate([by_key[key][0, y, p] for key in ordered], axis=0)
                for p in range(at_once)
                for y in range(per_y)
            ],
            axis=1,
        )
        total = lax.dot_general(
            block, block, (((1,), (1,)), ((), ())), preferred_element_type=F32
        )

        @pl.when(i == 0)
        def _():
            out[:, :bands_all] = total

        @pl.when(i > 0)
        def _():
            out[:, :bands_all] += total

        @pl.when(i == steps - 1)
        def _():
            direct_blocks(info_ref, out)
            for ref, core in ((mine, info_ref[0] & 1), (other, 1 - (info_ref[0] & 1))):
                where = pl.ds(pl.multiple_of(core * (half // 2), half // 2), half // 2)
                ref[...] = out[where, : 3 * half]

    def kernel(info_ref, *refs):
        mine, other, packed, rows, out = refs[len(pieces) :]
        parts = info_ref[4]
        i = pl.program_id(0)
        for (r, t, c), piece in zip(pieces, refs):
            source = lax.rem(info_ref[3] + parts - t, parts)
            fill(info_ref, rows, piece.at[0], source, 0, 0, r, c, bands, group)
            if t == 0 and (r, c) in packs:
                packed[packs.index((r, c))] = piece[0]
        block = jnp.concatenate(
            [rows[p, y] for p in range(at_once) for y in range(per_y)], axis=1
        )
        total = lax.dot_general(
            block, block, (((1,), (1,)), ((), ())), preferred_element_type=F32
        )

        total = [total[:half, :half], total[half:, :half], total[half:, half:]]
        total = jnp.concatenate(total, axis=1)

        @pl.when(i == 0)
        def _():
            out[...] = total

        @pl.when(i > 0)
        def _():
            out[...] += total

        @pl.when(i == steps - 1)
        def _():
            for ref, core in ((mine, info_ref[0] & 1), (other, 1 - (info_ref[0] & 1))):
                ref[...] = out[pl.ds(pl.multiple_of(core * (half // 2), half // 2), half // 2)]

    def spec(index):
        return pl.BlockSpec(
            (1, per_y, at_once, chunk, rows_z), lambda i, info_ref: (index, 0, i, 0, 0)
        )

    return pl.pallas_call(
        direct_kernel if direct else kernel,
        grid_spec=pltpu.PrefetchScalarGridSpec(
            num_scalar_prefetch=1,
            grid=(steps,),
            in_specs=[spec(index) for _, index in pieces.values()],
            out_specs=[pl.BlockSpec((half // 2, 3 * half), lambda i, info_ref: (0, 0))] * 2
            + [
                pl.BlockSpec(
                    (len(packs), per_y, at_once, chunk, rows_z),
                    lambda i, info_ref: (0, 0, i, 0, 0),
                ),
            ],
            scratch_shapes=[
                pltpu.VMEM((1 if direct else at_once, per_y, bands_all, rows_z), BF16),
                pltpu.VMEM((bands_all if direct else half, 3 * half), F32),
            ],
        ),
        out_shape=[jax.ShapeDtypeStruct((half // 2, 3 * half), F32)] * 2
        + [jax.ShapeDtypeStruct((len(packs), per_y, per_p, chunk, rows_z), BF16)],
        name="gram",
        **params(28),
    )(info, *[value for value, _ in pieces.values()])


def inverse_factor(info, mine, other, cells):
    half = 2 * mine.shape[0]
    count = 2 * half

    def exact(a, b, transposed):
        dims = (((1,), (1 if transposed else 0,)), ((), ()))
        return lax.dot_general(
            a, b, dims, precision=lax.Precision.HIGHEST, preferred_element_type=F32
        )

    def eliminate(block):
        groups = half // 8
        row = lax.broadcasted_iota(jnp.int32, (8, half), 0)
        column = lax.broadcasted_iota(jnp.int32, (8, half), 1)
        left = [block[8 * g : 8 * g + 8] for g in range(groups)]
        right = [jnp.where(column == row + 8 * g, 1.0, 0.0).astype(F32) for g in range(groups)]
        for at in range(groups):
            later = range(at, groups)
            spread = [
                [
                    jnp.broadcast_to(left[g][:, 8 * at + k : 8 * at + k + 1], (8, half))
                    for g in later
                ]
                for k in range(8)
            ]
            factors, rows_left, rows_right = [], [], []
            for k in range(8):
                pivot = jnp.broadcast_to(spread[k][0][k : k + 1], (8, half))
                scale = lax.rsqrt(pivot)
                scale = scale * (1.5 - 0.5 * pivot * scale * scale)
                factor = [value * scale for value in spread[k]]
                for m in range(k + 1, 8):
                    other = jnp.broadcast_to(factor[0][m : m + 1], (8, half))
                    spread[m] = [value - f * other for value, f in zip(spread[m], factor)]
                row_left = jnp.broadcast_to(left[at][k : k + 1], (8, half)) * scale
                row_right = jnp.broadcast_to(right[at][k : k + 1], (8, half)) * scale
                inside = jnp.where(row > k, factor[0], 0.0)
                left[at] = jnp.where(row == k, row_left, left[at] - inside * row_left)
                right[at] = jnp.where(row == k, row_right, right[at] - inside * row_right)
                factors.append(factor)
                rows_left.append(row_left)
                rows_right.append(row_right)
            for g in range(at + 1, groups):
                for k in range(8):
                    left[g] = left[g] - factors[k][g - at] * rows_left[k]
                    right[g] = right[g] - factors[k][g - at] * rows_right[k]
        return jnp.concatenate(right, axis=0)

    def kernel(info_ref, mine_ref, other_ref, out, blocks):
        for ref, core in ((mine_ref, info_ref[0] & 1), (other_ref, 1 - (info_ref[0] & 1))):
            where = pl.ds(pl.multiple_of(core * (half // 2), half // 2), half // 2)
            blocks[where] = ref[...] * (1.0 / cells)
        top = eliminate(blocks[:, :half])
        below = exact(blocks[:, half:count], top, True)
        rest = blocks[:, count:] - exact(below, below, True)
        bottom = eliminate(rest)
        out[:half, :half] = top.astype(BF16)
        out[:half, half:] = jnp.zeros((half, half), BF16)
        out[half:, :half] = (-exact(bottom, exact(below, top, False), False)).astype(BF16)
        out[half:, half:] = bottom.astype(BF16)

    return pl.pallas_call(
        kernel,
        grid_spec=pltpu.PrefetchScalarGridSpec(
            num_scalar_prefetch=1,
            grid=(1,),
            in_specs=[pl.BlockSpec(mine.shape, lambda i, info_ref: (0, 0))] * 2,
            out_specs=pl.BlockSpec((count, count), lambda i, info_ref: (0, 0)),
            scratch_shapes=[pltpu.VMEM((half, 3 * half), F32)],
        ),
        out_shape=jax.ShapeDtypeStruct((count, count), BF16),
        name="inverse_factor",
        **params(16),
    )(info, mine, other)


def rotate(info, rotation, pieces, bands, bands_all, planes, rows_y, only, before):
    group = 1 + max(r for r, t, u, c in pieces)
    _, per_y, per_p, _, rows_z = next(iter(pieces.values()))[0].shape
    swap = swap_matrix()
    cuts_y = rows_y // per_y
    at_once = 2 if only is not None and per_p % 2 == 0 else 1 if only is not None else per_p
    steps = per_p // at_once
    span = at_once if only is not None else planes
    given = [] if before is None else [before]
    arrays = {id(value): value for value, _ in pieces.values()}
    slots = {key: k for k, key in enumerate(arrays)}

    def start_of(info_ref, r, t, c):
        source = lax.rem(info_ref[3] + info_ref[4] - t, info_ref[4])
        return source * bands + (info_ref[0] ^ r) * (bands // group) + c * chunk

    def kernel(info_ref, *refs):
        rotation_ref, swap_ref = refs[len(arrays) :][:2]
        out, rows, mixed, turned = refs[-4:]
        me, parts = info_ref[3], info_ref[4]
        if only is None:
            for (r, t, u, c), (value, index) in pieces.items():
                source = lax.rem(me + parts - t, parts)
                part = lax.rem(me + u, parts)
                first_p, first_y = part // cuts_y * per_p, lax.rem(part, cuts_y) * per_y
                piece = refs[slots[id(value)]].at[index]
                fill(info_ref, rows, piece, source, first_p, first_y, r, c, bands, group)
            turned[...] = rotation_ref[...]
        else:

            @pl.when(pl.program_id(0) == 0)
            def _():
                place = lax.broadcasted_iota(jnp.int32, (bands_all, bands_all), 1)
                wanted = lax.broadcasted_iota(jnp.int32, (bands_all, bands_all), 0)
                from_row = place & (chunk - 1)
                for k, (r, t, _, c) in enumerate(pieces):
                    start = jnp.where(place // chunk == k, start_of(info_ref, r, t, c), 0)
                    from_row = from_row + start
                order = jnp.where(wanted == from_row, 1.0, 0.0).astype(BF16)
                value = jnp.dot(rotation_ref[...], order, preferred_element_type=F32)
                turned[...] = value.astype(BF16)

        def row(p, y):
            if only is None:
                return rows[p, y]
            held = [refs[slots[id(value)]][index, y, p] for value, index in pieces.values()]
            return jnp.concatenate(held, axis=0)

        def plane(p):
            for y in range(0, rows_y, 2):
                pair = jnp.concatenate([row(p, y), row(p, y + 1)], axis=1)
                value = jnp.dot(turned[...], pair, preferred_element_type=F32)
                value = value.astype(BF16)
                for k in range(bands // 16):
                    for b in range(2):
                        mixed[k, y + b] = value[
                            16 * k : 16 * k + 16, b * rows_z : (b + 1) * rows_z
                        ]
            for k in range(0, bands // 16, 2):
                pair = [mixed[k + b].reshape(16 * rows_y, rows_z) for b in range(2)]
                moved = jnp.dot(
                    swap_ref[...], jnp.concatenate(pair, axis=1), preferred_element_type=F32
                ).astype(BF16)
                for b in range(2):
                    part = moved[:, b * rows_z : (b + 1) * rows_z].reshape(16, rows_y, rows_z)
                    out[16 * (k + b) : 16 * (k + b) + 16, p] = part

        if only is not None:
            for p in range(span):
                plane(p)
        else:
            pl.loop(0, span)(plane)

    def spec(value):
        return pl.BlockSpec(
            (value.shape[0], per_y, at_once, chunk, rows_z), lambda i, info_ref: (0, 0, i, 0, 0)
        )

    def out_index(i, info_ref):
        if only is None:
            return (0, 0, 0, 0)
        return (0, lax.rem(info_ref[3] + only, info_ref[4]) * steps + i, 0, 0)

    return pl.pallas_call(
        kernel,
        grid_spec=pltpu.PrefetchScalarGridSpec(
            num_scalar_prefetch=1,
            grid=(steps,),
            in_specs=[spec(value) for value in arrays.values()]
            + [
                pl.BlockSpec((bands, bands_all), lambda i, info_ref: (info_ref[3], 0)),
                pl.BlockSpec(swap.shape, lambda i, info_ref: (0, 0)),
            ]
            + [pl.BlockSpec(memory_space=pl.ANY)] * len(given),
            out_specs=pl.BlockSpec((bands, span, rows_y, rows_z), out_index),
            scratch_shapes=[
                pltpu.VMEM((span if only is None else 1, rows_y, bands_all, rows_z), BF16),
                pltpu.VMEM((bands // 16, rows_y, 16, rows_z), BF16),
                pltpu.VMEM((bands, bands_all), BF16),
            ],
        ),
        out_shape=jax.ShapeDtypeStruct((bands, planes, rows_y, rows_z), BF16),
        input_output_aliases={3 + len(arrays): 0} if given else {},
        name="rotate",
        **params(60 if only is None else 28),
    )(info, *arrays.values(), rotation, swap, *given)


def pairwise_sum(value, axis, count, low, high):
    bit = max(low, 1)
    while bit < high:
        value = value + lax.ppermute(value, axis, [(i, i ^ bit) for i in range(count)])
        bit *= 2
    return value


def body(orbital_block, block_scale, potential):
    bands, planes, rows_y, rows_z = orbital_block.shape
    parts, slabs = lax.axis_size("band"), lax.axis_size("domain")
    bands_all = bands * parts
    group = 4 if bands // 4 >= chunk else 2
    chunks = bands // group // chunk
    where, band = lax.axis_index("domain"), lax.axis_index("band")
    info = jnp.stack(
        [
            lax.rem(where, group),
            (where < group).astype(jnp.int32),
            (where >= slabs - group).astype(jnp.int32),
            band,
            jnp.int32(parts),
            jnp.int32(0),
        ]
    ).astype(jnp.int32)
    paired = info.at[5].set(lax.rem(where // group, 2))

    def send(value, r, t):
        if r == 0 and t == 0:
            return value
        pairs = [
            (q * slabs + i, (q + t) % parts * slabs + (i ^ r))
            for q in range(parts)
            for i in range(slabs)
        ]
        return lax.ppermute(value, ("band", "domain"), pairs)

    scale = jnp.broadcast_to(block_scale[:, :, None], (bands, planes, rows_z))
    far_first = sorted(range(group), reverse=True)
    arrived = []
    for c in range(chunks):
        pieces = prepare(info, orbital_block, scale, potential, c, group, c == 0)
        sent = {r: send(pieces[r], r, 0) for r in far_first}
        arrived.append([sent[r] for r in range(group)])
    def after(value, *others):
        return lax.optimization_barrier((value, *others))[0] if others else value

    def swapped(value, odd):
        lower = [i for i in range(slabs - group) if i // group % 2 == odd]
        pairs = [(i, i + group) for i in lower] + [(i + group, i) for i in lower]
        return lax.ppermute(value, "domain", pairs)

    def shifted(value, by):
        pairs = [(i, i + by) for i in range(slabs) if 0 <= i + by < slabs]
        return lax.ppermute(value, "domain", pairs)

    sides = []
    for c in range(chunks):
        first, second = edges(paired if c else info, arrived[c], 1 if c else 2)
        if c == 0:
            sides.append(
                [[shifted(end, -group) for end in second], [shifted(end, group) for end in first]]
            )
        else:
            sides.append([[swapped(end, 0) for end in first], [swapped(end, 1) for end in second]])
        last_end = first[0]
    pieces, own, moved, crossed = {}, {}, {}, {}
    ready = [last_end]
    for c in range(chunks):
        order = after(paired if c else info, *ready)
        filtered = chebyshev(order, sides[c], arrived[c], sides[0], arrived[0], parts)
        ready = [filtered[0][0]]
        for a in reversed(range(group // 2)):
            for t in reversed(range(parts)):
                value = filtered[a][t]
                own[(a, t, c)] = value
                moved[(a, t, c)] = send(value, 2 * a, t)
    for c in range(chunks):
        keys = [(a, t) for t in range(parts) for a in range(group // 2)]
        there = {key: after(moved[(*key, c)], *ready) for key in keys}
        crossed[c] = send(jnp.stack([there[key][1] for key in keys]), 1, 0)
        for k, (a, t) in enumerate(keys):
            pieces[(2 * a, t, c)] = (there[(a, t)], 0)
            pieces[(2 * a + 1, t, c)] = (crossed[c], k)

    known = {(r, t, 0, c): value for (r, t, c), value in pieces.items()}
    late = {}
    last = [value for (a, t, c), value in moved.items() if c == chunks - 1]
    early = parts == 2 and chunks > 1 and group == 4
    if early:
        late[(1, 1, 0)] = send(after(own[(1, 1, 0)], *last), 2, 0)
        chosen = [(r, *pieces[(r, 0, 0)]) for r in (1, 2, 3)]
        sent = jnp.stack([value[index] for _, value, index in chosen])
        sent = lax.ppermute(after(sent, *last), "band", [(0, 1)])
        for k, (r, _, _) in enumerate(chosen):
            known[(r, 1, 1, 0)] = (sent, k)
    packs = [
        (r, c)
        for c in range(chunks)
        for r in range(group)
        if (r, 1, 1, c) not in known or parts > 2
    ]
    mine, other, buffer = gram(info, pieces, packs, bands, bands_all)
    mine = mine + send(other, 1, 0)
    mine = after(mine, *late.values())
    mine = pairwise_sum(mine, "domain", slabs, 2, group)
    for key, value in own.items():
        if key[1] > 0 and key not in late:
            late[key] = send(after(value, mine), 2 * key[0], 0)
    if early:
        mine = after(mine, sent)
    mine = pairwise_sum(mine, "band", parts, 0, parts)

    def forward(buffer, t, packs):
        for s in range(1, parts):
            if t != s:
                sent = lax.ppermute(buffer, "band", [(q, q + s) for q in range(parts - s)])
                for k, (r, c) in enumerate(packs):
                    known[(r, s, (t - s) % parts, c)] = (sent, k)

    forward(after(buffer, mine), 0, packs)
    mine = pairwise_sum(mine, "domain", slabs, group, slabs)
    rotation = inverse_factor(info, mine, send(mine, 1, 0), planes * rows_y * rows_z * slabs)
    for t in range(1, parts):
        keys = [(a, c) for c in range(chunks) for a in range(group // 2)]
        far = send(jnp.stack([after(late[(a, t, c)], rotation)[1] for a, c in keys]), 1, 0)
        for k, (a, c) in enumerate(keys):
            known[(2 * a, 0, t, c)] = (late[(a, t, c)], 0)
            known[(2 * a + 1, 0, t, c)] = (far, k)
        if parts > 2:
            chosen = [known[(r, 0, t, c)] for r, c in packs]
            forward(jnp.stack([value[index] for value, index in chosen]), t, packs)
    out = None
    for only in range(parts) if parts == 2 and planes % 2 == 0 else [None]:
        chosen = {key: value for key, value in known.items() if only in (None, key[2])}
        out = rotate(info, rotation, chosen, bands, bands_all, planes, rows_y, only, out)
    return out


def solution(mesh):
    in_specs = (P("band", "domain", None, None), P("band", "domain"), P("domain", None, None))
    out_specs = P("band", "domain", None, None)
    return jax.shard_map(body, mesh=mesh, in_specs=in_specs, out_specs=out_specs, check_vma=False)
```

```python
import math

import jax
import jax.numpy as jnp
import numpy as np
from jax import lax
from jax.experimental import pallas as pl
from jax.experimental.pallas import tpu as pltpu
from jax.sharding import PartitionSpec as P

grid_step = 0.5
stencil_coef = (
    -5369.0 / 1800.0,
    12.0 / 7.0,
    -15.0 / 56.0,
    10.0 / 189.0,
    -1.0 / 112.0,
    2.0 / 1925.0,
    -1.0 / 16632.0,
)
lower_end = -4.0
cut_energy = 6.0
upper_end = 43.0
kinetic = -0.5 / (grid_step * grid_step)
coef_scale = 7.0
reach = 6
edge = 3 * reach
chunk = 16
F32, BF16 = jnp.float32, jnp.bfloat16


def filter_terms():
    width_e = (upper_end - cut_energy) / 2.0
    centre = (upper_end + cut_energy) / 2.0
    sigma_one = width_e / (lower_end - centre)
    gamma_term = 2.0 / sigma_one
    sigma_two = 1.0 / (gamma_term - sigma_one)
    sigma_three = 1.0 / (gamma_term - sigma_two)
    return (width_e, centre, sigma_one, sigma_two, sigma_three)


def stencil_line(count):
    line = np.zeros((count, count), np.float64)
    for offset in range(1, reach + 1):
        value = kinetic * stencil_coef[offset] * coef_scale
        line += value * (np.eye(count, k=offset) + np.eye(count, k=-offset))
    return line


def xy_matrix(planes, rows_y):
    along_x = np.zeros((planes, planes + 2 * reach), np.float64)
    along_x[:, :] = stencil_line(planes + 2 * reach)[reach : reach + planes]
    middle = np.eye(planes, planes + 2 * reach, k=reach)
    full = np.kron(along_x, np.eye(rows_y)) + np.kron(middle, stencil_line(rows_y))
    return jnp.asarray(full, BF16)


def z_matrix(count_z):
    return jnp.asarray(np.kron(np.eye(2), stencil_line(count_z)), BF16)


def swap_matrix():
    full = np.zeros((256, 256), np.float32)
    for a in range(16):
        for b in range(16):
            full[a * 16 + b, b * 16 + a] = 1.0
    return jnp.asarray(full, BF16)


def params(mebibytes):
    return dict(
        compiler_params=pltpu.CompilerParams(
            vmem_limit_bytes=mebibytes * 2**20, dimension_semantics=("arbitrary",)
        ),
        cost_estimate=pl.CostEstimate(flops=1, bytes_accessed=1, transcendentals=0),
    )


def prepare(info, orbitals, scale, potential, part, group, with_potential):
    bands, planes, rows_y, rows_z = orbitals.shape
    own = bands // group
    at_once = 8
    steps = chunk // at_once
    total = chunk + (2 if with_potential else 0)

    def kernel(info_ref, *refs):
        sources, scales, potential_ref = refs[:group], refs[group : 2 * group], refs[2 * group]
        outs = refs[2 * group + 1 :]
        i = pl.program_id(0)
        for r in range(group):
            for b in range(at_once):
                value = sources[r][b].astype(F32) * scales[r][b][:, None, :]
                outs[r][i * at_once + b] = value.astype(BF16)

        if with_potential:

            @pl.when(i == 0)
            def _():
                high = potential_ref[...].astype(BF16)
                low = (potential_ref[...] - high.astype(F32)).astype(BF16)
                for r in range(group):
                    outs[r][chunk] = high
                    outs[r][chunk + 1] = low

    def first(r, i, info_ref):
        return ((info_ref[0] ^ r) * own + part * chunk) // at_once + i

    def source_spec(r):
        return pl.BlockSpec(
            (at_once, planes, rows_y, rows_z),
            lambda i, info_ref: (first(r, i, info_ref), 0, 0, 0),
        )

    def scale_spec(r):
        return pl.BlockSpec(
            (at_once, planes, rows_z), lambda i, info_ref: (first(r, i, info_ref), 0, 0)
        )

    shape = jax.ShapeDtypeStruct((total, planes, rows_y, rows_z), BF16)
    return pl.pallas_call(
        kernel,
        grid_spec=pltpu.PrefetchScalarGridSpec(
            num_scalar_prefetch=1,
            grid=(steps,),
            in_specs=[source_spec(r) for r in range(group)]
            + [scale_spec(r) for r in range(group)]
            + [pl.BlockSpec((planes, rows_y, rows_z), lambda i, info_ref: (0, 0, 0))],
            out_specs=[pl.BlockSpec(shape.shape, lambda i, info_ref: (0, 0, 0, 0))] * group,
        ),
        out_shape=[shape] * group,
        name="prepare",
        **params(24),
    )(info, *([orbitals] * group), *([scale] * group), potential)


def edges(info, pieces, cuts):
    group = len(pieces)
    total, planes, rows_y, rows_z = pieces[0].shape
    rest = edge - planes
    width = edge // cuts
    at_once = 6 if total % 6 == 0 else 4

    def kernel(info_ref, *refs):
        sources, outs = refs[:group], refs[group:]

        def put(targets, to, source, begin, count):
            while count:
                size = min(count, width - to % width)
                target = targets[to // width]
                target[:, to % width : to % width + size] = source[:, begin : begin + size]
                to, begin, count = to + size, begin + size, count - size

        for odd in range(2):
            up, down = (outs[k * cuts : (k + 1) * cuts] for k in (odd, 1 - odd))
            for r in range(group):
                slab = jnp.where(info_ref[5] == odd, info_ref[0] ^ r, -1)

                @pl.when(slab == group - 1)
                def _():
                    put(up, rest, sources[r], 0, planes)

                @pl.when(slab == group - 2)
                def _():
                    put(up, 0, sources[r], planes - rest, rest)

                @pl.when(slab == 0)
                def _():
                    put(down, 0, sources[r], 0, planes)

                @pl.when(slab == 1)
                def _():
                    put(down, planes, sources[r], 0, rest)

    def spec(count):
        return pl.BlockSpec((at_once, count, rows_y, rows_z), lambda i, info_ref: (i, 0, 0, 0))

    flat = pl.pallas_call(
        kernel,
        grid_spec=pltpu.PrefetchScalarGridSpec(
            num_scalar_prefetch=1,
            grid=(total // at_once,),
            in_specs=[spec(planes)] * group,
            out_specs=[spec(width)] * (2 * cuts),
        ),
        out_shape=[jax.ShapeDtypeStruct((total, width, rows_y, rows_z), BF16)] * (2 * cuts),
        name="edges",
        **params(16),
    )(info, *pieces)
    return flat[:cuts], flat[cuts:]


def chebyshev(info, sides, pieces, sides_pot, pieces_pot, parts):
    group = len(pieces)
    _, planes, rows_y, rows_z = pieces[0].shape
    slab = group * planes
    per_p, per_y, cuts_y = shares(planes, rows_y, parts)
    at_once = 2 if per_p % 2 == 0 else 1
    steps = chunk // 2
    count_out = group // 2 * parts
    flat_sides, flat_pot = ([value for side in both for value in side] for both in (sides, sides_pot))
    cuts, cuts_pot = len(sides[0]), len(sides_pot[0])
    width, width_pot = edge // cuts, edge // cuts_pot
    width_e, centre, sigma_one, sigma_two, sigma_three = filter_terms()
    diagonal = 3.0 * stencil_coef[0] * kinetic - centre
    tile_rows = planes * rows_y
    xy, zz, swap = xy_matrix(planes, rows_y), z_matrix(rows_z), swap_matrix()
    count_0, count_1, count_2 = slab + 6 * reach, slab + 4 * reach, slab + 2 * reach

    def kernel(info_ref, *refs):
        side_refs, refs = refs[: 2 * cuts], refs[2 * cuts :]
        side_pot_refs, refs = refs[: 2 * cuts_pot], refs[2 * cuts_pot :]
        piece_refs, pot_refs = refs[:group], refs[group : 2 * group]
        xy_ref, zz_ref, swap_ref = refs[2 * group : 3 + 2 * group]
        outs = refs[3 + 2 * group : 3 + 2 * group + count_out]
        field, first, second, energy, result = refs[3 + 2 * group + count_out :]
        i = pl.program_id(0)
        me = info_ref[0]
        at_left, at_right = info_ref[1] == 1, info_ref[2] == 1

        @pl.when(i == 0)
        def _():
            def store(start, source):
                total = source[0].astype(F32) + source[1].astype(F32)
                energy[pl.ds(start, source.shape[1])] = coef_scale * (total + diagonal)

            for side, base, low, high in (
                (side_pot_refs[cuts_pot:], -reach, 0, 2 * reach),
                (side_pot_refs[:cuts_pot], slab + 2 * reach, slab + 2 * reach, count_1),
            ):
                for k, ref in enumerate(side):
                    start = base + k * width_pot
                    begin, end = max(start, low), min(start + width_pot, high)
                    if begin < end:
                        store(begin, ref.at[:, begin - start : end - start])
            for r in range(group):
                store(2 * reach + planes * (me ^ r), pot_refs[r])

        for b in range(2):
            lanes = slice(b * rows_z, (b + 1) * rows_z)
            for k in range(2):
                start = (1 - (info_ref[5] ^ k)) * (edge + slab)
                for n in range(cuts):
                    where = pl.ds(start + n * width, width)
                    field[where, :, lanes] = side_refs[k * cuts + n][b]
            for r in range(group):
                field[pl.ds(edge + planes * (me ^ r), planes), :, lanes] = piece_refs[r][b]

        def apply(source, start, energy_start):
            rows = source[pl.ds(start, planes + 2 * reach)].reshape(-1, 2 * rows_z)
            middle = source[pl.ds(start + reach, planes)].reshape(tile_rows, 2 * rows_z)
            total = jnp.dot(xy_ref[...], rows, preferred_element_type=F32)
            total += jnp.dot(middle, zz_ref[...], preferred_element_type=F32)
            factor = energy[pl.ds(energy_start, planes)].reshape(tile_rows, rows_z)
            factor = jnp.concatenate([factor, factor], axis=1)
            return total + factor * middle.astype(F32)

        def block(value):
            return value.astype(BF16).reshape(planes, rows_y, 2 * rows_z)

        def previous(source, start):
            return source[pl.ds(start, planes)].reshape(tile_rows, 2 * rows_z).astype(F32)

        for t in range(count_1 // planes):
            at = t * planes
            value = apply(field, at, at) * (sigma_one / width_e / coef_scale)
            first[at : at + planes] = block(value)

        @pl.when(at_left)
        def _():
            first[: 2 * reach] = jnp.zeros((2 * reach, rows_y, 2 * rows_z), BF16)

        @pl.when(at_right)
        def _():
            first[count_1 - 2 * reach :] = jnp.zeros((2 * reach, rows_y, 2 * rows_z), BF16)

        for t in range(count_2 // planes):
            at = t * planes
            value = apply(first, at, at + reach) * (2.0 * sigma_two / width_e / coef_scale)
            value -= sigma_one * sigma_two * previous(field, at + 2 * reach)
            second[at : at + planes] = block(value)

        @pl.when(at_left)
        def _():
            second[:reach] = jnp.zeros((reach, rows_y, 2 * rows_z), BF16)

        @pl.when(at_right)
        def _():
            second[count_2 - reach :] = jnp.zeros((reach, rows_y, 2 * rows_z), BF16)

        for t in range(group):
            at = t * planes
            value = apply(second, at, at + 2 * reach) * (2.0 * sigma_three / width_e / coef_scale)
            value -= sigma_two * sigma_three * previous(first, at + 2 * reach)
            value = block(value)
            for b in range(2):
                part = value[:, :, b * rows_z : (b + 1) * rows_z]
                result[at : at + planes, 2 * i + b] = part

        @pl.when(i == steps - 1)
        def _():
            for t in range(parts):
                part = lax.rem(info_ref[3] + t, parts)
                begin = lax.rem(part, cuts_y) * (per_y * chunk)
                begin = pl.multiple_of(begin, per_y * chunk)
                for r in range(group):
                    start = planes * (me ^ r) + part // cuts_y * per_p
                    for p in range(0, per_p, at_once):
                        pair = [
                            result[start + p + k].reshape(chunk * rows_y, rows_z)
                            for k in range(at_once)
                        ]
                        moved = jnp.dot(
                            swap_ref[pl.ds(begin, per_y * chunk), :],
                            jnp.concatenate(pair, axis=1),
                            preferred_element_type=F32,
                        ).astype(BF16)
                        for k in range(at_once):
                            value = moved[:, k * rows_z : (k + 1) * rows_z]
                            out = outs[r // 2 * parts + t]
                            out[r % 2, :, p + k] = value.reshape(per_y, chunk, rows_z)

    def block_spec(count, index):
        return pl.BlockSpec((2, count, rows_y, rows_z), index)

    def whole_spec(shape):
        return pl.BlockSpec(shape, lambda i, info_ref: (0,) * len(shape))

    moving = lambda i, info_ref: (i, 0, 0, 0)
    fixed = lambda i, info_ref: (steps, 0, 0, 0)
    shape = jax.ShapeDtypeStruct((2, per_y, per_p, chunk, rows_z), BF16)
    flat = pl.pallas_call(
        kernel,
        grid_spec=pltpu.PrefetchScalarGridSpec(
            num_scalar_prefetch=1,
            grid=(steps,),
            in_specs=[block_spec(width, moving)] * (2 * cuts)
            + [block_spec(width_pot, fixed)] * (2 * cuts_pot)
            + [block_spec(planes, moving)] * group
            + [block_spec(planes, fixed)] * group
            + [whole_spec(xy.shape), whole_spec(zz.shape), whole_spec(swap.shape)],
            out_specs=[whole_spec(shape.shape)] * count_out,
            scratch_shapes=[
                pltpu.VMEM((count_0, rows_y, 2 * rows_z), BF16),
                pltpu.VMEM((count_1, rows_y, 2 * rows_z), BF16),
                pltpu.VMEM((count_2, rows_y, 2 * rows_z), BF16),
                pltpu.VMEM((count_1, rows_y, rows_z), F32),
                pltpu.VMEM((slab, chunk, rows_y, rows_z), BF16),
            ],
        ),
        out_shape=[shape] * count_out,
        name="chebyshev",
        **params(28),
    )(info, *flat_sides, *flat_pot, *pieces, *pieces_pot, xy, zz, swap)
    return [flat[a * parts : (a + 1) * parts] for a in range(group // 2)]


def shares(planes, rows_y, parts):
    cuts_p = math.gcd(planes, parts)
    cuts_y = parts // cuts_p
    return planes // cuts_p, rows_y // cuts_y, cuts_y


def fill(info_ref, rows, piece, source, first_p, first_y, r, c, bands, group):
    own = bands // group
    start = source * bands + (info_ref[0] ^ r) * own + c * chunk
    where = pl.ds(pl.multiple_of(start, chunk), chunk)
    for p in range(piece.shape[1]):
        rows[first_p + p, pl.ds(first_y, piece.shape[0]), where, :] = piece[:, p]


def gram(info, pieces, packs, bands, bands_all):
    group = 1 + max(r for r, t, c in pieces)
    _, per_y, per_p, _, rows_z = next(iter(pieces.values()))[0].shape
    at_once = 2 if per_p % 2 == 0 else 1
    steps = per_p // at_once
    half = bands_all // 2
    direct = half == bands
    own = bands // group
    ordered = sorted(pieces, key=lambda key: (key[1], key[0], key[2]))

    def in_order(info_ref, value, by_rows):
        axis = 0 if by_rows else 1
        count = value.shape[axis]
        place = lax.broadcasted_iota(jnp.int32, value.shape, axis)
        bit = 1
        while bit < group:
            step = bit * own
            if by_rows:
                blocks = [value[k : k + step] for k in range(0, count, step)]
                blocks = [blocks[k ^ 1] for k in range(len(blocks))]
                moved = jnp.concatenate(blocks, axis=0)
            else:
                low = pltpu.roll(value, count - step, 1)
                high = pltpu.roll(value, step, 1)
                moved = jnp.where(place & step == 0, low, high)
            value = jnp.where((info_ref[0] & bit) != 0, moved, value)
            bit *= 2
        return value

    def direct_blocks(info_ref, out):
        for odd in range(2):

            @pl.when(info_ref[3] == odd)
            def _():
                below = out[half:, :half] if odd == 0 else out[:half, half:bands_all]
                blocks = [out[:half, :half], below, out[half:, half:bands_all]]
                for k, block in enumerate(blocks if odd == 0 else blocks[::-1]):
                    value = in_order(info_ref, in_order(info_ref, block, True), False)
                    out[:half, k * half : (k + 1) * half] = value

    def direct_kernel(info_ref, *refs):
        mine, other, packed, _, out = refs[len(pieces) :]
        by_key = dict(zip(pieces, refs))
        i = pl.program_id(0)
        for k, (r, c) in enumerate(packs):
            packed[k] = by_key[(r, 0, c)][0]
        block = jnp.concatenate(
            [
                jnp.concatenate([by_key[key][0, y, p] for key in ordered], axis=0)
                for p in range(at_once)
                for y in range(per_y)
            ],
            axis=1,
        )
        total = lax.dot_general(
            block, block, (((1,), (1,)), ((), ())), preferred_element_type=F32
        )

        @pl.when(i == 0)
        def _():
            out[:, :bands_all] = total

        @pl.when(i > 0)
        def _():
            out[:, :bands_all] += total

        @pl.when(i == steps - 1)
        def _():
            direct_blocks(info_ref, out)
            for ref, core in ((mine, info_ref[0] & 1), (other, 1 - (info_ref[0] & 1))):
                where = pl.ds(pl.multiple_of(core * (half // 2), half // 2), half // 2)
                ref[...] = out[where, : 3 * half]

    def kernel(info_ref, *refs):
        mine, other, packed, rows, out = refs[len(pieces) :]
        parts = info_ref[4]
        i = pl.program_id(0)
        for (r, t, c), piece in zip(pieces, refs):
            source = lax.rem(info_ref[3] + parts - t, parts)
            fill(info_ref, rows, piece.at[0], source, 0, 0, r, c, bands, group)
            if t == 0 and (r, c) in packs:
                packed[packs.index((r, c))] = piece[0]
        block = jnp.concatenate(
            [rows[p, y] for p in range(at_once) for y in range(per_y)], axis=1
        )
        total = lax.dot_general(
            block, block, (((1,), (1,)), ((), ())), preferred_element_type=F32
        )

        total = [total[:half, :half], total[half:, :half], total[half:, half:]]
        total = jnp.concatenate(total, axis=1)

        @pl.when(i == 0)
        def _():
            out[...] = total

        @pl.when(i > 0)
        def _():
            out[...] += total

        @pl.when(i == steps - 1)
        def _():
            for ref, core in ((mine, info_ref[0] & 1), (other, 1 - (info_ref[0] & 1))):
                ref[...] = out[pl.ds(pl.multiple_of(core * (half // 2), half // 2), half // 2)]

    def spec(index):
        return pl.BlockSpec(
            (1, per_y, at_once, chunk, rows_z), lambda i, info_ref: (index, 0, i, 0, 0)
        )

    return pl.pallas_call(
        direct_kernel if direct else kernel,
        grid_spec=pltpu.PrefetchScalarGridSpec(
            num_scalar_prefetch=1,
            grid=(steps,),
            in_specs=[spec(index) for _, index in pieces.values()],
            out_specs=[pl.BlockSpec((half // 2, 3 * half), lambda i, info_ref: (0, 0))] * 2
            + [
                pl.BlockSpec(
                    (len(packs), per_y, at_once, chunk, rows_z),
                    lambda i, info_ref: (0, 0, i, 0, 0),
                ),
            ],
            scratch_shapes=[
                pltpu.VMEM((1 if direct else at_once, per_y, bands_all, rows_z), BF16),
                pltpu.VMEM((bands_all if direct else half, 3 * half), F32),
            ],
        ),
        out_shape=[jax.ShapeDtypeStruct((half // 2, 3 * half), F32)] * 2
        + [jax.ShapeDtypeStruct((len(packs), per_y, per_p, chunk, rows_z), BF16)],
        name="gram",
        **params(28),
    )(info, *[value for value, _ in pieces.values()])


def inverse_factor(info, mine, other, cells):
    half = 2 * mine.shape[0]
    count = 2 * half

    def exact(a, b, transposed):
        dims = (((1,), (1 if transposed else 0,)), ((), ()))
        return lax.dot_general(
            a, b, dims, precision=lax.Precision.HIGHEST, preferred_element_type=F32
        )

    def eliminate(block):
        groups = half // 8
        row = lax.broadcasted_iota(jnp.int32, (8, half), 0)
        column = lax.broadcasted_iota(jnp.int32, (8, half), 1)
        left = [block[8 * g : 8 * g + 8] for g in range(groups)]
        right = [jnp.where(column == row + 8 * g, 1.0, 0.0).astype(F32) for g in range(groups)]
        for at in range(groups):
            later = range(at, groups)
            spread = [
                [
                    jnp.broadcast_to(left[g][:, 8 * at + k : 8 * at + k + 1], (8, half))
                    for g in later
                ]
                for k in range(8)
            ]
            factors, rows_left, rows_right = [], [], []
            for k in range(8):
                pivot = jnp.broadcast_to(spread[k][0][k : k + 1], (8, half))
                scale = lax.rsqrt(pivot)
                scale = scale * (1.5 - 0.5 * pivot * scale * scale)
                factor = [value * scale for value in spread[k]]
                for m in range(k + 1, 8):
                    other = jnp.broadcast_to(factor[0][m : m + 1], (8, half))
                    spread[m] = [value - f * other for value, f in zip(spread[m], factor)]
                row_left = jnp.broadcast_to(left[at][k : k + 1], (8, half)) * scale
                row_right = jnp.broadcast_to(right[at][k : k + 1], (8, half)) * scale
                inside = jnp.where(row > k, factor[0], 0.0)
                left[at] = jnp.where(row == k, row_left, left[at] - inside * row_left)
                right[at] = jnp.where(row == k, row_right, right[at] - inside * row_right)
                factors.append(factor)
                rows_left.append(row_left)
                rows_right.append(row_right)
            for g in range(at + 1, groups):
                for k in range(8):
                    left[g] = left[g] - factors[k][g - at] * rows_left[k]
                    right[g] = right[g] - factors[k][g - at] * rows_right[k]
        return jnp.concatenate(right, axis=0)

    def kernel(info_ref, mine_ref, other_ref, out, blocks):
        for ref, core in ((mine_ref, info_ref[0] & 1), (other_ref, 1 - (info_ref[0] & 1))):
            where = pl.ds(pl.multiple_of(core * (half // 2), half // 2), half // 2)
            blocks[where] = ref[...] * (1.0 / cells)
        top = eliminate(blocks[:, :half])
        below = exact(blocks[:, half:count], top, True)
        rest = blocks[:, count:] - exact(below, below, True)
        bottom = eliminate(rest)
        out[:half, :half] = top.astype(BF16)
        out[:half, half:] = jnp.zeros((half, half), BF16)
        out[half:, :half] = (-exact(bottom, exact(below, top, False), False)).astype(BF16)
        out[half:, half:] = bottom.astype(BF16)

    return pl.pallas_call(
        kernel,
        grid_spec=pltpu.PrefetchScalarGridSpec(
            num_scalar_prefetch=1,
            grid=(1,),
            in_specs=[pl.BlockSpec(mine.shape, lambda i, info_ref: (0, 0))] * 2,
            out_specs=pl.BlockSpec((count, count), lambda i, info_ref: (0, 0)),
            scratch_shapes=[pltpu.VMEM((half, 3 * half), F32)],
        ),
        out_shape=jax.ShapeDtypeStruct((count, count), BF16),
        name="inverse_factor",
        **params(16),
    )(info, mine, other)


def rotate(info, rotation, pieces, bands, bands_all, planes, rows_y, only, before):
    group = 1 + max(r for r, t, u, c in pieces)
    _, per_y, per_p, _, rows_z = next(iter(pieces.values()))[0].shape
    swap = swap_matrix()
    cuts_y = rows_y // per_y
    at_once = 2 if only is not None and per_p % 2 == 0 else 1 if only is not None else per_p
    steps = per_p // at_once
    span = at_once if only is not None else planes
    given = [] if before is None else [before]
    arrays = {id(value): value for value, _ in pieces.values()}
    slots = {key: k for k, key in enumerate(arrays)}

    def start_of(info_ref, r, t, c):
        source = lax.rem(info_ref[3] + info_ref[4] - t, info_ref[4])
        return source * bands + (info_ref[0] ^ r) * (bands // group) + c * chunk

    def kernel(info_ref, *refs):
        rotation_ref, swap_ref = refs[len(arrays) :][:2]
        out, rows, mixed, turned = refs[-4:]
        me, parts = info_ref[3], info_ref[4]
        if only is None:
            for (r, t, u, c), (value, index) in pieces.items():
                source = lax.rem(me + parts - t, parts)
                part = lax.rem(me + u, parts)
                first_p, first_y = part // cuts_y * per_p, lax.rem(part, cuts_y) * per_y
                piece = refs[slots[id(value)]].at[index]
                fill(info_ref, rows, piece, source, first_p, first_y, r, c, bands, group)
            turned[...] = rotation_ref[...]
        else:

            @pl.when(pl.program_id(0) == 0)
            def _():
                place = lax.broadcasted_iota(jnp.int32, (bands_all, bands_all), 1)
                wanted = lax.broadcasted_iota(jnp.int32, (bands_all, bands_all), 0)
                from_row = place & (chunk - 1)
                for k, (r, t, _, c) in enumerate(pieces):
                    start = jnp.where(place // chunk == k, start_of(info_ref, r, t, c), 0)
                    from_row = from_row + start
                order = jnp.where(wanted == from_row, 1.0, 0.0).astype(BF16)
                value = jnp.dot(rotation_ref[...], order, preferred_element_type=F32)
                turned[...] = value.astype(BF16)

        def row(p, y):
            if only is None:
                return rows[p, y]
            held = [refs[slots[id(value)]][index, y, p] for value, index in pieces.values()]
            return jnp.concatenate(held, axis=0)

        def plane(p):
            for y in range(0, rows_y, 2):
                pair = jnp.concatenate([row(p, y), row(p, y + 1)], axis=1)
                value = jnp.dot(turned[...], pair, preferred_element_type=F32)
                value = value.astype(BF16)
                for k in range(bands // 16):
                    for b in range(2):
                        mixed[k, y + b] = value[
                            16 * k : 16 * k + 16, b * rows_z : (b + 1) * rows_z
                        ]
            for k in range(0, bands // 16, 2):
                pair = [mixed[k + b].reshape(16 * rows_y, rows_z) for b in range(2)]
                moved = jnp.dot(
                    swap_ref[...], jnp.concatenate(pair, axis=1), preferred_element_type=F32
                ).astype(BF16)
                for b in range(2):
                    part = moved[:, b * rows_z : (b + 1) * rows_z].reshape(16, rows_y, rows_z)
                    out[16 * (k + b) : 16 * (k + b) + 16, p] = part

        if only is not None:
            for p in range(span):
                plane(p)
        else:
            pl.loop(0, span)(plane)

    def spec(value):
        return pl.BlockSpec(
            (value.shape[0], per_y, at_once, chunk, rows_z), lambda i, info_ref: (0, 0, i, 0, 0)
        )

    def out_index(i, info_ref):
        if only is None:
            return (0, 0, 0, 0)
        return (0, lax.rem(info_ref[3] + only, info_ref[4]) * steps + i, 0, 0)

    return pl.pallas_call(
        kernel,
        grid_spec=pltpu.PrefetchScalarGridSpec(
            num_scalar_prefetch=1,
            grid=(steps,),
            in_specs=[spec(value) for value in arrays.values()]
            + [
                pl.BlockSpec((bands, bands_all), lambda i, info_ref: (info_ref[3], 0)),
                pl.BlockSpec(swap.shape, lambda i, info_ref: (0, 0)),
            ]
            + [pl.BlockSpec(memory_space=pl.ANY)] * len(given),
            out_specs=pl.BlockSpec((bands, span, rows_y, rows_z), out_index),
            scratch_shapes=[
                pltpu.VMEM((span if only is None else 1, rows_y, bands_all, rows_z), BF16),
                pltpu.VMEM((bands // 16, rows_y, 16, rows_z), BF16),
                pltpu.VMEM((bands, bands_all), BF16),
            ],
        ),
        out_shape=jax.ShapeDtypeStruct((bands, planes, rows_y, rows_z), BF16),
        input_output_aliases={3 + len(arrays): 0} if given else {},
        name="rotate",
        **params(60 if only is None else 28),
    )(info, *arrays.values(), rotation, swap, *given)


def pairwise_sum(value, axis, count, low, high):
    bit = max(low, 1)
    while bit < high:
        value = value + lax.ppermute(value, axis, [(i, i ^ bit) for i in range(count)])
        bit *= 2
    return value


def body(orbital_block, block_scale, potential):
    bands, planes, rows_y, rows_z = orbital_block.shape
    parts, slabs = lax.axis_size("band"), lax.axis_size("domain")
    bands_all = bands * parts
    group = 4 if bands // 4 >= chunk else 2
    chunks = bands // group // chunk
    where, band = lax.axis_index("domain"), lax.axis_index("band")
    info = jnp.stack(
        [
            lax.rem(where, group),
            (where < group).astype(jnp.int32),
            (where >= slabs - group).astype(jnp.int32),
            band,
            jnp.int32(parts),
            jnp.int32(0),
        ]
    ).astype(jnp.int32)
    paired = info.at[5].set(lax.rem(where // group, 2))

    def send(value, r, t):
        if r == 0 and t == 0:
            return value
        pairs = [
            (q * slabs + i, (q + t) % parts * slabs + (i ^ r))
            for q in range(parts)
            for i in range(slabs)
        ]
        return lax.ppermute(value, ("band", "domain"), pairs)

    scale = jnp.broadcast_to(block_scale[:, :, None], (bands, planes, rows_z))
    far_first = sorted(range(group), reverse=True)
    arrived = []
    for c in range(chunks):
        pieces = prepare(info, orbital_block, scale, potential, c, group, c == 0)
        sent = {r: send(pieces[r], r, 0) for r in far_first}
        arrived.append([sent[r] for r in range(group)])
    def after(value, *others):
        return lax.optimization_barrier((value, *others))[0] if others else value

    def swapped(value, odd):
        lower = [i for i in range(slabs - group) if i // group % 2 == odd]
        pairs = [(i, i + group) for i in lower] + [(i + group, i) for i in lower]
        return lax.ppermute(value, "domain", pairs)

    def shifted(value, by):
        pairs = [(i, i + by) for i in range(slabs) if 0 <= i + by < slabs]
        return lax.ppermute(value, "domain", pairs)

    sides = []
    for c in range(chunks):
        first, second = edges(paired if c else info, arrived[c], 1 if c else 2)
        if c == 0:
            sides.append(
                [[shifted(end, -group) for end in second], [shifted(end, group) for end in first]]
            )
        else:
            sides.append([[swapped(end, 0) for end in first], [swapped(end, 1) for end in second]])
        last_end = first[0]
    pieces, own, moved, crossed = {}, {}, {}, {}
    ready = [last_end]
    for c in range(chunks):
        order = after(paired if c else info, *ready)
        filtered = chebyshev(order, sides[c], arrived[c], sides[0], arrived[0], parts)
        ready = [filtered[0][0]]
        for a in reversed(range(group // 2)):
            for t in reversed(range(parts)):
                value = filtered[a][t]
                own[(a, t, c)] = value
                moved[(a, t, c)] = send(value, 2 * a, t)
    for c in range(chunks):
        keys = [(a, t) for t in range(parts) for a in range(group // 2)]
        there = {key: after(moved[(*key, c)], *ready) for key in keys}
        crossed[c] = send(jnp.stack([there[key][1] for key in keys]), 1, 0)
        for k, (a, t) in enumerate(keys):
            pieces[(2 * a, t, c)] = (there[(a, t)], 0)
            pieces[(2 * a + 1, t, c)] = (crossed[c], k)

    known = {(r, t, 0, c): value for (r, t, c), value in pieces.items()}
    late = {}
    early = parts == 2 and chunks > 1 and group == 4
    if early:
        came = [moved[(a, 1, chunks - 1)] for a in range(2)]
        first = lax.ppermute(after(own[(0, 0, 0)][0], *came), "band", [(0, 1)])
        known[(0, 1, 1, 0)] = (first[None], 0)
        chosen = [(r, c, *pieces[(r, 0, c)]) for r, c in ((0, chunks - 1), (1, 0))]
        sent = jnp.stack([value[index] for _, _, value, index in chosen])
        sent = lax.ppermute(after(sent, *came), "band", [(0, 1)])
        for k, (r, c, _, _) in enumerate(chosen):
            known[(r, 1, 1, c)] = (sent, k)
    packs = [
        (r, c)
        for c in range(chunks)
        for r in range(group)
        if parts > 2 or (r, 1, 1, c) not in known
    ]
    mine, other, buffer = gram(after(info, *([first] if early else [])), pieces, packs, bands, bands_all)
    mine = mine + send(other, 1, 0)
    mine = pairwise_sum(mine, "domain", slabs, 2, group)
    for key, value in own.items():
        if key[1] > 0:
            late[key] = send(after(value, mine), 2 * key[0], 0)
    if early:
        mine = after(mine, sent)
    mine = pairwise_sum(mine, "band", parts, 0, parts)

    def forward(buffer, t, packs):
        for s in range(1, parts):
            if t != s:
                sent = lax.ppermute(buffer, "band", [(q, q + s) for q in range(parts - s)])
                for k, (r, c) in enumerate(packs):
                    known[(r, s, (t - s) % parts, c)] = (sent, k)

    forward(after(buffer, mine), 0, packs)
    mine = pairwise_sum(mine, "domain", slabs, group, slabs)
    rotation = inverse_factor(info, mine, send(mine, 1, 0), planes * rows_y * rows_z * slabs)
    for t in range(1, parts):
        keys = [(a, c) for c in range(chunks) for a in range(group // 2)]
        far = send(jnp.stack([after(late[(a, t, c)], rotation)[1] for a, c in keys]), 1, 0)
        for k, (a, c) in enumerate(keys):
            known[(2 * a, 0, t, c)] = (late[(a, t, c)], 0)
            known[(2 * a + 1, 0, t, c)] = (far, k)
        if parts > 2:
            chosen = [known[(r, 0, t, c)] for r, c in packs]
            forward(jnp.stack([value[index] for value, index in chosen]), t, packs)
    out = None
    for only in range(parts) if parts == 2 and planes % 2 == 0 else [None]:
        chosen = {key: value for key, value in known.items() if only in (None, key[2])}
        out = rotate(info, rotation, chosen, bands, bands_all, planes, rows_y, only, out)
    return out


def solution(mesh):
    in_specs = (P("band", "domain", None, None), P("band", "domain"), P("domain", None, None))
    out_specs = P("band", "domain", None, None)
    return jax.shard_map(body, mesh=mesh, in_specs=in_specs, out_specs=out_specs, check_vma=False)
```

```python
import math

import jax
import jax.numpy as jnp
import numpy as np
from jax import lax
from jax.experimental import pallas as pl
from jax.experimental.pallas import tpu as pltpu
from jax.sharding import PartitionSpec as P

grid_step = 0.5
stencil_coef = (
    -5369.0 / 1800.0,
    12.0 / 7.0,
    -15.0 / 56.0,
    10.0 / 189.0,
    -1.0 / 112.0,
    2.0 / 1925.0,
    -1.0 / 16632.0,
)
lower_end = -4.0
cut_energy = 6.0
upper_end = 43.0
kinetic = -0.5 / (grid_step * grid_step)
coef_scale = 7.0
reach = 6
edge = 3 * reach
chunk = 16
F32, BF16 = jnp.float32, jnp.bfloat16


def filter_terms():
    width_e = (upper_end - cut_energy) / 2.0
    centre = (upper_end + cut_energy) / 2.0
    sigma_one = width_e / (lower_end - centre)
    gamma_term = 2.0 / sigma_one
    sigma_two = 1.0 / (gamma_term - sigma_one)
    sigma_three = 1.0 / (gamma_term - sigma_two)
    return (width_e, centre, sigma_one, sigma_two, sigma_three)


def stencil_line(count):
    line = np.zeros((count, count), np.float64)
    for offset in range(1, reach + 1):
        value = kinetic * stencil_coef[offset] * coef_scale
        line += value * (np.eye(count, k=offset) + np.eye(count, k=-offset))
    return line


def xy_matrix(planes, rows_y):
    along_x = np.zeros((planes, planes + 2 * reach), np.float64)
    along_x[:, :] = stencil_line(planes + 2 * reach)[reach : reach + planes]
    middle = np.eye(planes, planes + 2 * reach, k=reach)
    full = np.kron(along_x, np.eye(rows_y)) + np.kron(middle, stencil_line(rows_y))
    return jnp.asarray(full, BF16)


def z_matrix(count_z):
    return jnp.asarray(np.kron(np.eye(2), stencil_line(count_z)), BF16)


def swap_matrix():
    full = np.zeros((256, 256), np.float32)
    for a in range(16):
        for b in range(16):
            full[a * 16 + b, b * 16 + a] = 1.0
    return jnp.asarray(full, BF16)


def params(mebibytes):
    return dict(
        compiler_params=pltpu.CompilerParams(
            vmem_limit_bytes=mebibytes * 2**20, dimension_semantics=("arbitrary",)
        ),
        cost_estimate=pl.CostEstimate(flops=1, bytes_accessed=1, transcendentals=0),
    )


def prepare(info, orbitals, scale, potential, part, group, with_potential):
    bands, planes, rows_y, rows_z = orbitals.shape
    own = bands // group
    at_once = 8
    steps = chunk // at_once
    total = chunk + (2 if with_potential else 0)

    def kernel(info_ref, *refs):
        sources, scales, potential_ref = refs[:group], refs[group : 2 * group], refs[2 * group]
        outs = refs[2 * group + 1 :]
        i = pl.program_id(0)
        for r in range(group):
            for b in range(at_once):
                value = sources[r][b].astype(F32) * scales[r][b][:, None, :]
                outs[r][i * at_once + b] = value.astype(BF16)

        if with_potential:

            @pl.when(i == 0)
            def _():
                high = potential_ref[...].astype(BF16)
                low = (potential_ref[...] - high.astype(F32)).astype(BF16)
                for r in range(group):
                    outs[r][chunk] = high
                    outs[r][chunk + 1] = low

    def first(r, i, info_ref):
        return ((info_ref[0] ^ r) * own + part * chunk) // at_once + i

    def source_spec(r):
        return pl.BlockSpec(
            (at_once, planes, rows_y, rows_z),
            lambda i, info_ref: (first(r, i, info_ref), 0, 0, 0),
        )

    def scale_spec(r):
        return pl.BlockSpec(
            (at_once, planes, rows_z), lambda i, info_ref: (first(r, i, info_ref), 0, 0)
        )

    shape = jax.ShapeDtypeStruct((total, planes, rows_y, rows_z), BF16)
    return pl.pallas_call(
        kernel,
        grid_spec=pltpu.PrefetchScalarGridSpec(
            num_scalar_prefetch=1,
            grid=(steps,),
            in_specs=[source_spec(r) for r in range(group)]
            + [scale_spec(r) for r in range(group)]
            + [pl.BlockSpec((planes, rows_y, rows_z), lambda i, info_ref: (0, 0, 0))],
            out_specs=[pl.BlockSpec(shape.shape, lambda i, info_ref: (0, 0, 0, 0))] * group,
        ),
        out_shape=[shape] * group,
        name="prepare",
        **params(14),
    )(info, *([orbitals] * group), *([scale] * group), potential)


def edges(info, pieces, cuts):
    group = len(pieces)
    total, planes, rows_y, rows_z = pieces[0].shape
    rest = edge - planes
    width = edge // cuts
    at_once = 6 if total % 6 == 0 else 4

    def kernel(info_ref, *refs):
        sources, outs = refs[:group], refs[group:]

        def put(targets, to, source, begin, count):
            while count:
                size = min(count, width - to % width)
                target = targets[to // width]
                target[:, to % width : to % width + size] = source[:, begin : begin + size]
                to, begin, count = to + size, begin + size, count - size

        for odd in range(2):
            up, down = (outs[k * cuts : (k + 1) * cuts] for k in (odd, 1 - odd))
            for r in range(group):
                slab = jnp.where(info_ref[5] == odd, info_ref[0] ^ r, -1)

                @pl.when(slab == group - 1)
                def _():
                    put(up, rest, sources[r], 0, planes)

                @pl.when(slab == group - 2)
                def _():
                    put(up, 0, sources[r], planes - rest, rest)

                @pl.when(slab == 0)
                def _():
                    put(down, 0, sources[r], 0, planes)

                @pl.when(slab == 1)
                def _():
                    put(down, planes, sources[r], 0, rest)

    def spec(count):
        return pl.BlockSpec((at_once, count, rows_y, rows_z), lambda i, info_ref: (i, 0, 0, 0))

    flat = pl.pallas_call(
        kernel,
        grid_spec=pltpu.PrefetchScalarGridSpec(
            num_scalar_prefetch=1,
            grid=(total // at_once,),
            in_specs=[spec(planes)] * group,
            out_specs=[spec(width)] * (2 * cuts),
        ),
        out_shape=[jax.ShapeDtypeStruct((total, width, rows_y, rows_z), BF16)] * (2 * cuts),
        name="edges",
        **params(8),
    )(info, *pieces)
    return flat[:cuts], flat[cuts:]


def chebyshev(info, sides, pieces, sides_pot, pieces_pot, parts):
    group = len(pieces)
    _, planes, rows_y, rows_z = pieces[0].shape
    slab = group * planes
    per_p, per_y, cuts_y = shares(planes, rows_y, parts)
    at_once = 2 if per_p % 2 == 0 else 1
    steps = chunk // 2
    count_out = group // 2 * parts
    flat_sides, flat_pot = ([value for side in both for value in side] for both in (sides, sides_pot))
    cuts, cuts_pot = len(sides[0]), len(sides_pot[0])
    width, width_pot = edge // cuts, edge // cuts_pot
    width_e, centre, sigma_one, sigma_two, sigma_three = filter_terms()
    diagonal = 3.0 * stencil_coef[0] * kinetic - centre
    tile_rows = planes * rows_y
    xy, zz, swap = xy_matrix(planes, rows_y), z_matrix(rows_z), swap_matrix()
    count_0, count_1, count_2 = slab + 6 * reach, slab + 4 * reach, slab + 2 * reach

    def kernel(info_ref, *refs):
        side_refs, refs = refs[: 2 * cuts], refs[2 * cuts :]
        side_pot_refs, refs = refs[: 2 * cuts_pot], refs[2 * cuts_pot :]
        piece_refs, pot_refs = refs[:group], refs[group : 2 * group]
        xy_ref, zz_ref, swap_ref = refs[2 * group : 3 + 2 * group]
        outs = refs[3 + 2 * group : 3 + 2 * group + count_out]
        field, first, second, energy, result = refs[3 + 2 * group + count_out :]
        i = pl.program_id(0)
        me = info_ref[0]
        at_left, at_right = info_ref[1] == 1, info_ref[2] == 1

        @pl.when(i == 0)
        def _():
            def store(start, source):
                total = source[0].astype(F32) + source[1].astype(F32)
                energy[pl.ds(start, source.shape[1])] = coef_scale * (total + diagonal)

            for side, base, low, high in (
                (side_pot_refs[cuts_pot:], -reach, 0, 2 * reach),
                (side_pot_refs[:cuts_pot], slab + 2 * reach, slab + 2 * reach, count_1),
            ):
                for k, ref in enumerate(side):
                    start = base + k * width_pot
                    begin, end = max(start, low), min(start + width_pot, high)
                    if begin < end:
                        store(begin, ref.at[:, begin - start : end - start])
            for r in range(group):
                store(2 * reach + planes * (me ^ r), pot_refs[r])

        for b in range(2):
            lanes = slice(b * rows_z, (b + 1) * rows_z)
            for k in range(2):
                start = (1 - (info_ref[5] ^ k)) * (edge + slab)
                for n in range(cuts):
                    where = pl.ds(start + n * width, width)
                    field[where, :, lanes] = side_refs[k * cuts + n][b]
            for r in range(group):
                field[pl.ds(edge + planes * (me ^ r), planes), :, lanes] = piece_refs[r][b]

        def apply(source, start, energy_start):
            rows = source[pl.ds(start, planes + 2 * reach)].reshape(-1, 2 * rows_z)
            middle = source[pl.ds(start + reach, planes)].reshape(tile_rows, 2 * rows_z)
            total = jnp.dot(xy_ref[...], rows, preferred_element_type=F32)
            total += jnp.dot(middle, zz_ref[...], preferred_element_type=F32)
            factor = energy[pl.ds(energy_start, planes)].reshape(tile_rows, rows_z)
            factor = jnp.concatenate([factor, factor], axis=1)
            return total + factor * middle.astype(F32)

        def block(value):
            return value.astype(BF16).reshape(planes, rows_y, 2 * rows_z)

        def previous(source, start):
            return source[pl.ds(start, planes)].reshape(tile_rows, 2 * rows_z).astype(F32)

        for t in range(count_1 // planes):
            at = t * planes
            value = apply(field, at, at) * (sigma_one / width_e / coef_scale)
            first[at : at + planes] = block(value)

        @pl.when(at_left)
        def _():
            first[: 2 * reach] = jnp.zeros((2 * reach, rows_y, 2 * rows_z), BF16)

        @pl.when(at_right)
        def _():
            first[count_1 - 2 * reach :] = jnp.zeros((2 * reach, rows_y, 2 * rows_z), BF16)

        for t in range(count_2 // planes):
            at = t * planes
            value = apply(first, at, at + reach) * (2.0 * sigma_two / width_e / coef_scale)
            value -= sigma_one * sigma_two * previous(field, at + 2 * reach)
            second[at : at + planes] = block(value)

        @pl.when(at_left)
        def _():
            second[:reach] = jnp.zeros((reach, rows_y, 2 * rows_z), BF16)

        @pl.when(at_right)
        def _():
            second[count_2 - reach :] = jnp.zeros((reach, rows_y, 2 * rows_z), BF16)

        for t in range(group):
            at = t * planes
            value = apply(second, at, at + 2 * reach) * (2.0 * sigma_three / width_e / coef_scale)
            value -= sigma_two * sigma_three * previous(first, at + 2 * reach)
            value = block(value)
            for b in range(2):
                part = value[:, :, b * rows_z : (b + 1) * rows_z]
                result[at : at + planes, 2 * i + b] = part

        @pl.when(i == steps - 1)
        def _():
            for t in range(parts):
                part = lax.rem(info_ref[3] + t, parts)
                begin = lax.rem(part, cuts_y) * (per_y * chunk)
                begin = pl.multiple_of(begin, per_y * chunk)
                for r in range(group):
                    start = planes * (me ^ r) + part // cuts_y * per_p
                    for p in range(0, per_p, at_once):
                        pair = [
                            result[start + p + k].reshape(chunk * rows_y, rows_z)
                            for k in range(at_once)
                        ]
                        moved = jnp.dot(
                            swap_ref[pl.ds(begin, per_y * chunk), :],
                            jnp.concatenate(pair, axis=1),
                            preferred_element_type=F32,
                        ).astype(BF16)
                        for k in range(at_once):
                            value = moved[:, k * rows_z : (k + 1) * rows_z]
                            out = outs[r // 2 * parts + t]
                            out[r % 2, :, p + k] = value.reshape(per_y, chunk, rows_z)

    def block_spec(count, index):
        return pl.BlockSpec((2, count, rows_y, rows_z), index)

    def whole_spec(shape):
        return pl.BlockSpec(shape, lambda i, info_ref: (0,) * len(shape))

    moving = lambda i, info_ref: (i, 0, 0, 0)
    fixed = lambda i, info_ref: (steps, 0, 0, 0)
    shape = jax.ShapeDtypeStruct((2, per_y, per_p, chunk, rows_z), BF16)
    flat = pl.pallas_call(
        kernel,
        grid_spec=pltpu.PrefetchScalarGridSpec(
            num_scalar_prefetch=1,
            grid=(steps,),
            in_specs=[block_spec(width, moving)] * (2 * cuts)
            + [block_spec(width_pot, fixed)] * (2 * cuts_pot)
            + [block_spec(planes, moving)] * group
            + [block_spec(planes, fixed)] * group
            + [whole_spec(xy.shape), whole_spec(zz.shape), whole_spec(swap.shape)],
            out_specs=[whole_spec(shape.shape)] * count_out,
            scratch_shapes=[
                pltpu.VMEM((count_0, rows_y, 2 * rows_z), BF16),
                pltpu.VMEM((count_1, rows_y, 2 * rows_z), BF16),
                pltpu.VMEM((count_2, rows_y, 2 * rows_z), BF16),
                pltpu.VMEM((count_1, rows_y, rows_z), F32),
                pltpu.VMEM((slab, chunk, rows_y, rows_z), BF16),
            ],
        ),
        out_shape=[shape] * count_out,
        name="chebyshev",
        **params(18),
    )(info, *flat_sides, *flat_pot, *pieces, *pieces_pot, xy, zz, swap)
    return [flat[a * parts : (a + 1) * parts] for a in range(group // 2)]


def shares(planes, rows_y, parts):
    cuts_p = math.gcd(planes, parts)
    cuts_y = parts // cuts_p
    return planes // cuts_p, rows_y // cuts_y, cuts_y


def fill(info_ref, rows, piece, source, first_p, first_y, r, c, bands, group):
    own = bands // group
    start = source * bands + (info_ref[0] ^ r) * own + c * chunk
    where = pl.ds(pl.multiple_of(start, chunk), chunk)
    for p in range(piece.shape[1]):
        rows[first_p + p, pl.ds(first_y, piece.shape[0]), where, :] = piece[:, p]


def gram(info, pieces, packs, bands, bands_all):
    group = 1 + max(r for r, t, c in pieces)
    _, per_y, per_p, _, rows_z = next(iter(pieces.values()))[0].shape
    at_once = 2 if per_p % 2 == 0 else 1
    steps = per_p // at_once
    half = bands_all // 2
    direct = half == bands
    own = bands // group
    ordered = sorted(pieces, key=lambda key: (key[1], key[0], key[2]))

    def in_order(info_ref, value, by_rows):
        axis = 0 if by_rows else 1
        count = value.shape[axis]
        place = lax.broadcasted_iota(jnp.int32, value.shape, axis)
        bit = 1
        while bit < group:
            step = bit * own
            if by_rows:
                blocks = [value[k : k + step] for k in range(0, count, step)]
                blocks = [blocks[k ^ 1] for k in range(len(blocks))]
                moved = jnp.concatenate(blocks, axis=0)
            else:
                low = pltpu.roll(value, count - step, 1)
                high = pltpu.roll(value, step, 1)
                moved = jnp.where(place & step == 0, low, high)
            value = jnp.where((info_ref[0] & bit) != 0, moved, value)
            bit *= 2
        return value

    def direct_blocks(info_ref, out):
        for odd in range(2):

            @pl.when(info_ref[3] == odd)
            def _():
                below = out[half:, :half] if odd == 0 else out[:half, half:bands_all]
                blocks = [out[:half, :half], below, out[half:, half:bands_all]]
                for k, block in enumerate(blocks if odd == 0 else blocks[::-1]):
                    value = in_order(info_ref, in_order(info_ref, block, True), False)
                    out[:half, k * half : (k + 1) * half] = value

    def direct_kernel(info_ref, *refs):
        mine, other, packed, _, out = refs[len(pieces) :]
        by_key = dict(zip(pieces, refs))
        i = pl.program_id(0)
        for k, (r, c) in enumerate(packs):
            packed[k] = by_key[(r, 0, c)][0]
        block = jnp.concatenate(
            [
                jnp.concatenate([by_key[key][0, y, p] for key in ordered], axis=0)
                for p in range(at_once)
                for y in range(per_y)
            ],
            axis=1,
        )
        total = lax.dot_general(
            block, block, (((1,), (1,)), ((), ())), preferred_element_type=F32
        )

        @pl.when(i == 0)
        def _():
            out[:, :bands_all] = total

        @pl.when(i > 0)
        def _():
            out[:, :bands_all] += total

        @pl.when(i == steps - 1)
        def _():
            direct_blocks(info_ref, out)
            for ref, core in ((mine, info_ref[0] & 1), (other, 1 - (info_ref[0] & 1))):
                where = pl.ds(pl.multiple_of(core * (half // 2), half // 2), half // 2)
                ref[...] = out[where, : 3 * half]

    def kernel(info_ref, *refs):
        mine, other, packed, rows, out = refs[len(pieces) :]
        parts = info_ref[4]
        i = pl.program_id(0)
        for (r, t, c), piece in zip(pieces, refs):
            source = lax.rem(info_ref[3] + parts - t, parts)
            fill(info_ref, rows, piece.at[0], source, 0, 0, r, c, bands, group)
            if t == 0 and (r, c) in packs:
                packed[packs.index((r, c))] = piece[0]
        block = jnp.concatenate(
            [rows[p, y] for p in range(at_once) for y in range(per_y)], axis=1
        )
        total = lax.dot_general(
            block, block, (((1,), (1,)), ((), ())), preferred_element_type=F32
        )

        total = [total[:half, :half], total[half:, :half], total[half:, half:]]
        total = jnp.concatenate(total, axis=1)

        @pl.when(i == 0)
        def _():
            out[...] = total

        @pl.when(i > 0)
        def _():
            out[...] += total

        @pl.when(i == steps - 1)
        def _():
            for ref, core in ((mine, info_ref[0] & 1), (other, 1 - (info_ref[0] & 1))):
                ref[...] = out[pl.ds(pl.multiple_of(core * (half // 2), half // 2), half // 2)]

    def spec(index):
        return pl.BlockSpec(
            (1, per_y, at_once, chunk, rows_z), lambda i, info_ref: (index, 0, i, 0, 0)
        )

    return pl.pallas_call(
        direct_kernel if direct else kernel,
        grid_spec=pltpu.PrefetchScalarGridSpec(
            num_scalar_prefetch=1,
            grid=(steps,),
            in_specs=[spec(index) for _, index in pieces.values()],
            out_specs=[pl.BlockSpec((half // 2, 3 * half), lambda i, info_ref: (0, 0))] * 2
            + [
                pl.BlockSpec(
                    (len(packs), per_y, at_once, chunk, rows_z),
                    lambda i, info_ref: (0, 0, i, 0, 0),
                ),
            ],
            scratch_shapes=[
                pltpu.VMEM((1 if direct else at_once, per_y, bands_all, rows_z), BF16),
                pltpu.VMEM((bands_all if direct else half, 3 * half), F32),
            ],
        ),
        out_shape=[jax.ShapeDtypeStruct((half // 2, 3 * half), F32)] * 2
        + [jax.ShapeDtypeStruct((len(packs), per_y, per_p, chunk, rows_z), BF16)],
        name="gram",
        **params(16),
    )(info, *[value for value, _ in pieces.values()])


def inverse_factor(info, mine, other, cells):
    half = 2 * mine.shape[0]
    count = 2 * half

    def exact(a, b, transposed):
        dims = (((1,), (1 if transposed else 0,)), ((), ()))
        return lax.dot_general(
            a, b, dims, precision=lax.Precision.HIGHEST, preferred_element_type=F32
        )

    def eliminate(block):
        groups = half // 8
        row = lax.broadcasted_iota(jnp.int32, (8, half), 0)
        column = lax.broadcasted_iota(jnp.int32, (8, half), 1)
        left = [block[8 * g : 8 * g + 8] for g in range(groups)]
        right = [jnp.where(column == row + 8 * g, 1.0, 0.0).astype(F32) for g in range(groups)]
        for at in range(groups):
            later = range(at, groups)
            spread = [
                [
                    jnp.broadcast_to(left[g][:, 8 * at + k : 8 * at + k + 1], (8, half))
                    for g in later
                ]
                for k in range(8)
            ]
            factors, rows_left, rows_right = [], [], []
            for k in range(8):
                pivot = jnp.broadcast_to(spread[k][0][k : k + 1], (8, half))
                scale = lax.rsqrt(pivot)
                scale = scale * (1.5 - 0.5 * pivot * scale * scale)
                factor = [value * scale for value in spread[k]]
                for m in range(k + 1, 8):
                    other = jnp.broadcast_to(factor[0][m : m + 1], (8, half))
                    spread[m] = [value - f * other for value, f in zip(spread[m], factor)]
                row_left = jnp.broadcast_to(left[at][k : k + 1], (8, half)) * scale
                row_right = jnp.broadcast_to(right[at][k : k + 1], (8, half)) * scale
                inside = jnp.where(row > k, factor[0], 0.0)
                left[at] = jnp.where(row == k, row_left, left[at] - inside * row_left)
                right[at] = jnp.where(row == k, row_right, right[at] - inside * row_right)
                factors.append(factor)
                rows_left.append(row_left)
                rows_right.append(row_right)
            for g in range(at + 1, groups):
                for k in range(8):
                    left[g] = left[g] - factors[k][g - at] * rows_left[k]
                    right[g] = right[g] - factors[k][g - at] * rows_right[k]
        return jnp.concatenate(right, axis=0)

    def kernel(info_ref, mine_ref, other_ref, out, blocks):
        for ref, core in ((mine_ref, info_ref[0] & 1), (other_ref, 1 - (info_ref[0] & 1))):
            where = pl.ds(pl.multiple_of(core * (half // 2), half // 2), half // 2)
            blocks[where] = ref[...] * (1.0 / cells)
        top = eliminate(blocks[:, :half])
        below = exact(blocks[:, half:count], top, True)
        rest = blocks[:, count:] - exact(below, below, True)
        bottom = eliminate(rest)
        out[:half, :half] = top.astype(BF16)
        out[:half, half:] = jnp.zeros((half, half), BF16)
        out[half:, :half] = (-exact(bottom, exact(below, top, False), False)).astype(BF16)
        out[half:, half:] = bottom.astype(BF16)

    return pl.pallas_call(
        kernel,
        grid_spec=pltpu.PrefetchScalarGridSpec(
            num_scalar_prefetch=1,
            grid=(1,),
            in_specs=[pl.BlockSpec(mine.shape, lambda i, info_ref: (0, 0))] * 2,
            out_specs=pl.BlockSpec((count, count), lambda i, info_ref: (0, 0)),
            scratch_shapes=[pltpu.VMEM((half, 3 * half), F32)],
        ),
        out_shape=jax.ShapeDtypeStruct((count, count), BF16),
        name="inverse_factor",
        **params(8),
    )(info, mine, other)


def rotate(info, rotation, pieces, bands, bands_all, planes, rows_y, only, before):
    group = 1 + max(r for r, t, u, c in pieces)
    _, per_y, per_p, _, rows_z = next(iter(pieces.values()))[0].shape
    swap = swap_matrix()
    cuts_y = rows_y // per_y
    at_once = 2 if only is not None and per_p % 2 == 0 else 1 if only is not None else per_p
    steps = per_p // at_once
    span = at_once if only is not None else planes
    given = [] if before is None else [before]
    arrays = {id(value): value for value, _ in pieces.values()}
    slots = {key: k for k, key in enumerate(arrays)}

    def start_of(info_ref, r, t, c):
        source = lax.rem(info_ref[3] + info_ref[4] - t, info_ref[4])
        return source * bands + (info_ref[0] ^ r) * (bands // group) + c * chunk

    def kernel(info_ref, *refs):
        rotation_ref, swap_ref = refs[len(arrays) :][:2]
        out, rows, mixed, turned = refs[-4:]
        me, parts = info_ref[3], info_ref[4]
        if only is None:
            for (r, t, u, c), (value, index) in pieces.items():
                source = lax.rem(me + parts - t, parts)
                part = lax.rem(me + u, parts)
                first_p, first_y = part // cuts_y * per_p, lax.rem(part, cuts_y) * per_y
                piece = refs[slots[id(value)]].at[index]
                fill(info_ref, rows, piece, source, first_p, first_y, r, c, bands, group)
            turned[...] = rotation_ref[...]
        else:

            @pl.when(pl.program_id(0) == 0)
            def _():
                place = lax.broadcasted_iota(jnp.int32, (bands_all, bands_all), 1)
                wanted = lax.broadcasted_iota(jnp.int32, (bands_all, bands_all), 0)
                from_row = place & (chunk - 1)
                for k, (r, t, _, c) in enumerate(pieces):
                    start = jnp.where(place // chunk == k, start_of(info_ref, r, t, c), 0)
                    from_row = from_row + start
                order = jnp.where(wanted == from_row, 1.0, 0.0).astype(BF16)
                value = jnp.dot(rotation_ref[...], order, preferred_element_type=F32)
                turned[...] = value.astype(BF16)

        def row(p, y):
            if only is None:
                return rows[p, y]
            held = [refs[slots[id(value)]][index, y, p] for value, index in pieces.values()]
            return jnp.concatenate(held, axis=0)

        def plane(p):
            for y in range(0, rows_y, 2):
                pair = jnp.concatenate([row(p, y), row(p, y + 1)], axis=1)
                value = jnp.dot(turned[...], pair, preferred_element_type=F32)
                value = value.astype(BF16)
                for k in range(bands // 16):
                    for b in range(2):
                        mixed[k, y + b] = value[
                            16 * k : 16 * k + 16, b * rows_z : (b + 1) * rows_z
                        ]
            for k in range(0, bands // 16, 2):
                pair = [mixed[k + b].reshape(16 * rows_y, rows_z) for b in range(2)]
                moved = jnp.dot(
                    swap_ref[...], jnp.concatenate(pair, axis=1), preferred_element_type=F32
                ).astype(BF16)
                for b in range(2):
                    part = moved[:, b * rows_z : (b + 1) * rows_z].reshape(16, rows_y, rows_z)
                    out[16 * (k + b) : 16 * (k + b) + 16, p] = part

        if only is not None:
            for p in range(span):
                plane(p)
        else:
            pl.loop(0, span)(plane)

    def spec(value):
        return pl.BlockSpec(
            (value.shape[0], per_y, at_once, chunk, rows_z), lambda i, info_ref: (0, 0, i, 0, 0)
        )

    def out_index(i, info_ref):
        if only is None:
            return (0, 0, 0, 0)
        return (0, lax.rem(info_ref[3] + only, info_ref[4]) * steps + i, 0, 0)

    return pl.pallas_call(
        kernel,
        grid_spec=pltpu.PrefetchScalarGridSpec(
            num_scalar_prefetch=1,
            grid=(steps,),
            in_specs=[spec(value) for value in arrays.values()]
            + [
                pl.BlockSpec((bands, bands_all), lambda i, info_ref: (info_ref[3], 0)),
                pl.BlockSpec(swap.shape, lambda i, info_ref: (0, 0)),
            ]
            + [pl.BlockSpec(memory_space=pl.ANY)] * len(given),
            out_specs=pl.BlockSpec((bands, span, rows_y, rows_z), out_index),
            scratch_shapes=[
                pltpu.VMEM((span if only is None else 1, rows_y, bands_all, rows_z), BF16),
                pltpu.VMEM((bands // 16, rows_y, 16, rows_z), BF16),
                pltpu.VMEM((bands, bands_all), BF16),
            ],
        ),
        out_shape=jax.ShapeDtypeStruct((bands, planes, rows_y, rows_z), BF16),
        input_output_aliases={3 + len(arrays): 0} if given else {},
        name="rotate",
        **params(60 if only is None else 14),
    )(info, *arrays.values(), rotation, swap, *given)


def pairwise_sum(value, axis, count, low, high):
    bit = max(low, 1)
    while bit < high:
        value = value + lax.ppermute(value, axis, [(i, i ^ bit) for i in range(count)])
        bit *= 2
    return value


def body(orbital_block, block_scale, potential):
    bands, planes, rows_y, rows_z = orbital_block.shape
    parts, slabs = lax.axis_size("band"), lax.axis_size("domain")
    bands_all = bands * parts
    group = 4 if bands // 4 >= chunk else 2
    chunks = bands // group // chunk
    where, band = lax.axis_index("domain"), lax.axis_index("band")
    info = jnp.stack(
        [
            lax.rem(where, group),
            (where < group).astype(jnp.int32),
            (where >= slabs - group).astype(jnp.int32),
            band,
            jnp.int32(parts),
            jnp.int32(0),
        ]
    ).astype(jnp.int32)
    paired = info.at[5].set(lax.rem(where // group, 2))

    def send(value, r, t):
        if r == 0 and t == 0:
            return value
        pairs = [
            (q * slabs + i, (q + t) % parts * slabs + (i ^ r))
            for q in range(parts)
            for i in range(slabs)
        ]
        return lax.ppermute(value, ("band", "domain"), pairs)

    scale = jnp.broadcast_to(block_scale[:, :, None], (bands, planes, rows_z))
    far_first = sorted(range(group), reverse=True)
    arrived = []
    for c in range(chunks):
        pieces = prepare(info, orbital_block, scale, potential, c, group, c == 0)
        sent = {r: send(pieces[r], r, 0) for r in far_first}
        arrived.append([sent[r] for r in range(group)])
    def after(value, *others):
        return lax.optimization_barrier((value, *others))[0] if others else value

    def swapped(value, odd):
        lower = [i for i in range(slabs - group) if i // group % 2 == odd]
        pairs = [(i, i + group) for i in lower] + [(i + group, i) for i in lower]
        return lax.ppermute(value, "domain", pairs)

    def shifted(value, by):
        pairs = [(i, i + by) for i in range(slabs) if 0 <= i + by < slabs]
        return lax.ppermute(value, "domain", pairs)

    sides = []
    for c in range(chunks):
        first, second = edges(paired if c else info, arrived[c], 1 if c else 2)
        if c == 0:
            sides.append(
                [[shifted(end, -group) for end in second], [shifted(end, group) for end in first]]
            )
        else:
            sides.append([[swapped(end, 0) for end in first], [swapped(end, 1) for end in second]])
        last_end = first[0]
    pieces, own, moved, crossed = {}, {}, {}, {}
    ready = [last_end]
    for c in range(chunks):
        order = after(paired if c else info, *ready)
        filtered = chebyshev(order, sides[c], arrived[c], sides[0], arrived[0], parts)
        ready = [filtered[0][0]]
        for a in reversed(range(group // 2)):
            for t in reversed(range(parts)):
                value = filtered[a][t]
                own[(a, t, c)] = value
                moved[(a, t, c)] = send(value, 2 * a, t)
    known = {}
    early = parts == 2 and chunks > 1 and group == 4
    if early:
        first = lax.ppermute(after(own[(0, 0, 0)][0], *ready), "band", [(0, 1)])
        known[(0, 1, 1, 0)] = (first[None], 0)
    for c in range(chunks):
        keys = [(a, t) for t in range(parts) for a in range(group // 2)]
        wait = [first] if early and c == chunks - 1 else []
        there = {key: after(moved[(*key, c)], *ready, *wait) for key in keys}
        crossed[c] = send(jnp.stack([there[key][1] for key in keys]), 1, 0)
        for k, (a, t) in enumerate(keys):
            pieces[(2 * a, t, c)] = (there[(a, t)], 0)
            pieces[(2 * a + 1, t, c)] = (crossed[c], k)

    known |= {(r, t, 0, c): value for (r, t, c), value in pieces.items()}
    late = {}
    if early:
        came = [moved[(a, 1, chunks - 1)] for a in range(2)]
        chosen = [(r, c, *pieces[(r, 0, c)]) for r, c in ((0, chunks - 1), (1, 0))]
        sent = jnp.stack([value[index] for _, _, value, index in chosen])
        sent = lax.ppermute(after(sent, *came), "band", [(0, 1)])
        for k, (r, c, _, _) in enumerate(chosen):
            known[(r, 1, 1, c)] = (sent, k)
    packs = [
        (r, c)
        for c in range(chunks)
        for r in range(group)
        if parts > 2 or (r, 1, 1, c) not in known
    ]
    mine, other, buffer = gram(info, pieces, packs, bands, bands_all)
    mine = mine + send(other, 1, 0)
    mine = pairwise_sum(mine, "domain", slabs, 2, group)
    for key, value in own.items():
        if key[1] > 0:
            late[key] = send(after(value, mine), 2 * key[0], 0)
    if early:
        mine = after(mine, sent)
    mine = pairwise_sum(mine, "band", parts, 0, parts)

    def forward(buffer, t, packs):
        for s in range(1, parts):
            if t != s:
                sent = lax.ppermute(buffer, "band", [(q, q + s) for q in range(parts - s)])
                for k, (r, c) in enumerate(packs):
                    known[(r, s, (t - s) % parts, c)] = (sent, k)

    forward(after(buffer, mine), 0, packs)
    mine = pairwise_sum(mine, "domain", slabs, group, slabs)
    rotation = inverse_factor(info, mine, send(mine, 1, 0), planes * rows_y * rows_z * slabs)
    for t in range(1, parts):
        keys = [(a, c) for c in range(chunks) for a in range(group // 2)]
        far = send(jnp.stack([after(late[(a, t, c)], rotation)[1] for a, c in keys]), 1, 0)
        for k, (a, c) in enumerate(keys):
            known[(2 * a, 0, t, c)] = (late[(a, t, c)], 0)
            known[(2 * a + 1, 0, t, c)] = (far, k)
        if parts > 2:
            chosen = [known[(r, 0, t, c)] for r, c in packs]
            forward(jnp.stack([value[index] for value, index in chosen]), t, packs)
    out = None
    for only in range(parts) if parts == 2 and planes % 2 == 0 else [None]:
        chosen = {key: value for key, value in known.items() if only in (None, key[2])}
        out = rotate(info, rotation, chosen, bands, bands_all, planes, rows_y, only, out)
    return out


def solution(mesh):
    in_specs = (P("band", "domain", None, None), P("band", "domain"), P("domain", None, None))
    out_specs = P("band", "domain", None, None)
    return jax.shard_map(body, mesh=mesh, in_specs=in_specs, out_specs=out_specs, check_vma=False)
```

```python
import math

import jax
import jax.numpy as jnp
import numpy as np
from jax import lax
from jax.experimental import pallas as pl
from jax.experimental.pallas import tpu as pltpu
from jax.sharding import PartitionSpec as P

grid_step = 0.5
stencil_coef = (
    -5369.0 / 1800.0,
    12.0 / 7.0,
    -15.0 / 56.0,
    10.0 / 189.0,
    -1.0 / 112.0,
    2.0 / 1925.0,
    -1.0 / 16632.0,
)
lower_end = -4.0
cut_energy = 6.0
upper_end = 43.0
kinetic = -0.5 / (grid_step * grid_step)
coef_scale = 7.0
reach = 6
edge = 3 * reach
chunk = 16
deep = 16
F32, BF16 = jnp.float32, jnp.bfloat16


def filter_terms():
    width_e = (upper_end - cut_energy) / 2.0
    centre = (upper_end + cut_energy) / 2.0
    sigma_one = width_e / (lower_end - centre)
    gamma_term = 2.0 / sigma_one
    sigma_two = 1.0 / (gamma_term - sigma_one)
    sigma_three = 1.0 / (gamma_term - sigma_two)
    return (width_e, centre, sigma_one, sigma_two, sigma_three)


def stencil_line(count):
    line = np.zeros((count, count), np.float64)
    for offset in range(1, reach + 1):
        value = kinetic * stencil_coef[offset] * coef_scale
        line += value * (np.eye(count, k=offset) + np.eye(count, k=-offset))
    return line


def xy_matrix(rows_y):
    along_x = stencil_line(deep + 2 * reach)[:, reach : reach + deep]
    middle = np.eye(deep + 2 * reach, deep, k=-reach)
    full = np.kron(along_x, np.eye(rows_y)) + np.kron(middle, stencil_line(rows_y))
    return jnp.asarray(full, BF16)


def z_matrix(count_z):
    return jnp.asarray(np.kron(np.eye(2), stencil_line(count_z)), BF16)


def swap_matrix():
    full = np.zeros((256, 256), np.float32)
    for a in range(16):
        for b in range(16):
            full[a * 16 + b, b * 16 + a] = 1.0
    return jnp.asarray(full, BF16)


def params(mebibytes):
    return dict(
        compiler_params=pltpu.CompilerParams(
            vmem_limit_bytes=mebibytes * 2**20, dimension_semantics=("arbitrary",)
        ),
        cost_estimate=pl.CostEstimate(flops=1, bytes_accessed=1, transcendentals=0),
    )


def prepare(info, orbitals, scale, potential, part, group, with_potential):
    bands, planes, rows_y, rows_z = orbitals.shape
    own = bands // group
    at_once = 8
    steps = chunk // at_once
    total = chunk + (2 if with_potential else 0)

    def kernel(info_ref, *refs):
        sources, scales, potential_ref = refs[:group], refs[group : 2 * group], refs[2 * group]
        outs = refs[2 * group + 1 :]
        i = pl.program_id(0)
        for r in range(group):
            for b in range(at_once):
                value = sources[r][b].astype(F32) * scales[r][b][:, None, :]
                outs[r][i * at_once + b] = value.astype(BF16)

        if with_potential:

            @pl.when(i == 0)
            def _():
                high = potential_ref[...].astype(BF16)
                low = (potential_ref[...] - high.astype(F32)).astype(BF16)
                for r in range(group):
                    outs[r][chunk] = high
                    outs[r][chunk + 1] = low

    def first(r, i, info_ref):
        return ((info_ref[0] ^ r) * own + part * chunk) // at_once + i

    def source_spec(r):
        return pl.BlockSpec(
            (at_once, planes, rows_y, rows_z),
            lambda i, info_ref: (first(r, i, info_ref), 0, 0, 0),
        )

    def scale_spec(r):
        return pl.BlockSpec(
            (at_once, planes, rows_z), lambda i, info_ref: (first(r, i, info_ref), 0, 0)
        )

    shape = jax.ShapeDtypeStruct((total, planes, rows_y, rows_z), BF16)
    return pl.pallas_call(
        kernel,
        grid_spec=pltpu.PrefetchScalarGridSpec(
            num_scalar_prefetch=1,
            grid=(steps,),
            in_specs=[source_spec(r) for r in range(group)]
            + [scale_spec(r) for r in range(group)]
            + [pl.BlockSpec((planes, rows_y, rows_z), lambda i, info_ref: (0, 0, 0))],
            out_specs=[pl.BlockSpec(shape.shape, lambda i, info_ref: (0, 0, 0, 0))] * group,
        ),
        out_shape=[shape] * group,
        name="prepare",
        **params(14),
    )(info, *([orbitals] * group), *([scale] * group), potential)


def edges(info, pieces, cuts):
    group = len(pieces)
    total, planes, rows_y, rows_z = pieces[0].shape
    rest = edge - planes
    width = edge // cuts
    at_once = 6 if total % 6 == 0 else 4

    def kernel(info_ref, *refs):
        sources, outs = refs[:group], refs[group:]

        def put(targets, to, source, begin, count):
            while count:
                size = min(count, width - to % width)
                target = targets[to // width]
                target[:, to % width : to % width + size] = source[:, begin : begin + size]
                to, begin, count = to + size, begin + size, count - size

        for odd in range(2):
            up, down = (outs[k * cuts : (k + 1) * cuts] for k in (odd, 1 - odd))
            for r in range(group):
                slab = jnp.where(info_ref[5] == odd, info_ref[0] ^ r, -1)

                @pl.when(slab == group - 1)
                def _():
                    put(up, rest, sources[r], 0, planes)

                @pl.when(slab == group - 2)
                def _():
                    put(up, 0, sources[r], planes - rest, rest)

                @pl.when(slab == 0)
                def _():
                    put(down, 0, sources[r], 0, planes)

                @pl.when(slab == 1)
                def _():
                    put(down, planes, sources[r], 0, rest)

    def spec(count):
        return pl.BlockSpec((at_once, count, rows_y, rows_z), lambda i, info_ref: (i, 0, 0, 0))

    flat = pl.pallas_call(
        kernel,
        grid_spec=pltpu.PrefetchScalarGridSpec(
            num_scalar_prefetch=1,
            grid=(total // at_once,),
            in_specs=[spec(planes)] * group,
            out_specs=[spec(width)] * (2 * cuts),
        ),
        out_shape=[jax.ShapeDtypeStruct((total, width, rows_y, rows_z), BF16)] * (2 * cuts),
        name="edges",
        **params(8),
    )(info, *pieces)
    return flat[:cuts], flat[cuts:]


def chebyshev(info, sides, pieces, sides_pot, pieces_pot, parts):
    group = len(pieces)
    _, planes, rows_y, rows_z = pieces[0].shape
    slab = group * planes
    per_p, per_y, cuts_y = shares(planes, rows_y, parts)
    at_once = 2 if per_p % 2 == 0 else 1
    steps = chunk // 2
    count_out = group // 2 * parts
    flat_sides, flat_pot = ([value for side in both for value in side] for both in (sides, sides_pot))
    cuts, cuts_pot = len(sides[0]), len(sides_pot[0])
    width, width_pot = edge // cuts, edge // cuts_pot
    width_e, centre, sigma_one, sigma_two, sigma_three = filter_terms()
    diagonal = 3.0 * stencil_coef[0] * kinetic - centre
    xy, zz, swap = xy_matrix(rows_y), z_matrix(rows_z), swap_matrix()
    count_0, count_1, count_2 = slab + 6 * reach, slab + 4 * reach, slab + 2 * reach

    def kernel(info_ref, *refs):
        side_refs, refs = refs[: 2 * cuts], refs[2 * cuts :]
        side_pot_refs, refs = refs[: 2 * cuts_pot], refs[2 * cuts_pot :]
        piece_refs, pot_refs = refs[:group], refs[group : 2 * group]
        xy_ref, zz_ref, swap_ref = refs[2 * group : 3 + 2 * group]
        outs = refs[3 + 2 * group : 3 + 2 * group + count_out]
        field, first, second, energy, result = refs[3 + 2 * group + count_out :]
        i = pl.program_id(0)
        me = info_ref[0]
        at_left, at_right = info_ref[1] == 1, info_ref[2] == 1

        @pl.when(i == 0)
        def _():
            def store(start, source):
                total = source[0].astype(F32) + source[1].astype(F32)
                energy[pl.ds(start, source.shape[1])] = coef_scale * (total + diagonal)

            for side, base, low, high in (
                (side_pot_refs[cuts_pot:], -reach, 0, 2 * reach),
                (side_pot_refs[:cuts_pot], slab + 2 * reach, slab + 2 * reach, count_1),
            ):
                for k, ref in enumerate(side):
                    start = base + k * width_pot
                    begin, end = max(start, low), min(start + width_pot, high)
                    if begin < end:
                        store(begin, ref.at[:, begin - start : end - start])
            for r in range(group):
                store(2 * reach + planes * (me ^ r), pot_refs[r])

        for b in range(2):
            lanes = slice(b * rows_z, (b + 1) * rows_z)
            for k in range(2):
                start = (1 - (info_ref[5] ^ k)) * (edge + slab)
                for n in range(cuts):
                    where = pl.ds(start + n * width, width)
                    field[where, :, lanes] = side_refs[k * cuts + n][b]
            for r in range(group):
                field[pl.ds(edge + planes * (me ^ r), planes), :, lanes] = piece_refs[r][b]

        def flat(source, start, stop):
            return source[start:stop].reshape((stop - start) * rows_y, 2 * rows_z)

        def apply(source, count, energy_start):
            inner = count - 2 * reach
            along_z = jnp.dot(
                flat(source, reach, reach + inner), zz_ref[...], preferred_element_type=F32
            )
            carry = None
            for at in range(0, count, deep):
                size = min(deep, count - at)
                low, high = max(at - 2 * reach, 0), min(at + size, inner)
                skip = (low - at + 2 * reach) * rows_y
                share = xy_ref[skip : skip + (high - low) * rows_y, : size * rows_y]
                total = jnp.dot(share, flat(source, at, at + size), preferred_element_type=F32)
                if carry is not None:
                    begun = carry.shape[0]
                    sums = [total[:begun] + carry]
                    total = jnp.concatenate(sums + [total[begun:]][: total.shape[0] > begun], axis=0)
                done = high if at + size == count else at + deep - 2 * reach
                rows = (done - low) * rows_y
                carry = total[rows:] if done < high else None
                factor = energy[energy_start + low : energy_start + done]
                factor = factor.reshape(rows, rows_z)
                middle = flat(source, reach + low, reach + done).astype(F32)
                yield low, done, (
                    total[:rows]
                    + along_z[low * rows_y : done * rows_y]
                    + jnp.concatenate([factor, factor], axis=1) * middle
                )

        def block(value):
            return value.astype(BF16).reshape(-1, rows_y, 2 * rows_z)

        def previous(source, start, stop):
            return flat(source, start + 2 * reach, stop + 2 * reach).astype(F32)

        for low, high, value in apply(field, count_0, 0):
            first[low:high] = block(value * (sigma_one / width_e / coef_scale))

        @pl.when(at_left)
        def _():
            first[: 2 * reach] = jnp.zeros((2 * reach, rows_y, 2 * rows_z), BF16)

        @pl.when(at_right)
        def _():
            first[count_1 - 2 * reach :] = jnp.zeros((2 * reach, rows_y, 2 * rows_z), BF16)

        for low, high, value in apply(first, count_1, reach):
            value = value * (2.0 * sigma_two / width_e / coef_scale)
            value -= sigma_one * sigma_two * previous(field, low, high)
            second[low:high] = block(value)

        @pl.when(at_left)
        def _():
            second[:reach] = jnp.zeros((reach, rows_y, 2 * rows_z), BF16)

        @pl.when(at_right)
        def _():
            second[count_2 - reach :] = jnp.zeros((reach, rows_y, 2 * rows_z), BF16)

        for low, high, value in apply(second, count_2, 2 * reach):
            value = value * (2.0 * sigma_three / width_e / coef_scale)
            value -= sigma_two * sigma_three * previous(first, low, high)
            value = block(value)
            for b in range(2):
                part = value[:, :, b * rows_z : (b + 1) * rows_z]
                result[low:high, 2 * i + b] = part

        @pl.when(i == steps - 1)
        def _():
            for t in range(parts):
                part = lax.rem(info_ref[3] + t, parts)
                begin = lax.rem(part, cuts_y) * (per_y * chunk)
                begin = pl.multiple_of(begin, per_y * chunk)
                for r in range(group):
                    start = planes * (me ^ r) + part // cuts_y * per_p
                    for p in range(0, per_p, at_once):
                        pair = [
                            result[start + p + k].reshape(chunk * rows_y, rows_z)
                            for k in range(at_once)
                        ]
                        moved = jnp.dot(
                            swap_ref[pl.ds(begin, per_y * chunk), :],
                            jnp.concatenate(pair, axis=1),
                            preferred_element_type=F32,
                        ).astype(BF16)
                        for k in range(at_once):
                            value = moved[:, k * rows_z : (k + 1) * rows_z]
                            out = outs[r // 2 * parts + t]
                            out[r % 2, :, p + k] = value.reshape(per_y, chunk, rows_z)

    def block_spec(count, index):
        return pl.BlockSpec((2, count, rows_y, rows_z), index)

    def whole_spec(shape):
        return pl.BlockSpec(shape, lambda i, info_ref: (0,) * len(shape))

    moving = lambda i, info_ref: (i, 0, 0, 0)
    fixed = lambda i, info_ref: (steps, 0, 0, 0)
    shape = jax.ShapeDtypeStruct((2, per_y, per_p, chunk, rows_z), BF16)
    flat = pl.pallas_call(
        kernel,
        grid_spec=pltpu.PrefetchScalarGridSpec(
            num_scalar_prefetch=1,
            grid=(steps,),
            in_specs=[block_spec(width, moving)] * (2 * cuts)
            + [block_spec(width_pot, fixed)] * (2 * cuts_pot)
            + [block_spec(planes, moving)] * group
            + [block_spec(planes, fixed)] * group
            + [whole_spec(xy.shape), whole_spec(zz.shape), whole_spec(swap.shape)],
            out_specs=[whole_spec(shape.shape)] * count_out,
            scratch_shapes=[
                pltpu.VMEM((count_0, rows_y, 2 * rows_z), BF16),
                pltpu.VMEM((count_1, rows_y, 2 * rows_z), BF16),
                pltpu.VMEM((count_2, rows_y, 2 * rows_z), BF16),
                pltpu.VMEM((count_1, rows_y, rows_z), F32),
                pltpu.VMEM((slab, chunk, rows_y, rows_z), BF16),
            ],
        ),
        out_shape=[shape] * count_out,
        name="chebyshev",
        **params(24),
    )(info, *flat_sides, *flat_pot, *pieces, *pieces_pot, xy, zz, swap)
    return [flat[a * parts : (a + 1) * parts] for a in range(group // 2)]


def shares(planes, rows_y, parts):
    cuts_p = math.gcd(planes, parts)
    cuts_y = parts // cuts_p
    return planes // cuts_p, rows_y // cuts_y, cuts_y


def fill(info_ref, rows, piece, source, first_p, first_y, r, c, bands, group):
    own = bands // group
    start = source * bands + (info_ref[0] ^ r) * own + c * chunk
    where = pl.ds(pl.multiple_of(start, chunk), chunk)
    for p in range(piece.shape[1]):
        rows[first_p + p, pl.ds(first_y, piece.shape[0]), where, :] = piece[:, p]


def gram(info, pieces, packs, bands, bands_all):
    group = 1 + max(r for r, t, c in pieces)
    _, per_y, per_p, _, rows_z = next(iter(pieces.values()))[0].shape
    at_once = 2 if per_p % 2 == 0 else 1
    steps = per_p // at_once
    half = bands_all // 2
    direct = half == bands
    own = bands // group
    ordered = sorted(pieces, key=lambda key: (key[1], key[0], key[2]))

    def in_order(info_ref, value, by_rows):
        axis = 0 if by_rows else 1
        count = value.shape[axis]
        place = lax.broadcasted_iota(jnp.int32, value.shape, axis)
        bit = 1
        while bit < group:
            step = bit * own
            if by_rows:
                blocks = [value[k : k + step] for k in range(0, count, step)]
                blocks = [blocks[k ^ 1] for k in range(len(blocks))]
                moved = jnp.concatenate(blocks, axis=0)
            else:
                low = pltpu.roll(value, count - step, 1)
                high = pltpu.roll(value, step, 1)
                moved = jnp.where(place & step == 0, low, high)
            value = jnp.where((info_ref[0] & bit) != 0, moved, value)
            bit *= 2
        return value

    def direct_blocks(info_ref, out):
        for odd in range(2):

            @pl.when(info_ref[3] == odd)
            def _():
                below = out[half:, :half] if odd == 0 else out[:half, half:bands_all]
                blocks = [out[:half, :half], below, out[half:, half:bands_all]]
                for k, block in enumerate(blocks if odd == 0 else blocks[::-1]):
                    value = in_order(info_ref, in_order(info_ref, block, True), False)
                    out[:half, k * half : (k + 1) * half] = value

    def direct_kernel(info_ref, *refs):
        mine, other, packed, _, out = refs[len(pieces) :]
        by_key = dict(zip(pieces, refs))
        i = pl.program_id(0)
        for k, (r, c) in enumerate(packs):
            packed[k] = by_key[(r, 0, c)][0]
        block = jnp.concatenate(
            [
                jnp.concatenate([by_key[key][0, y, p] for key in ordered], axis=0)
                for p in range(at_once)
                for y in range(per_y)
            ],
            axis=1,
        )
        total = lax.dot_general(
            block, block, (((1,), (1,)), ((), ())), preferred_element_type=F32
        )

        @pl.when(i == 0)
        def _():
            out[:, :bands_all] = total

        @pl.when(i > 0)
        def _():
            out[:, :bands_all] += total

        @pl.when(i == steps - 1)
        def _():
            direct_blocks(info_ref, out)
            for ref, core in ((mine, info_ref[0] & 1), (other, 1 - (info_ref[0] & 1))):
                where = pl.ds(pl.multiple_of(core * (half // 2), half // 2), half // 2)
                ref[...] = out[where, : 3 * half]

    def kernel(info_ref, *refs):
        mine, other, packed, rows, out = refs[len(pieces) :]
        parts = info_ref[4]
        i = pl.program_id(0)
        for (r, t, c), piece in zip(pieces, refs):
            source = lax.rem(info_ref[3] + parts - t, parts)
            fill(info_ref, rows, piece.at[0], source, 0, 0, r, c, bands, group)
            if t == 0 and (r, c) in packs:
                packed[packs.index((r, c))] = piece[0]
        block = jnp.concatenate(
            [rows[p, y] for p in range(at_once) for y in range(per_y)], axis=1
        )
        total = lax.dot_general(
            block, block, (((1,), (1,)), ((), ())), preferred_element_type=F32
        )

        total = [total[:half, :half], total[half:, :half], total[half:, half:]]
        total = jnp.concatenate(total, axis=1)

        @pl.when(i == 0)
        def _():
            out[...] = total

        @pl.when(i > 0)
        def _():
            out[...] += total

        @pl.when(i == steps - 1)
        def _():
            for ref, core in ((mine, info_ref[0] & 1), (other, 1 - (info_ref[0] & 1))):
                ref[...] = out[pl.ds(pl.multiple_of(core * (half // 2), half // 2), half // 2)]

    def spec(index):
        return pl.BlockSpec(
            (1, per_y, at_once, chunk, rows_z), lambda i, info_ref: (index, 0, i, 0, 0)
        )

    return pl.pallas_call(
        direct_kernel if direct else kernel,
        grid_spec=pltpu.PrefetchScalarGridSpec(
            num_scalar_prefetch=1,
            grid=(steps,),
            in_specs=[spec(index) for _, index in pieces.values()],
            out_specs=[pl.BlockSpec((half // 2, 3 * half), lambda i, info_ref: (0, 0))] * 2
            + [
                pl.BlockSpec(
                    (len(packs), per_y, at_once, chunk, rows_z),
                    lambda i, info_ref: (0, 0, i, 0, 0),
                ),
            ],
            scratch_shapes=[
                pltpu.VMEM((1 if direct else at_once, per_y, bands_all, rows_z), BF16),
                pltpu.VMEM((bands_all if direct else half, 3 * half), F32),
            ],
        ),
        out_shape=[jax.ShapeDtypeStruct((half // 2, 3 * half), F32)] * 2
        + [jax.ShapeDtypeStruct((len(packs), per_y, per_p, chunk, rows_z), BF16)],
        name="gram",
        **params(16),
    )(info, *[value for value, _ in pieces.values()])


def inverse_factor(info, mine, other, cells):
    half = 2 * mine.shape[0]
    count = 2 * half

    def exact(a, b, transposed):
        dims = (((1,), (1 if transposed else 0,)), ((), ()))
        return lax.dot_general(
            a, b, dims, precision=lax.Precision.HIGHEST, preferred_element_type=F32
        )

    def eliminate(block):
        groups = half // 8
        row = lax.broadcasted_iota(jnp.int32, (8, half), 0)
        column = lax.broadcasted_iota(jnp.int32, (8, half), 1)
        left = [block[8 * g : 8 * g + 8] for g in range(groups)]
        right = [jnp.where(column == row + 8 * g, 1.0, 0.0).astype(F32) for g in range(groups)]
        for at in range(groups):
            later = range(at, groups)
            spread = [
                [
                    jnp.broadcast_to(left[g][:, 8 * at + k : 8 * at + k + 1], (8, half))
                    for g in later
                ]
                for k in range(8)
            ]
            factors, rows_left, rows_right = [], [], []
            for k in range(8):
                pivot = jnp.broadcast_to(spread[k][0][k : k + 1], (8, half))
                scale = lax.rsqrt(pivot)
                scale = scale * (1.5 - 0.5 * pivot * scale * scale)
                factor = [value * scale for value in spread[k]]
                for m in range(k + 1, 8):
                    other = jnp.broadcast_to(factor[0][m : m + 1], (8, half))
                    spread[m] = [value - f * other for value, f in zip(spread[m], factor)]
                row_left = jnp.broadcast_to(left[at][k : k + 1], (8, half)) * scale
                row_right = jnp.broadcast_to(right[at][k : k + 1], (8, half)) * scale
                inside = jnp.where(row > k, factor[0], 0.0)
                left[at] = jnp.where(row == k, row_left, left[at] - inside * row_left)
                right[at] = jnp.where(row == k, row_right, right[at] - inside * row_right)
                factors.append(factor)
                rows_left.append(row_left)
                rows_right.append(row_right)
            for g in range(at + 1, groups):
                for k in range(8):
                    left[g] = left[g] - factors[k][g - at] * rows_left[k]
                    right[g] = right[g] - factors[k][g - at] * rows_right[k]
        return jnp.concatenate(right, axis=0)

    def kernel(info_ref, mine_ref, other_ref, out, blocks):
        for ref, core in ((mine_ref, info_ref[0] & 1), (other_ref, 1 - (info_ref[0] & 1))):
            where = pl.ds(pl.multiple_of(core * (half // 2), half // 2), half // 2)
            blocks[where] = ref[...] * (1.0 / cells)
        top = eliminate(blocks[:, :half])
        below = exact(blocks[:, half:count], top, True)
        rest = blocks[:, count:] - exact(below, below, True)
        bottom = eliminate(rest)
        out[:half, :half] = top.astype(BF16)
        out[:half, half:] = jnp.zeros((half, half), BF16)
        out[half:, :half] = (-exact(bottom, exact(below, top, False), False)).astype(BF16)
        out[half:, half:] = bottom.astype(BF16)

    return pl.pallas_call(
        kernel,
        grid_spec=pltpu.PrefetchScalarGridSpec(
            num_scalar_prefetch=1,
            grid=(1,),
            in_specs=[pl.BlockSpec(mine.shape, lambda i, info_ref: (0, 0))] * 2,
            out_specs=pl.BlockSpec((count, count), lambda i, info_ref: (0, 0)),
            scratch_shapes=[pltpu.VMEM((half, 3 * half), F32)],
        ),
        out_shape=jax.ShapeDtypeStruct((count, count), BF16),
        name="inverse_factor",
        **params(8),
    )(info, mine, other)


def rotate(info, rotation, pieces, bands, bands_all, planes, rows_y, only, before):
    group = 1 + max(r for r, t, u, c in pieces)
    _, per_y, per_p, _, rows_z = next(iter(pieces.values()))[0].shape
    swap = swap_matrix()
    cuts_y = rows_y // per_y
    at_once = 2 if only is not None and per_p % 2 == 0 else 1 if only is not None else per_p
    steps = per_p // at_once
    span = at_once if only is not None else planes
    given = [] if before is None else [before]
    arrays = {id(value): value for value, _ in pieces.values()}
    slots = {key: k for k, key in enumerate(arrays)}

    def start_of(info_ref, r, t, c):
        source = lax.rem(info_ref[3] + info_ref[4] - t, info_ref[4])
        return source * bands + (info_ref[0] ^ r) * (bands // group) + c * chunk

    def kernel(info_ref, *refs):
        rotation_ref, swap_ref = refs[len(arrays) :][:2]
        out, rows, mixed, turned = refs[-4:]
        me, parts = info_ref[3], info_ref[4]
        if only is None:
            for (r, t, u, c), (value, index) in pieces.items():
                source = lax.rem(me + parts - t, parts)
                part = lax.rem(me + u, parts)
                first_p, first_y = part // cuts_y * per_p, lax.rem(part, cuts_y) * per_y
                piece = refs[slots[id(value)]].at[index]
                fill(info_ref, rows, piece, source, first_p, first_y, r, c, bands, group)
            turned[...] = rotation_ref[...]
        else:

            @pl.when(pl.program_id(0) == 0)
            def _():
                place = lax.broadcasted_iota(jnp.int32, (bands_all, bands_all), 1)
                wanted = lax.broadcasted_iota(jnp.int32, (bands_all, bands_all), 0)
                from_row = place & (chunk - 1)
                for k, (r, t, _, c) in enumerate(pieces):
                    start = jnp.where(place // chunk == k, start_of(info_ref, r, t, c), 0)
                    from_row = from_row + start
                order = jnp.where(wanted == from_row, 1.0, 0.0).astype(BF16)
                value = jnp.dot(rotation_ref[...], order, preferred_element_type=F32)
                turned[...] = value.astype(BF16)

        def row(p, y):
            if only is None:
                return rows[p, y]
            held = [refs[slots[id(value)]][index, y, p] for value, index in pieces.values()]
            return jnp.concatenate(held, axis=0)

        def plane(p):
            for y in range(0, rows_y, 2):
                pair = jnp.concatenate([row(p, y), row(p, y + 1)], axis=1)
                value = jnp.dot(turned[...], pair, preferred_element_type=F32)
                value = value.astype(BF16)
                for k in range(bands // 16):
                    for b in range(2):
                        mixed[k, y + b] = value[
                            16 * k : 16 * k + 16, b * rows_z : (b + 1) * rows_z
                        ]
            for k in range(0, bands // 16, 2):
                pair = [mixed[k + b].reshape(16 * rows_y, rows_z) for b in range(2)]
                moved = jnp.dot(
                    swap_ref[...], jnp.concatenate(pair, axis=1), preferred_element_type=F32
                ).astype(BF16)
                for b in range(2):
                    part = moved[:, b * rows_z : (b + 1) * rows_z].reshape(16, rows_y, rows_z)
                    out[16 * (k + b) : 16 * (k + b) + 16, p] = part

        if only is not None:
            for p in range(span):
                plane(p)
        else:
            pl.loop(0, span)(plane)

    def spec(value):
        return pl.BlockSpec(
            (value.shape[0], per_y, at_once, chunk, rows_z), lambda i, info_ref: (0, 0, i, 0, 0)
        )

    def out_index(i, info_ref):
        if only is None:
            return (0, 0, 0, 0)
        return (0, lax.rem(info_ref[3] + only, info_ref[4]) * steps + i, 0, 0)

    return pl.pallas_call(
        kernel,
        grid_spec=pltpu.PrefetchScalarGridSpec(
            num_scalar_prefetch=1,
            grid=(steps,),
            in_specs=[spec(value) for value in arrays.values()]
            + [
                pl.BlockSpec((bands, bands_all), lambda i, info_ref: (info_ref[3], 0)),
                pl.BlockSpec(swap.shape, lambda i, info_ref: (0, 0)),
            ]
            + [pl.BlockSpec(memory_space=pl.ANY)] * len(given),
            out_specs=pl.BlockSpec((bands, span, rows_y, rows_z), out_index),
            scratch_shapes=[
                pltpu.VMEM((span if only is None else 1, rows_y, bands_all, rows_z), BF16),
                pltpu.VMEM((bands // 16, rows_y, 16, rows_z), BF16),
                pltpu.VMEM((bands, bands_all), BF16),
            ],
        ),
        out_shape=jax.ShapeDtypeStruct((bands, planes, rows_y, rows_z), BF16),
        input_output_aliases={3 + len(arrays): 0} if given else {},
        name="rotate",
        **params(60 if only is None else 14),
    )(info, *arrays.values(), rotation, swap, *given)


def pairwise_sum(value, axis, count, low, high):
    bit = max(low, 1)
    while bit < high:
        value = value + lax.ppermute(value, axis, [(i, i ^ bit) for i in range(count)])
        bit *= 2
    return value


def body(orbital_block, block_scale, potential):
    bands, planes, rows_y, rows_z = orbital_block.shape
    parts, slabs = lax.axis_size("band"), lax.axis_size("domain")
    bands_all = bands * parts
    group = 4 if bands // 4 >= chunk else 2
    chunks = bands // group // chunk
    where, band = lax.axis_index("domain"), lax.axis_index("band")
    info = jnp.stack(
        [
            lax.rem(where, group),
            (where < group).astype(jnp.int32),
            (where >= slabs - group).astype(jnp.int32),
            band,
            jnp.int32(parts),
            jnp.int32(0),
        ]
    ).astype(jnp.int32)
    paired = info.at[5].set(lax.rem(where // group, 2))

    def send(value, r, t):
        if r == 0 and t == 0:
            return value
        pairs = [
            (q * slabs + i, (q + t) % parts * slabs + (i ^ r))
            for q in range(parts)
            for i in range(slabs)
        ]
        return lax.ppermute(value, ("band", "domain"), pairs)

    scale = jnp.broadcast_to(block_scale[:, :, None], (bands, planes, rows_z))
    far_first = sorted(range(group), reverse=True)
    arrived = []
    for c in range(chunks):
        pieces = prepare(info, orbital_block, scale, potential, c, group, c == 0)
        sent = {r: send(pieces[r], r, 0) for r in far_first}
        arrived.append([sent[r] for r in range(group)])
    def after(value, *others):
        return lax.optimization_barrier((value, *others))[0] if others else value

    def swapped(value, odd):
        lower = [i for i in range(slabs - group) if i // group % 2 == odd]
        pairs = [(i, i + group) for i in lower] + [(i + group, i) for i in lower]
        return lax.ppermute(value, "domain", pairs)

    def shifted(value, by):
        pairs = [(i, i + by) for i in range(slabs) if 0 <= i + by < slabs]
        return lax.ppermute(value, "domain", pairs)

    sides = []
    for c in range(chunks):
        first, second = edges(paired if c else info, arrived[c], 1 if c else 2)
        if c == 0:
            sides.append(
                [[shifted(end, -group) for end in second], [shifted(end, group) for end in first]]
            )
        else:
            sides.append([[swapped(end, 0) for end in first], [swapped(end, 1) for end in second]])
        last_end = first[0]
    pieces, own, moved, crossed = {}, {}, {}, {}
    ready = [last_end]
    for c in range(chunks):
        order = after(paired if c else info, *ready)
        filtered = chebyshev(order, sides[c], arrived[c], sides[0], arrived[0], parts)
        ready = [filtered[0][0]]
        for a in reversed(range(group // 2)):
            for t in reversed(range(parts)):
                value = filtered[a][t]
                own[(a, t, c)] = value
                moved[(a, t, c)] = send(value, 2 * a, t)
    known = {}
    early = parts == 2 and chunks > 1 and group == 4
    if early:
        first = lax.ppermute(after(own[(0, 0, 0)][0], *ready), "band", [(0, 1)])
        known[(0, 1, 1, 0)] = (first[None], 0)
    for c in range(chunks):
        keys = [(a, t) for t in range(parts) for a in range(group // 2)]
        wait = [first] if early and c == chunks - 1 else []
        there = {key: after(moved[(*key, c)], *ready, *wait) for key in keys}
        crossed[c] = send(jnp.stack([there[key][1] for key in keys]), 1, 0)
        for k, (a, t) in enumerate(keys):
            pieces[(2 * a, t, c)] = (there[(a, t)], 0)
            pieces[(2 * a + 1, t, c)] = (crossed[c], k)

    known |= {(r, t, 0, c): value for (r, t, c), value in pieces.items()}
    late = {}
    if early:
        came = [moved[(a, 1, chunks - 1)] for a in range(2)]
        chosen = [(r, c, *pieces[(r, 0, c)]) for r, c in ((0, chunks - 1), (1, 0))]
        sent = jnp.stack([value[index] for _, _, value, index in chosen])
        sent = lax.ppermute(after(sent, *came), "band", [(0, 1)])
        for k, (r, c, _, _) in enumerate(chosen):
            known[(r, 1, 1, c)] = (sent, k)
    packs = [
        (r, c)
        for c in range(chunks)
        for r in range(group)
        if parts > 2 or (r, 1, 1, c) not in known
    ]
    mine, other, buffer = gram(info, pieces, packs, bands, bands_all)
    mine = mine + send(other, 1, 0)
    mine = pairwise_sum(mine, "domain", slabs, 2, group)
    for key, value in own.items():
        if key[1] > 0:
            late[key] = send(after(value, mine), 2 * key[0], 0)
    if early:
        mine = after(mine, sent)
    mine = pairwise_sum(mine, "band", parts, 0, parts)

    def forward(buffer, t, packs):
        for s in range(1, parts):
            if t != s:
                sent = lax.ppermute(buffer, "band", [(q, q + s) for q in range(parts - s)])
                for k, (r, c) in enumerate(packs):
                    known[(r, s, (t - s) % parts, c)] = (sent, k)

    forward(after(buffer, mine), 0, packs)
    mine = pairwise_sum(mine, "domain", slabs, group, slabs)
    rotation = inverse_factor(info, mine, send(mine, 1, 0), planes * rows_y * rows_z * slabs)
    for t in range(1, parts):
        keys = [(a, c) for c in range(chunks) for a in range(group // 2)]
        far = send(jnp.stack([after(late[(a, t, c)], rotation)[1] for a, c in keys]), 1, 0)
        for k, (a, c) in enumerate(keys):
            known[(2 * a, 0, t, c)] = (late[(a, t, c)], 0)
            known[(2 * a + 1, 0, t, c)] = (far, k)
        if parts > 2:
            chosen = [known[(r, 0, t, c)] for r, c in packs]
            forward(jnp.stack([value[index] for value, index in chosen]), t, packs)
    out = None
    for only in range(parts) if parts == 2 and planes % 2 == 0 else [None]:
        chosen = {key: value for key, value in known.items() if only in (None, key[2])}
        out = rotate(info, rotation, chosen, bands, bands_all, planes, rows_y, only, out)
    return out


def solution(mesh):
    in_specs = (P("band", "domain", None, None), P("band", "domain"), P("domain", None, None))
    out_specs = P("band", "domain", None, None)
    return jax.shard_map(body, mesh=mesh, in_specs=in_specs, out_specs=out_specs, check_vma=False)
```

```python
import math

import jax
import jax.numpy as jnp
import numpy as np
from jax import lax
from jax.experimental import pallas as pl
from jax.experimental.pallas import tpu as pltpu
from jax.sharding import PartitionSpec as P

grid_step = 0.5
stencil_coef = (
    -5369.0 / 1800.0,
    12.0 / 7.0,
    -15.0 / 56.0,
    10.0 / 189.0,
    -1.0 / 112.0,
    2.0 / 1925.0,
    -1.0 / 16632.0,
)
lower_end = -4.0
cut_energy = 6.0
upper_end = 43.0
kinetic = -0.5 / (grid_step * grid_step)
coef_scale = 7.0
reach = 6
edge = 3 * reach
chunk = 16
F32, BF16 = jnp.float32, jnp.bfloat16


def filter_terms():
    width_e = (upper_end - cut_energy) / 2.0
    centre = (upper_end + cut_energy) / 2.0
    sigma_one = width_e / (lower_end - centre)
    gamma_term = 2.0 / sigma_one
    sigma_two = 1.0 / (gamma_term - sigma_one)
    sigma_three = 1.0 / (gamma_term - sigma_two)
    return (width_e, centre, sigma_one, sigma_two, sigma_three)


def stencil_line(count):
    line = np.zeros((count, count), np.float64)
    for offset in range(1, reach + 1):
        value = kinetic * stencil_coef[offset] * coef_scale
        line += value * (np.eye(count, k=offset) + np.eye(count, k=-offset))
    return line


def xy_matrix(planes, rows_y):
    along_x = np.zeros((planes, planes + 2 * reach), np.float64)
    along_x[:, :] = stencil_line(planes + 2 * reach)[reach : reach + planes]
    middle = np.eye(planes, planes + 2 * reach, k=reach)
    full = np.kron(along_x, np.eye(rows_y)) + np.kron(middle, stencil_line(rows_y))
    return jnp.asarray(full, BF16)


def z_matrix(count_z):
    return jnp.asarray(np.kron(np.eye(2), stencil_line(count_z)), BF16)


def swap_matrix():
    full = np.zeros((256, 256), np.float32)
    for a in range(16):
        for b in range(16):
            full[a * 16 + b, b * 16 + a] = 1.0
    return jnp.asarray(full, BF16)


def params(mebibytes):
    return dict(
        compiler_params=pltpu.CompilerParams(
            vmem_limit_bytes=mebibytes * 2**20, dimension_semantics=("arbitrary",)
        ),
        cost_estimate=pl.CostEstimate(flops=1, bytes_accessed=1, transcendentals=0),
    )


def prepare(info, orbitals, scale, potential, part, group, with_potential):
    bands, planes, rows_y, rows_z = orbitals.shape
    own = bands // group
    at_once = 8
    steps = chunk // at_once
    total = chunk + (2 if with_potential else 0)

    def kernel(info_ref, *refs):
        sources, scales, potential_ref = refs[:group], refs[group : 2 * group], refs[2 * group]
        outs = refs[2 * group + 1 :]
        i = pl.program_id(0)
        for r in range(group):
            for b in range(at_once):
                value = sources[r][b].astype(F32) * scales[r][b][:, None, :]
                outs[r][i * at_once + b] = value.astype(BF16)

        if with_potential:

            @pl.when(i == 0)
            def _():
                high = potential_ref[...].astype(BF16)
                low = (potential_ref[...] - high.astype(F32)).astype(BF16)
                for r in range(group):
                    outs[r][chunk] = high
                    outs[r][chunk + 1] = low

    def first(r, i, info_ref):
        return ((info_ref[0] ^ r) * own + part * chunk) // at_once + i

    def source_spec(r):
        return pl.BlockSpec(
            (at_once, planes, rows_y, rows_z),
            lambda i, info_ref: (first(r, i, info_ref), 0, 0, 0),
        )

    def scale_spec(r):
        return pl.BlockSpec(
            (at_once, planes, rows_z), lambda i, info_ref: (first(r, i, info_ref), 0, 0)
        )

    shape = jax.ShapeDtypeStruct((total, planes, rows_y, rows_z), BF16)
    return pl.pallas_call(
        kernel,
        grid_spec=pltpu.PrefetchScalarGridSpec(
            num_scalar_prefetch=1,
            grid=(steps,),
            in_specs=[source_spec(r) for r in range(group)]
            + [scale_spec(r) for r in range(group)]
            + [pl.BlockSpec((planes, rows_y, rows_z), lambda i, info_ref: (0, 0, 0))],
            out_specs=[pl.BlockSpec(shape.shape, lambda i, info_ref: (0, 0, 0, 0))] * group,
        ),
        out_shape=[shape] * group,
        name="prepare",
        **params(14),
    )(info, *([orbitals] * group), *([scale] * group), potential)


def edges(info, pieces, cuts):
    group = len(pieces)
    total, planes, rows_y, rows_z = pieces[0].shape
    rest = edge - planes
    width = edge // cuts
    at_once = 6 if total % 6 == 0 else 4

    def kernel(info_ref, *refs):
        sources, outs = refs[:group], refs[group:]

        def put(targets, to, source, begin, count):
            while count:
                size = min(count, width - to % width)
                target = targets[to // width]
                target[:, to % width : to % width + size] = source[:, begin : begin + size]
                to, begin, count = to + size, begin + size, count - size

        for odd in range(2):
            up, down = (outs[k * cuts : (k + 1) * cuts] for k in (odd, 1 - odd))
            for r in range(group):
                slab = jnp.where(info_ref[5] == odd, info_ref[0] ^ r, -1)

                @pl.when(slab == group - 1)
                def _():
                    put(up, rest, sources[r], 0, planes)

                @pl.when(slab == group - 2)
                def _():
                    put(up, 0, sources[r], planes - rest, rest)

                @pl.when(slab == 0)
                def _():
                    put(down, 0, sources[r], 0, planes)

                @pl.when(slab == 1)
                def _():
                    put(down, planes, sources[r], 0, rest)

    def spec(count):
        return pl.BlockSpec((at_once, count, rows_y, rows_z), lambda i, info_ref: (i, 0, 0, 0))

    flat = pl.pallas_call(
        kernel,
        grid_spec=pltpu.PrefetchScalarGridSpec(
            num_scalar_prefetch=1,
            grid=(total // at_once,),
            in_specs=[spec(planes)] * group,
            out_specs=[spec(width)] * (2 * cuts),
        ),
        out_shape=[jax.ShapeDtypeStruct((total, width, rows_y, rows_z), BF16)] * (2 * cuts),
        name="edges",
        **params(8),
    )(info, *pieces)
    return flat[:cuts], flat[cuts:]


def chebyshev(info, sides, pieces, sides_pot, pieces_pot, parts):
    group = len(pieces)
    _, planes, rows_y, rows_z = pieces[0].shape
    slab = group * planes
    per_p, per_y, cuts_y = shares(planes, rows_y, parts)
    at_once = 2 if per_p % 2 == 0 else 1
    steps = chunk // 2
    count_out = group // 2 * parts
    flat_sides, flat_pot = ([value for side in both for value in side] for both in (sides, sides_pot))
    cuts, cuts_pot = len(sides[0]), len(sides_pot[0])
    width, width_pot = edge // cuts, edge // cuts_pot
    width_e, centre, sigma_one, sigma_two, sigma_three = filter_terms()
    diagonal = 3.0 * stencil_coef[0] * kinetic - centre
    tile_rows = planes * rows_y
    xy, zz, swap = xy_matrix(planes, rows_y), z_matrix(rows_z), swap_matrix()
    count_0, count_1, count_2 = slab + 6 * reach, slab + 4 * reach, slab + 2 * reach

    def kernel(info_ref, *refs):
        side_refs, refs = refs[: 2 * cuts], refs[2 * cuts :]
        side_pot_refs, refs = refs[: 2 * cuts_pot], refs[2 * cuts_pot :]
        piece_refs, pot_refs = refs[:group], refs[group : 2 * group]
        xy_ref, zz_ref, swap_ref = refs[2 * group : 3 + 2 * group]
        outs = refs[3 + 2 * group : 3 + 2 * group + count_out]
        field, first, second, energy, result = refs[3 + 2 * group + count_out :]
        i = pl.program_id(0)
        me = info_ref[0]
        at_left, at_right = info_ref[1] == 1, info_ref[2] == 1

        @pl.when(i == 0)
        def _():
            def store(start, source):
                total = source[0].astype(F32) + source[1].astype(F32)
                energy[pl.ds(start, source.shape[1])] = coef_scale * (total + diagonal)

            for odd in range(2):

                @pl.when(info_ref[5] == odd)
                def _():
                    halves = side_pot_refs[:cuts_pot], side_pot_refs[cuts_pot:]
                    for side, base, low, high in (
                        (halves[1 - odd], -reach, 0, 2 * reach),
                        (halves[odd], slab + 2 * reach, slab + 2 * reach, count_1),
                    ):
                        for k, ref in enumerate(side):
                            start = base + k * width_pot
                            begin, end = max(start, low), min(start + width_pot, high)
                            if begin < end:
                                store(begin, ref.at[:, begin - start : end - start])

            for r in range(group):
                store(2 * reach + planes * (me ^ r), pot_refs[r])

        for b in range(2):
            lanes = slice(b * rows_z, (b + 1) * rows_z)
            for k in range(2):
                start = (1 - (info_ref[5] ^ k)) * (edge + slab)
                for n in range(cuts):
                    where = pl.ds(start + n * width, width)
                    field[where, :, lanes] = side_refs[k * cuts + n][b]
            for r in range(group):
                field[pl.ds(edge + planes * (me ^ r), planes), :, lanes] = piece_refs[r][b]

        def apply(source, start, energy_start):
            rows = source[pl.ds(start, planes + 2 * reach)].reshape(-1, 2 * rows_z)
            middle = source[pl.ds(start + reach, planes)].reshape(tile_rows, 2 * rows_z)
            total = jnp.dot(xy_ref[...], rows, preferred_element_type=F32)
            total += jnp.dot(middle, zz_ref[...], preferred_element_type=F32)
            factor = energy[pl.ds(energy_start, planes)].reshape(tile_rows, rows_z)
            factor = jnp.concatenate([factor, factor], axis=1)
            return total + factor * middle.astype(F32)

        def block(value):
            return value.astype(BF16).reshape(planes, rows_y, 2 * rows_z)

        def previous(source, start):
            return source[pl.ds(start, planes)].reshape(tile_rows, 2 * rows_z).astype(F32)

        for t in range(count_1 // planes):
            at = t * planes
            value = apply(field, at, at) * (sigma_one / width_e / coef_scale)
            first[at : at + planes] = block(value)

        @pl.when(at_left)
        def _():
            first[: 2 * reach] = jnp.zeros((2 * reach, rows_y, 2 * rows_z), BF16)

        @pl.when(at_right)
        def _():
            first[count_1 - 2 * reach :] = jnp.zeros((2 * reach, rows_y, 2 * rows_z), BF16)

        for t in range(count_2 // planes):
            at = t * planes
            value = apply(first, at, at + reach) * (2.0 * sigma_two / width_e / coef_scale)
            value -= sigma_one * sigma_two * previous(field, at + 2 * reach)
            second[at : at + planes] = block(value)

        @pl.when(at_left)
        def _():
            second[:reach] = jnp.zeros((reach, rows_y, 2 * rows_z), BF16)

        @pl.when(at_right)
        def _():
            second[count_2 - reach :] = jnp.zeros((reach, rows_y, 2 * rows_z), BF16)

        for t in range(group):
            at = t * planes
            value = apply(second, at, at + 2 * reach) * (2.0 * sigma_three / width_e / coef_scale)
            value -= sigma_two * sigma_three * previous(first, at + 2 * reach)
            value = block(value)
            for b in range(2):
                part = value[:, :, b * rows_z : (b + 1) * rows_z]
                result[at : at + planes, 2 * i + b] = part

        @pl.when(i == steps - 1)
        def _():
            for t in range(parts):
                part = lax.rem(info_ref[3] + t, parts)
                begin = lax.rem(part, cuts_y) * (per_y * chunk)
                begin = pl.multiple_of(begin, per_y * chunk)
                for r in range(group):
                    start = planes * (me ^ r) + part // cuts_y * per_p
                    for p in range(0, per_p, at_once):
                        pair = [
                            result[start + p + k].reshape(chunk * rows_y, rows_z)
                            for k in range(at_once)
                        ]
                        moved = jnp.dot(
                            swap_ref[pl.ds(begin, per_y * chunk), :],
                            jnp.concatenate(pair, axis=1),
                            preferred_element_type=F32,
                        ).astype(BF16)
                        for k in range(at_once):
                            value = moved[:, k * rows_z : (k + 1) * rows_z]
                            out = outs[r // 2 * parts + t]
                            out[r % 2, :, p + k] = value.reshape(per_y, chunk, rows_z)

    def block_spec(count, index):
        return pl.BlockSpec((2, count, rows_y, rows_z), index)

    def whole_spec(shape):
        return pl.BlockSpec(shape, lambda i, info_ref: (0,) * len(shape))

    moving = lambda i, info_ref: (i, 0, 0, 0)
    fixed = lambda i, info_ref: (steps, 0, 0, 0)
    shape = jax.ShapeDtypeStruct((2, per_y, per_p, chunk, rows_z), BF16)
    flat = pl.pallas_call(
        kernel,
        grid_spec=pltpu.PrefetchScalarGridSpec(
            num_scalar_prefetch=1,
            grid=(steps,),
            in_specs=[block_spec(width, moving)] * (2 * cuts)
            + [block_spec(width_pot, fixed)] * (2 * cuts_pot)
            + [block_spec(planes, moving)] * group
            + [block_spec(planes, fixed)] * group
            + [whole_spec(xy.shape), whole_spec(zz.shape), whole_spec(swap.shape)],
            out_specs=[whole_spec(shape.shape)] * count_out,
            scratch_shapes=[
                pltpu.VMEM((count_0, rows_y, 2 * rows_z), BF16),
                pltpu.VMEM((count_1, rows_y, 2 * rows_z), BF16),
                pltpu.VMEM((count_2, rows_y, 2 * rows_z), BF16),
                pltpu.VMEM((count_1, rows_y, rows_z), F32),
                pltpu.VMEM((slab, chunk, rows_y, rows_z), BF16),
            ],
        ),
        out_shape=[shape] * count_out,
        name="chebyshev",
        **params(18),
    )(info, *flat_sides, *flat_pot, *pieces, *pieces_pot, xy, zz, swap)
    return [flat[a * parts : (a + 1) * parts] for a in range(group // 2)]


def shares(planes, rows_y, parts):
    cuts_p = math.gcd(planes, parts)
    cuts_y = parts // cuts_p
    return planes // cuts_p, rows_y // cuts_y, cuts_y


def fill(info_ref, rows, piece, source, first_p, first_y, r, c, bands, group):
    own = bands // group
    start = source * bands + (info_ref[0] ^ r) * own + c * chunk
    where = pl.ds(pl.multiple_of(start, chunk), chunk)
    for p in range(piece.shape[1]):
        rows[first_p + p, pl.ds(first_y, piece.shape[0]), where, :] = piece[:, p]


def gram(info, pieces, packs, bands, bands_all):
    group = 1 + max(r for r, t, c in pieces)
    _, per_y, per_p, _, rows_z = next(iter(pieces.values()))[0].shape
    at_once = 2 if per_p % 2 == 0 else 1
    steps = per_p // at_once
    half = bands_all // 2
    direct = half == bands
    own = bands // group
    ordered = sorted(pieces, key=lambda key: (key[1], key[0], key[2]))

    def in_order(info_ref, value, by_rows):
        axis = 0 if by_rows else 1
        count = value.shape[axis]
        place = lax.broadcasted_iota(jnp.int32, value.shape, axis)
        bit = 1
        while bit < group:
            step = bit * own
            if by_rows:
                blocks = [value[k : k + step] for k in range(0, count, step)]
                blocks = [blocks[k ^ 1] for k in range(len(blocks))]
                moved = jnp.concatenate(blocks, axis=0)
            else:
                low = pltpu.roll(value, count - step, 1)
                high = pltpu.roll(value, step, 1)
                moved = jnp.where(place & step == 0, low, high)
            value = jnp.where((info_ref[0] & bit) != 0, moved, value)
            bit *= 2
        return value

    def direct_blocks(info_ref, out):
        for odd in range(2):

            @pl.when(info_ref[3] == odd)
            def _():
                below = out[half:, :half] if odd == 0 else out[:half, half:bands_all]
                blocks = [out[:half, :half], below, out[half:, half:bands_all]]
                for k, block in enumerate(blocks if odd == 0 else blocks[::-1]):
                    value = in_order(info_ref, in_order(info_ref, block, True), False)
                    out[:half, k * half : (k + 1) * half] = value

    def direct_kernel(info_ref, *refs):
        mine, other, packed, _, out = refs[len(pieces) :]
        by_key = dict(zip(pieces, refs))
        i = pl.program_id(0)
        for k, (r, c) in enumerate(packs):
            packed[k] = by_key[(r, 0, c)][0]
        block = jnp.concatenate(
            [
                jnp.concatenate([by_key[key][0, y, p] for key in ordered], axis=0)
                for p in range(at_once)
                for y in range(per_y)
            ],
            axis=1,
        )
        total = lax.dot_general(
            block, block, (((1,), (1,)), ((), ())), preferred_element_type=F32
        )

        @pl.when(i == 0)
        def _():
            out[:, :bands_all] = total

        @pl.when(i > 0)
        def _():
            out[:, :bands_all] += total

        @pl.when(i == steps - 1)
        def _():
            direct_blocks(info_ref, out)
            for ref, core in ((mine, info_ref[0] & 1), (other, 1 - (info_ref[0] & 1))):
                where = pl.ds(pl.multiple_of(core * (half // 2), half // 2), half // 2)
                ref[...] = out[where, : 3 * half]

    def kernel(info_ref, *refs):
        mine, other, packed, rows, out = refs[len(pieces) :]
        parts = info_ref[4]
        i = pl.program_id(0)
        for (r, t, c), piece in zip(pieces, refs):
            source = lax.rem(info_ref[3] + parts - t, parts)
            fill(info_ref, rows, piece.at[0], source, 0, 0, r, c, bands, group)
            if t == 0 and (r, c) in packs:
                packed[packs.index((r, c))] = piece[0]
        block = jnp.concatenate(
            [rows[p, y] for p in range(at_once) for y in range(per_y)], axis=1
        )
        total = lax.dot_general(
            block, block, (((1,), (1,)), ((), ())), preferred_element_type=F32
        )

        total = [total[:half, :half], total[half:, :half], total[half:, half:]]
        total = jnp.concatenate(total, axis=1)

        @pl.when(i == 0)
        def _():
            out[...] = total

        @pl.when(i > 0)
        def _():
            out[...] += total

        @pl.when(i == steps - 1)
        def _():
            for ref, core in ((mine, info_ref[0] & 1), (other, 1 - (info_ref[0] & 1))):
                ref[...] = out[pl.ds(pl.multiple_of(core * (half // 2), half // 2), half // 2)]

    def spec(index):
        return pl.BlockSpec(
            (1, per_y, at_once, chunk, rows_z), lambda i, info_ref: (index, 0, i, 0, 0)
        )

    return pl.pallas_call(
        direct_kernel if direct else kernel,
        grid_spec=pltpu.PrefetchScalarGridSpec(
            num_scalar_prefetch=1,
            grid=(steps,),
            in_specs=[spec(index) for _, index in pieces.values()],
            out_specs=[pl.BlockSpec((half // 2, 3 * half), lambda i, info_ref: (0, 0))] * 2
            + [
                pl.BlockSpec(
                    (len(packs), per_y, at_once, chunk, rows_z),
                    lambda i, info_ref: (0, 0, i, 0, 0),
                ),
            ],
            scratch_shapes=[
                pltpu.VMEM((1 if direct else at_once, per_y, bands_all, rows_z), BF16),
                pltpu.VMEM((bands_all if direct else half, 3 * half), F32),
            ],
        ),
        out_shape=[jax.ShapeDtypeStruct((half // 2, 3 * half), F32)] * 2
        + [jax.ShapeDtypeStruct((len(packs), per_y, per_p, chunk, rows_z), BF16)],
        name="gram",
        **params(16),
    )(info, *[value for value, _ in pieces.values()])


def inverse_factor(info, mine, other, cells):
    half = 2 * mine.shape[0]
    count = 2 * half

    def exact(a, b, transposed):
        dims = (((1,), (1 if transposed else 0,)), ((), ()))
        return lax.dot_general(
            a, b, dims, precision=lax.Precision.HIGHEST, preferred_element_type=F32
        )

    def eliminate(block):
        groups = half // 8
        row = lax.broadcasted_iota(jnp.int32, (8, half), 0)
        column = lax.broadcasted_iota(jnp.int32, (8, half), 1)
        left = [block[8 * g : 8 * g + 8] for g in range(groups)]
        right = [jnp.where(column == row + 8 * g, 1.0, 0.0).astype(F32) for g in range(groups)]
        for at in range(groups):
            later = range(at, groups)
            spread = [
                [
                    jnp.broadcast_to(left[g][:, 8 * at + k : 8 * at + k + 1], (8, half))
                    for g in later
                ]
                for k in range(8)
            ]
            factors, rows_left, rows_right = [], [], []
            for k in range(8):
                pivot = jnp.broadcast_to(spread[k][0][k : k + 1], (8, half))
                scale = lax.rsqrt(pivot)
                scale = scale * (1.5 - 0.5 * pivot * scale * scale)
                factor = [value * scale for value in spread[k]]
                for m in range(k + 1, 8):
                    other = jnp.broadcast_to(factor[0][m : m + 1], (8, half))
                    spread[m] = [value - f * other for value, f in zip(spread[m], factor)]
                row_left = jnp.broadcast_to(left[at][k : k + 1], (8, half)) * scale
                row_right = jnp.broadcast_to(right[at][k : k + 1], (8, half)) * scale
                inside = jnp.where(row > k, factor[0], 0.0)
                left[at] = jnp.where(row == k, row_left, left[at] - inside * row_left)
                right[at] = jnp.where(row == k, row_right, right[at] - inside * row_right)
                factors.append(factor)
                rows_left.append(row_left)
                rows_right.append(row_right)
            for g in range(at + 1, groups):
                for k in range(8):
                    left[g] = left[g] - factors[k][g - at] * rows_left[k]
                    right[g] = right[g] - factors[k][g - at] * rows_right[k]
        return jnp.concatenate(right, axis=0)

    def kernel(info_ref, mine_ref, other_ref, out, blocks):
        for ref, core in ((mine_ref, info_ref[0] & 1), (other_ref, 1 - (info_ref[0] & 1))):
            where = pl.ds(pl.multiple_of(core * (half // 2), half // 2), half // 2)
            blocks[where] = ref[...] * (1.0 / cells)
        top = eliminate(blocks[:, :half])
        below = exact(blocks[:, half:count], top, True)
        rest = blocks[:, count:] - exact(below, below, True)
        bottom = eliminate(rest)
        out[:half, :half] = top.astype(BF16)
        out[:half, half:] = jnp.zeros((half, half), BF16)
        out[half:, :half] = (-exact(bottom, exact(below, top, False), False)).astype(BF16)
        out[half:, half:] = bottom.astype(BF16)

    return pl.pallas_call(
        kernel,
        grid_spec=pltpu.PrefetchScalarGridSpec(
            num_scalar_prefetch=1,
            grid=(1,),
            in_specs=[pl.BlockSpec(mine.shape, lambda i, info_ref: (0, 0))] * 2,
            out_specs=pl.BlockSpec((count, count), lambda i, info_ref: (0, 0)),
            scratch_shapes=[pltpu.VMEM((half, 3 * half), F32)],
        ),
        out_shape=jax.ShapeDtypeStruct((count, count), BF16),
        name="inverse_factor",
        **params(8),
    )(info, mine, other)


def rotate(info, rotation, pieces, bands, bands_all, planes, rows_y, only, before):
    group = 1 + max(r for r, t, u, c in pieces)
    _, per_y, per_p, _, rows_z = next(iter(pieces.values()))[0].shape
    swap = swap_matrix()
    cuts_y = rows_y // per_y
    at_once = 2 if only is not None and per_p % 2 == 0 else 1 if only is not None else per_p
    steps = per_p // at_once
    span = at_once if only is not None else planes
    given = [] if before is None else [before]
    arrays = {id(value): value for value, _ in pieces.values()}
    slots = {key: k for k, key in enumerate(arrays)}

    def start_of(info_ref, r, t, c):
        source = lax.rem(info_ref[3] + info_ref[4] - t, info_ref[4])
        return source * bands + (info_ref[0] ^ r) * (bands // group) + c * chunk

    def kernel(info_ref, *refs):
        rotation_ref, swap_ref = refs[len(arrays) :][:2]
        out, rows, mixed, turned = refs[-4:]
        me, parts = info_ref[3], info_ref[4]
        if only is None:
            for (r, t, u, c), (value, index) in pieces.items():
                source = lax.rem(me + parts - t, parts)
                part = lax.rem(me + u, parts)
                first_p, first_y = part // cuts_y * per_p, lax.rem(part, cuts_y) * per_y
                piece = refs[slots[id(value)]].at[index]
                fill(info_ref, rows, piece, source, first_p, first_y, r, c, bands, group)
            turned[...] = rotation_ref[...]
        else:

            @pl.when(pl.program_id(0) == 0)
            def _():
                place = lax.broadcasted_iota(jnp.int32, (bands_all, bands_all), 1)
                wanted = lax.broadcasted_iota(jnp.int32, (bands_all, bands_all), 0)
                from_row = place & (chunk - 1)
                for k, (r, t, _, c) in enumerate(pieces):
                    start = jnp.where(place // chunk == k, start_of(info_ref, r, t, c), 0)
                    from_row = from_row + start
                order = jnp.where(wanted == from_row, 1.0, 0.0).astype(BF16)
                value = jnp.dot(rotation_ref[...], order, preferred_element_type=F32)
                turned[...] = value.astype(BF16)

        def row(p, y):
            if only is None:
                return rows[p, y]
            held = [refs[slots[id(value)]][index, y, p] for value, index in pieces.values()]
            return jnp.concatenate(held, axis=0)

        def plane(p):
            for y in range(0, rows_y, 2):
                pair = jnp.concatenate([row(p, y), row(p, y + 1)], axis=1)
                value = jnp.dot(turned[...], pair, preferred_element_type=F32)
                value = value.astype(BF16)
                for k in range(bands // 16):
                    for b in range(2):
                        mixed[k, y + b] = value[
                            16 * k : 16 * k + 16, b * rows_z : (b + 1) * rows_z
                        ]
            for k in range(0, bands // 16, 2):
                pair = [mixed[k + b].reshape(16 * rows_y, rows_z) for b in range(2)]
                moved = jnp.dot(
                    swap_ref[...], jnp.concatenate(pair, axis=1), preferred_element_type=F32
                ).astype(BF16)
                for b in range(2):
                    part = moved[:, b * rows_z : (b + 1) * rows_z].reshape(16, rows_y, rows_z)
                    out[16 * (k + b) : 16 * (k + b) + 16, p] = part

        if only is not None:
            for p in range(span):
                plane(p)
        else:
            pl.loop(0, span)(plane)

    def spec(value):
        return pl.BlockSpec(
            (value.shape[0], per_y, at_once, chunk, rows_z), lambda i, info_ref: (0, 0, i, 0, 0)
        )

    def out_index(i, info_ref):
        if only is None:
            return (0, 0, 0, 0)
        return (0, lax.rem(info_ref[3] + only, info_ref[4]) * steps + i, 0, 0)

    return pl.pallas_call(
        kernel,
        grid_spec=pltpu.PrefetchScalarGridSpec(
            num_scalar_prefetch=1,
            grid=(steps,),
            in_specs=[spec(value) for value in arrays.values()]
            + [
                pl.BlockSpec((bands, bands_all), lambda i, info_ref: (info_ref[3], 0)),
                pl.BlockSpec(swap.shape, lambda i, info_ref: (0, 0)),
            ]
            + [pl.BlockSpec(memory_space=pl.ANY)] * len(given),
            out_specs=pl.BlockSpec((bands, span, rows_y, rows_z), out_index),
            scratch_shapes=[
                pltpu.VMEM((span if only is None else 1, rows_y, bands_all, rows_z), BF16),
                pltpu.VMEM((bands // 16, rows_y, 16, rows_z), BF16),
                pltpu.VMEM((bands, bands_all), BF16),
            ],
        ),
        out_shape=jax.ShapeDtypeStruct((bands, planes, rows_y, rows_z), BF16),
        input_output_aliases={3 + len(arrays): 0} if given else {},
        name="rotate",
        **params(60 if only is None else 14),
    )(info, *arrays.values(), rotation, swap, *given)


def pairwise_sum(value, axis, count, low, high):
    bit = max(low, 1)
    while bit < high:
        value = value + lax.ppermute(value, axis, [(i, i ^ bit) for i in range(count)])
        bit *= 2
    return value


def body(orbital_block, block_scale, potential):
    bands, planes, rows_y, rows_z = orbital_block.shape
    parts, slabs = lax.axis_size("band"), lax.axis_size("domain")
    bands_all = bands * parts
    group = 4 if bands // 4 >= chunk else 2
    chunks = bands // group // chunk
    where, band = lax.axis_index("domain"), lax.axis_index("band")
    info = jnp.stack(
        [
            lax.rem(where, group),
            (where < group).astype(jnp.int32),
            (where >= slabs - group).astype(jnp.int32),
            band,
            jnp.int32(parts),
            lax.rem(where // group, 2),
        ]
    ).astype(jnp.int32)

    def send(value, r, t):
        if r == 0 and t == 0:
            return value
        pairs = [
            (q * slabs + i, (q + t) % parts * slabs + (i ^ r))
            for q in range(parts)
            for i in range(slabs)
        ]
        return lax.ppermute(value, ("band", "domain"), pairs)

    scale = jnp.broadcast_to(block_scale[:, :, None], (bands, planes, rows_z))
    far_first = sorted(range(group), reverse=True)
    arrived = []
    for c in range(chunks):
        pieces = prepare(info, orbital_block, scale, potential, c, group, c == 0)
        sent = {r: send(pieces[r], r, 0) for r in far_first}
        arrived.append([sent[r] for r in range(group)])
    def after(value, *others):
        return lax.optimization_barrier((value, *others))[0] if others else value

    def swapped(value, odd):
        lower = [i for i in range(slabs - group) if i // group % 2 == odd]
        pairs = [(i, i + group) for i in lower] + [(i + group, i) for i in lower]
        return lax.ppermute(value, "domain", pairs)

    sides = []
    pieces, own, moved, crossed = {}, {}, {}, {}
    ready = []
    for c in range(chunks):
        ends = edges(after(info, *ready), arrived[c], 1)
        sides.append([[swapped(end, odd) for end in ends[odd]] for odd in range(2)])
        filtered = chebyshev(info, sides[c], arrived[c], sides[0], arrived[0], parts)
        ready = [filtered[0][0]]
        for a in reversed(range(group // 2)):
            for t in reversed(range(parts)):
                value = filtered[a][t]
                own[(a, t, c)] = value
                moved[(a, t, c)] = send(value, 2 * a, t)
    known = {}
    early = parts == 2 and chunks > 1 and group == 4
    if early:
        first = lax.ppermute(own[(0, 0, 0)][0], "band", [(0, 1), (1, 0)])
        known[(0, 1, 1, 0)] = (first[None], 0)
    for c in range(chunks):
        keys = [(a, t) for t in range(parts) for a in range(group // 2)]
        wait = [first] if early and c == 0 else []
        there = {key: after(moved[(*key, c)], *ready, *wait) for key in keys}
        crossed[c] = send(jnp.stack([there[key][1] for key in keys]), 1, 0)
        for k, (a, t) in enumerate(keys):
            pieces[(2 * a, t, c)] = (there[(a, t)], 0)
            pieces[(2 * a + 1, t, c)] = (crossed[c], k)

    known |= {(r, t, 0, c): value for (r, t, c), value in pieces.items()}
    late = {}
    if early:
        came = [moved[(a, 1, chunks - 1)] for a in range(2)]
        chosen = [(r, c, *pieces[(r, 0, c)]) for r, c in ((0, chunks - 1), (1, 0))]
        sent = jnp.stack([value[index] for _, _, value, index in chosen])
        sent = lax.ppermute(after(sent, *came), "band", [(0, 1), (1, 0)])
        for k, (r, c, _, _) in enumerate(chosen):
            known[(r, 1, 1, c)] = (sent, k)
    packs = [
        (r, c)
        for c in range(chunks)
        for r in range(group)
        if parts > 2 or (r, 1, 1, c) not in known
    ]
    mine, other, buffer = gram(info, pieces, packs, bands, bands_all)
    mine = mine + send(other, 1, 0)
    mine = pairwise_sum(mine, "domain", slabs, 2, group)
    for key, value in own.items():
        if key[1] > 0:
            late[key] = send(after(value, mine), 2 * key[0], 0)
    if early:
        mine = after(mine, sent)
    mine = pairwise_sum(mine, "band", parts, 0, parts)

    def forward(buffer, t, packs):
        for s in range(1, parts):
            if t != s:
                pairs = [(q, (q + s) % parts) for q in range(parts)]
                sent = lax.ppermute(buffer, "band", pairs)
                for k, (r, c) in enumerate(packs):
                    known[(r, s, (t - s) % parts, c)] = (sent, k)

    forward(after(buffer, mine), 0, packs)
    mine = pairwise_sum(mine, "domain", slabs, group, slabs)
    rotation = inverse_factor(info, mine, send(mine, 1, 0), planes * rows_y * rows_z * slabs)
    for t in range(1, parts):
        keys = [(a, c) for c in range(chunks) for a in range(group // 2)]
        far = send(jnp.stack([after(late[(a, t, c)], rotation)[1] for a, c in keys]), 1, 0)
        for k, (a, c) in enumerate(keys):
            known[(2 * a, 0, t, c)] = (late[(a, t, c)], 0)
            known[(2 * a + 1, 0, t, c)] = (far, k)
        if parts > 2:
            chosen = [known[(r, 0, t, c)] for r, c in packs]
            forward(jnp.stack([value[index] for value, index in chosen]), t, packs)
    out = None
    for only in range(parts) if parts == 2 and planes % 2 == 0 else [None]:
        chosen = {key: value for key, value in known.items() if only in (None, key[2])}
        out = rotate(info, rotation, chosen, bands, bands_all, planes, rows_y, only, out)
    return out


def solution(mesh):
    in_specs = (P("band", "domain", None, None), P("band", "domain"), P("domain", None, None))
    out_specs = P("band", "domain", None, None)
    return jax.shard_map(body, mesh=mesh, in_specs=in_specs, out_specs=out_specs, check_vma=False)
```

```python
import math

import jax
import jax.numpy as jnp
import numpy as np
from jax import lax
from jax.experimental import pallas as pl
from jax.experimental.pallas import tpu as pltpu
from jax.sharding import PartitionSpec as P

grid_step = 0.5
stencil_coef = (
    -5369.0 / 1800.0,
    12.0 / 7.0,
    -15.0 / 56.0,
    10.0 / 189.0,
    -1.0 / 112.0,
    2.0 / 1925.0,
    -1.0 / 16632.0,
)
lower_end = -4.0
cut_energy = 6.0
upper_end = 43.0
kinetic = -0.5 / (grid_step * grid_step)
coef_scale = 7.0
reach = 6
edge = 3 * reach
chunk = 16
F32, BF16 = jnp.float32, jnp.bfloat16


def filter_terms():
    width_e = (upper_end - cut_energy) / 2.0
    centre = (upper_end + cut_energy) / 2.0
    sigma_one = width_e / (lower_end - centre)
    gamma_term = 2.0 / sigma_one
    sigma_two = 1.0 / (gamma_term - sigma_one)
    sigma_three = 1.0 / (gamma_term - sigma_two)
    return (width_e, centre, sigma_one, sigma_two, sigma_three)


def stencil_line(count):
    line = np.zeros((count, count), np.float64)
    for offset in range(1, reach + 1):
        value = kinetic * stencil_coef[offset] * coef_scale
        line += value * (np.eye(count, k=offset) + np.eye(count, k=-offset))
    return line


def xy_matrix(planes, rows_y):
    along_x = np.zeros((planes, planes + 2 * reach), np.float64)
    along_x[:, :] = stencil_line(planes + 2 * reach)[reach : reach + planes]
    middle = np.eye(planes, planes + 2 * reach, k=reach)
    full = np.kron(along_x, np.eye(rows_y)) + np.kron(middle, stencil_line(rows_y))
    return jnp.asarray(full, BF16)


def z_matrix(count_z):
    return jnp.asarray(np.kron(np.eye(2), stencil_line(count_z)), BF16)


def swap_matrix():
    full = np.zeros((256, 256), np.float32)
    for a in range(16):
        for b in range(16):
            full[a * 16 + b, b * 16 + a] = 1.0
    return jnp.asarray(full, BF16)


def params(mebibytes):
    return dict(
        compiler_params=pltpu.CompilerParams(
            vmem_limit_bytes=mebibytes * 2**20, dimension_semantics=("arbitrary",)
        ),
        cost_estimate=pl.CostEstimate(flops=1, bytes_accessed=1, transcendentals=0),
    )


def prepare(info, orbitals, scale, potential, part, group, with_potential):
    bands, planes, rows_y, rows_z = orbitals.shape
    own = bands // group
    at_once = 8
    steps = chunk // at_once
    total = chunk + (1 if with_potential else 0)

    def kernel(info_ref, *refs):
        sources, scales, potential_ref = refs[:group], refs[group : 2 * group], refs[2 * group]
        outs = refs[2 * group + 1 :]
        i = pl.program_id(0)
        for r in range(group):
            for b in range(at_once):
                value = sources[r][b].astype(F32) * scales[r][b][:, None, :]
                outs[r][i * at_once + b] = value.astype(BF16)

        if with_potential:

            @pl.when(i == 0)
            def _():
                for r in range(group):
                    outs[r][chunk] = potential_ref[...].astype(BF16)

    def first(r, i, info_ref):
        return ((info_ref[0] ^ r) * own + part * chunk) // at_once + i

    def source_spec(r):
        return pl.BlockSpec(
            (at_once, planes, rows_y, rows_z),
            lambda i, info_ref: (first(r, i, info_ref), 0, 0, 0),
        )

    def scale_spec(r):
        return pl.BlockSpec(
            (at_once, planes, rows_z), lambda i, info_ref: (first(r, i, info_ref), 0, 0)
        )

    shape = jax.ShapeDtypeStruct((total, planes, rows_y, rows_z), BF16)
    return pl.pallas_call(
        kernel,
        grid_spec=pltpu.PrefetchScalarGridSpec(
            num_scalar_prefetch=1,
            grid=(steps,),
            in_specs=[source_spec(r) for r in range(group)]
            + [scale_spec(r) for r in range(group)]
            + [pl.BlockSpec((planes, rows_y, rows_z), lambda i, info_ref: (0, 0, 0))],
            out_specs=[pl.BlockSpec(shape.shape, lambda i, info_ref: (0, 0, 0, 0))] * group,
        ),
        out_shape=[shape] * group,
        name="prepare",
        **params(14),
    )(info, *([orbitals] * group), *([scale] * group), potential)


def edges(info, pieces, cuts):
    group = len(pieces)
    total, planes, rows_y, rows_z = pieces[0].shape
    rest = edge - planes
    width = edge // cuts

    def kernel(info_ref, *refs):
        sources, outs = refs[:group], refs[group:]

        def put(targets, to, source, begin, count):
            while count:
                size = min(count, width - to % width)
                target = targets[to // width]
                target[:, to % width : to % width + size] = source[:, begin : begin + size]
                to, begin, count = to + size, begin + size, count - size

        for odd in range(2):
            up, down = (outs[k * cuts : (k + 1) * cuts] for k in (odd, 1 - odd))
            for r in range(group):
                slab = jnp.where(info_ref[5] == odd, info_ref[0] ^ r, -1)

                @pl.when(slab == group - 1)
                def _():
                    put(up, rest, sources[r], 0, planes)

                @pl.when(slab == group - 2)
                def _():
                    put(up, 0, sources[r], planes - rest, rest)

                @pl.when(slab == 0)
                def _():
                    put(down, 0, sources[r], 0, planes)

                @pl.when(slab == 1)
                def _():
                    put(down, planes, sources[r], 0, rest)

    whole = pl.BlockSpec(memory_space=pltpu.VMEM)
    flat = pl.pallas_call(
        kernel,
        grid_spec=pltpu.PrefetchScalarGridSpec(
            num_scalar_prefetch=1,
            grid=(1,),
            in_specs=[whole] * group,
            out_specs=[whole] * (2 * cuts),
        ),
        out_shape=[jax.ShapeDtypeStruct((total, width, rows_y, rows_z), BF16)] * (2 * cuts),
        name="edges",
        **params(8),
    )(info, *pieces)
    return flat[:cuts], flat[cuts:]


def chebyshev(info, sides, pieces, sides_pot, pieces_pot, parts):
    group = len(pieces)
    _, planes, rows_y, rows_z = pieces[0].shape
    slab = group * planes
    per_p, per_y, cuts_y = shares(planes, rows_y, parts)
    at_once = 2 if per_p % 2 == 0 else 1
    steps = chunk // 2
    count_out = group // 2 * parts
    flat_sides, flat_pot = ([value for side in both for value in side] for both in (sides, sides_pot))
    cuts, cuts_pot = len(sides[0]), len(sides_pot[0])
    width, width_pot = edge // cuts, edge // cuts_pot
    width_e, centre, sigma_one, sigma_two, sigma_three = filter_terms()
    diagonal = 3.0 * stencil_coef[0] * kinetic - centre
    tile_rows = planes * rows_y
    xy, zz, swap = xy_matrix(planes, rows_y), z_matrix(rows_z), swap_matrix()
    count_0, count_1, count_2 = slab + 6 * reach, slab + 4 * reach, slab + 2 * reach

    def kernel(info_ref, *refs):
        side_refs, refs = refs[: 2 * cuts], refs[2 * cuts :]
        side_pot_refs, refs = refs[: 2 * cuts_pot], refs[2 * cuts_pot :]
        piece_refs, pot_refs = refs[:group], refs[group : 2 * group]
        xy_ref, zz_ref, swap_ref = refs[2 * group : 3 + 2 * group]
        outs = refs[3 + 2 * group : 3 + 2 * group + count_out]
        field, first, second, energy, result = refs[3 + 2 * group + count_out :]
        i = pl.program_id(0)
        me = info_ref[0]
        at_left, at_right = info_ref[1] == 1, info_ref[2] == 1

        @pl.when(i == 0)
        def _():
            def store(start, source):
                total = source[0].astype(F32)
                energy[pl.ds(start, source.shape[1])] = coef_scale * (total + diagonal)

            for odd in range(2):

                @pl.when(info_ref[5] == odd)
                def _():
                    halves = side_pot_refs[:cuts_pot], side_pot_refs[cuts_pot:]
                    for side, base, low, high in (
                        (halves[1 - odd], -reach, 0, 2 * reach),
                        (halves[odd], slab + 2 * reach, slab + 2 * reach, count_1),
                    ):
                        for k, ref in enumerate(side):
                            start = base + k * width_pot
                            begin, end = max(start, low), min(start + width_pot, high)
                            if begin < end:
                                store(begin, ref.at[:, begin - start : end - start])

            for r in range(group):
                store(2 * reach + planes * (me ^ r), pot_refs[r])

        for b in range(2):
            lanes = slice(b * rows_z, (b + 1) * rows_z)
            for k in range(2):
                start = (1 - (info_ref[5] ^ k)) * (edge + slab)
                for n in range(cuts):
                    where = pl.ds(start + n * width, width)
                    field[where, :, lanes] = side_refs[k * cuts + n][b]
            for r in range(group):
                field[pl.ds(edge + planes * (me ^ r), planes), :, lanes] = piece_refs[r][b]

        def apply(source, start, energy_start):
            rows = source[pl.ds(start, planes + 2 * reach)].reshape(-1, 2 * rows_z)
            middle = source[pl.ds(start + reach, planes)].reshape(tile_rows, 2 * rows_z)
            total = jnp.dot(xy_ref[...], rows, preferred_element_type=F32)
            total += jnp.dot(middle, zz_ref[...], preferred_element_type=F32)
            factor = energy[pl.ds(energy_start, planes)].reshape(tile_rows, rows_z)
            factor = jnp.concatenate([factor, factor], axis=1)
            return total + factor * middle.astype(F32)

        def block(value):
            return value.astype(BF16).reshape(planes, rows_y, 2 * rows_z)

        def previous(source, start):
            return source[pl.ds(start, planes)].reshape(tile_rows, 2 * rows_z).astype(F32)

        for t in range(count_1 // planes):
            at = t * planes
            value = apply(field, at, at) * (sigma_one / width_e / coef_scale)
            first[at : at + planes] = block(value)

        @pl.when(at_left)
        def _():
            first[: 2 * reach] = jnp.zeros((2 * reach, rows_y, 2 * rows_z), BF16)

        @pl.when(at_right)
        def _():
            first[count_1 - 2 * reach :] = jnp.zeros((2 * reach, rows_y, 2 * rows_z), BF16)

        for t in range(count_2 // planes):
            at = t * planes
            value = apply(first, at, at + reach) * (2.0 * sigma_two / width_e / coef_scale)
            value -= sigma_one * sigma_two * previous(field, at + 2 * reach)
            second[at : at + planes] = block(value)

        @pl.when(at_left)
        def _():
            second[:reach] = jnp.zeros((reach, rows_y, 2 * rows_z), BF16)

        @pl.when(at_right)
        def _():
            second[count_2 - reach :] = jnp.zeros((reach, rows_y, 2 * rows_z), BF16)

        for t in range(group):
            at = t * planes
            value = apply(second, at, at + 2 * reach) * (2.0 * sigma_three / width_e / coef_scale)
            value -= sigma_two * sigma_three * previous(first, at + 2 * reach)
            value = block(value)
            for b in range(2):
                part = value[:, :, b * rows_z : (b + 1) * rows_z]
                result[at : at + planes, 2 * i + b] = part

        @pl.when(i == steps - 1)
        def _():
            for t in range(parts):
                part = lax.rem(info_ref[3] + t, parts)
                begin = lax.rem(part, cuts_y) * (per_y * chunk)
                begin = pl.multiple_of(begin, per_y * chunk)
                for r in range(group):
                    start = planes * (me ^ r) + part // cuts_y * per_p
                    for p in range(0, per_p, at_once):
                        pair = [
                            result[start + p + k].reshape(chunk * rows_y, rows_z)
                            for k in range(at_once)
                        ]
                        moved = jnp.dot(
                            swap_ref[pl.ds(begin, per_y * chunk), :],
                            jnp.concatenate(pair, axis=1),
                            preferred_element_type=F32,
                        ).astype(BF16)
                        for k in range(at_once):
                            value = moved[:, k * rows_z : (k + 1) * rows_z]
                            out = outs[r // 2 * parts + t]
                            out[r % 2, :, p + k] = value.reshape(per_y, chunk, rows_z)

    def block_spec(count, index, bands=2):
        return pl.BlockSpec((bands, count, rows_y, rows_z), index)

    def whole_spec(shape):
        return pl.BlockSpec(shape, lambda i, info_ref: (0,) * len(shape))

    moving = lambda i, info_ref: (i, 0, 0, 0)
    fixed = lambda i, info_ref: (chunk, 0, 0, 0)
    shape = jax.ShapeDtypeStruct((2, per_y, per_p, chunk, rows_z), BF16)
    flat = pl.pallas_call(
        kernel,
        grid_spec=pltpu.PrefetchScalarGridSpec(
            num_scalar_prefetch=1,
            grid=(steps,),
            in_specs=[block_spec(width, moving)] * (2 * cuts)
            + [block_spec(width_pot, fixed, 1)] * (2 * cuts_pot)
            + [block_spec(planes, moving)] * group
            + [block_spec(planes, fixed, 1)] * group
            + [whole_spec(xy.shape), whole_spec(zz.shape), whole_spec(swap.shape)],
            out_specs=[whole_spec(shape.shape)] * count_out,
            scratch_shapes=[
                pltpu.VMEM((count_0, rows_y, 2 * rows_z), BF16),
                pltpu.VMEM((count_1, rows_y, 2 * rows_z), BF16),
                pltpu.VMEM((count_2, rows_y, 2 * rows_z), BF16),
                pltpu.VMEM((count_1, rows_y, rows_z), F32),
                pltpu.VMEM((slab, chunk, rows_y, rows_z), BF16),
            ],
        ),
        out_shape=[shape] * count_out,
        name="chebyshev",
        **params(18),
    )(info, *flat_sides, *flat_pot, *pieces, *pieces_pot, xy, zz, swap)
    return [flat[a * parts : (a + 1) * parts] for a in range(group // 2)]


def shares(planes, rows_y, parts):
    cuts_p = math.gcd(planes, parts)
    cuts_y = parts // cuts_p
    return planes // cuts_p, rows_y // cuts_y, cuts_y


def fill(info_ref, rows, piece, source, first_p, first_y, r, c, bands, group):
    own = bands // group
    start = source * bands + (info_ref[0] ^ r) * own + c * chunk
    where = pl.ds(pl.multiple_of(start, chunk), chunk)
    for p in range(piece.shape[1]):
        rows[first_p + p, pl.ds(first_y, piece.shape[0]), where, :] = piece[:, p]


def gram(info, pieces, packs, bands, bands_all):
    group = 1 + max(r for r, t, c in pieces)
    _, per_y, per_p, _, rows_z = next(iter(pieces.values()))[0].shape
    at_once = 2 if per_p % 2 == 0 else 1
    steps = per_p // at_once
    half = bands_all // 2
    direct = half == bands
    own = bands // group
    ordered = sorted(pieces, key=lambda key: (key[1], key[0], key[2]))

    def in_order(info_ref, value, by_rows):
        axis = 0 if by_rows else 1
        count = value.shape[axis]
        place = lax.broadcasted_iota(jnp.int32, value.shape, axis)
        bit = 1
        while bit < group:
            step = bit * own
            if by_rows:
                blocks = [value[k : k + step] for k in range(0, count, step)]
                blocks = [blocks[k ^ 1] for k in range(len(blocks))]
                moved = jnp.concatenate(blocks, axis=0)
            else:
                low = pltpu.roll(value, count - step, 1)
                high = pltpu.roll(value, step, 1)
                moved = jnp.where(place & step == 0, low, high)
            value = jnp.where((info_ref[0] & bit) != 0, moved, value)
            bit *= 2
        return value

    def direct_blocks(info_ref, out):
        for odd in range(2):

            @pl.when(info_ref[3] == odd)
            def _():
                below = out[half:, :half] if odd == 0 else out[:half, half:bands_all]
                blocks = [out[:half, :half], below, out[half:, half:bands_all]]
                for k, block in enumerate(blocks if odd == 0 else blocks[::-1]):
                    value = in_order(info_ref, in_order(info_ref, block, True), False)
                    out[:half, k * half : (k + 1) * half] = value

    def direct_kernel(info_ref, *refs):
        mine, other, packed, _, out = refs[len(pieces) :]
        by_key = dict(zip(pieces, refs))
        i = pl.program_id(0)
        for k, (r, c) in enumerate(packs):
            packed[k] = by_key[(r, 0, c)][0]
        block = jnp.concatenate(
            [
                jnp.concatenate([by_key[key][0, y, p] for key in ordered], axis=0)
                for p in range(at_once)
                for y in range(per_y)
            ],
            axis=1,
        )
        total = lax.dot_general(
            block, block, (((1,), (1,)), ((), ())), preferred_element_type=F32
        )

        @pl.when(i == 0)
        def _():
            out[:, :bands_all] = total

        @pl.when(i > 0)
        def _():
            out[:, :bands_all] += total

        @pl.when(i == steps - 1)
        def _():
            direct_blocks(info_ref, out)
            for ref, core in ((mine, info_ref[0] & 1), (other, 1 - (info_ref[0] & 1))):
                where = pl.ds(pl.multiple_of(core * (half // 2), half // 2), half // 2)
                ref[...] = out[where, : 3 * half]

    def kernel(info_ref, *refs):
        mine, other, packed, rows, out = refs[len(pieces) :]
        parts = info_ref[4]
        i = pl.program_id(0)
        for (r, t, c), piece in zip(pieces, refs):
            source = lax.rem(info_ref[3] + parts - t, parts)
            fill(info_ref, rows, piece.at[0], source, 0, 0, r, c, bands, group)
            if t == 0 and (r, c) in packs:
                packed[packs.index((r, c))] = piece[0]
        block = jnp.concatenate(
            [rows[p, y] for p in range(at_once) for y in range(per_y)], axis=1
        )
        total = lax.dot_general(
            block, block, (((1,), (1,)), ((), ())), preferred_element_type=F32
        )

        total = [total[:half, :half], total[half:, :half], total[half:, half:]]
        total = jnp.concatenate(total, axis=1)

        @pl.when(i == 0)
        def _():
            out[...] = total

        @pl.when(i > 0)
        def _():
            out[...] += total

        @pl.when(i == steps - 1)
        def _():
            for ref, core in ((mine, info_ref[0] & 1), (other, 1 - (info_ref[0] & 1))):
                ref[...] = out[pl.ds(pl.multiple_of(core * (half // 2), half // 2), half // 2)]

    def spec(index):
        return pl.BlockSpec(
            (1, per_y, at_once, chunk, rows_z), lambda i, info_ref: (index, 0, i, 0, 0)
        )

    return pl.pallas_call(
        direct_kernel if direct else kernel,
        grid_spec=pltpu.PrefetchScalarGridSpec(
            num_scalar_prefetch=1,
            grid=(steps,),
            in_specs=[spec(index) for _, index in pieces.values()],
            out_specs=[pl.BlockSpec((half // 2, 3 * half), lambda i, info_ref: (0, 0))] * 2
            + [
                pl.BlockSpec(
                    (len(packs), per_y, at_once, chunk, rows_z),
                    lambda i, info_ref: (0, 0, i, 0, 0),
                ),
            ],
            scratch_shapes=[
                pltpu.VMEM((1 if direct else at_once, per_y, bands_all, rows_z), BF16),
                pltpu.VMEM((bands_all if direct else half, 3 * half), F32),
            ],
        ),
        out_shape=[jax.ShapeDtypeStruct((half // 2, 3 * half), F32)] * 2
        + [jax.ShapeDtypeStruct((len(packs), per_y, per_p, chunk, rows_z), BF16)],
        name="gram",
        **params(16),
    )(info, *[value for value, _ in pieces.values()])


def inverse_factor(info, mine, other, cells):
    half = 2 * mine.shape[0]
    count = 2 * half

    def exact(a, b, transposed):
        dims = (((1,), (1 if transposed else 0,)), ((), ()))
        return lax.dot_general(
            a, b, dims, precision=lax.Precision.HIGHEST, preferred_element_type=F32
        )

    def eliminate(block):
        groups = half // 8
        row = lax.broadcasted_iota(jnp.int32, (8, half), 0)
        column = lax.broadcasted_iota(jnp.int32, (8, half), 1)
        left = [block[8 * g : 8 * g + 8] for g in range(groups)]
        right = [jnp.where(column == row + 8 * g, 1.0, 0.0).astype(F32) for g in range(groups)]
        for at in range(groups):
            later = range(at, groups)
            spread = [
                [
                    jnp.broadcast_to(left[g][:, 8 * at + k : 8 * at + k + 1], (8, half))
                    for g in later
                ]
                for k in range(8)
            ]
            factors, rows_left, rows_right = [], [], []
            for k in range(8):
                pivot = jnp.broadcast_to(spread[k][0][k : k + 1], (8, half))
                scale = lax.rsqrt(pivot)
                scale = scale * (1.5 - 0.5 * pivot * scale * scale)
                factor = [value * scale for value in spread[k]]
                for m in range(k + 1, 8):
                    other = jnp.broadcast_to(factor[0][m : m + 1], (8, half))
                    spread[m] = [value - f * other for value, f in zip(spread[m], factor)]
                row_left = jnp.broadcast_to(left[at][k : k + 1], (8, half)) * scale
                row_right = jnp.broadcast_to(right[at][k : k + 1], (8, half)) * scale
                inside = jnp.where(row > k, factor[0], 0.0)
                left[at] = jnp.where(row == k, row_left, left[at] - inside * row_left)
                right[at] = jnp.where(row == k, row_right, right[at] - inside * row_right)
                factors.append(factor)
                rows_left.append(row_left)
                rows_right.append(row_right)
            for g in range(at + 1, groups):
                for k in range(8):
                    left[g] = left[g] - factors[k][g - at] * rows_left[k]
                    right[g] = right[g] - factors[k][g - at] * rows_right[k]
        return jnp.concatenate(right, axis=0)

    def kernel(info_ref, mine_ref, other_ref, out, blocks):
        for ref, core in ((mine_ref, info_ref[0] & 1), (other_ref, 1 - (info_ref[0] & 1))):
            where = pl.ds(pl.multiple_of(core * (half // 2), half // 2), half // 2)
            blocks[where] = ref[...] * (1.0 / cells)
        top = eliminate(blocks[:, :half])
        below = exact(blocks[:, half:count], top, True)
        rest = blocks[:, count:] - exact(below, below, True)
        bottom = eliminate(rest)
        out[:half, :half] = top.astype(BF16)
        out[:half, half:] = jnp.zeros((half, half), BF16)
        out[half:, :half] = (-exact(bottom, exact(below, top, False), False)).astype(BF16)
        out[half:, half:] = bottom.astype(BF16)

    return pl.pallas_call(
        kernel,
        grid_spec=pltpu.PrefetchScalarGridSpec(
            num_scalar_prefetch=1,
            grid=(1,),
            in_specs=[pl.BlockSpec(mine.shape, lambda i, info_ref: (0, 0))] * 2,
            out_specs=pl.BlockSpec((count, count), lambda i, info_ref: (0, 0)),
            scratch_shapes=[pltpu.VMEM((half, 3 * half), F32)],
        ),
        out_shape=jax.ShapeDtypeStruct((count, count), BF16),
        name="inverse_factor",
        **params(8),
    )(info, mine, other)


def rotate(info, rotation, pieces, bands, bands_all, planes, rows_y, only, before):
    group = 1 + max(r for r, t, u, c in pieces)
    _, per_y, per_p, _, rows_z = next(iter(pieces.values()))[0].shape
    swap = swap_matrix()
    cuts_y = rows_y // per_y
    at_once = 2 if only is not None and per_p % 2 == 0 else 1 if only is not None else per_p
    steps = per_p // at_once
    span = at_once if only is not None else planes
    given = [] if before is None else [before]
    arrays = {id(value): value for value, _ in pieces.values()}
    slots = {key: k for k, key in enumerate(arrays)}

    def start_of(info_ref, r, t, c):
        source = lax.rem(info_ref[3] + info_ref[4] - t, info_ref[4])
        return source * bands + (info_ref[0] ^ r) * (bands // group) + c * chunk

    def kernel(info_ref, *refs):
        rotation_ref, swap_ref = refs[len(arrays) :][:2]
        out, rows, mixed, turned = refs[-4:]
        me, parts = info_ref[3], info_ref[4]
        if only is None:
            for (r, t, u, c), (value, index) in pieces.items():
                source = lax.rem(me + parts - t, parts)
                part = lax.rem(me + u, parts)
                first_p, first_y = part // cuts_y * per_p, lax.rem(part, cuts_y) * per_y
                piece = refs[slots[id(value)]].at[index]
                fill(info_ref, rows, piece, source, first_p, first_y, r, c, bands, group)
            turned[...] = rotation_ref[...]
        else:

            @pl.when(pl.program_id(0) == 0)
            def _():
                place = lax.broadcasted_iota(jnp.int32, (bands_all, bands_all), 1)
                wanted = lax.broadcasted_iota(jnp.int32, (bands_all, bands_all), 0)
                from_row = place & (chunk - 1)
                for k, (r, t, _, c) in enumerate(pieces):
                    start = jnp.where(place // chunk == k, start_of(info_ref, r, t, c), 0)
                    from_row = from_row + start
                order = jnp.where(wanted == from_row, 1.0, 0.0).astype(BF16)
                value = jnp.dot(rotation_ref[...], order, preferred_element_type=F32)
                turned[...] = value.astype(BF16)

        def row(p, y):
            if only is None:
                return rows[p, y]
            held = [refs[slots[id(value)]][index, y, p] for value, index in pieces.values()]
            return jnp.concatenate(held, axis=0)

        def plane(p):
            for y in range(0, rows_y, 2):
                pair = jnp.concatenate([row(p, y), row(p, y + 1)], axis=1)
                value = jnp.dot(turned[...], pair, preferred_element_type=F32)
                value = value.astype(BF16)
                for k in range(bands // 16):
                    for b in range(2):
                        mixed[k, y + b] = value[
                            16 * k : 16 * k + 16, b * rows_z : (b + 1) * rows_z
                        ]
            for k in range(0, bands // 16, 2):
                pair = [mixed[k + b].reshape(16 * rows_y, rows_z) for b in range(2)]
                moved = jnp.dot(
                    swap_ref[...], jnp.concatenate(pair, axis=1), preferred_element_type=F32
                ).astype(BF16)
                for b in range(2):
                    part = moved[:, b * rows_z : (b + 1) * rows_z].reshape(16, rows_y, rows_z)
                    out[16 * (k + b) : 16 * (k + b) + 16, p] = part

        if only is not None:
            for p in range(span):
                plane(p)
        else:
            pl.loop(0, span)(plane)

    def spec(value):
        return pl.BlockSpec(
            (value.shape[0], per_y, at_once, chunk, rows_z), lambda i, info_ref: (0, 0, i, 0, 0)
        )

    def out_index(i, info_ref):
        if only is None:
            return (0, 0, 0, 0)
        return (0, lax.rem(info_ref[3] + only, info_ref[4]) * steps + i, 0, 0)

    return pl.pallas_call(
        kernel,
        grid_spec=pltpu.PrefetchScalarGridSpec(
            num_scalar_prefetch=1,
            grid=(steps,),
            in_specs=[spec(value) for value in arrays.values()]
            + [
                pl.BlockSpec((bands, bands_all), lambda i, info_ref: (info_ref[3], 0)),
                pl.BlockSpec(swap.shape, lambda i, info_ref: (0, 0)),
            ]
            + [pl.BlockSpec(memory_space=pl.ANY)] * len(given),
            out_specs=pl.BlockSpec((bands, span, rows_y, rows_z), out_index),
            scratch_shapes=[
                pltpu.VMEM((span if only is None else 1, rows_y, bands_all, rows_z), BF16),
                pltpu.VMEM((bands // 16, rows_y, 16, rows_z), BF16),
                pltpu.VMEM((bands, bands_all), BF16),
            ],
        ),
        out_shape=jax.ShapeDtypeStruct((bands, planes, rows_y, rows_z), BF16),
        input_output_aliases={3 + len(arrays): 0} if given else {},
        name="rotate",
        **params(60 if only is None else 14),
    )(info, *arrays.values(), rotation, swap, *given)


def pairwise_sum(value, axis, count, low, high):
    bit = max(low, 1)
    while bit < high:
        value = value + lax.ppermute(value, axis, [(i, i ^ bit) for i in range(count)])
        bit *= 2
    return value


def body(orbital_block, block_scale, potential):
    bands, planes, rows_y, rows_z = orbital_block.shape
    parts, slabs = lax.axis_size("band"), lax.axis_size("domain")
    bands_all = bands * parts
    group = 4 if bands // 4 >= chunk else 2
    chunks = bands // group // chunk
    where, band = lax.axis_index("domain"), lax.axis_index("band")
    info = jnp.stack(
        [
            lax.rem(where, group),
            (where < group).astype(jnp.int32),
            (where >= slabs - group).astype(jnp.int32),
            band,
            jnp.int32(parts),
            lax.rem(where // group, 2),
        ]
    ).astype(jnp.int32)

    def send(value, r, t):
        if r == 0 and t == 0:
            return value
        pairs = [
            (q * slabs + i, (q + t) % parts * slabs + (i ^ r))
            for q in range(parts)
            for i in range(slabs)
        ]
        return lax.ppermute(value, ("band", "domain"), pairs)

    scale = jnp.broadcast_to(block_scale[:, :, None], (bands, planes, rows_z))
    far_first = sorted(range(group), reverse=True)
    arrived = []
    for c in range(chunks):
        pieces = prepare(info, orbital_block, scale, potential, c, group, c == 0)
        sent = {r: send(pieces[r], r, 0) for r in far_first}
        arrived.append([sent[r] for r in range(group)])
    def after(value, *others):
        return lax.optimization_barrier((value, *others))[0] if others else value

    def swapped(value, odd):
        lower = [i for i in range(slabs - group) if i // group % 2 == odd]
        pairs = [(i, i + group) for i in lower] + [(i + group, i) for i in lower]
        return lax.ppermute(value, "domain", pairs)

    sides = []
    pieces, own, moved, crossed = {}, {}, {}, {}
    ready = []
    for c in range(chunks):
        ends = edges(after(info, *ready), arrived[c], 1)
        sides.append([[swapped(end, odd) for end in ends[odd]] for odd in range(2)])
        filtered = chebyshev(info, sides[c], arrived[c], sides[0], arrived[0], parts)
        ready = [filtered[0][0]]
        for a in reversed(range(group // 2)):
            for t in reversed(range(parts)):
                value = filtered[a][t]
                own[(a, t, c)] = value
                moved[(a, t, c)] = send(value, 2 * a, t)
    known = {}
    early = parts == 2 and chunks > 1 and group == 4
    if early:
        first = [
            lax.ppermute(own[(0, 0, c)][0], "band", [(0, 1), (1, 0)]) for c in (0, chunks - 1)
        ]
        known[(0, 1, 1, 0)] = (first[0][None], 0)
        known[(0, 1, 1, chunks - 1)] = (first[1][None], 0)
    for c in range(chunks):
        keys = [(a, t) for t in range(parts) for a in range(group // 2)]
        wait = [first[min(c, 1)]] if early and c in (0, chunks - 1) else []
        there = {key: after(moved[(*key, c)], *ready, *wait) for key in keys}
        crossed[c] = send(jnp.stack([there[key][1] for key in keys]), 1, 0)
        for k, (a, t) in enumerate(keys):
            pieces[(2 * a, t, c)] = (there[(a, t)], 0)
            pieces[(2 * a + 1, t, c)] = (crossed[c], k)

    known |= {(r, t, 0, c): value for (r, t, c), value in pieces.items()}
    late = {}
    if early:
        came = [moved[(a, 1, chunks - 1)] for a in range(2)]
        chosen = [(r, c, *pieces[(r, 0, c)]) for r, c in ((1, 0), (2, 0))]
        sent = jnp.stack([value[index] for _, _, value, index in chosen])
        sent = lax.ppermute(after(sent, *came), "band", [(0, 1), (1, 0)])
        for k, (r, c, _, _) in enumerate(chosen):
            known[(r, 1, 1, c)] = (sent, k)
    packs = [
        (r, c)
        for c in range(chunks)
        for r in range(group)
        if parts > 2 or (r, 1, 1, c) not in known
    ]
    mine, other, buffer = gram(info, pieces, packs, bands, bands_all)
    mine = mine + send(other, 1, 0)
    mine = pairwise_sum(mine, "domain", slabs, 2, group)
    for key, value in own.items():
        if key[1] > 0:
            late[key] = send(after(value, mine), 2 * key[0], 0)
    if early:
        mine = after(mine, sent)
    mine = pairwise_sum(mine, "band", parts, 0, parts)

    def forward(buffer, t, packs):
        for s in range(1, parts):
            if t != s:
                pairs = [(q, (q + s) % parts) for q in range(parts)]
                sent = lax.ppermute(buffer, "band", pairs)
                for k, (r, c) in enumerate(packs):
                    known[(r, s, (t - s) % parts, c)] = (sent, k)

    forward(after(buffer, mine), 0, packs)
    mine = pairwise_sum(mine, "domain", slabs, group, slabs)
    rotation = inverse_factor(info, mine, send(mine, 1, 0), planes * rows_y * rows_z * slabs)
    for t in range(1, parts):
        keys = [(a, c) for c in range(chunks) for a in range(group // 2)]
        far = send(jnp.stack([after(late[(a, t, c)], rotation)[1] for a, c in keys]), 1, 0)
        for k, (a, c) in enumerate(keys):
            known[(2 * a, 0, t, c)] = (late[(a, t, c)], 0)
            known[(2 * a + 1, 0, t, c)] = (far, k)
        if parts > 2:
            chosen = [known[(r, 0, t, c)] for r, c in packs]
            forward(jnp.stack([value[index] for value, index in chosen]), t, packs)
    out = None
    for only in range(parts) if parts == 2 and planes % 2 == 0 else [None]:
        chosen = {key: value for key, value in known.items() if only in (None, key[2])}
        out = rotate(info, rotation, chosen, bands, bands_all, planes, rows_y, only, out)
    return out


def solution(mesh):
    in_specs = (P("band", "domain", None, None), P("band", "domain"), P("domain", None, None))
    out_specs = P("band", "domain", None, None)
    return jax.shard_map(body, mesh=mesh, in_specs=in_specs, out_specs=out_specs, check_vma=False)
```

```python
import math

import jax
import jax.numpy as jnp
import numpy as np
from jax import lax
from jax.experimental import pallas as pl
from jax.experimental.pallas import tpu as pltpu
from jax.sharding import PartitionSpec as P

grid_step = 0.5
stencil_coef = (
    -5369.0 / 1800.0,
    12.0 / 7.0,
    -15.0 / 56.0,
    10.0 / 189.0,
    -1.0 / 112.0,
    2.0 / 1925.0,
    -1.0 / 16632.0,
)
lower_end = -4.0
cut_energy = 6.0
upper_end = 43.0
kinetic = -0.5 / (grid_step * grid_step)
coef_scale = 7.0
reach = 6
edge = 3 * reach
chunk = 16
F32, BF16 = jnp.float32, jnp.bfloat16


def filter_terms():
    width_e = (upper_end - cut_energy) / 2.0
    centre = (upper_end + cut_energy) / 2.0
    sigma_one = width_e / (lower_end - centre)
    gamma_term = 2.0 / sigma_one
    sigma_two = 1.0 / (gamma_term - sigma_one)
    sigma_three = 1.0 / (gamma_term - sigma_two)
    return (width_e, centre, sigma_one, sigma_two, sigma_three)


def stencil_line(count):
    line = np.zeros((count, count), np.float64)
    for offset in range(1, reach + 1):
        value = kinetic * stencil_coef[offset] * coef_scale
        line += value * (np.eye(count, k=offset) + np.eye(count, k=-offset))
    return line


def xy_matrix(planes, rows_y):
    along_x = np.zeros((planes, planes + 2 * reach), np.float64)
    along_x[:, :] = stencil_line(planes + 2 * reach)[reach : reach + planes]
    middle = np.eye(planes, planes + 2 * reach, k=reach)
    full = np.kron(along_x, np.eye(rows_y)) + np.kron(middle, stencil_line(rows_y))
    return jnp.asarray(full, BF16)


def z_matrix(count_z):
    return jnp.asarray(np.kron(np.eye(2), stencil_line(count_z)), BF16)


def swap_matrix():
    full = np.zeros((256, 256), np.float32)
    for a in range(16):
        for b in range(16):
            full[a * 16 + b, b * 16 + a] = 1.0
    return jnp.asarray(full, BF16)


def params(mebibytes):
    return dict(
        compiler_params=pltpu.CompilerParams(
            vmem_limit_bytes=mebibytes * 2**20, dimension_semantics=("arbitrary",)
        ),
        cost_estimate=pl.CostEstimate(flops=1, bytes_accessed=1, transcendentals=0),
    )


def prepare(info, orbitals, scale, potential, part, group, with_potential):
    bands, planes, rows_y, rows_z = orbitals.shape
    own = bands // group
    at_once = 8
    steps = chunk // at_once
    total = chunk + (1 if with_potential else 0)

    def kernel(info_ref, *refs):
        sources, scales, potential_ref = refs[:group], refs[group : 2 * group], refs[2 * group]
        outs = refs[2 * group + 1 :]
        i = pl.program_id(0)
        for r in range(group):
            for b in range(at_once):
                value = sources[r][b].astype(F32) * scales[r][b][:, None, :]
                outs[r][i * at_once + b] = value.astype(BF16)

        if with_potential:

            @pl.when(i == 0)
            def _():
                for r in range(group):
                    outs[r][chunk] = potential_ref[...].astype(BF16)

    def first(r, i, info_ref):
        return ((info_ref[0] ^ r) * own + part * chunk) // at_once + i

    def source_spec(r):
        return pl.BlockSpec(
            (at_once, planes, rows_y, rows_z),
            lambda i, info_ref: (first(r, i, info_ref), 0, 0, 0),
        )

    def scale_spec(r):
        return pl.BlockSpec(
            (at_once, planes, rows_z), lambda i, info_ref: (first(r, i, info_ref), 0, 0)
        )

    shape = jax.ShapeDtypeStruct((total, planes, rows_y, rows_z), BF16)
    return pl.pallas_call(
        kernel,
        grid_spec=pltpu.PrefetchScalarGridSpec(
            num_scalar_prefetch=1,
            grid=(steps,),
            in_specs=[source_spec(r) for r in range(group)]
            + [scale_spec(r) for r in range(group)]
            + [pl.BlockSpec((planes, rows_y, rows_z), lambda i, info_ref: (0, 0, 0))],
            out_specs=[pl.BlockSpec(shape.shape, lambda i, info_ref: (0, 0, 0, 0))] * group,
        ),
        out_shape=[shape] * group,
        name="prepare",
        **params(14),
    )(info, *([orbitals] * group), *([scale] * group), potential)


def edges(info, pieces, cuts):
    group = len(pieces)
    total, planes, rows_y, rows_z = pieces[0].shape
    rest = edge - planes
    width = edge // cuts

    def kernel(info_ref, *refs):
        sources, outs = refs[:group], refs[group:]

        def put(targets, to, source, begin, count):
            while count:
                size = min(count, width - to % width)
                target = targets[to // width]
                target[:, to % width : to % width + size] = source[:, begin : begin + size]
                to, begin, count = to + size, begin + size, count - size

        for odd in range(2):
            up, down = (outs[k * cuts : (k + 1) * cuts] for k in (odd, 1 - odd))
            for r in range(group):
                slab = jnp.where(info_ref[5] == odd, info_ref[0] ^ r, -1)

                @pl.when(slab == group - 1)
                def _():
                    put(up, rest, sources[r], 0, planes)

                @pl.when(slab == group - 2)
                def _():
                    put(up, 0, sources[r], planes - rest, rest)

                @pl.when(slab == 0)
                def _():
                    put(down, 0, sources[r], 0, planes)

                @pl.when(slab == 1)
                def _():
                    put(down, planes, sources[r], 0, rest)

    whole = pl.BlockSpec(memory_space=pltpu.VMEM)
    flat = pl.pallas_call(
        kernel,
        grid_spec=pltpu.PrefetchScalarGridSpec(
            num_scalar_prefetch=1,
            grid=(1,),
            in_specs=[whole] * group,
            out_specs=[whole] * (2 * cuts),
        ),
        out_shape=[jax.ShapeDtypeStruct((total, width, rows_y, rows_z), BF16)] * (2 * cuts),
        name="edges",
        **params(8),
    )(info, *pieces)
    return flat[:cuts], flat[cuts:]


def chebyshev(info, sides, pieces, sides_pot, pieces_pot, parts):
    group = len(pieces)
    _, planes, rows_y, rows_z = pieces[0].shape
    slab = group * planes
    per_p, per_y, cuts_y = shares(planes, rows_y, parts)
    at_once = 2 if per_p % 2 == 0 else 1
    steps = chunk // 2
    count_out = group // 2 * parts
    flat_sides, flat_pot = ([value for side in both for value in side] for both in (sides, sides_pot))
    cuts, cuts_pot = len(sides[0]), len(sides_pot[0])
    width, width_pot = edge // cuts, edge // cuts_pot
    width_e, centre, sigma_one, sigma_two, sigma_three = filter_terms()
    diagonal = 3.0 * stencil_coef[0] * kinetic - centre
    tile_rows = planes * rows_y
    xy, zz, swap = xy_matrix(planes, rows_y), z_matrix(rows_z), swap_matrix()
    count_0, count_1, count_2 = slab + 6 * reach, slab + 4 * reach, slab + 2 * reach

    def kernel(info_ref, *refs):
        side_refs, refs = refs[: 2 * cuts], refs[2 * cuts :]
        side_pot_refs, refs = refs[: 2 * cuts_pot], refs[2 * cuts_pot :]
        piece_refs, pot_refs = refs[:group], refs[group : 2 * group]
        xy_ref, zz_ref, swap_ref = refs[2 * group : 3 + 2 * group]
        outs = refs[3 + 2 * group : 3 + 2 * group + count_out]
        field, first, second, energy, result = refs[3 + 2 * group + count_out :]
        i = pl.program_id(0)
        me = info_ref[0]
        at_left, at_right = info_ref[1] == 1, info_ref[2] == 1

        @pl.when(i == 0)
        def _():
            def store(start, source):
                total = source[0].astype(F32)
                energy[pl.ds(start, source.shape[1])] = coef_scale * (total + diagonal)

            for odd in range(2):

                @pl.when(info_ref[5] == odd)
                def _():
                    halves = side_pot_refs[:cuts_pot], side_pot_refs[cuts_pot:]
                    for side, base, low, high in (
                        (halves[1 - odd], -reach, 0, 2 * reach),
                        (halves[odd], slab + 2 * reach, slab + 2 * reach, count_1),
                    ):
                        for k, ref in enumerate(side):
                            start = base + k * width_pot
                            begin, end = max(start, low), min(start + width_pot, high)
                            if begin < end:
                                store(begin, ref.at[:, begin - start : end - start])

            for r in range(group):
                store(2 * reach + planes * (me ^ r), pot_refs[r])

        for b in range(2):
            lanes = slice(b * rows_z, (b + 1) * rows_z)
            for k in range(2):
                start = (1 - (info_ref[5] ^ k)) * (edge + slab)
                for n in range(cuts):
                    where = pl.ds(start + n * width, width)
                    field[where, :, lanes] = side_refs[k * cuts + n][b]
            for r in range(group):
                field[pl.ds(edge + planes * (me ^ r), planes), :, lanes] = piece_refs[r][b]

        def apply(source, start, energy_start):
            rows = source[pl.ds(start, planes + 2 * reach)].reshape(-1, 2 * rows_z)
            middle = source[pl.ds(start + reach, planes)].reshape(tile_rows, 2 * rows_z)
            total = jnp.dot(xy_ref[...], rows, preferred_element_type=F32)
            total += jnp.dot(middle, zz_ref[...], preferred_element_type=F32)
            factor = energy[pl.ds(energy_start, planes)].reshape(tile_rows, rows_z)
            factor = jnp.concatenate([factor, factor], axis=1)
            return total + factor * middle.astype(F32)

        def block(value):
            return value.astype(BF16).reshape(planes, rows_y, 2 * rows_z)

        def previous(source, start):
            return source[pl.ds(start, planes)].reshape(tile_rows, 2 * rows_z).astype(F32)

        for t in range(count_1 // planes):
            at = t * planes
            value = apply(field, at, at) * (sigma_one / width_e / coef_scale)
            first[at : at + planes] = block(value)

        @pl.when(at_left)
        def _():
            first[: 2 * reach] = jnp.zeros((2 * reach, rows_y, 2 * rows_z), BF16)

        @pl.when(at_right)
        def _():
            first[count_1 - 2 * reach :] = jnp.zeros((2 * reach, rows_y, 2 * rows_z), BF16)

        for t in range(count_2 // planes):
            at = t * planes
            value = apply(first, at, at + reach) * (2.0 * sigma_two / width_e / coef_scale)
            value -= sigma_one * sigma_two * previous(field, at + 2 * reach)
            second[at : at + planes] = block(value)

        @pl.when(at_left)
        def _():
            second[:reach] = jnp.zeros((reach, rows_y, 2 * rows_z), BF16)

        @pl.when(at_right)
        def _():
            second[count_2 - reach :] = jnp.zeros((reach, rows_y, 2 * rows_z), BF16)

        for t in range(group):
            at = t * planes
            value = apply(second, at, at + 2 * reach) * (2.0 * sigma_three / width_e / coef_scale)
            value -= sigma_two * sigma_three * previous(first, at + 2 * reach)
            value = block(value)
            for b in range(2):
                part = value[:, :, b * rows_z : (b + 1) * rows_z]
                result[at : at + planes, 2 * i + b] = part

        @pl.when(i == steps - 1)
        def _():
            for t in range(parts):
                part = lax.rem(info_ref[3] + t, parts)
                begin = lax.rem(part, cuts_y) * (per_y * chunk)
                begin = pl.multiple_of(begin, per_y * chunk)
                for r in range(group):
                    start = planes * (me ^ r) + part // cuts_y * per_p
                    for p in range(0, per_p, at_once):
                        pair = [
                            result[start + p + k].reshape(chunk * rows_y, rows_z)
                            for k in range(at_once)
                        ]
                        moved = jnp.dot(
                            swap_ref[pl.ds(begin, per_y * chunk), :],
                            jnp.concatenate(pair, axis=1),
                            preferred_element_type=F32,
                        ).astype(BF16)
                        for k in range(at_once):
                            value = moved[:, k * rows_z : (k + 1) * rows_z]
                            out = outs[r // 2 * parts + t]
                            out[r % 2, :, p + k] = value.reshape(per_y, chunk, rows_z)

    def block_spec(count, index, bands=2):
        return pl.BlockSpec((bands, count, rows_y, rows_z), index)

    def whole_spec(shape):
        return pl.BlockSpec(shape, lambda i, info_ref: (0,) * len(shape))

    moving = lambda i, info_ref: (i, 0, 0, 0)
    fixed = lambda i, info_ref: (chunk, 0, 0, 0)
    shape = jax.ShapeDtypeStruct((2, per_y, per_p, chunk, rows_z), BF16)
    flat = pl.pallas_call(
        kernel,
        grid_spec=pltpu.PrefetchScalarGridSpec(
            num_scalar_prefetch=1,
            grid=(steps,),
            in_specs=[block_spec(width, moving)] * (2 * cuts)
            + [block_spec(width_pot, fixed, 1)] * (2 * cuts_pot)
            + [block_spec(planes, moving)] * group
            + [block_spec(planes, fixed, 1)] * group
            + [whole_spec(xy.shape), whole_spec(zz.shape), whole_spec(swap.shape)],
            out_specs=[whole_spec(shape.shape)] * count_out,
            scratch_shapes=[
                pltpu.VMEM((count_0, rows_y, 2 * rows_z), BF16),
                pltpu.VMEM((count_1, rows_y, 2 * rows_z), BF16),
                pltpu.VMEM((count_2, rows_y, 2 * rows_z), BF16),
                pltpu.VMEM((count_1, rows_y, rows_z), F32),
                pltpu.VMEM((slab, chunk, rows_y, rows_z), BF16),
            ],
        ),
        out_shape=[shape] * count_out,
        name="chebyshev",
        **params(18),
    )(info, *flat_sides, *flat_pot, *pieces, *pieces_pot, xy, zz, swap)
    return [flat[a * parts : (a + 1) * parts] for a in range(group // 2)]


def shares(planes, rows_y, parts):
    cuts_p = math.gcd(planes, parts)
    cuts_y = parts // cuts_p
    return planes // cuts_p, rows_y // cuts_y, cuts_y


def fill(info_ref, rows, piece, source, first_p, first_y, r, c, bands, group):
    own = bands // group
    start = source * bands + (info_ref[0] ^ r) * own + c * chunk
    where = pl.ds(pl.multiple_of(start, chunk), chunk)
    for p in range(piece.shape[1]):
        rows[first_p + p, pl.ds(first_y, piece.shape[0]), where, :] = piece[:, p]


def gram(info, pieces, packs, bands, bands_all):
    group = 1 + max(r for r, t, c in pieces)
    _, per_y, per_p, _, rows_z = next(iter(pieces.values()))[0].shape
    at_once = 2 if per_p % 2 == 0 else 1
    steps = per_p // at_once
    half = bands_all // 2
    direct = half == bands
    own = bands // group
    ordered = sorted(pieces, key=lambda key: (key[1], key[0], key[2]))

    def in_order(info_ref, value, by_rows):
        axis = 0 if by_rows else 1
        count = value.shape[axis]
        place = lax.broadcasted_iota(jnp.int32, value.shape, axis)
        bit = 1
        while bit < group:
            step = bit * own
            if by_rows:
                blocks = [value[k : k + step] for k in range(0, count, step)]
                blocks = [blocks[k ^ 1] for k in range(len(blocks))]
                moved = jnp.concatenate(blocks, axis=0)
            else:
                low = pltpu.roll(value, count - step, 1)
                high = pltpu.roll(value, step, 1)
                moved = jnp.where(place & step == 0, low, high)
            value = jnp.where((info_ref[0] & bit) != 0, moved, value)
            bit *= 2
        return value

    def direct_blocks(info_ref, out):
        for odd in range(2):

            @pl.when(info_ref[3] == odd)
            def _():
                below = out[half:, :half] if odd == 0 else out[:half, half:bands_all]
                blocks = [out[:half, :half], below, out[half:, half:bands_all]]
                for k, block in enumerate(blocks if odd == 0 else blocks[::-1]):
                    value = in_order(info_ref, in_order(info_ref, block, True), False)
                    out[:half, k * half : (k + 1) * half] = value

    def direct_kernel(info_ref, *refs):
        mine, other, packed, _, out = refs[len(pieces) :]
        by_key = dict(zip(pieces, refs))
        i = pl.program_id(0)
        for k, (r, c) in enumerate(packs):
            packed[k] = by_key[(r, 0, c)][0]
        block = jnp.concatenate(
            [
                jnp.concatenate([by_key[key][0, y, p] for key in ordered], axis=0)
                for p in range(at_once)
                for y in range(per_y)
            ],
            axis=1,
        )
        total = lax.dot_general(
            block, block, (((1,), (1,)), ((), ())), preferred_element_type=F32
        )

        @pl.when(i == 0)
        def _():
            out[:, :bands_all] = total

        @pl.when(i > 0)
        def _():
            out[:, :bands_all] += total

        @pl.when(i == steps - 1)
        def _():
            direct_blocks(info_ref, out)
            for ref, core in ((mine, info_ref[0] & 1), (other, 1 - (info_ref[0] & 1))):
                where = pl.ds(pl.multiple_of(core * (half // 2), half // 2), half // 2)
                ref[...] = out[where, : 3 * half]

    def kernel(info_ref, *refs):
        mine, other, packed, rows, out = refs[len(pieces) :]
        parts = info_ref[4]
        i = pl.program_id(0)
        for (r, t, c), piece in zip(pieces, refs):
            source = lax.rem(info_ref[3] + parts - t, parts)
            fill(info_ref, rows, piece.at[0], source, 0, 0, r, c, bands, group)
            if t == 0 and (r, c) in packs:
                packed[packs.index((r, c))] = piece[0]
        block = jnp.concatenate(
            [rows[p, y] for p in range(at_once) for y in range(per_y)], axis=1
        )
        total = lax.dot_general(
            block, block, (((1,), (1,)), ((), ())), preferred_element_type=F32
        )

        total = [total[:half, :half], total[half:, :half], total[half:, half:]]
        total = jnp.concatenate(total, axis=1)

        @pl.when(i == 0)
        def _():
            out[...] = total

        @pl.when(i > 0)
        def _():
            out[...] += total

        @pl.when(i == steps - 1)
        def _():
            for ref, core in ((mine, info_ref[0] & 1), (other, 1 - (info_ref[0] & 1))):
                ref[...] = out[pl.ds(pl.multiple_of(core * (half // 2), half // 2), half // 2)]

    def spec(index):
        return pl.BlockSpec(
            (1, per_y, at_once, chunk, rows_z), lambda i, info_ref: (index, 0, i, 0, 0)
        )

    return pl.pallas_call(
        direct_kernel if direct else kernel,
        grid_spec=pltpu.PrefetchScalarGridSpec(
            num_scalar_prefetch=1,
            grid=(steps,),
            in_specs=[spec(index) for _, index in pieces.values()],
            out_specs=[pl.BlockSpec((half // 2, 3 * half), lambda i, info_ref: (0, 0))] * 2
            + [
                pl.BlockSpec(
                    (len(packs), per_y, at_once, chunk, rows_z),
                    lambda i, info_ref: (0, 0, i, 0, 0),
                ),
            ],
            scratch_shapes=[
                pltpu.VMEM((1 if direct else at_once, per_y, bands_all, rows_z), BF16),
                pltpu.VMEM((bands_all if direct else half, 3 * half), F32),
            ],
        ),
        out_shape=[jax.ShapeDtypeStruct((half // 2, 3 * half), F32)] * 2
        + [jax.ShapeDtypeStruct((len(packs), per_y, per_p, chunk, rows_z), BF16)],
        name="gram",
        **params(16),
    )(info, *[value for value, _ in pieces.values()])


def inverse_factor(info, mine, other, cells):
    half = 2 * mine.shape[0]
    count = 2 * half

    def exact(a, b, transposed):
        dims = (((1,), (1 if transposed else 0,)), ((), ()))
        return lax.dot_general(
            a, b, dims, precision=lax.Precision.HIGHEST, preferred_element_type=F32
        )

    def eliminate(block):
        groups = half // 8
        row = lax.broadcasted_iota(jnp.int32, (8, half), 0)
        column = lax.broadcasted_iota(jnp.int32, (8, half), 1)
        left = [block[8 * g : 8 * g + 8] for g in range(groups)]
        right = [jnp.where(column == row + 8 * g, 1.0, 0.0).astype(F32) for g in range(groups)]
        for at in range(groups):
            later = range(at, groups)
            spread = [
                [
                    jnp.broadcast_to(left[g][:, 8 * at + k : 8 * at + k + 1], (8, half))
                    for g in later
                ]
                for k in range(8)
            ]
            factors, rows_left, rows_right = [], [], []
            for k in range(8):
                pivot = jnp.broadcast_to(spread[k][0][k : k + 1], (8, half))
                scale = lax.rsqrt(pivot)
                scale = scale * (1.5 - 0.5 * pivot * scale * scale)
                factor = [value * scale for value in spread[k]]
                for m in range(k + 1, 8):
                    other = jnp.broadcast_to(factor[0][m : m + 1], (8, half))
                    spread[m] = [value - f * other for value, f in zip(spread[m], factor)]
                row_left = jnp.broadcast_to(left[at][k : k + 1], (8, half)) * scale
                row_right = jnp.broadcast_to(right[at][k : k + 1], (8, half)) * scale
                inside = jnp.where(row > k, factor[0], 0.0)
                left[at] = jnp.where(row == k, row_left, left[at] - inside * row_left)
                right[at] = jnp.where(row == k, row_right, right[at] - inside * row_right)
                factors.append(factor)
                rows_left.append(row_left)
                rows_right.append(row_right)
            for g in range(at + 1, groups):
                for k in range(8):
                    left[g] = left[g] - factors[k][g - at] * rows_left[k]
                    right[g] = right[g] - factors[k][g - at] * rows_right[k]
        return jnp.concatenate(right, axis=0)

    def kernel(info_ref, mine_ref, other_ref, out, blocks):
        for ref, core in ((mine_ref, info_ref[0] & 1), (other_ref, 1 - (info_ref[0] & 1))):
            where = pl.ds(pl.multiple_of(core * (half // 2), half // 2), half // 2)
            blocks[where] = ref[...] * (1.0 / cells)
        top = eliminate(blocks[:, :half])
        below = exact(blocks[:, half:count], top, True)
        rest = blocks[:, count:] - exact(below, below, True)
        bottom = eliminate(rest)
        out[:half, :half] = top.astype(BF16)
        out[:half, half:] = jnp.zeros((half, half), BF16)
        out[half:, :half] = (-exact(bottom, exact(below, top, False), False)).astype(BF16)
        out[half:, half:] = bottom.astype(BF16)

    return pl.pallas_call(
        kernel,
        grid_spec=pltpu.PrefetchScalarGridSpec(
            num_scalar_prefetch=1,
            grid=(1,),
            in_specs=[pl.BlockSpec(mine.shape, lambda i, info_ref: (0, 0))] * 2,
            out_specs=pl.BlockSpec((count, count), lambda i, info_ref: (0, 0)),
            scratch_shapes=[pltpu.VMEM((half, 3 * half), F32)],
        ),
        out_shape=jax.ShapeDtypeStruct((count, count), BF16),
        name="inverse_factor",
        **params(8),
    )(info, mine, other)


def rotate(info, rotation, pieces, bands, bands_all, planes, rows_y, only, before):
    group = 1 + max(r for r, t, u, c in pieces)
    _, per_y, per_p, _, rows_z = next(iter(pieces.values()))[0].shape
    swap = swap_matrix()
    cuts_y = rows_y // per_y
    at_once = 2 if only is not None and per_p % 2 == 0 else 1 if only is not None else per_p
    steps = per_p // at_once
    span = at_once if only is not None else planes
    given = [] if before is None else [before]
    arrays = {id(value): value for value, _ in pieces.values()}
    slots = {key: k for k, key in enumerate(arrays)}

    def start_of(info_ref, r, t, c):
        source = lax.rem(info_ref[3] + info_ref[4] - t, info_ref[4])
        return source * bands + (info_ref[0] ^ r) * (bands // group) + c * chunk

    def kernel(info_ref, *refs):
        rotation_ref, swap_ref = refs[len(arrays) :][:2]
        out, rows, mixed, turned = refs[-4:]
        me, parts = info_ref[3], info_ref[4]
        if only is None:
            for (r, t, u, c), (value, index) in pieces.items():
                source = lax.rem(me + parts - t, parts)
                part = lax.rem(me + u, parts)
                first_p, first_y = part // cuts_y * per_p, lax.rem(part, cuts_y) * per_y
                piece = refs[slots[id(value)]].at[index]
                fill(info_ref, rows, piece, source, first_p, first_y, r, c, bands, group)
            turned[...] = rotation_ref[...]
        else:

            @pl.when(pl.program_id(0) == 0)
            def _():
                place = lax.broadcasted_iota(jnp.int32, (bands_all, bands_all), 1)
                wanted = lax.broadcasted_iota(jnp.int32, (bands_all, bands_all), 0)
                from_row = place & (chunk - 1)
                for k, (r, t, _, c) in enumerate(pieces):
                    start = jnp.where(place // chunk == k, start_of(info_ref, r, t, c), 0)
                    from_row = from_row + start
                order = jnp.where(wanted == from_row, 1.0, 0.0).astype(BF16)
                value = jnp.dot(rotation_ref[...], order, preferred_element_type=F32)
                turned[...] = value.astype(BF16)

        def row(p, y):
            if only is None:
                return rows[p, y]
            held = [refs[slots[id(value)]][index, y, p] for value, index in pieces.values()]
            return jnp.concatenate(held, axis=0)

        def plane(p):
            for y in range(0, rows_y, 2):
                pair = jnp.concatenate([row(p, y), row(p, y + 1)], axis=1)
                value = jnp.dot(turned[...], pair, preferred_element_type=F32)
                value = value.astype(BF16)
                for k in range(bands // 16):
                    for b in range(2):
                        mixed[k, y + b] = value[
                            16 * k : 16 * k + 16, b * rows_z : (b + 1) * rows_z
                        ]
            for k in range(0, bands // 16, 2):
                pair = [mixed[k + b].reshape(16 * rows_y, rows_z) for b in range(2)]
                moved = jnp.dot(
                    swap_ref[...], jnp.concatenate(pair, axis=1), preferred_element_type=F32
                ).astype(BF16)
                for b in range(2):
                    part = moved[:, b * rows_z : (b + 1) * rows_z].reshape(16, rows_y, rows_z)
                    out[16 * (k + b) : 16 * (k + b) + 16, p] = part

        if only is not None:
            for p in range(span):
                plane(p)
        else:
            pl.loop(0, span)(plane)

    def spec(value):
        return pl.BlockSpec(
            (value.shape[0], per_y, at_once, chunk, rows_z), lambda i, info_ref: (0, 0, i, 0, 0)
        )

    def out_index(i, info_ref):
        if only is None:
            return (0, 0, 0, 0)
        return (0, lax.rem(info_ref[3] + only, info_ref[4]) * steps + i, 0, 0)

    return pl.pallas_call(
        kernel,
        grid_spec=pltpu.PrefetchScalarGridSpec(
            num_scalar_prefetch=1,
            grid=(steps,),
            in_specs=[spec(value) for value in arrays.values()]
            + [
                pl.BlockSpec((bands, bands_all), lambda i, info_ref: (info_ref[3], 0)),
                pl.BlockSpec(swap.shape, lambda i, info_ref: (0, 0)),
            ]
            + [pl.BlockSpec(memory_space=pl.ANY)] * len(given),
            out_specs=pl.BlockSpec((bands, span, rows_y, rows_z), out_index),
            scratch_shapes=[
                pltpu.VMEM((span if only is None else 1, rows_y, bands_all, rows_z), BF16),
                pltpu.VMEM((bands // 16, rows_y, 16, rows_z), BF16),
                pltpu.VMEM((bands, bands_all), BF16),
            ],
        ),
        out_shape=jax.ShapeDtypeStruct((bands, planes, rows_y, rows_z), BF16),
        input_output_aliases={3 + len(arrays): 0} if given else {},
        name="rotate",
        **params(60 if only is None else 14),
    )(info, *arrays.values(), rotation, swap, *given)


def pairwise_sum(value, axis, count, low, high):
    bit = max(low, 1)
    while bit < high:
        value = value + lax.ppermute(value, axis, [(i, i ^ bit) for i in range(count)])
        bit *= 2
    return value


def body(orbital_block, block_scale, potential):
    bands, planes, rows_y, rows_z = orbital_block.shape
    parts, slabs = lax.axis_size("band"), lax.axis_size("domain")
    bands_all = bands * parts
    group = 4 if bands // 4 >= chunk else 2
    chunks = bands // group // chunk
    where, band = lax.axis_index("domain"), lax.axis_index("band")
    info = jnp.stack(
        [
            lax.rem(where, group),
            (where < group).astype(jnp.int32),
            (where >= slabs - group).astype(jnp.int32),
            band,
            jnp.int32(parts),
            lax.rem(where // group, 2),
        ]
    ).astype(jnp.int32)

    def send(value, r, t):
        if r == 0 and t == 0:
            return value
        pairs = [
            (q * slabs + i, (q + t) % parts * slabs + (i ^ r))
            for q in range(parts)
            for i in range(slabs)
        ]
        return lax.ppermute(value, ("band", "domain"), pairs)

    scale = jnp.broadcast_to(block_scale[:, :, None], (bands, planes, rows_z))
    far_first = sorted(range(group), reverse=True)
    arrived = []
    for c in range(chunks):
        pieces = prepare(info, orbital_block, scale, potential, c, group, c == 0)
        sent = {r: send(pieces[r], r, 0) for r in far_first}
        arrived.append([sent[r] for r in range(group)])
    def after(value, *others):
        return lax.optimization_barrier((value, *others))[0] if others else value

    def swapped(value, odd):
        lower = [i for i in range(slabs - group) if i // group % 2 == odd]
        pairs = [(i, i + group) for i in lower] + [(i + group, i) for i in lower]
        return lax.ppermute(value, "domain", pairs)

    sides = []
    pieces, own, moved, crossed = {}, {}, {}, {}
    ready = []
    for c in range(chunks):
        ends = edges(after(info, *ready), arrived[c], 1)
        sides.append([[swapped(end, odd) for end in ends[odd]] for odd in range(2)])
        filtered = chebyshev(info, sides[c], arrived[c], sides[0], arrived[0], parts)
        ready = [filtered[0][0]]
        for a in reversed(range(group // 2)):
            for t in reversed(range(parts)):
                value = filtered[a][t]
                own[(a, t, c)] = value
                moved[(a, t, c)] = send(value, 2 * a, t)
    known = {}
    early = parts == 2 and chunks > 1 and group == 4
    if early:
        first = lax.ppermute(own[(0, 0, 0)][0], "band", [(0, 1), (1, 0)])
        known[(0, 1, 1, 0)] = (first[None], 0)
    for c in range(chunks):
        keys = [(a, t) for t in range(parts) for a in range(group // 2)]
        wait = [first] if early and c == 0 else []
        there = {key: after(moved[(*key, c)], *ready, *wait) for key in keys}
        crossed[c] = send(jnp.stack([there[key][1] for key in keys]), 1, 0)
        for k, (a, t) in enumerate(keys):
            pieces[(2 * a, t, c)] = (there[(a, t)], 0)
            pieces[(2 * a + 1, t, c)] = (crossed[c], k)

    known |= {(r, t, 0, c): value for (r, t, c), value in pieces.items()}
    late = {}
    if early:
        came = [moved[(a, 1, chunks - 1)] for a in range(2)]
        chosen = [(r, c, *pieces[(r, 0, c)]) for r, c in ((0, chunks - 1), (1, 0))]
        sent = jnp.stack([value[index] for _, _, value, index in chosen])
        sent = lax.ppermute(after(sent, *came), "band", [(0, 1), (1, 0)])
        for k, (r, c, _, _) in enumerate(chosen):
            known[(r, 1, 1, c)] = (sent, k)
    packs = [
        (r, c)
        for c in range(chunks)
        for r in range(group)
        if parts > 2 or (r, 1, 1, c) not in known
    ]
    mine, other, buffer = gram(info, pieces, packs, bands, bands_all)
    mine = mine + send(other, 1, 0)
    mine = pairwise_sum(mine, "domain", slabs, 2, group)
    for key, value in own.items():
        if key[1] > 0:
            late[key] = send(after(value, mine), 2 * key[0], 0)
    if early:
        mine = after(mine, sent)
    mine = pairwise_sum(mine, "band", parts, 0, parts)

    def forward(buffer, t, packs):
        for s in range(1, parts):
            if t != s:
                pairs = [(q, (q + s) % parts) for q in range(parts)]
                sent = lax.ppermute(buffer, "band", pairs)
                for k, (r, c) in enumerate(packs):
                    known[(r, s, (t - s) % parts, c)] = (sent, k)

    forward(after(buffer, mine), 0, packs)
    mine = pairwise_sum(mine, "domain", slabs, group, slabs)
    rotation = inverse_factor(info, mine, send(mine, 1, 0), planes * rows_y * rows_z * slabs)
    for t in range(1, parts):
        keys = [(a, c) for c in range(chunks) for a in range(group // 2)]
        far = send(jnp.stack([after(late[(a, t, c)], rotation)[1] for a, c in keys]), 1, 0)
        for k, (a, c) in enumerate(keys):
            known[(2 * a, 0, t, c)] = (late[(a, t, c)], 0)
            known[(2 * a + 1, 0, t, c)] = (far, k)
        if parts > 2:
            chosen = [known[(r, 0, t, c)] for r, c in packs]
            forward(jnp.stack([value[index] for value, index in chosen]), t, packs)
    out = None
    for only in range(parts) if parts == 2 and planes % 2 == 0 else [None]:
        chosen = {key: value for key, value in known.items() if only in (None, key[2])}
        out = rotate(info, rotation, chosen, bands, bands_all, planes, rows_y, only, out)
    return out


def solution(mesh):
    in_specs = (P("band", "domain", None, None), P("band", "domain"), P("domain", None, None))
    out_specs = P("band", "domain", None, None)
    return jax.shard_map(body, mesh=mesh, in_specs=in_specs, out_specs=out_specs, check_vma=False)
```

```python
import math

import jax
import jax.numpy as jnp
import numpy as np
from jax import lax
from jax.experimental import pallas as pl
from jax.experimental.pallas import tpu as pltpu
from jax.sharding import PartitionSpec as P

grid_step = 0.5
stencil_coef = (
    -5369.0 / 1800.0,
    12.0 / 7.0,
    -15.0 / 56.0,
    10.0 / 189.0,
    -1.0 / 112.0,
    2.0 / 1925.0,
    -1.0 / 16632.0,
)
lower_end = -4.0
cut_energy = 6.0
upper_end = 43.0
kinetic = -0.5 / (grid_step * grid_step)
coef_scale = 7.0
reach = 6
edge = 3 * reach
chunk = 16
F32, BF16 = jnp.float32, jnp.bfloat16


def filter_terms():
    width_e = (upper_end - cut_energy) / 2.0
    centre = (upper_end + cut_energy) / 2.0
    sigma_one = width_e / (lower_end - centre)
    gamma_term = 2.0 / sigma_one
    sigma_two = 1.0 / (gamma_term - sigma_one)
    sigma_three = 1.0 / (gamma_term - sigma_two)
    return (width_e, centre, sigma_one, sigma_two, sigma_three)


def filter_sign():
    _, _, sigma_one, sigma_two, sigma_three = filter_terms()
    return math.copysign(1.0, sigma_one * sigma_two * sigma_three)


def stencil_line(count):
    line = np.zeros((count, count), np.float64)
    for offset in range(1, reach + 1):
        value = kinetic * stencil_coef[offset] * coef_scale
        line += value * (np.eye(count, k=offset) + np.eye(count, k=-offset))
    return line


def xy_matrix(planes, rows_y):
    along_x = np.zeros((planes, planes + 2 * reach), np.float64)
    along_x[:, :] = stencil_line(planes + 2 * reach)[reach : reach + planes]
    middle = np.eye(planes, planes + 2 * reach, k=reach)
    full = np.kron(along_x, np.eye(rows_y)) + np.kron(middle, stencil_line(rows_y))
    return jnp.asarray(full, BF16)


def z_matrix(count_z):
    return jnp.asarray(np.kron(np.eye(2), stencil_line(count_z)), BF16)


def swap_matrix():
    full = np.zeros((256, 256), np.float32)
    for a in range(16):
        for b in range(16):
            full[a * 16 + b, b * 16 + a] = 1.0
    return jnp.asarray(full, BF16)


def params(mebibytes):
    return dict(
        compiler_params=pltpu.CompilerParams(
            vmem_limit_bytes=mebibytes * 2**20, dimension_semantics=("arbitrary",)
        ),
        cost_estimate=pl.CostEstimate(flops=1, bytes_accessed=1, transcendentals=0),
    )


def prepare(info, orbitals, scale, potential, part, group, with_potential):
    bands, planes, rows_y, rows_z = orbitals.shape
    own = bands // group
    at_once = 8
    steps = chunk // at_once
    total = chunk + (1 if with_potential else 0)

    def kernel(info_ref, *refs):
        sources, scales, potential_ref = refs[:group], refs[group : 2 * group], refs[2 * group]
        outs = refs[2 * group + 1 :]
        i = pl.program_id(0)
        for r in range(group):
            for b in range(at_once):
                value = sources[r][b].astype(F32) * scales[r][b][:, None, :]
                outs[r][i * at_once + b] = value.astype(BF16)

        if with_potential:

            @pl.when(i == 0)
            def _():
                for r in range(group):
                    outs[r][chunk] = potential_ref[...].astype(BF16)

    def first(r, i, info_ref):
        return ((info_ref[0] ^ r) * own + part * chunk) // at_once + i

    def source_spec(r):
        return pl.BlockSpec(
            (at_once, planes, rows_y, rows_z),
            lambda i, info_ref: (first(r, i, info_ref), 0, 0, 0),
        )

    def scale_spec(r):
        return pl.BlockSpec(
            (at_once, planes, rows_z), lambda i, info_ref: (first(r, i, info_ref), 0, 0)
        )

    shape = jax.ShapeDtypeStruct((total, planes, rows_y, rows_z), BF16)
    return pl.pallas_call(
        kernel,
        grid_spec=pltpu.PrefetchScalarGridSpec(
            num_scalar_prefetch=1,
            grid=(steps,),
            in_specs=[source_spec(r) for r in range(group)]
            + [scale_spec(r) for r in range(group)]
            + [pl.BlockSpec((planes, rows_y, rows_z), lambda i, info_ref: (0, 0, 0))],
            out_specs=[pl.BlockSpec(shape.shape, lambda i, info_ref: (0, 0, 0, 0))] * group,
        ),
        out_shape=[shape] * group,
        name="prepare",
        **params(14),
    )(info, *([orbitals] * group), *([scale] * group), potential)


def edges(info, pieces, cuts):
    group = len(pieces)
    total, planes, rows_y, rows_z = pieces[0].shape
    rest = edge - planes
    width = edge // cuts

    def kernel(info_ref, *refs):
        sources, outs = refs[:group], refs[group:]

        def put(targets, to, source, begin, count):
            while count:
                size = min(count, width - to % width)
                target = targets[to // width]
                target[:, to % width : to % width + size] = source[:, begin : begin + size]
                to, begin, count = to + size, begin + size, count - size

        for odd in range(2):
            up, down = (outs[k * cuts : (k + 1) * cuts] for k in (odd, 1 - odd))
            for r in range(group):
                slab = jnp.where(info_ref[5] == odd, info_ref[0] ^ r, -1)

                @pl.when(slab == group - 1)
                def _():
                    put(up, rest, sources[r], 0, planes)

                @pl.when(slab == group - 2)
                def _():
                    put(up, 0, sources[r], planes - rest, rest)

                @pl.when(slab == 0)
                def _():
                    put(down, 0, sources[r], 0, planes)

                @pl.when(slab == 1)
                def _():
                    put(down, planes, sources[r], 0, rest)

    whole = pl.BlockSpec(memory_space=pltpu.VMEM)
    flat = pl.pallas_call(
        kernel,
        grid_spec=pltpu.PrefetchScalarGridSpec(
            num_scalar_prefetch=1,
            grid=(1,),
            in_specs=[whole] * group,
            out_specs=[whole] * (2 * cuts),
        ),
        out_shape=[jax.ShapeDtypeStruct((total, width, rows_y, rows_z), BF16)] * (2 * cuts),
        name="edges",
        **params(8),
    )(info, *pieces)
    return flat[:cuts], flat[cuts:]


def chebyshev(info, sides, pieces, sides_pot, pieces_pot, parts):
    group = len(pieces)
    _, planes, rows_y, rows_z = pieces[0].shape
    slab = group * planes
    per_p, per_y, cuts_y = shares(planes, rows_y, parts)
    at_once = 2 if per_p % 2 == 0 else 1
    steps = chunk // 2
    count_out = group // 2 * parts
    flat_sides, flat_pot = ([value for side in both for value in side] for both in (sides, sides_pot))
    cuts, cuts_pot = len(sides[0]), len(sides_pot[0])
    width, width_pot = edge // cuts, edge // cuts_pot
    width_e, centre, sigma_one, sigma_two, sigma_three = filter_terms()
    diagonal = 3.0 * stencil_coef[0] * kinetic - centre
    fold = (coef_scale * width_e) ** 2 / 4.0
    tile_rows = planes * rows_y
    xy, zz, swap = xy_matrix(planes, rows_y), z_matrix(rows_z), swap_matrix()
    count_0, count_1, count_2 = slab + 6 * reach, slab + 4 * reach, slab + 2 * reach

    def kernel(info_ref, *refs):
        side_refs, refs = refs[: 2 * cuts], refs[2 * cuts :]
        side_pot_refs, refs = refs[: 2 * cuts_pot], refs[2 * cuts_pot :]
        piece_refs, pot_refs = refs[:group], refs[group : 2 * group]
        xy_ref, zz_ref, swap_ref = refs[2 * group : 3 + 2 * group]
        outs = refs[3 + 2 * group : 3 + 2 * group + count_out]
        field, first, second, energy, result = refs[3 + 2 * group + count_out :]
        i = pl.program_id(0)
        me = info_ref[0]
        at_left, at_right = info_ref[1] == 1, info_ref[2] == 1

        @pl.when(i == 0)
        def _():
            def store(start, source):
                total = source[0].astype(F32)
                energy[pl.ds(start, source.shape[1])] = coef_scale * (total + diagonal)

            for odd in range(2):

                @pl.when(info_ref[5] == odd)
                def _():
                    halves = side_pot_refs[:cuts_pot], side_pot_refs[cuts_pot:]
                    for side, base, low, high in (
                        (halves[1 - odd], -reach, 0, 2 * reach),
                        (halves[odd], slab + 2 * reach, slab + 2 * reach, count_1),
                    ):
                        for k, ref in enumerate(side):
                            start = base + k * width_pot
                            begin, end = max(start, low), min(start + width_pot, high)
                            if begin < end:
                                store(begin, ref.at[:, begin - start : end - start])

            for r in range(group):
                store(2 * reach + planes * (me ^ r), pot_refs[r])

        for b in range(2):
            lanes = slice(b * rows_z, (b + 1) * rows_z)
            for k in range(2):
                start = (1 - (info_ref[5] ^ k)) * (edge + slab)
                for n in range(cuts):
                    where = pl.ds(start + n * width, width)
                    field[where, :, lanes] = side_refs[k * cuts + n][b]
            for r in range(group):
                field[pl.ds(edge + planes * (me ^ r), planes), :, lanes] = piece_refs[r][b]

        def apply(source, start, energy_start):
            rows = source[pl.ds(start, planes + 2 * reach)].reshape(-1, 2 * rows_z)
            middle = source[pl.ds(start + reach, planes)].reshape(tile_rows, 2 * rows_z)
            total = jnp.dot(xy_ref[...], rows, preferred_element_type=F32)
            total += jnp.dot(middle, zz_ref[...], preferred_element_type=F32)
            factor = energy[pl.ds(energy_start, planes)].reshape(tile_rows, rows_z)
            factor = jnp.concatenate([factor, factor], axis=1)
            return total + factor * middle.astype(F32)

        def block(value):
            return value.astype(BF16).reshape(planes, rows_y, 2 * rows_z)

        def previous(source, start):
            return source[pl.ds(start, planes)].reshape(tile_rows, 2 * rows_z).astype(F32)

        for t in range(count_1 // planes):
            at = t * planes
            first[at : at + planes] = block(apply(field, at, at))

        @pl.when(at_left)
        def _():
            first[: 2 * reach] = jnp.zeros((2 * reach, rows_y, 2 * rows_z), BF16)

        @pl.when(at_right)
        def _():
            first[count_1 - 2 * reach :] = jnp.zeros((2 * reach, rows_y, 2 * rows_z), BF16)

        for t in range(count_2 // planes):
            at = t * planes
            value = apply(first, at, at + reach)
            value -= 2.0 * fold * previous(field, at + 2 * reach)
            second[at : at + planes] = block(value)

        @pl.when(at_left)
        def _():
            second[:reach] = jnp.zeros((reach, rows_y, 2 * rows_z), BF16)

        @pl.when(at_right)
        def _():
            second[count_2 - reach :] = jnp.zeros((reach, rows_y, 2 * rows_z), BF16)

        for t in range(group):
            at = t * planes
            value = apply(second, at, at + 2 * reach)
            value -= fold * previous(first, at + 2 * reach)
            value = block(value)
            for b in range(2):
                part = value[:, :, b * rows_z : (b + 1) * rows_z]
                result[at : at + planes, 2 * i + b] = part

        @pl.when(i == steps - 1)
        def _():
            for t in range(parts):
                part = lax.rem(info_ref[3] + t, parts)
                begin = lax.rem(part, cuts_y) * (per_y * chunk)
                begin = pl.multiple_of(begin, per_y * chunk)
                for r in range(group):
                    start = planes * (me ^ r) + part // cuts_y * per_p
                    for p in range(0, per_p, at_once):
                        pair = [
                            result[start + p + k].reshape(chunk * rows_y, rows_z)
                            for k in range(at_once)
                        ]
                        moved = jnp.dot(
                            swap_ref[pl.ds(begin, per_y * chunk), :],
                            jnp.concatenate(pair, axis=1),
                            preferred_element_type=F32,
                        ).astype(BF16)
                        for k in range(at_once):
                            value = moved[:, k * rows_z : (k + 1) * rows_z]
                            out = outs[r // 2 * parts + t]
                            out[r % 2, :, p + k] = value.reshape(per_y, chunk, rows_z)

    def block_spec(count, index, bands=2):
        return pl.BlockSpec((bands, count, rows_y, rows_z), index)

    def whole_spec(shape):
        return pl.BlockSpec(shape, lambda i, info_ref: (0,) * len(shape))

    moving = lambda i, info_ref: (i, 0, 0, 0)
    fixed = lambda i, info_ref: (chunk, 0, 0, 0)
    shape = jax.ShapeDtypeStruct((2, per_y, per_p, chunk, rows_z), BF16)
    flat = pl.pallas_call(
        kernel,
        grid_spec=pltpu.PrefetchScalarGridSpec(
            num_scalar_prefetch=1,
            grid=(steps,),
            in_specs=[block_spec(width, moving)] * (2 * cuts)
            + [block_spec(width_pot, fixed, 1)] * (2 * cuts_pot)
            + [block_spec(planes, moving)] * group
            + [block_spec(planes, fixed, 1)] * group
            + [whole_spec(xy.shape), whole_spec(zz.shape), whole_spec(swap.shape)],
            out_specs=[whole_spec(shape.shape)] * count_out,
            scratch_shapes=[
                pltpu.VMEM((count_0, rows_y, 2 * rows_z), BF16),
                pltpu.VMEM((count_1, rows_y, 2 * rows_z), BF16),
                pltpu.VMEM((count_2, rows_y, 2 * rows_z), BF16),
                pltpu.VMEM((count_1, rows_y, rows_z), F32),
                pltpu.VMEM((slab, chunk, rows_y, rows_z), BF16),
            ],
        ),
        out_shape=[shape] * count_out,
        name="chebyshev",
        **params(18),
    )(info, *flat_sides, *flat_pot, *pieces, *pieces_pot, xy, zz, swap)
    return [flat[a * parts : (a + 1) * parts] for a in range(group // 2)]


def shares(planes, rows_y, parts):
    cuts_p = math.gcd(planes, parts)
    cuts_y = parts // cuts_p
    return planes // cuts_p, rows_y // cuts_y, cuts_y


def fill(info_ref, rows, piece, source, first_p, first_y, r, c, bands, group):
    own = bands // group
    start = source * bands + (info_ref[0] ^ r) * own + c * chunk
    where = pl.ds(pl.multiple_of(start, chunk), chunk)
    for p in range(piece.shape[1]):
        rows[first_p + p, pl.ds(first_y, piece.shape[0]), where, :] = piece[:, p]


def gram(info, pieces, packs, bands, bands_all):
    group = 1 + max(r for r, t, c in pieces)
    _, per_y, per_p, _, rows_z = next(iter(pieces.values()))[0].shape
    at_once = 2 if per_p % 2 == 0 else 1
    steps = per_p // at_once
    half = bands_all // 2
    direct = half == bands
    own = bands // group
    ordered = sorted(pieces, key=lambda key: (key[1], key[0], key[2]))

    def in_order(info_ref, value, by_rows):
        axis = 0 if by_rows else 1
        count = value.shape[axis]
        place = lax.broadcasted_iota(jnp.int32, value.shape, axis)
        bit = 1
        while bit < group:
            step = bit * own
            if by_rows:
                blocks = [value[k : k + step] for k in range(0, count, step)]
                blocks = [blocks[k ^ 1] for k in range(len(blocks))]
                moved = jnp.concatenate(blocks, axis=0)
            else:
                low = pltpu.roll(value, count - step, 1)
                high = pltpu.roll(value, step, 1)
                moved = jnp.where(place & step == 0, low, high)
            value = jnp.where((info_ref[0] & bit) != 0, moved, value)
            bit *= 2
        return value

    def direct_blocks(info_ref, out):
        for odd in range(2):

            @pl.when(info_ref[3] == odd)
            def _():
                below = out[half:, :half] if odd == 0 else out[:half, half:bands_all]
                blocks = [out[:half, :half], below, out[half:, half:bands_all]]
                for k, block in enumerate(blocks if odd == 0 else blocks[::-1]):
                    value = in_order(info_ref, in_order(info_ref, block, True), False)
                    out[:half, k * half : (k + 1) * half] = value

    def direct_kernel(info_ref, *refs):
        mine, other, packed, _, out = refs[len(pieces) :]
        by_key = dict(zip(pieces, refs))
        i = pl.program_id(0)
        for k, (r, c) in enumerate(packs):
            packed[k] = by_key[(r, 0, c)][0]
        block = jnp.concatenate(
            [
                jnp.concatenate([by_key[key][0, y, p] for key in ordered], axis=0)
                for p in range(at_once)
                for y in range(per_y)
            ],
            axis=1,
        )
        total = lax.dot_general(
            block, block, (((1,), (1,)), ((), ())), preferred_element_type=F32
        )

        @pl.when(i == 0)
        def _():
            out[:, :bands_all] = total

        @pl.when(i > 0)
        def _():
            out[:, :bands_all] += total

        @pl.when(i == steps - 1)
        def _():
            direct_blocks(info_ref, out)
            for ref, core in ((mine, info_ref[0] & 1), (other, 1 - (info_ref[0] & 1))):
                where = pl.ds(pl.multiple_of(core * (half // 2), half // 2), half // 2)
                ref[...] = out[where, : 3 * half]

    def kernel(info_ref, *refs):
        mine, other, packed, rows, out = refs[len(pieces) :]
        parts = info_ref[4]
        i = pl.program_id(0)
        for (r, t, c), piece in zip(pieces, refs):
            source = lax.rem(info_ref[3] + parts - t, parts)
            fill(info_ref, rows, piece.at[0], source, 0, 0, r, c, bands, group)
            if t == 0 and (r, c) in packs:
                packed[packs.index((r, c))] = piece[0]
        block = jnp.concatenate(
            [rows[p, y] for p in range(at_once) for y in range(per_y)], axis=1
        )
        total = lax.dot_general(
            block, block, (((1,), (1,)), ((), ())), preferred_element_type=F32
        )

        total = [total[:half, :half], total[half:, :half], total[half:, half:]]
        total = jnp.concatenate(total, axis=1)

        @pl.when(i == 0)
        def _():
            out[...] = total

        @pl.when(i > 0)
        def _():
            out[...] += total

        @pl.when(i == steps - 1)
        def _():
            for ref, core in ((mine, info_ref[0] & 1), (other, 1 - (info_ref[0] & 1))):
                ref[...] = out[pl.ds(pl.multiple_of(core * (half // 2), half // 2), half // 2)]

    def spec(index):
        return pl.BlockSpec(
            (1, per_y, at_once, chunk, rows_z), lambda i, info_ref: (index, 0, i, 0, 0)
        )

    return pl.pallas_call(
        direct_kernel if direct else kernel,
        grid_spec=pltpu.PrefetchScalarGridSpec(
            num_scalar_prefetch=1,
            grid=(steps,),
            in_specs=[spec(index) for _, index in pieces.values()],
            out_specs=[pl.BlockSpec((half // 2, 3 * half), lambda i, info_ref: (0, 0))] * 2
            + [
                pl.BlockSpec(
                    (len(packs), per_y, at_once, chunk, rows_z),
                    lambda i, info_ref: (0, 0, i, 0, 0),
                ),
            ],
            scratch_shapes=[
                pltpu.VMEM((1 if direct else at_once, per_y, bands_all, rows_z), BF16),
                pltpu.VMEM((bands_all if direct else half, 3 * half), F32),
            ],
        ),
        out_shape=[jax.ShapeDtypeStruct((half // 2, 3 * half), F32)] * 2
        + [jax.ShapeDtypeStruct((len(packs), per_y, per_p, chunk, rows_z), BF16)],
        name="gram",
        **params(16),
    )(info, *[value for value, _ in pieces.values()])


def inverse_factor(info, mine, other, cells):
    half = 2 * mine.shape[0]
    sign = filter_sign()
    count = 2 * half

    def exact(a, b, transposed):
        dims = (((1,), (1 if transposed else 0,)), ((), ()))
        return lax.dot_general(
            a, b, dims, precision=lax.Precision.HIGHEST, preferred_element_type=F32
        )

    def eliminate(block):
        groups = half // 8
        row = lax.broadcasted_iota(jnp.int32, (8, half), 0)
        column = lax.broadcasted_iota(jnp.int32, (8, half), 1)
        left = [block[8 * g : 8 * g + 8] for g in range(groups)]
        right = [jnp.where(column == row + 8 * g, 1.0, 0.0).astype(F32) for g in range(groups)]
        for at in range(groups):
            later = range(at, groups)
            spread = [
                [
                    jnp.broadcast_to(left[g][:, 8 * at + k : 8 * at + k + 1], (8, half))
                    for g in later
                ]
                for k in range(8)
            ]
            factors, rows_left, rows_right = [], [], []
            for k in range(8):
                pivot = jnp.broadcast_to(spread[k][0][k : k + 1], (8, half))
                scale = lax.rsqrt(pivot)
                scale = scale * (1.5 - 0.5 * pivot * scale * scale)
                factor = [value * scale for value in spread[k]]
                for m in range(k + 1, 8):
                    other = jnp.broadcast_to(factor[0][m : m + 1], (8, half))
                    spread[m] = [value - f * other for value, f in zip(spread[m], factor)]
                row_left = jnp.broadcast_to(left[at][k : k + 1], (8, half)) * scale
                row_right = jnp.broadcast_to(right[at][k : k + 1], (8, half)) * scale
                inside = jnp.where(row > k, factor[0], 0.0)
                left[at] = jnp.where(row == k, row_left, left[at] - inside * row_left)
                right[at] = jnp.where(row == k, row_right, right[at] - inside * row_right)
                factors.append(factor)
                rows_left.append(row_left)
                rows_right.append(row_right)
            for g in range(at + 1, groups):
                for k in range(8):
                    left[g] = left[g] - factors[k][g - at] * rows_left[k]
                    right[g] = right[g] - factors[k][g - at] * rows_right[k]
        return jnp.concatenate(right, axis=0)

    def kernel(info_ref, mine_ref, other_ref, out, blocks):
        for ref, core in ((mine_ref, info_ref[0] & 1), (other_ref, 1 - (info_ref[0] & 1))):
            where = pl.ds(pl.multiple_of(core * (half // 2), half // 2), half // 2)
            blocks[where] = ref[...] * (1.0 / cells)
        top = eliminate(blocks[:, :half])
        below = exact(blocks[:, half:count], top, True)
        rest = blocks[:, count:] - exact(below, below, True)
        bottom = eliminate(rest)
        out[:half, :half] = (sign * top).astype(BF16)
        out[:half, half:] = jnp.zeros((half, half), BF16)
        out[half:, :half] = (-sign * exact(bottom, exact(below, top, False), False)).astype(BF16)
        out[half:, half:] = (sign * bottom).astype(BF16)

    return pl.pallas_call(
        kernel,
        grid_spec=pltpu.PrefetchScalarGridSpec(
            num_scalar_prefetch=1,
            grid=(1,),
            in_specs=[pl.BlockSpec(mine.shape, lambda i, info_ref: (0, 0))] * 2,
            out_specs=pl.BlockSpec((count, count), lambda i, info_ref: (0, 0)),
            scratch_shapes=[pltpu.VMEM((half, 3 * half), F32)],
        ),
        out_shape=jax.ShapeDtypeStruct((count, count), BF16),
        name="inverse_factor",
        **params(8),
    )(info, mine, other)


def rotate(info, rotation, pieces, bands, bands_all, planes, rows_y, only, before):
    group = 1 + max(r for r, t, u, c in pieces)
    _, per_y, per_p, _, rows_z = next(iter(pieces.values()))[0].shape
    swap = swap_matrix()
    cuts_y = rows_y // per_y
    at_once = 2 if only is not None and per_p % 2 == 0 else 1 if only is not None else per_p
    steps = per_p // at_once
    span = at_once if only is not None else planes
    given = [] if before is None else [before]
    arrays = {id(value): value for value, _ in pieces.values()}
    slots = {key: k for k, key in enumerate(arrays)}

    def start_of(info_ref, r, t, c):
        source = lax.rem(info_ref[3] + info_ref[4] - t, info_ref[4])
        return source * bands + (info_ref[0] ^ r) * (bands // group) + c * chunk

    def kernel(info_ref, *refs):
        rotation_ref, swap_ref = refs[len(arrays) :][:2]
        out, rows, mixed, turned = refs[-4:]
        me, parts = info_ref[3], info_ref[4]
        if only is None:
            for (r, t, u, c), (value, index) in pieces.items():
                source = lax.rem(me + parts - t, parts)
                part = lax.rem(me + u, parts)
                first_p, first_y = part // cuts_y * per_p, lax.rem(part, cuts_y) * per_y
                piece = refs[slots[id(value)]].at[index]
                fill(info_ref, rows, piece, source, first_p, first_y, r, c, bands, group)
            turned[...] = rotation_ref[...]
        else:

            @pl.when(pl.program_id(0) == 0)
            def _():
                place = lax.broadcasted_iota(jnp.int32, (bands_all, bands_all), 1)
                wanted = lax.broadcasted_iota(jnp.int32, (bands_all, bands_all), 0)
                from_row = place & (chunk - 1)
                for k, (r, t, _, c) in enumerate(pieces):
                    start = jnp.where(place // chunk == k, start_of(info_ref, r, t, c), 0)
                    from_row = from_row + start
                order = jnp.where(wanted == from_row, 1.0, 0.0).astype(BF16)
                value = jnp.dot(rotation_ref[...], order, preferred_element_type=F32)
                turned[...] = value.astype(BF16)

        def row(p, y):
            if only is None:
                return rows[p, y]
            held = [refs[slots[id(value)]][index, y, p] for value, index in pieces.values()]
            return jnp.concatenate(held, axis=0)

        def plane(p):
            for y in range(0, rows_y, 2):
                pair = jnp.concatenate([row(p, y), row(p, y + 1)], axis=1)
                value = jnp.dot(turned[...], pair, preferred_element_type=F32)
                value = value.astype(BF16)
                for k in range(bands // 16):
                    for b in range(2):
                        mixed[k, y + b] = value[
                            16 * k : 16 * k + 16, b * rows_z : (b + 1) * rows_z
                        ]
            for k in range(0, bands // 16, 2):
                pair = [mixed[k + b].reshape(16 * rows_y, rows_z) for b in range(2)]
                moved = jnp.dot(
                    swap_ref[...], jnp.concatenate(pair, axis=1), preferred_element_type=F32
                ).astype(BF16)
                for b in range(2):
                    part = moved[:, b * rows_z : (b + 1) * rows_z].reshape(16, rows_y, rows_z)
                    out[16 * (k + b) : 16 * (k + b) + 16, p] = part

        if only is not None:
            for p in range(span):
                plane(p)
        else:
            pl.loop(0, span)(plane)

    def spec(value):
        return pl.BlockSpec(
            (value.shape[0], per_y, at_once, chunk, rows_z), lambda i, info_ref: (0, 0, i, 0, 0)
        )

    def out_index(i, info_ref):
        if only is None:
            return (0, 0, 0, 0)
        return (0, lax.rem(info_ref[3] + only, info_ref[4]) * steps + i, 0, 0)

    return pl.pallas_call(
        kernel,
        grid_spec=pltpu.PrefetchScalarGridSpec(
            num_scalar_prefetch=1,
            grid=(steps,),
            in_specs=[spec(value) for value in arrays.values()]
            + [
                pl.BlockSpec((bands, bands_all), lambda i, info_ref: (info_ref[3], 0)),
                pl.BlockSpec(swap.shape, lambda i, info_ref: (0, 0)),
            ]
            + [pl.BlockSpec(memory_space=pl.ANY)] * len(given),
            out_specs=pl.BlockSpec((bands, span, rows_y, rows_z), out_index),
            scratch_shapes=[
                pltpu.VMEM((span if only is None else 1, rows_y, bands_all, rows_z), BF16),
                pltpu.VMEM((bands // 16, rows_y, 16, rows_z), BF16),
                pltpu.VMEM((bands, bands_all), BF16),
            ],
        ),
        out_shape=jax.ShapeDtypeStruct((bands, planes, rows_y, rows_z), BF16),
        input_output_aliases={3 + len(arrays): 0} if given else {},
        name="rotate",
        **params(60 if only is None else 14),
    )(info, *arrays.values(), rotation, swap, *given)


def pairwise_sum(value, axis, count, low, high):
    bit = max(low, 1)
    while bit < high:
        value = value + lax.ppermute(value, axis, [(i, i ^ bit) for i in range(count)])
        bit *= 2
    return value


def body(orbital_block, block_scale, potential):
    bands, planes, rows_y, rows_z = orbital_block.shape
    parts, slabs = lax.axis_size("band"), lax.axis_size("domain")
    bands_all = bands * parts
    group = 4 if bands // 4 >= chunk else 2
    chunks = bands // group // chunk
    where, band = lax.axis_index("domain"), lax.axis_index("band")
    info = jnp.stack(
        [
            lax.rem(where, group),
            (where < group).astype(jnp.int32),
            (where >= slabs - group).astype(jnp.int32),
            band,
            jnp.int32(parts),
            lax.rem(where // group, 2),
        ]
    ).astype(jnp.int32)

    def send(value, r, t):
        if r == 0 and t == 0:
            return value
        pairs = [
            (q * slabs + i, (q + t) % parts * slabs + (i ^ r))
            for q in range(parts)
            for i in range(slabs)
        ]
        return lax.ppermute(value, ("band", "domain"), pairs)

    scale = jnp.broadcast_to(block_scale[:, :, None], (bands, planes, rows_z))
    far_first = sorted(range(group), reverse=True)
    arrived = []
    for c in range(chunks):
        pieces = prepare(info, orbital_block, scale, potential, c, group, c == 0)
        sent = {r: send(pieces[r], r, 0) for r in far_first}
        arrived.append([sent[r] for r in range(group)])
    def after(value, *others):
        return lax.optimization_barrier((value, *others))[0] if others else value

    def swapped(value, odd):
        lower = [i for i in range(slabs - group) if i // group % 2 == odd]
        pairs = [(i, i + group) for i in lower] + [(i + group, i) for i in lower]
        return lax.ppermute(value, "domain", pairs)

    sides = []
    pieces, own, moved, crossed = {}, {}, {}, {}
    ready = []
    for c in range(chunks):
        ends = edges(after(info, *ready), arrived[c], 1)
        sides.append([[swapped(end, odd) for end in ends[odd]] for odd in range(2)])
        filtered = chebyshev(info, sides[c], arrived[c], sides[0], arrived[0], parts)
        ready = [filtered[0][0]]
        for a in reversed(range(group // 2)):
            for t in reversed(range(parts)):
                value = filtered[a][t]
                own[(a, t, c)] = value
                moved[(a, t, c)] = send(value, 2 * a, t)
    known = {}
    early = parts == 2 and chunks > 1 and group == 4
    if early:
        first = lax.ppermute(own[(0, 0, 0)][0], "band", [(0, 1), (1, 0)])
        known[(0, 1, 1, 0)] = (first[None], 0)
    for c in range(chunks):
        keys = [(a, t) for t in range(parts) for a in range(group // 2)]
        wait = [first] if early and c == 0 else []
        there = {key: after(moved[(*key, c)], *ready, *wait) for key in keys}
        crossed[c] = send(jnp.stack([there[key][1] for key in keys]), 1, 0)
        for k, (a, t) in enumerate(keys):
            pieces[(2 * a, t, c)] = (there[(a, t)], 0)
            pieces[(2 * a + 1, t, c)] = (crossed[c], k)

    known |= {(r, t, 0, c): value for (r, t, c), value in pieces.items()}
    late = {}
    if early:
        came = [moved[(a, 1, chunks - 1)] for a in range(2)]
        chosen = [(r, c, *pieces[(r, 0, c)]) for r, c in ((0, chunks - 1), (1, 0))]
        sent = jnp.stack([value[index] for _, _, value, index in chosen])
        sent = lax.ppermute(after(sent, *came), "band", [(0, 1), (1, 0)])
        for k, (r, c, _, _) in enumerate(chosen):
            known[(r, 1, 1, c)] = (sent, k)
    packs = [
        (r, c)
        for c in range(chunks)
        for r in range(group)
        if parts > 2 or (r, 1, 1, c) not in known
    ]
    mine, other, buffer = gram(info, pieces, packs, bands, bands_all)
    mine = mine + send(other, 1, 0)
    mine = pairwise_sum(mine, "domain", slabs, 2, group)
    for key, value in own.items():
        if key[1] > 0:
            late[key] = send(after(value, mine), 2 * key[0], 0)
    if early:
        mine = after(mine, sent)
    mine = pairwise_sum(mine, "band", parts, 0, parts)

    def forward(buffer, t, packs):
        for s in range(1, parts):
            if t != s:
                pairs = [(q, (q + s) % parts) for q in range(parts)]
                sent = lax.ppermute(buffer, "band", pairs)
                for k, (r, c) in enumerate(packs):
                    known[(r, s, (t - s) % parts, c)] = (sent, k)

    forward(after(buffer, mine), 0, packs)
    mine = pairwise_sum(mine, "domain", slabs, group, slabs)
    rotation = inverse_factor(info, mine, send(mine, 1, 0), planes * rows_y * rows_z * slabs)
    for t in range(1, parts):
        keys = [(a, c) for c in range(chunks) for a in range(group // 2)]
        far = send(jnp.stack([after(late[(a, t, c)], rotation)[1] for a, c in keys]), 1, 0)
        for k, (a, c) in enumerate(keys):
            known[(2 * a, 0, t, c)] = (late[(a, t, c)], 0)
            known[(2 * a + 1, 0, t, c)] = (far, k)
        if parts > 2:
            chosen = [known[(r, 0, t, c)] for r, c in packs]
            forward(jnp.stack([value[index] for value, index in chosen]), t, packs)
    out = None
    for only in range(parts) if parts == 2 and planes % 2 == 0 else [None]:
        chosen = {key: value for key, value in known.items() if only in (None, key[2])}
        out = rotate(info, rotation, chosen, bands, bands_all, planes, rows_y, only, out)
    return out


def solution(mesh):
    in_specs = (P("band", "domain", None, None), P("band", "domain"), P("domain", None, None))
    out_specs = P("band", "domain", None, None)
    return jax.shard_map(body, mesh=mesh, in_specs=in_specs, out_specs=out_specs, check_vma=False)
```
